32 devices in a mesh: row: 4 (over y, x), seq: 4 (over z), tp: 2 (over core).
Axes of the slice: x: 2, y: 2, z: 4, core: 2. Of those that a mesh axis runs over, the one named last changes fastest.
Arguments:
- block_input: bfloat16 [4, 1024, 2048], P('row', 'seq'), may hold values from -6 to 6
- grad_out: bfloat16 [4, 1024, 2048], P('row', 'seq'), may hold values from -6 to 6
- doc_lengths: int32 [4, 8], P('row'), may hold values from 1 to 896, as said below
- attn_gain: float32 [2048], replicated, may hold values from 0.5 to 1.5
- mlp_gain: float32 [2048], replicated, may hold values from 0.5 to 1.5
- out_gain: float32 [128], replicated, may hold values from 0.5 to 1.5
- conv_weight: float32 [3, 4, 2048], P(None, None, 'tp'), may hold values from -3 to 3
- qkv_weight: bfloat16 [3, 2048, 2048], P(None, ('row', 'seq'), 'tp'), may hold values from -0.125 to 0.125
- beta_weight: bfloat16 [2048, 16], P(('row', 'seq'), 'tp'), may hold values from -0.125 to 0.125
- o_weight: bfloat16 [2048, 2048], P('tp', ('row', 'seq')), may hold values from -0.125 to 0.125
- gate_up_weight: bfloat16 [2, 2048, 5632], P(None, ('row', 'seq'), 'tp'), may hold values from -0.125 to 0.125
- down_weight: bfloat16 [5632, 2048], P('tp', ('row', 'seq')), may hold values from -0.078125 to 0.078125
Outputs:
- block_output: bfloat16 [4, 1024, 2048], P('row', 'seq')
- input_grad: bfloat16 [4, 1024, 2048], P('row', 'seq')
- attn_gain_grad: float32 [2048], replicated
- mlp_gain_grad: float32 [2048], replicated
- out_gain_grad: float32 [128], replicated
- conv_grad: float32 [3, 4, 2048], replicated
- qkv_grad: float32 [3, 2048, 2048], P(None, ('row', 'seq'), 'tp')
- beta_grad: float32 [2048, 16], P(('row', 'seq'), 'tp')
- o_grad: float32 [2048, 2048], P('tp', ('row', 'seq'))
- gate_up_grad: float32 [2, 2048, 5632], P(None, ('row', 'seq'), 'tp')
- down_grad: float32 [5632, 2048], P('tp', ('row', 'seq'))
The draws below stay inside these ranges and needn't reach their ends.
Inputs may be any that keep to these rules, and one draw needn't show every extreme that they name: `doc_lengths`: the 8 documents of each row lie one after another from position 0 and sum to less than 1024; the positions after them are padding; one document of each row has exactly 896 positions.
All inputs are finite; a program needn't handle non-finite values.
Results may differ from the reference program's by a relative error of at most 0.023.
Values may be sent and summed in bfloat16 or wider, within the bound.
A program may use at most 256 MiB of HBM per device.

```python
import jax
import jax.numpy as jnp
from jax import lax

D = 2048
H = 16
DK = 128
FF = 5632
KW = 4
GROUP = 64
DOCS = 8
TOK_DEV = 256
ROWS = 4
SEQ_LEN = 1024


def draw_doc_lengths(key, part):
    key = jax.random.fold_in(key, 11)
    limit = max(TOK_DEV // 16, 2)
    key_one, key_two, key_slot = jax.random.split(key, 3)
    first_part = jax.random.randint(key_one, (ROWS, DOCS), 0, limit)
    second_part = jax.random.randint(key_two, (ROWS, DOCS), 0, limit)
    short_docs = 1 + first_part * second_part // (limit - 1)
    long_slot = jax.random.randint(key_slot, (ROWS, 1), 0, DOCS)
    slots = jnp.arange(DOCS, dtype=jnp.int32)[None, :]
    is_long = slots == long_slot
    long_doc = jnp.full((ROWS, DOCS), SEQ_LEN - TOK_DEV // 2, jnp.int32)
    return jnp.where(is_long, long_doc, short_docs).astype(jnp.int32)


def shard_levels(key, extent, cuts, smallest, top_value):
    level, own = 1.0, jax.random.fold_in(key, 6)
    for axis_at, parts in cuts:
        steps = jnp.exp(jax.random.uniform(jax.random.fold_in(own, axis_at), (parts,), jnp.float32, smallest / len(cuts), top_value / len(cuts)))
        level = level * jnp.repeat(steps, extent[axis_at] // parts).reshape([-1 if axis == axis_at else 1 for axis in range(len(extent))])
    return level


def gaussian(rng, dims, width, most, cuts=(), held_as=jnp.bfloat16):
    values = jax.random.normal(rng, dims, jnp.float32) * width
    if len(cuts) > 0:
        values = shard_levels(rng, dims, cuts, -0.22, 0.18) * values
    return jnp.clip(values, min=-most, max=most).astype(held_as)


def setup_inputs(seed: int = 0) -> dict:
    streams_of = jax.random.split(jax.random.key(seed), 13)
    return {
        "block_input": gaussian(streams_of[0], (ROWS, SEQ_LEN, D), 1.0, 6.0, ((0, 4), (1, 4))),
        "grad_out": gaussian(streams_of[1], (ROWS, SEQ_LEN, D), 1.0, 6.0, ((0, 4), (1, 4))),
        "doc_lengths": draw_doc_lengths(jax.random.fold_in(streams_of[12], 71), 0),
        "attn_gain": jnp.clip(1.0 + 0.1 * jax.random.normal(streams_of[3], (D,), jnp.float32), 0.5, 1.5),
        "mlp_gain": jnp.clip(1.0 + 0.1 * jax.random.normal(streams_of[4], (D,), jnp.float32), 0.5, 1.5),
        "out_gain": jnp.clip(1.0 + 0.1 * jax.random.normal(streams_of[5], (DK,), jnp.float32), 0.5, 1.5),
        "conv_weight": gaussian(streams_of[6], (3, KW, D), 0.5, 3.0, ((2, 2),), jnp.float32),
        "qkv_weight": gaussian(streams_of[7], (3, D, D), D ** -0.5, 0.125, ((1, 16), (2, 2))),
        "beta_weight": gaussian(streams_of[8], (D, H), D ** -0.5, 0.125, ((0, 16), (1, 2))),
        "o_weight": gaussian(streams_of[9], (D, D), D ** -0.5, 0.125, ((0, 2), (1, 16))),
        "gate_up_weight": gaussian(streams_of[10], (2, D, FF), D ** -0.5, 0.125, ((1, 16), (2, 2))),
        "down_weight": gaussian(streams_of[11], (FF, D), FF ** -0.5, 0.078125, ((0, 2), (1, 16))),
    }


eps = 1e-06
mix_floor = 0.01
precise = lax.Precision.HIGHEST

@jax.custom_vjp
def low(v):
    return lax.optimization_barrier(v.astype(jnp.bfloat16)).astype(jnp.float32)

@jax.custom_vjp
def low_back(v):
    return v

def low_keep(v):
    return (low(v), None)

def low_pass(kept, grad):
    return (grad,)

def back_keep(v):
    return (v, None)

def back_low(kept, grad):
    return (low(grad),)
low.defvjp(low_keep, low_pass)
low_back.defvjp(back_keep, back_low)

def rms_norm(values, gain):
    return values * lax.rsqrt(lax.optimization_barrier(jnp.mean(values * values, axis=-1, keepdims=True)) + eps) * gain

def floored_norm(values, gain):
    return values * lax.rsqrt(jnp.maximum(lax.optimization_barrier(jnp.mean(values * values, axis=-1, keepdims=True)), mix_floor)) * gain

def unit_rows(values):
    total = lax.optimization_barrier(jnp.sum(values * values, axis=-1, keepdims=True))
    return values * lax.rsqrt(jnp.maximum(total, DK / 16.0))

def delta_rule(queries, key_rows, value_rows, rates, keep):
    blocks = SEQ_LEN // GROUP

    def arrange(array):
        shaped = array.reshape((ROWS, blocks, GROUP) + array.shape[2:])
        return jnp.moveaxis(shaped, (1, 2), (0, 1))

    def token_step(state_now, inputs):
        query_t, key_t, value_t, rate_t, keep_t = inputs
        state_now = state_now * keep_t[:, None, None, None]
        guess = jnp.einsum('rhkv,rhk->rhv', state_now, key_t, precision=precise)
        change = rate_t[..., None] * (value_t - guess)
        state_now = state_now + key_t[..., None] * change[..., None, :]
        return (state_now, jnp.einsum('rhkv,rhk->rhv', state_now, query_t, precision=precise))

    def block_step(state_now, inputs):
        return lax.scan(token_step, state_now, inputs)
    start = jnp.zeros((ROWS, H, DK, DK), jnp.float32)
    inputs = (arrange(queries), arrange(key_rows), arrange(value_rows), arrange(rates), arrange(keep))
    final, outputs = lax.scan(jax.checkpoint(block_step), start, inputs)
    return jnp.moveaxis(outputs, (0, 1), (1, 2)).reshape(ROWS, SEQ_LEN, H, DK)

def reference(block_input, grad_out, doc_lengths, attn_gain, mlp_gain, out_gain, conv_weight, qkv_weight, beta_weight, o_weight, gate_up_weight, down_weight):
    ends = jnp.cumsum(doc_lengths, axis=1).astype(jnp.int32)
    places = jnp.arange(SEQ_LEN, dtype=jnp.int32)
    doc_ids = lax.optimization_barrier(jnp.sum((places[None, :, None] >= ends[:, None, :]).astype(jnp.int32), axis=2)).astype(jnp.int32)
    padded_ids = jnp.concatenate([jnp.full((ROWS, KW - 1), -1, jnp.int32), doc_ids], axis=1)
    valid = (doc_ids < DOCS).astype(jnp.float32)
    keep = (padded_ids[:, KW - 2:KW - 2 + SEQ_LEN] == doc_ids).astype(jnp.float32)
    tap_masks = [(padded_ids[:, KW - 1 - tap:KW - 1 - tap + SEQ_LEN] == doc_ids).astype(jnp.float32) for tap in range(KW)]

    def forward(x_in, gain_one, gain_two, gain_out, conv_in, qkv_in, beta_in, o_in, gate_up_in, down_in):
        normed_one = low(rms_norm(x_in, gain_one))
        proj = low_back(low(jnp.einsum('rld,cde->crle', normed_one, qkv_in, precision=precise)))
        logit = low_back(jnp.einsum('rld,dh->rlh', normed_one, beta_in, precision=precise))
        extended = jnp.pad(proj, ((0, 0), (0, 0), (KW - 1, 0), (0, 0)))
        conv_out = jnp.zeros_like(proj)
        for tap in range(KW):
            window = extended[:, :, KW - 1 - tap:KW - 1 - tap + SEQ_LEN]
            conv_out = conv_out + conv_in[:, tap][:, None, None, :] * window * tap_masks[tap][None, :, :, None]
        activated = jax.nn.silu(conv_out)
        queries = unit_rows(activated[0].reshape(ROWS, SEQ_LEN, H, DK))
        key_rows = unit_rows(activated[1].reshape(ROWS, SEQ_LEN, H, DK))
        value_rows = activated[2].reshape(ROWS, SEQ_LEN, H, DK)
        rates = jax.nn.sigmoid(logit) * valid[..., None]
        mixed = delta_rule(queries, key_rows, value_rows, rates, keep) * valid[..., None, None]
        normed_mix = low(floored_norm(mixed, gain_out)).reshape(ROWS, SEQ_LEN, D)
        attn = low_back(jnp.einsum('rle,ed->rld', normed_mix, o_in, precision=precise))
        resid = x_in + attn
        normed_two = low(rms_norm(resid, gain_two))
        gate_up = low_back(jnp.einsum('rld,cdf->crlf', normed_two, gate_up_in, precision=precise))
        hidden = low(jax.nn.silu(gate_up[0]) * gate_up[1])
        return resid + jnp.einsum('rlf,fd->rld', hidden, down_in, precision=precise)
    primals = tuple((array.astype(jnp.float32) for array in (block_input, attn_gain, mlp_gain, out_gain, conv_weight, qkv_weight, beta_weight, o_weight, gate_up_weight, down_weight)))
    result, pullback = jax.vjp(forward, *primals)
    grads = pullback(grad_out.astype(jnp.float32))
    return (result.astype(jnp.bfloat16), grads[0].astype(jnp.bfloat16), grads[1], grads[2], grads[3], grads[4], grads[5], grads[6], grads[7], grads[8], grads[9])
```

```python
import jax
import jax.numpy as jnp
from jax import lax
from jax.sharding import PartitionSpec as P

DK = 128
KW = 4
GROUP = 64
DOCS = 8


eps = 1e-06
mix_floor = 0.01
precise = lax.Precision.HIGHEST


def from_behind(shard, axis, by):
    devices = lax.axis_size(axis)
    pairs = [(i, i + by) for i in range(devices) if 0 <= i + by < devices]
    return lax.ppermute(shard, axis, pairs)


def prefix(shard, axis, combine, identity, reverse):
    devices, place = (lax.axis_size(axis), lax.axis_index(axis))
    everything = jax.tree.map(
        lambda part, kind: lax.all_gather(part.astype(kind), axis),
        shard,
        (jnp.bfloat16, jnp.bfloat16),
    )
    start = jax.tree.map(
        lambda part, zero: jnp.broadcast_to(jnp.asarray(zero, part.dtype), part.shape),
        shard,
        identity,
    )

    def step(k, before):
        at = devices - 1 - k if reverse else k
        reached = at > place if reverse else at < place
        new = combine(
            before, jax.tree.map(lambda part, own: part[at].astype(own.dtype), everything, shard)
        )
        return jax.tree.map(lambda a, b: jnp.where(reached, a, b), new, before)

    return lax.fori_loop(0, devices, step, start)


def norm_scale(values):
    return lax.rsqrt(jnp.mean(values * values, axis=-1, keepdims=True) + eps)


def norm_back(values, scale, gain, grad):
    weighted = gain * grad
    return scale * weighted - values * scale**3 * jnp.mean(
        weighted * values, axis=-1, keepdims=True
    )


def batch_mul(left, right):
    return jnp.einsum("hij,hjk->hik", left, right, precision=precise)


def batch_mul_t(left, right):
    return jnp.einsum("hji,hjk->hik", left, right, precision=precise)


def compose(earlier, later):
    return (batch_mul(later[0], earlier[0]), batch_mul(later[0], earlier[1]) + later[1])


def over_heads(function, shared):
    return jax.vmap(jax.vmap(function), in_axes=shared)


def tp_total(term):
    return lax.psum(term.astype(jnp.bfloat16), "tp").astype(jnp.float32)


def group_parts(key_rows, value_rows, rates, same_doc, carry_mask):
    size = key_rows.shape[0]
    strict = jnp.tril(jnp.ones((size, size), jnp.float32), -1) * same_doc
    inner = jnp.dot(key_rows, key_rows.T, precision=precise)
    system = jnp.eye(size, dtype=jnp.float32) + rates[:, None] * inner * strict
    right_side = jnp.concatenate(
        [rates[:, None] * value_rows, (rates * carry_mask)[:, None] * key_rows], axis=1
    )
    solved = jax.scipy.linalg.solve_triangular(system, right_side, lower=True)
    base_rows = solved[:, : value_rows.shape[1]]
    wy_rows = solved[:, value_rows.shape[1] :]
    tail_keys = same_doc[size - 1][:, None] * key_rows
    identity_mat = jnp.eye(key_rows.shape[1], dtype=jnp.float32)
    transition = carry_mask[size - 1] * identity_mat - jnp.dot(
        tail_keys.T, wy_rows, precision=precise
    )
    contribution = jnp.dot(tail_keys.T, base_rows, precision=precise)
    return (transition, contribution, base_rows, wy_rows)


def group_output(queries, key_rows, same_doc, carry_mask, base_rows, wy_rows, state_in):
    size = key_rows.shape[0]
    lower = jnp.tril(jnp.ones((size, size), jnp.float32)) * same_doc
    written = base_rows - jnp.dot(wy_rows, state_in, precision=precise)
    scores = jnp.dot(queries, key_rows.T, precision=precise) * lower
    carried = carry_mask[:, None] * jnp.dot(queries, state_in, precision=precise)
    return carried + jnp.dot(scores, written, precision=precise)


def group_full(queries, key_rows, value_rows, rates, same_doc, carry_mask, state_in):
    transition, contribution, base_rows, wy_rows = group_parts(
        key_rows, value_rows, rates, same_doc, carry_mask
    )
    outputs = group_output(queries, key_rows, same_doc, carry_mask, base_rows, wy_rows, state_in)
    return (outputs, jnp.dot(transition, state_in, precision=precise) + contribution)


def state_pull(queries, key_rows, same_doc, carry_mask, wy_rows, grad_rows):
    size = key_rows.shape[0]
    lower = jnp.tril(jnp.ones((size, size), jnp.float32)) * same_doc
    scores = jnp.dot(queries, key_rows.T, precision=precise) * lower
    pulled = jnp.dot(scores.T, grad_rows, precision=precise)
    direct = jnp.dot((carry_mask[:, None] * queries).T, grad_rows, precision=precise)
    return direct - jnp.dot(wy_rows.T, pulled, precision=precise)


def group_grads(
    queries, key_rows, value_rows, rates, same_doc, carry_mask, state_in, grad_rows, grad_end
):

    def group_local(query_in, key_in, value_in, rate_in):
        return group_full(query_in, key_in, value_in, rate_in, same_doc, carry_mask, state_in)

    outputs, pullback = jax.vjp(group_local, queries, key_rows, value_rows, rates)
    return pullback((grad_rows, grad_end))


def local_pieces(
    block_input,
    grad_out,
    doc_lengths,
    attn_gain,
    mlp_gain,
    out_gain,
    conv_weight,
    qkv_weight,
    beta_weight,
    o_weight,
    gate_up_weight,
    down_weight,
):
    tok_rows = block_input.shape[1]
    model_width = block_input.shape[2]
    blocks = tok_rows // GROUP
    unit_floor = DK / 16.0
    x_rows = block_input[0].astype(jnp.float32)
    grad_rows_out = grad_out[0]
    qkv_full, beta_full, o_full, gate_up_full, down_full = (
        lax.all_gather(qkv_weight, ("row", "seq"), axis=1, tiled=True),
        lax.all_gather(beta_weight, ("row", "seq"), axis=0, tiled=True),
        lax.all_gather(o_weight, ("row", "seq"), axis=1, tiled=True),
        lax.all_gather(gate_up_weight, ("row", "seq"), axis=1, tiled=True),
        lax.all_gather(down_weight, ("row", "seq"), axis=1, tiled=True),
    )
    local_width = qkv_full.shape[2]
    head_count = local_width // DK
    lead_mask = (lax.axis_index("tp") == 0).astype(jnp.float32)
    ends = jnp.cumsum(doc_lengths[0])
    places = (
        lax.axis_index("seq") * tok_rows + jnp.arange(tok_rows + KW - 1, dtype=jnp.int32) - (KW - 1)
    )
    doc_ids = jnp.sum((places[:, None] >= ends[None, :]).astype(jnp.int32), axis=1)
    doc_ids = jnp.where(places < 0, -1, doc_ids)
    own_docs = doc_ids[KW - 1 :]
    prior_docs = doc_ids[KW - 2 : KW - 2 + tok_rows]
    valid = (own_docs < DOCS).astype(jnp.float32)
    fresh = (own_docs != prior_docs).astype(jnp.int32)
    tap_masks = [
        (doc_ids[KW - 1 - tap : KW - 1 - tap + tok_rows] == own_docs).astype(jnp.float32)
        for tap in range(KW)
    ]
    own_blocks = own_docs.reshape(blocks, GROUP)
    same_doc = (own_blocks[:, :, None] == own_blocks[:, None, :]).astype(jnp.float32)
    carry_mask = (jnp.cumsum(fresh.reshape(blocks, GROUP), axis=1) == 0).astype(jnp.float32)

    def to_blocks(array):
        return array.reshape(blocks, GROUP, head_count, -1).transpose(2, 0, 1, 3)

    def from_blocks(array):
        return array.transpose(1, 2, 0, 3).reshape(tok_rows, head_count, -1)

    scale_one = norm_scale(x_rows)
    normed_one = (x_rows * scale_one * attn_gain).astype(jnp.bfloat16)
    proj_low = jnp.einsum(
        "td,cde->cte", normed_one, qkv_full, preferred_element_type=jnp.float32
    ).astype(jnp.bfloat16)
    logit = jnp.dot(normed_one, beta_full, preferred_element_type=jnp.float32)
    rim_rows = from_behind(proj_low[:, tok_rows - (KW - 1) :, :], "seq", 1)
    extended = jnp.concatenate([rim_rows, proj_low], axis=1).astype(jnp.float32)
    conv_out = jnp.zeros((3, tok_rows, local_width), jnp.float32)
    for tap in range(KW):
        window = extended[:, KW - 1 - tap : KW - 1 - tap + tok_rows]
        conv_out = (
            conv_out + conv_weight[:, tap][:, None, :] * window * tap_masks[tap][None, :, None]
        )
    conv_sig = jax.nn.sigmoid(conv_out)
    activated = conv_out * conv_sig
    query_raw = activated[0].reshape(tok_rows, head_count, DK)
    key_raw = activated[1].reshape(tok_rows, head_count, DK)
    query_sq = jnp.sum(query_raw * query_raw, axis=-1, keepdims=True)
    key_sq = jnp.sum(key_raw * key_raw, axis=-1, keepdims=True)
    query_scale = lax.rsqrt(jnp.maximum(query_sq, unit_floor))
    key_scale = lax.rsqrt(jnp.maximum(key_sq, unit_floor))
    query_live = (query_sq > unit_floor).astype(jnp.float32)
    key_live = (key_sq > unit_floor).astype(jnp.float32)
    query_blocks = to_blocks(query_raw * query_scale)
    key_blocks = to_blocks(key_raw * key_scale)
    value_blocks = to_blocks(activated[2].reshape(tok_rows, head_count, DK))
    rate_sig = jax.nn.sigmoid(logit)
    rate_blocks = (rate_sig * valid[:, None]).reshape(blocks, GROUP, head_count).transpose(2, 0, 1)
    transition, contribution, base_rows, wy_rows = over_heads(group_parts, (0, 0, 0, None, None))(
        key_blocks, value_blocks, rate_blocks, same_doc, carry_mask
    )
    identity_mat = jnp.broadcast_to(jnp.eye(DK, dtype=jnp.float32), (head_count, DK, DK))
    zero_state = jnp.zeros((head_count, DK, DK), jnp.float32)
    transition_steps = jnp.moveaxis(transition, 1, 0)

    def chain(running, pair):
        product, partial_state = running
        step_trans, step_contrib = pair
        advanced = (
            batch_mul(step_trans, product),
            batch_mul(step_trans, partial_state) + step_contrib,
        )
        return (advanced, (product, partial_state))

    (dev_trans, dev_state), (products, partials) = lax.scan(
        chain, (identity_mat, zero_state), (transition_steps, jnp.moveaxis(contribution, 1, 0))
    )
    incoming = prefix((dev_trans, dev_state), "seq", compose, (identity_mat, zero_state), False)[1]
    group_starts = partials + jnp.einsum("nhij,hjk->nhik", products, incoming, precision=precise)
    start_blocks = jnp.moveaxis(group_starts, 0, 1)
    mix_blocks = over_heads(group_output, (0, 0, None, None, 0, 0, 0))(
        query_blocks, key_blocks, same_doc, carry_mask, base_rows, wy_rows, start_blocks
    )
    mixed = from_blocks(mix_blocks) * valid[:, None, None]
    mix_sq = jnp.mean(mixed * mixed, axis=-1, keepdims=True)
    mix_scale = lax.rsqrt(jnp.maximum(mix_sq, mix_floor))
    mix_live = (mix_sq > mix_floor).astype(jnp.float32)
    normed_mix = (mixed * mix_scale * out_gain).astype(jnp.bfloat16).reshape(tok_rows, local_width)
    o_term = jnp.dot(normed_mix, o_full, preferred_element_type=jnp.float32)
    resid = x_rows + tp_total(o_term)
    scale_two = norm_scale(resid)
    normed_local = (resid * scale_two * mlp_gain).astype(jnp.bfloat16)
    gate_up = jnp.einsum(
        "td,cdf->ctf", normed_local, gate_up_full, preferred_element_type=jnp.float32
    )
    gate_sig = jax.nn.sigmoid(gate_up[0])
    gate_act = gate_up[0] * gate_sig
    hidden = (gate_act * gate_up[1]).astype(jnp.bfloat16)
    down_term = jnp.dot(hidden, down_full, preferred_element_type=jnp.float32)
    mlp_out = tp_total(down_term)
    result = (resid + mlp_out).astype(jnp.bfloat16)
    grad_hidden = jnp.einsum(
        "td,fd->tf", grad_rows_out, down_full, preferred_element_type=jnp.float32
    )
    grad_gate = grad_hidden * gate_up[1] * gate_sig * (1.0 + gate_up[0] * (1.0 - gate_sig))
    grad_up = grad_hidden * gate_act
    grad_gate_up = jnp.stack([grad_gate, grad_up]).astype(jnp.bfloat16)
    down_part = jnp.einsum("tf,td->fd", hidden, grad_rows_out, preferred_element_type=jnp.float32)
    gate_up_part = jnp.einsum(
        "td,ctf->cdf", normed_local, grad_gate_up, preferred_element_type=jnp.float32
    )
    two_term = jnp.einsum(
        "ctf,cdf->td", grad_gate_up, gate_up_full, preferred_element_type=jnp.float32
    )
    grad_two = tp_total(two_term)
    mlp_gain_part = jnp.sum(grad_two * resid * scale_two, axis=0)
    grad_resid = grad_rows_out.astype(jnp.float32) + norm_back(resid, scale_two, mlp_gain, grad_two)
    grad_attn_local = grad_resid.astype(jnp.bfloat16)
    o_part = jnp.einsum(
        "te,td->ed", normed_mix, grad_attn_local, preferred_element_type=jnp.float32
    )
    grad_normed = jnp.einsum(
        "td,ed->te", grad_attn_local, o_full, preferred_element_type=jnp.float32
    ).reshape(tok_rows, head_count, DK)
    out_gain_part = jnp.sum(grad_normed * mixed * mix_scale, axis=(0, 1))
    weighted_mix = out_gain * grad_normed
    grad_mixed = (
        mix_scale * weighted_mix
        - mixed * mix_scale**3 * mix_live * jnp.mean(weighted_mix * mixed, axis=-1, keepdims=True)
    ) * valid[:, None, None]
    grad_blocks = to_blocks(grad_mixed)
    pulls = over_heads(state_pull, (0, 0, None, None, 0, 0))(
        query_blocks, key_blocks, same_doc, carry_mask, wy_rows, grad_blocks
    )

    def back_chain(running, pair):
        grad_end, product = running
        step_trans, step_pull = pair
        advanced = (step_pull + batch_mul_t(step_trans, grad_end), batch_mul_t(step_trans, product))
        return (advanced, (grad_end, product))

    (dev_pull, dev_back), (grad_ends, back_products) = lax.scan(
        back_chain,
        (zero_state, identity_mat),
        (transition_steps, jnp.moveaxis(pulls, 1, 0)),
        reverse=True,
    )
    outgoing = prefix((dev_back, dev_pull), "seq", compose, (identity_mat, zero_state), True)[1]
    end_grads = grad_ends + jnp.einsum("nhij,hjk->nhik", back_products, outgoing, precision=precise)
    grad_query, grad_key, grad_value, grad_rate = over_heads(
        group_grads, (0, 0, 0, 0, None, None, 0, 0, 0)
    )(
        query_blocks,
        key_blocks,
        value_blocks,
        rate_blocks,
        same_doc,
        carry_mask,
        start_blocks,
        grad_blocks,
        jnp.moveaxis(end_grads, 0, 1),
    )
    grad_query = from_blocks(grad_query)
    grad_key = from_blocks(grad_key)
    grad_query_raw = query_scale * grad_query - query_raw * query_scale**3 * query_live * jnp.sum(
        query_raw * grad_query, axis=-1, keepdims=True
    )
    grad_key_raw = key_scale * grad_key - key_raw * key_scale**3 * key_live * jnp.sum(
        key_raw * grad_key, axis=-1, keepdims=True
    )
    grad_activated = jnp.stack(
        [
            grad_query_raw.reshape(tok_rows, local_width),
            grad_key_raw.reshape(tok_rows, local_width),
            from_blocks(grad_value).reshape(tok_rows, local_width),
        ]
    )
    grad_conv = grad_activated * conv_sig * (1.0 + conv_out * (1.0 - conv_sig))
    grad_extended = jnp.zeros((3, tok_rows + KW - 1, local_width), jnp.float32)
    tap_grads = []
    for tap in range(KW):
        masked = grad_conv * tap_masks[tap][None, :, None]
        window = extended[:, KW - 1 - tap : KW - 1 - tap + tok_rows]
        tap_grads.append(jnp.sum(masked * window, axis=1))
        grad_extended = grad_extended + jnp.pad(
            conv_weight[:, tap][:, None, :] * masked, ((0, 0), (KW - 1 - tap, tap), (0, 0))
        )
    conv_part = jnp.stack(tap_grads, axis=1)
    rim_back = from_behind(grad_extended[:, : KW - 1], "seq", -1)
    grad_proj = jnp.concatenate(
        [grad_extended[:, KW - 1 : tok_rows], grad_extended[:, tok_rows:] + rim_back], axis=1
    ).astype(jnp.bfloat16)
    rate_grad = grad_rate.transpose(1, 2, 0).reshape(tok_rows, head_count)
    grad_logit = (rate_grad * valid[:, None] * rate_sig * (1.0 - rate_sig)).astype(jnp.bfloat16)
    qkv_part = jnp.einsum("td,cte->cde", normed_one, grad_proj, preferred_element_type=jnp.float32)
    beta_part = jnp.einsum("td,th->dh", normed_one, grad_logit, preferred_element_type=jnp.float32)
    grad_one_part = jnp.einsum(
        "cte,cde->td", grad_proj, qkv_full, preferred_element_type=jnp.float32
    ) + jnp.einsum("th,dh->td", grad_logit, beta_full, preferred_element_type=jnp.float32)
    grad_one = tp_total(grad_one_part)
    attn_gain_part = jnp.sum(grad_one * x_rows * scale_one, axis=0)
    input_local = (grad_resid + norm_back(x_rows, scale_one, attn_gain, grad_one)).astype(
        jnp.bfloat16
    )
    conv_whole = lax.dynamic_update_slice(
        jnp.zeros((3, KW, model_width), jnp.float32),
        conv_part,
        (0, 0, lax.axis_index("tp") * local_width),
    )
    attn_gain_grad, mlp_gain_grad, out_gain_grad, conv_grad = lax.psum(
        (attn_gain_part * lead_mask, mlp_gain_part * lead_mask, out_gain_part, conv_whole),
        ("row", "seq", "tp"),
    )
    qkv_sum, beta_sum, o_sum, gate_up_sum, down_sum = (
        lax.psum_scatter(
            qkv_part.astype(jnp.bfloat16), ("row", "seq"), scatter_dimension=1, tiled=True
        ).astype(jnp.float32),
        lax.psum_scatter(
            beta_part.astype(jnp.bfloat16), ("row", "seq"), scatter_dimension=0, tiled=True
        ).astype(jnp.float32),
        lax.psum_scatter(
            o_part.astype(jnp.bfloat16), ("row", "seq"), scatter_dimension=1, tiled=True
        ).astype(jnp.float32),
        lax.psum_scatter(
            gate_up_part.astype(jnp.bfloat16), ("row", "seq"), scatter_dimension=1, tiled=True
        ).astype(jnp.float32),
        lax.psum_scatter(
            down_part.astype(jnp.bfloat16), ("row", "seq"), scatter_dimension=1, tiled=True
        ).astype(jnp.float32),
    )
    return (
        result[None],
        input_local[None],
        attn_gain_grad,
        mlp_gain_grad,
        out_gain_grad,
        conv_grad,
        qkv_sum,
        beta_sum,
        o_sum,
        gate_up_sum,
        down_sum,
    )


CHUNK = 128


def lower_inverse(strict_part):
    size = strict_part.shape[-1]
    at = jnp.arange(size, dtype=jnp.int32)

    def joins(half):
        outer = (at[:, None] // (2 * half)) == (at[None, :] // (2 * half))
        return jnp.where(outer & (at[:, None] // half != at[None, :] // half), strict_part, 0.0)

    inverse = jnp.eye(size, dtype=jnp.float32) - joins(1)
    half = 2
    while half < size:
        inverse = inverse - wide_mul(inverse, wide_mul(joins(half), inverse))
        half *= 2
    return inverse


def wide_mul(left, right):
    return jnp.einsum("...ij,...jk->...ik", left, right, precision=precise)


def wide_mul_nt(left, right):
    return jnp.einsum("...ij,...kj->...ik", left, right, precision=precise)


def wide_mul_tn(left, right):
    return jnp.einsum("...ji,...jk->...ik", left, right, precision=precise)


def row_masks(doc_ids):
    chunks = doc_ids.reshape(-1, CHUNK)
    same = chunks[:, :, None] == chunks[:, None, :]
    at = jnp.arange(CHUNK, dtype=jnp.int32)
    lower = at[:, None] >= at[None, :]
    strict = at[:, None] > at[None, :]
    prior = jnp.concatenate([jnp.full((1,), -1, jnp.int32), chunks[:-1, -1]])
    return (
        (same & lower).astype(jnp.float32),
        (same & strict).astype(jnp.float32),
        same[:, -1, :].astype(jnp.float32),
        (chunks == prior[:, None]).astype(jnp.float32),
    )


def mixer_forward(queries, key_rows, value_rows, rates, masks):
    lower, strict, tail, carry = masks
    system = rates[..., None] * wide_mul_nt(key_rows, key_rows) * strict
    inverse = lower_inverse(system)
    base = wide_mul(inverse, rates[..., None] * value_rows)
    read = wide_mul(inverse, (rates * carry)[..., None] * key_rows)
    scores = wide_mul_nt(queries, key_rows) * lower
    tail_keys = tail[:, :, None] * key_rows

    def step(state, parts):
        base_n, read_n, tail_n, carry_n = parts
        written = base_n - wide_mul(read_n, state)
        after = carry_n * state + wide_mul_tn(tail_n, written)
        return after, (state, written)

    heads = queries.shape[0]
    start = jnp.zeros((heads, DK, DK), jnp.float32)
    _, (states, written) = lax.scan(
        step,
        start,
        (
            jnp.moveaxis(base, 1, 0),
            jnp.moveaxis(read, 1, 0),
            jnp.moveaxis(tail_keys, 1, 0),
            carry[:, -1],
        ),
    )
    states, written = jnp.moveaxis(states, 0, 1), jnp.moveaxis(written, 0, 1)
    mixed = carry[:, :, None] * wide_mul(queries, states) + wide_mul(scores, written)
    return mixed, (inverse, states, written)


def mixer_backward(queries, key_rows, value_rows, rates, masks, saved, grads):
    lower, strict, tail, carry = masks
    inverse, states, written = saved
    rate_col = rates[..., None]
    carry_col = carry[:, :, None]
    scores = wide_mul_nt(queries, key_rows) * lower
    pulled = wide_mul_tn(scores, grads)
    tail_keys = tail[:, :, None] * key_rows
    direct = wide_mul_tn(carry_col * queries, grads)
    carried_keys = rate_col * carry_col * key_rows

    def step(grad_state, parts):
        pulled_n, tail_n, inverse_n, carried_n, direct_n, carry_n = parts
        grad_solved = wide_mul_tn(inverse_n, pulled_n + wide_mul(tail_n, grad_state))
        before = carry_n * grad_state + direct_n - wide_mul_tn(carried_n, grad_solved)
        return before, (grad_state, grad_solved)

    heads = queries.shape[0]
    _, (grad_states, grad_solved) = lax.scan(
        step,
        jnp.zeros((heads, DK, DK), jnp.float32),
        (
            jnp.moveaxis(pulled, 1, 0),
            jnp.moveaxis(tail_keys, 1, 0),
            jnp.moveaxis(inverse, 1, 0),
            jnp.moveaxis(carried_keys, 1, 0),
            jnp.moveaxis(direct, 1, 0),
            carry[:, -1],
        ),
        reverse=True,
    )
    grad_states, grad_solved = jnp.moveaxis(grad_states, 0, 1), jnp.moveaxis(grad_solved, 0, 1)
    grad_scores = wide_mul_nt(grads, written) * lower
    grad_query = carry_col * wide_mul_nt(grads, states) + wide_mul(grad_scores, key_rows)
    grad_key = wide_mul_tn(grad_scores, queries) + tail[:, :, None] * wide_mul_nt(
        written, grad_states
    )
    guess_error = value_rows - carry_col * wide_mul(key_rows, states)
    grad_value = rate_col * grad_solved
    gram = wide_mul_nt(key_rows, key_rows) * strict
    grad_system = -wide_mul_nt(grad_solved, written) * strict
    grad_rate = jnp.sum(grad_solved * guess_error, axis=-1) + jnp.sum(
        grad_system * gram, axis=-1
    )
    grad_gram = rate_col * grad_system
    grad_key = (
        grad_key
        - rate_col * carry_col * wide_mul_nt(grad_solved, states)
        + wide_mul(grad_gram, key_rows)
        + wide_mul_tn(grad_gram, key_rows)
    )
    return grad_query, grad_key, grad_value, grad_rate


def spread(shard, pieces, axis):
    rows, width = shard.shape
    parts = shard.reshape(rows, pieces, width // pieces).transpose(1, 0, 2)
    return lax.all_to_all(parts, axis, 0, 0, tiled=True)


def gathered(shard):
    pieces = lax.axis_size("seq")
    parts = spread(shard, pieces, "seq")
    whole = lax.all_gather(parts, "row", axis=0, tiled=True)
    return whole.reshape(-1, whole.shape[-1])


def returned(part):
    pieces = lax.axis_size("seq")
    rows = part.shape[0] // (pieces * lax.axis_size("row"))
    own = lax.psum_scatter(part, "row", scatter_dimension=0, tiled=True)
    own = own.reshape(pieces, rows, -1)
    return lax.all_to_all(own, "seq", 0, 0, tiled=True)


def token_gather(own):
    return lax.all_gather(own, ("seq", "tp"), axis=0, tiled=True)


def token_sum(term):
    return lax.psum_scatter(
        term.astype(jnp.bfloat16), ("seq", "tp"), scatter_dimension=0, tiled=True
    ).astype(jnp.float32)


def both_cores(own):
    cores = lax.axis_size("tp")
    if cores == 1:
        return own
    other = lax.ppermute(own, "tp", [(0, 1), (1, 0)])
    first = lax.axis_index("tp") == 0
    return jnp.concatenate([jnp.where(first, own, other), jnp.where(first, other, own)], axis=0)


def shifted(rows, by):
    if by == 0:
        return rows
    pad = jnp.zeros((abs(by),) + rows.shape[1:], rows.dtype)
    if by > 0:
        return jnp.concatenate([pad, rows[:-by]], axis=0)
    return jnp.concatenate([rows[-by:], pad], axis=0)


def local_heads(
    block_input,
    grad_out,
    doc_lengths,
    attn_gain,
    mlp_gain,
    out_gain,
    conv_weight,
    qkv_weight,
    beta_weight,
    o_weight,
    gate_up_weight,
    down_weight,
):
    tok_rows, model_width = block_input.shape[1:]
    pieces, cores = lax.axis_size("seq"), lax.axis_size("tp")
    piece, core = lax.axis_index("seq"), lax.axis_index("tp")
    row_len = pieces * tok_rows
    own_rows = tok_rows // cores
    unit_floor = DK / 16.0
    shard_rows = qkv_weight.shape[1]
    half_width = qkv_weight.shape[2]
    width = half_width // pieces
    heads = width // DK
    units = gate_up_weight.shape[2] // pieces
    chunks = row_len // CHUNK
    f32, b16 = jnp.float32, jnp.bfloat16

    qkv_parts = qkv_weight.reshape(3, shard_rows, pieces, width).transpose(1, 2, 0, 3)
    qkv_full = gathered(qkv_parts.reshape(shard_rows, -1))
    beta_full = lax.all_gather(beta_weight, ("row", "seq"), axis=0, tiled=True)
    beta_full = lax.dynamic_slice_in_dim(beta_full, piece * heads, heads, axis=1)
    o_full = gathered(o_weight.T)
    gate_up_parts = gate_up_weight.reshape(2, shard_rows, pieces, units).transpose(1, 2, 0, 3)
    gate_up_full = gathered(gate_up_parts.reshape(shard_rows, -1))
    down_full = gathered(down_weight.T)

    ends = jnp.cumsum(doc_lengths[0])
    places = jnp.arange(row_len, dtype=jnp.int32)
    docs = jnp.sum((places[:, None] >= ends[None, :]).astype(jnp.int32), axis=1)
    padded_docs = jnp.concatenate([jnp.full((KW - 1,), -1, jnp.int32), docs])
    valid = (docs < DOCS).astype(f32)
    tap_masks = [
        (padded_docs[KW - 1 - tap : KW - 1 - tap + row_len] == docs).astype(f32)[:, None]
        for tap in range(KW)
    ]
    masks = row_masks(docs)
    taps = lax.dynamic_slice_in_dim(conv_weight, piece * width, width, axis=2)
    taps = taps.transpose(1, 0, 2).reshape(KW, 3 * width)

    def to_chunks(array):
        return array.reshape(chunks, CHUNK, heads, -1).transpose(2, 0, 1, 3)

    def from_chunks(array):
        return array.transpose(1, 2, 0, 3).reshape(row_len, heads, -1)

    x_rows = lax.dynamic_slice_in_dim(block_input[0], core * own_rows, own_rows, axis=0)
    x_rows = x_rows.astype(f32)
    g_rows = lax.dynamic_slice_in_dim(grad_out[0], core * own_rows, own_rows, axis=0)
    scale_one = norm_scale(x_rows)
    normed_one = token_gather((x_rows * scale_one * attn_gain).astype(b16))
    g_full = token_gather(g_rows)
    proj = jnp.dot(normed_one, qkv_full, preferred_element_type=f32).astype(b16).astype(f32)
    logit = jnp.dot(normed_one, beta_full, preferred_element_type=f32)
    conv_out = sum(taps[tap] * shifted(proj, tap) * tap_masks[tap] for tap in range(KW))
    conv_sig = jax.nn.sigmoid(conv_out)
    activated = (conv_out * conv_sig).reshape(row_len, 3, heads, DK)
    query_raw, key_raw = activated[:, 0], activated[:, 1]
    query_sq = jnp.sum(query_raw * query_raw, axis=-1, keepdims=True)
    key_sq = jnp.sum(key_raw * key_raw, axis=-1, keepdims=True)
    query_scale = lax.rsqrt(jnp.maximum(query_sq, unit_floor))
    key_scale = lax.rsqrt(jnp.maximum(key_sq, unit_floor))
    query_live = (query_sq > unit_floor).astype(f32)
    key_live = (key_sq > unit_floor).astype(f32)
    query_chunks = to_chunks(query_raw * query_scale)
    key_chunks = to_chunks(key_raw * key_scale)
    value_chunks = to_chunks(activated[:, 2])
    rate_sig = jax.nn.sigmoid(logit)
    rate_chunks = (rate_sig * valid[:, None]).T.reshape(heads, chunks, CHUNK)
    mix_chunks, saved = mixer_forward(query_chunks, key_chunks, value_chunks, rate_chunks, masks)
    mixed = from_chunks(mix_chunks) * valid[:, None, None]
    mix_sq = jnp.mean(mixed * mixed, axis=-1, keepdims=True)
    mix_scale = lax.rsqrt(jnp.maximum(mix_sq, mix_floor))
    mix_live = (mix_sq > mix_floor).astype(f32)
    normed_mix = (mixed * mix_scale * out_gain).astype(b16).reshape(row_len, width)
    o_term = jnp.einsum("te,de->td", normed_mix, o_full, preferred_element_type=f32)
    resid = x_rows + token_sum(o_term)
    scale_two = norm_scale(resid)
    normed_two = token_gather((resid * scale_two * mlp_gain).astype(b16))
    gate_up = jnp.dot(normed_two, gate_up_full, preferred_element_type=f32)
    gate, up = gate_up[:, :units], gate_up[:, units:]
    gate_sig = jax.nn.sigmoid(gate)
    gate_act = gate * gate_sig
    hidden = (gate_act * up).astype(b16)
    grad_hidden = jnp.dot(g_full, down_full, preferred_element_type=f32)
    grad_gate = grad_hidden * up * gate_sig * (1.0 + gate * (1.0 - gate_sig))
    grad_up = grad_hidden * gate_act
    grad_gate_up = jnp.concatenate([grad_gate, grad_up], axis=1).astype(b16)
    two_term = jnp.einsum("tf,df->td", grad_gate_up, gate_up_full, preferred_element_type=f32)
    grad_two = token_sum(two_term)
    mlp_gain_part = jnp.sum(grad_two * resid * scale_two, axis=0)
    grad_resid = g_rows.astype(f32) + norm_back(resid, scale_two, mlp_gain, grad_two)
    grad_attn = token_gather(grad_resid.astype(b16))
    down_term = jnp.einsum("tf,df->td", hidden, down_full, preferred_element_type=f32)
    result = both_cores((resid + token_sum(down_term)).astype(b16))
    down_part = jnp.einsum("td,tf->df", g_full, hidden, preferred_element_type=f32)
    gate_up_part = jnp.einsum("td,tf->df", normed_two, grad_gate_up, preferred_element_type=f32)
    o_part = jnp.einsum("td,te->de", grad_attn, normed_mix, preferred_element_type=f32)
    grad_normed = jnp.dot(grad_attn, o_full, preferred_element_type=f32)
    grad_normed = grad_normed.reshape(row_len, heads, DK)
    out_gain_part = jnp.sum(grad_normed * mixed * mix_scale, axis=(0, 1))
    weighted_mix = out_gain * grad_normed
    grad_mixed = (
        mix_scale * weighted_mix
        - mixed * mix_scale**3 * mix_live * jnp.mean(weighted_mix * mixed, axis=-1, keepdims=True)
    ) * valid[:, None, None]
    grad_query, grad_key, grad_value, grad_rate = mixer_backward(
        query_chunks, key_chunks, value_chunks, rate_chunks, masks, saved, to_chunks(grad_mixed)
    )
    grad_query, grad_key = from_chunks(grad_query), from_chunks(grad_key)
    grad_query_raw = query_scale * grad_query - query_raw * query_scale**3 * query_live * jnp.sum(
        query_raw * grad_query, axis=-1, keepdims=True
    )
    grad_key_raw = key_scale * grad_key - key_raw * key_scale**3 * key_live * jnp.sum(
        key_raw * grad_key, axis=-1, keepdims=True
    )
    grad_activated = jnp.stack([grad_query_raw, grad_key_raw, from_chunks(grad_value)], axis=1)
    grad_conv = grad_activated.reshape(row_len, -1) * conv_sig * (1.0 + conv_out * (1.0 - conv_sig))
    grad_proj = jnp.zeros_like(proj)
    tap_grads = []
    for tap in range(KW):
        masked = grad_conv * tap_masks[tap]
        tap_grads.append(jnp.sum(masked * shifted(proj, tap), axis=0))
        grad_proj = grad_proj + taps[tap] * shifted(masked, -tap)
    grad_proj = grad_proj.astype(b16)
    conv_part = jnp.stack(tap_grads).reshape(KW, 3, width).transpose(1, 0, 2)
    rate_grad = grad_rate.reshape(heads, row_len).T
    grad_logit = (rate_grad * valid[:, None] * rate_sig * (1.0 - rate_sig)).astype(b16)
    one_term = jnp.einsum("te,de->td", grad_proj, qkv_full, preferred_element_type=f32)
    one_term = one_term + jnp.einsum("th,dh->td", grad_logit, beta_full, preferred_element_type=f32)
    grad_one = token_sum(one_term)
    attn_gain_part = jnp.sum(grad_one * x_rows * scale_one, axis=0)
    input_grad = both_cores(
        (grad_resid + norm_back(x_rows, scale_one, attn_gain, grad_one)).astype(b16)
    )
    qkv_part = jnp.einsum("td,te->de", normed_one, grad_proj, preferred_element_type=f32)
    beta_part = jnp.einsum("td,th->dh", normed_one, grad_logit, preferred_element_type=f32)
    beta_part = lax.dynamic_update_slice(
        jnp.zeros((model_width, pieces * heads), f32), beta_part, (0, piece * heads)
    )
    conv_whole = lax.dynamic_update_slice(
        jnp.zeros((3, KW, model_width), f32),
        conv_part,
        (0, 0, core * half_width + piece * width),
    )
    attn_gain_grad, mlp_gain_grad, out_gain_grad, conv_grad = lax.psum(
        (attn_gain_part, mlp_gain_part, out_gain_part, conv_whole), ("row", "seq", "tp")
    )
    down_sum = returned(down_part.astype(b16))
    gate_up_sum = returned(gate_up_part.astype(b16)).reshape(pieces, shard_rows, 2, units)
    o_sum = returned(o_part.astype(b16))
    qkv_sum = returned(qkv_part.astype(b16)).reshape(pieces, shard_rows, 3, width)
    beta_sum = lax.psum_scatter(
        beta_part.astype(b16), ("row", "seq"), scatter_dimension=0, tiled=True
    ).astype(f32)
    return (
        result[None],
        input_grad[None],
        attn_gain_grad,
        mlp_gain_grad,
        out_gain_grad,
        conv_grad,
        qkv_sum.transpose(2, 1, 0, 3).reshape(3, shard_rows, -1).astype(f32),
        beta_sum,
        o_sum.transpose(0, 2, 1).reshape(-1, shard_rows).astype(f32),
        gate_up_sum.transpose(2, 1, 0, 3).reshape(2, shard_rows, -1).astype(f32),
        down_sum.transpose(0, 2, 1).reshape(-1, shard_rows).astype(f32),
    )


def splits_heads(mesh, heads=16, units=5632):
    return (
        mesh.shape["tp"] == 2
        and heads % (mesh.shape["seq"] * 2) == 0
        and units % (mesh.shape["seq"] * 2) == 0
    )


def solution(mesh):
    in_specs = (
        P("row", "seq", None),
        P("row", "seq", None),
        P("row", None),
        P(),
        P(),
        P(),
        P(None, None, "tp"),
        P(None, ("row", "seq"), "tp"),
        P(("row", "seq"), "tp"),
        P("tp", ("row", "seq")),
        P(None, ("row", "seq"), "tp"),
        P("tp", ("row", "seq")),
    )
    out_specs = (
        P("row", "seq", None),
        P("row", "seq", None),
        P(),
        P(),
        P(),
        P(),
        P(None, ("row", "seq"), "tp"),
        P(("row", "seq"), "tp"),
        P("tp", ("row", "seq")),
        P(None, ("row", "seq"), "tp"),
        P("tp", ("row", "seq")),
    )
    local = local_heads if splits_heads(mesh) else local_pieces
    return jax.shard_map(local, mesh=mesh, in_specs=in_specs, out_specs=out_specs, check_vma=False)
```

```python
import functools

import jax
import jax.numpy as jnp
from jax import lax
from jax.experimental import pallas as pl
from jax.experimental.pallas import tpu as pltpu
from jax.sharding import PartitionSpec as P

DK = 128
KW = 4
GROUP = 64
DOCS = 8


eps = 1e-06
mix_floor = 0.01
precise = lax.Precision.HIGHEST


def from_behind(shard, axis, by):
    devices = lax.axis_size(axis)
    pairs = [(i, i + by) for i in range(devices) if 0 <= i + by < devices]
    return lax.ppermute(shard, axis, pairs)


def prefix(shard, axis, combine, identity, reverse):
    devices, place = (lax.axis_size(axis), lax.axis_index(axis))
    everything = jax.tree.map(
        lambda part, kind: lax.all_gather(part.astype(kind), axis),
        shard,
        (jnp.bfloat16, jnp.bfloat16),
    )
    start = jax.tree.map(
        lambda part, zero: jnp.broadcast_to(jnp.asarray(zero, part.dtype), part.shape),
        shard,
        identity,
    )

    def step(k, before):
        at = devices - 1 - k if reverse else k
        reached = at > place if reverse else at < place
        new = combine(
            before, jax.tree.map(lambda part, own: part[at].astype(own.dtype), everything, shard)
        )
        return jax.tree.map(lambda a, b: jnp.where(reached, a, b), new, before)

    return lax.fori_loop(0, devices, step, start)


def norm_scale(values):
    return lax.rsqrt(jnp.mean(values * values, axis=-1, keepdims=True) + eps)


def norm_back(values, scale, gain, grad):
    weighted = gain * grad
    return scale * weighted - values * scale**3 * jnp.mean(
        weighted * values, axis=-1, keepdims=True
    )


def batch_mul(left, right):
    return jnp.einsum("hij,hjk->hik", left, right, precision=precise)


def batch_mul_t(left, right):
    return jnp.einsum("hji,hjk->hik", left, right, precision=precise)


def compose(earlier, later):
    return (batch_mul(later[0], earlier[0]), batch_mul(later[0], earlier[1]) + later[1])


def over_heads(function, shared):
    return jax.vmap(jax.vmap(function), in_axes=shared)


def tp_total(term):
    return lax.psum(term.astype(jnp.bfloat16), "tp").astype(jnp.float32)


def group_parts(key_rows, value_rows, rates, same_doc, carry_mask):
    size = key_rows.shape[0]
    strict = jnp.tril(jnp.ones((size, size), jnp.float32), -1) * same_doc
    inner = jnp.dot(key_rows, key_rows.T, precision=precise)
    system = jnp.eye(size, dtype=jnp.float32) + rates[:, None] * inner * strict
    right_side = jnp.concatenate(
        [rates[:, None] * value_rows, (rates * carry_mask)[:, None] * key_rows], axis=1
    )
    solved = jax.scipy.linalg.solve_triangular(system, right_side, lower=True)
    base_rows = solved[:, : value_rows.shape[1]]
    wy_rows = solved[:, value_rows.shape[1] :]
    tail_keys = same_doc[size - 1][:, None] * key_rows
    identity_mat = jnp.eye(key_rows.shape[1], dtype=jnp.float32)
    transition = carry_mask[size - 1] * identity_mat - jnp.dot(
        tail_keys.T, wy_rows, precision=precise
    )
    contribution = jnp.dot(tail_keys.T, base_rows, precision=precise)
    return (transition, contribution, base_rows, wy_rows)


def group_output(queries, key_rows, same_doc, carry_mask, base_rows, wy_rows, state_in):
    size = key_rows.shape[0]
    lower = jnp.tril(jnp.ones((size, size), jnp.float32)) * same_doc
    written = base_rows - jnp.dot(wy_rows, state_in, precision=precise)
    scores = jnp.dot(queries, key_rows.T, precision=precise) * lower
    carried = carry_mask[:, None] * jnp.dot(queries, state_in, precision=precise)
    return carried + jnp.dot(scores, written, precision=precise)


def group_full(queries, key_rows, value_rows, rates, same_doc, carry_mask, state_in):
    transition, contribution, base_rows, wy_rows = group_parts(
        key_rows, value_rows, rates, same_doc, carry_mask
    )
    outputs = group_output(queries, key_rows, same_doc, carry_mask, base_rows, wy_rows, state_in)
    return (outputs, jnp.dot(transition, state_in, precision=precise) + contribution)


def state_pull(queries, key_rows, same_doc, carry_mask, wy_rows, grad_rows):
    size = key_rows.shape[0]
    lower = jnp.tril(jnp.ones((size, size), jnp.float32)) * same_doc
    scores = jnp.dot(queries, key_rows.T, precision=precise) * lower
    pulled = jnp.dot(scores.T, grad_rows, precision=precise)
    direct = jnp.dot((carry_mask[:, None] * queries).T, grad_rows, precision=precise)
    return direct - jnp.dot(wy_rows.T, pulled, precision=precise)


def group_grads(
    queries, key_rows, value_rows, rates, same_doc, carry_mask, state_in, grad_rows, grad_end
):

    def group_local(query_in, key_in, value_in, rate_in):
        return group_full(query_in, key_in, value_in, rate_in, same_doc, carry_mask, state_in)

    outputs, pullback = jax.vjp(group_local, queries, key_rows, value_rows, rates)
    return pullback((grad_rows, grad_end))


def local_pieces(
    block_input,
    grad_out,
    doc_lengths,
    attn_gain,
    mlp_gain,
    out_gain,
    conv_weight,
    qkv_weight,
    beta_weight,
    o_weight,
    gate_up_weight,
    down_weight,
):
    tok_rows = block_input.shape[1]
    model_width = block_input.shape[2]
    blocks = tok_rows // GROUP
    unit_floor = DK / 16.0
    x_rows = block_input[0].astype(jnp.float32)
    grad_rows_out = grad_out[0]
    qkv_full, beta_full, o_full, gate_up_full, down_full = (
        lax.all_gather(qkv_weight, ("row", "seq"), axis=1, tiled=True),
        lax.all_gather(beta_weight, ("row", "seq"), axis=0, tiled=True),
        lax.all_gather(o_weight, ("row", "seq"), axis=1, tiled=True),
        lax.all_gather(gate_up_weight, ("row", "seq"), axis=1, tiled=True),
        lax.all_gather(down_weight, ("row", "seq"), axis=1, tiled=True),
    )
    local_width = qkv_full.shape[2]
    head_count = local_width // DK
    lead_mask = (lax.axis_index("tp") == 0).astype(jnp.float32)
    ends = jnp.cumsum(doc_lengths[0])
    places = (
        lax.axis_index("seq") * tok_rows + jnp.arange(tok_rows + KW - 1, dtype=jnp.int32) - (KW - 1)
    )
    doc_ids = jnp.sum((places[:, None] >= ends[None, :]).astype(jnp.int32), axis=1)
    doc_ids = jnp.where(places < 0, -1, doc_ids)
    own_docs = doc_ids[KW - 1 :]
    prior_docs = doc_ids[KW - 2 : KW - 2 + tok_rows]
    valid = (own_docs < DOCS).astype(jnp.float32)
    fresh = (own_docs != prior_docs).astype(jnp.int32)
    tap_masks = [
        (doc_ids[KW - 1 - tap : KW - 1 - tap + tok_rows] == own_docs).astype(jnp.float32)
        for tap in range(KW)
    ]
    own_blocks = own_docs.reshape(blocks, GROUP)
    same_doc = (own_blocks[:, :, None] == own_blocks[:, None, :]).astype(jnp.float32)
    carry_mask = (jnp.cumsum(fresh.reshape(blocks, GROUP), axis=1) == 0).astype(jnp.float32)

    def to_blocks(array):
        return array.reshape(blocks, GROUP, head_count, -1).transpose(2, 0, 1, 3)

    def from_blocks(array):
        return array.transpose(1, 2, 0, 3).reshape(tok_rows, head_count, -1)

    scale_one = norm_scale(x_rows)
    normed_one = (x_rows * scale_one * attn_gain).astype(jnp.bfloat16)
    proj_low = jnp.einsum(
        "td,cde->cte", normed_one, qkv_full, preferred_element_type=jnp.float32
    ).astype(jnp.bfloat16)
    logit = jnp.dot(normed_one, beta_full, preferred_element_type=jnp.float32)
    rim_rows = from_behind(proj_low[:, tok_rows - (KW - 1) :, :], "seq", 1)
    extended = jnp.concatenate([rim_rows, proj_low], axis=1).astype(jnp.float32)
    conv_out = jnp.zeros((3, tok_rows, local_width), jnp.float32)
    for tap in range(KW):
        window = extended[:, KW - 1 - tap : KW - 1 - tap + tok_rows]
        conv_out = (
            conv_out + conv_weight[:, tap][:, None, :] * window * tap_masks[tap][None, :, None]
        )
    conv_sig = jax.nn.sigmoid(conv_out)
    activated = conv_out * conv_sig
    query_raw = activated[0].reshape(tok_rows, head_count, DK)
    key_raw = activated[1].reshape(tok_rows, head_count, DK)
    query_sq = jnp.sum(query_raw * query_raw, axis=-1, keepdims=True)
    key_sq = jnp.sum(key_raw * key_raw, axis=-1, keepdims=True)
    query_scale = lax.rsqrt(jnp.maximum(query_sq, unit_floor))
    key_scale = lax.rsqrt(jnp.maximum(key_sq, unit_floor))
    query_live = (query_sq > unit_floor).astype(jnp.float32)
    key_live = (key_sq > unit_floor).astype(jnp.float32)
    query_blocks = to_blocks(query_raw * query_scale)
    key_blocks = to_blocks(key_raw * key_scale)
    value_blocks = to_blocks(activated[2].reshape(tok_rows, head_count, DK))
    rate_sig = jax.nn.sigmoid(logit)
    rate_blocks = (rate_sig * valid[:, None]).reshape(blocks, GROUP, head_count).transpose(2, 0, 1)
    transition, contribution, base_rows, wy_rows = over_heads(group_parts, (0, 0, 0, None, None))(
        key_blocks, value_blocks, rate_blocks, same_doc, carry_mask
    )
    identity_mat = jnp.broadcast_to(jnp.eye(DK, dtype=jnp.float32), (head_count, DK, DK))
    zero_state = jnp.zeros((head_count, DK, DK), jnp.float32)
    transition_steps = jnp.moveaxis(transition, 1, 0)

    def chain(running, pair):
        product, partial_state = running
        step_trans, step_contrib = pair
        advanced = (
            batch_mul(step_trans, product),
            batch_mul(step_trans, partial_state) + step_contrib,
        )
        return (advanced, (product, partial_state))

    (dev_trans, dev_state), (products, partials) = lax.scan(
        chain, (identity_mat, zero_state), (transition_steps, jnp.moveaxis(contribution, 1, 0))
    )
    incoming = prefix((dev_trans, dev_state), "seq", compose, (identity_mat, zero_state), False)[1]
    group_starts = partials + jnp.einsum("nhij,hjk->nhik", products, incoming, precision=precise)
    start_blocks = jnp.moveaxis(group_starts, 0, 1)
    mix_blocks = over_heads(group_output, (0, 0, None, None, 0, 0, 0))(
        query_blocks, key_blocks, same_doc, carry_mask, base_rows, wy_rows, start_blocks
    )
    mixed = from_blocks(mix_blocks) * valid[:, None, None]
    mix_sq = jnp.mean(mixed * mixed, axis=-1, keepdims=True)
    mix_scale = lax.rsqrt(jnp.maximum(mix_sq, mix_floor))
    mix_live = (mix_sq > mix_floor).astype(jnp.float32)
    normed_mix = (mixed * mix_scale * out_gain).astype(jnp.bfloat16).reshape(tok_rows, local_width)
    o_term = jnp.dot(normed_mix, o_full, preferred_element_type=jnp.float32)
    resid = x_rows + tp_total(o_term)
    scale_two = norm_scale(resid)
    normed_local = (resid * scale_two * mlp_gain).astype(jnp.bfloat16)
    gate_up = jnp.einsum(
        "td,cdf->ctf", normed_local, gate_up_full, preferred_element_type=jnp.float32
    )
    gate_sig = jax.nn.sigmoid(gate_up[0])
    gate_act = gate_up[0] * gate_sig
    hidden = (gate_act * gate_up[1]).astype(jnp.bfloat16)
    down_term = jnp.dot(hidden, down_full, preferred_element_type=jnp.float32)
    mlp_out = tp_total(down_term)
    result = (resid + mlp_out).astype(jnp.bfloat16)
    grad_hidden = jnp.einsum(
        "td,fd->tf", grad_rows_out, down_full, preferred_element_type=jnp.float32
    )
    grad_gate = grad_hidden * gate_up[1] * gate_sig * (1.0 + gate_up[0] * (1.0 - gate_sig))
    grad_up = grad_hidden * gate_act
    grad_gate_up = jnp.stack([grad_gate, grad_up]).astype(jnp.bfloat16)
    down_part = jnp.einsum("tf,td->fd", hidden, grad_rows_out, preferred_element_type=jnp.float32)
    gate_up_part = jnp.einsum(
        "td,ctf->cdf", normed_local, grad_gate_up, preferred_element_type=jnp.float32
    )
    two_term = jnp.einsum(
        "ctf,cdf->td", grad_gate_up, gate_up_full, preferred_element_type=jnp.float32
    )
    grad_two = tp_total(two_term)
    mlp_gain_part = jnp.sum(grad_two * resid * scale_two, axis=0)
    grad_resid = grad_rows_out.astype(jnp.float32) + norm_back(resid, scale_two, mlp_gain, grad_two)
    grad_attn_local = grad_resid.astype(jnp.bfloat16)
    o_part = jnp.einsum(
        "te,td->ed", normed_mix, grad_attn_local, preferred_element_type=jnp.float32
    )
    grad_normed = jnp.einsum(
        "td,ed->te", grad_attn_local, o_full, preferred_element_type=jnp.float32
    ).reshape(tok_rows, head_count, DK)
    out_gain_part = jnp.sum(grad_normed * mixed * mix_scale, axis=(0, 1))
    weighted_mix = out_gain * grad_normed
    grad_mixed = (
        mix_scale * weighted_mix
        - mixed * mix_scale**3 * mix_live * jnp.mean(weighted_mix * mixed, axis=-1, keepdims=True)
    ) * valid[:, None, None]
    grad_blocks = to_blocks(grad_mixed)
    pulls = over_heads(state_pull, (0, 0, None, None, 0, 0))(
        query_blocks, key_blocks, same_doc, carry_mask, wy_rows, grad_blocks
    )

    def back_chain(running, pair):
        grad_end, product = running
        step_trans, step_pull = pair
        advanced = (step_pull + batch_mul_t(step_trans, grad_end), batch_mul_t(step_trans, product))
        return (advanced, (grad_end, product))

    (dev_pull, dev_back), (grad_ends, back_products) = lax.scan(
        back_chain,
        (zero_state, identity_mat),
        (transition_steps, jnp.moveaxis(pulls, 1, 0)),
        reverse=True,
    )
    outgoing = prefix((dev_back, dev_pull), "seq", compose, (identity_mat, zero_state), True)[1]
    end_grads = grad_ends + jnp.einsum("nhij,hjk->nhik", back_products, outgoing, precision=precise)
    grad_query, grad_key, grad_value, grad_rate = over_heads(
        group_grads, (0, 0, 0, 0, None, None, 0, 0, 0)
    )(
        query_blocks,
        key_blocks,
        value_blocks,
        rate_blocks,
        same_doc,
        carry_mask,
        start_blocks,
        grad_blocks,
        jnp.moveaxis(end_grads, 0, 1),
    )
    grad_query = from_blocks(grad_query)
    grad_key = from_blocks(grad_key)
    grad_query_raw = query_scale * grad_query - query_raw * query_scale**3 * query_live * jnp.sum(
        query_raw * grad_query, axis=-1, keepdims=True
    )
    grad_key_raw = key_scale * grad_key - key_raw * key_scale**3 * key_live * jnp.sum(
        key_raw * grad_key, axis=-1, keepdims=True
    )
    grad_activated = jnp.stack(
        [
            grad_query_raw.reshape(tok_rows, local_width),
            grad_key_raw.reshape(tok_rows, local_width),
            from_blocks(grad_value).reshape(tok_rows, local_width),
        ]
    )
    grad_conv = grad_activated * conv_sig * (1.0 + conv_out * (1.0 - conv_sig))
    grad_extended = jnp.zeros((3, tok_rows + KW - 1, local_width), jnp.float32)
    tap_grads = []
    for tap in range(KW):
        masked = grad_conv * tap_masks[tap][None, :, None]
        window = extended[:, KW - 1 - tap : KW - 1 - tap + tok_rows]
        tap_grads.append(jnp.sum(masked * window, axis=1))
        grad_extended = grad_extended + jnp.pad(
            conv_weight[:, tap][:, None, :] * masked, ((0, 0), (KW - 1 - tap, tap), (0, 0))
        )
    conv_part = jnp.stack(tap_grads, axis=1)
    rim_back = from_behind(grad_extended[:, : KW - 1], "seq", -1)
    grad_proj = jnp.concatenate(
        [grad_extended[:, KW - 1 : tok_rows], grad_extended[:, tok_rows:] + rim_back], axis=1
    ).astype(jnp.bfloat16)
    rate_grad = grad_rate.transpose(1, 2, 0).reshape(tok_rows, head_count)
    grad_logit = (rate_grad * valid[:, None] * rate_sig * (1.0 - rate_sig)).astype(jnp.bfloat16)
    qkv_part = jnp.einsum("td,cte->cde", normed_one, grad_proj, preferred_element_type=jnp.float32)
    beta_part = jnp.einsum("td,th->dh", normed_one, grad_logit, preferred_element_type=jnp.float32)
    grad_one_part = jnp.einsum(
        "cte,cde->td", grad_proj, qkv_full, preferred_element_type=jnp.float32
    ) + jnp.einsum("th,dh->td", grad_logit, beta_full, preferred_element_type=jnp.float32)
    grad_one = tp_total(grad_one_part)
    attn_gain_part = jnp.sum(grad_one * x_rows * scale_one, axis=0)
    input_local = (grad_resid + norm_back(x_rows, scale_one, attn_gain, grad_one)).astype(
        jnp.bfloat16
    )
    conv_whole = lax.dynamic_update_slice(
        jnp.zeros((3, KW, model_width), jnp.float32),
        conv_part,
        (0, 0, lax.axis_index("tp") * local_width),
    )
    attn_gain_grad, mlp_gain_grad, out_gain_grad, conv_grad = lax.psum(
        (attn_gain_part * lead_mask, mlp_gain_part * lead_mask, out_gain_part, conv_whole),
        ("row", "seq", "tp"),
    )
    qkv_sum, beta_sum, o_sum, gate_up_sum, down_sum = (
        lax.psum_scatter(
            qkv_part.astype(jnp.bfloat16), ("row", "seq"), scatter_dimension=1, tiled=True
        ).astype(jnp.float32),
        lax.psum_scatter(
            beta_part.astype(jnp.bfloat16), ("row", "seq"), scatter_dimension=0, tiled=True
        ).astype(jnp.float32),
        lax.psum_scatter(
            o_part.astype(jnp.bfloat16), ("row", "seq"), scatter_dimension=1, tiled=True
        ).astype(jnp.float32),
        lax.psum_scatter(
            gate_up_part.astype(jnp.bfloat16), ("row", "seq"), scatter_dimension=1, tiled=True
        ).astype(jnp.float32),
        lax.psum_scatter(
            down_part.astype(jnp.bfloat16), ("row", "seq"), scatter_dimension=1, tiled=True
        ).astype(jnp.float32),
    )
    return (
        result[None],
        input_local[None],
        attn_gain_grad,
        mlp_gain_grad,
        out_gain_grad,
        conv_grad,
        qkv_sum,
        beta_sum,
        o_sum,
        gate_up_sum,
        down_sum,
    )


CHUNK = 128
PAD = 8


def mul(left, right, dims, precision=None):
    return lax.dot_general(
        left, right, ((dims[:1], dims[1:]), ((), ())), precision=precision, preferred_element_type=jnp.float32
    )


def fine(left, right, dims=(1, 0)):
    return mul(left, right, dims, precise)


def plain(left, right, dims=(1, 0)):
    return mul(left.astype(jnp.bfloat16), right.astype(jnp.bfloat16), dims)


def chunk_masks(doc_col, doc_row):
    same = doc_col == doc_row
    down = lax.broadcasted_iota(jnp.int32, (CHUNK, CHUNK), 0)
    along = lax.broadcasted_iota(jnp.int32, (CHUNK, CHUNK), 1)
    lower = jnp.where(same & (down >= along), 1.0, 0.0)
    strict = jnp.where(same & (down > along), 1.0, 0.0)
    return lower, strict, down, along


def lower_inverse(systems, down, along):
    at_one = (down // 2 == along // 2) & (down != along)
    unit = jnp.where(down == along, 1.0, 0.0)
    inverses = [unit - jnp.where(at_one, system, 0.0) for system in systems]
    half = 2
    while half < CHUNK:
        joins = (down // (2 * half) == along // (2 * half)) & (down // half != along // half)
        inner = [
            fine(jnp.where(joins, system, 0.0), inverse)
            for system, inverse in zip(systems, inverses)
        ]
        inverses = [inverse - fine(inverse, part) for inverse, part in zip(inverses, inner)]
        half *= 2
    return inverses


def tap_mask(aux, tap):
    return 1.0 if tap == 0 else aux[:, 3 + tap : 4 + tap]


def convolved(window, taps, aux):
    total = 0.0
    for tap in range(KW):
        total = total + (
            taps[tap : tap + 1] * window[PAD - tap : PAD - tap + CHUNK] * tap_mask(aux, tap)
        )
    return total


def sigmoid(values):
    return 1.0 / (1.0 + jnp.exp(-values))


def unit_scale(values):
    total = jnp.sum(values * values, axis=1, keepdims=True)
    floor = DK / 16.0
    return lax.rsqrt(jnp.maximum(total, floor)), jnp.where(total > floor, 1.0, 0.0)


def mix_norm(mixed):
    mean = jnp.mean(mixed * mixed, axis=1, keepdims=True)
    return lax.rsqrt(jnp.maximum(mean, mix_floor)), jnp.where(mean > mix_floor, 1.0, 0.0)


def forward_kernel(
    heads,
    n1_ref,
    qkv_ref,
    beta_ref,
    taps_ref,
    aux_ref,
    docs_ref,
    gain_ref,
    proj_ref,
    logit_ref,
    mixed_ref,
    normed_ref,
    inverse_ref,
    states_ref,
    written_ref,
    window_ref,
    state_ref,
):
    width = heads * DK
    window_ref[0:PAD] = jnp.zeros((PAD, 3 * width), jnp.float32)
    state_ref[...] = jnp.zeros_like(state_ref)

    def chunk(n, _):
        rows = pl.ds(pl.multiple_of(n * CHUNK, CHUNK), CHUNK)
        n1 = n1_ref[rows]
        proj = mul(n1, qkv_ref[...], (1, 0)).astype(jnp.bfloat16)
        proj_ref[rows] = proj
        window_ref[PAD : PAD + CHUNK] = proj.astype(jnp.float32)
        logit = mul(n1, beta_ref[...], (1, 1))
        logit_ref[rows] = logit
        aux = aux_ref[rows]
        conv = convolved(window_ref[...], taps_ref[...], aux)
        act = conv * sigmoid(conv)
        window_ref[0:PAD] = window_ref[CHUNK : CHUNK + PAD]
        valid, carry, tail = aux[:, 1:2], aux[:, 2:3], aux[:, 3:4]
        carry_last = carry[CHUNK - 1 :]
        lower, strict, down, along = chunk_masks(aux[:, 0:1], docs_ref[pl.ds(n, 1)])
        rate_all = sigmoid(logit) * valid
        parts = []
        for h in range(heads):
            query = act[:, h * DK : (h + 1) * DK]
            key = act[:, width + h * DK : width + (h + 1) * DK]
            value = act[:, 2 * width + h * DK : 2 * width + (h + 1) * DK]
            query = query * unit_scale(query)[0]
            key = key * unit_scale(key)[0]
            rate = rate_all[:, h : h + 1]
            system = rate * fine(key, key, (1, 1)) * strict
            parts.append((query, key, value, rate, system))
        inverses = lower_inverse([part[4] for part in parts], down, along)
        for h, (query, key, value, rate, _) in enumerate(parts):
            inverse = inverses[h]
            state = state_ref[h]
            carried_key = carry * key
            right = rate * (value - fine(carried_key, state))
            written = fine(inverse, right)
            scores = plain(query, key, (1, 1)) * lower
            mixed = carry * plain(query, state) + plain(scores, written)
            mixed = mixed * valid
            states_ref[h, n] = state
            written_ref[h, n] = written
            inverse_ref[h, n] = inverse
            state_ref[h] = carry_last * state + fine(tail * key, written, (0, 0))
            columns = pl.ds(h * DK, DK)
            mixed_ref[rows, columns] = mixed
            normed_ref[rows, columns] = (
                mixed * mix_norm(mixed)[0] * gain_ref[...]
            ).astype(jnp.bfloat16)
        return 0

    lax.fori_loop(0, n1_ref.shape[0] // CHUNK, chunk, 0)


def backward_kernel(
    heads,
    grad_ref,
    o_ref,
    proj_ref,
    logit_ref,
    mixed_ref,
    inverse_ref,
    states_ref,
    written_ref,
    taps_ref,
    aux_ref,
    docs_ref,
    gain_ref,
    grad_proj_ref,
    grad_logit_ref,
    conv_grad_ref,
    gain_grad_ref,
    window_ref,
    masked_ref,
    state_ref,
):
    width = heads * DK
    chunks = grad_ref.shape[0] // CHUNK
    state_ref[...] = jnp.zeros_like(state_ref)
    masked_ref[...] = jnp.zeros_like(masked_ref)
    conv_grad_ref[...] = jnp.zeros_like(conv_grad_ref)
    gain_grad_ref[...] = jnp.zeros_like(gain_grad_ref)

    def chunk(step, _):
        n = chunks - 1 - step
        rows = pl.ds(pl.multiple_of(n * CHUNK, CHUNK), CHUNK)
        before = jnp.maximum(n - 1, 0)
        aux = aux_ref[rows]
        grad_normed = mul(grad_ref[rows], o_ref[...], (1, 0))
        prior = proj_ref[pl.ds(pl.multiple_of(before * CHUNK + CHUNK - 16, 16), 16)]
        window_ref[0:PAD] = prior.astype(jnp.float32)[16 - PAD :]
        window_ref[PAD : PAD + CHUNK] = proj_ref[rows].astype(jnp.float32)
        window = window_ref[...]
        taps = taps_ref[...]
        conv = convolved(window, taps, aux)
        conv_sig = sigmoid(conv)
        act = conv * conv_sig
        valid, carry, tail = aux[:, 1:2], aux[:, 2:3], aux[:, 3:4]
        carry_last = carry[CHUNK - 1 :]
        lower, strict, down, along = chunk_masks(aux[:, 0:1], docs_ref[pl.ds(n, 1)])
        rate_sig = sigmoid(logit_ref[rows])
        rate_all = rate_sig * valid
        lanes = lax.broadcasted_iota(jnp.int32, rate_all.shape, 1)
        grad_rates = jnp.zeros_like(rate_all)
        grads = [[], [], []]
        for h in range(heads):
            columns = pl.ds(h * DK, DK)
            mixed = mixed_ref[rows, columns]
            mix_scale, mix_live = mix_norm(mixed)
            grad_out = grad_normed[:, h * DK : (h + 1) * DK]
            scaled = mixed * mix_scale
            gain_grad_ref[...] += jnp.sum(grad_out * scaled, axis=0, keepdims=True)
            weighted = gain_ref[...] * grad_out
            grad_mix = (
                mix_scale * weighted
                - scaled
                * (mix_scale * mix_scale * mix_live)
                * jnp.mean(weighted * mixed, axis=1, keepdims=True)
            ) * valid
            query_raw = act[:, h * DK : (h + 1) * DK]
            key_raw = act[:, width + h * DK : width + (h + 1) * DK]
            value = act[:, 2 * width + h * DK : 2 * width + (h + 1) * DK]
            query_scale, query_live = unit_scale(query_raw)
            key_scale, key_live = unit_scale(key_raw)
            query = query_raw * query_scale
            key = key_raw * key_scale
            rate = rate_all[:, h : h + 1]
            inverse = inverse_ref[h, n]
            state = states_ref[h, n]
            written = written_ref[h, n]
            grad_state = state_ref[h]
            tail_key = tail * key
            carried_key = carry * key
            scores = plain(query, key, (1, 1)) * lower
            pulled = plain(scores, grad_mix, (0, 0)) + fine(tail_key, grad_state)
            solved = fine(inverse, pulled, (0, 0))
            state_ref[h] = (
                carry_last * grad_state
                + plain(carry * query, grad_mix, (0, 0))
                - fine(rate * carried_key, solved, (0, 0))
            )
            grad_scores = plain(grad_mix, written, (1, 1)) * lower
            grad_query = carry * plain(grad_mix, state, (1, 1)) + plain(grad_scores, key)
            guess_error = value - plain(carried_key, state)
            gram = plain(key, key, (1, 1)) * strict
            grad_system = plain(solved, written, (1, 1)) * strict
            grad_rate = jnp.sum(solved * guess_error, axis=1, keepdims=True) - jnp.sum(
                grad_system * gram, axis=1, keepdims=True
            )
            grad_gram = rate * grad_system
            grad_key = (
                plain(grad_scores, query, (0, 0))
                + tail * plain(written, grad_state, (1, 1))
                - rate * carry * plain(solved, state, (1, 1))
                - plain(grad_gram, key)
                - plain(grad_gram, key, (0, 0))
            )
            grads[0].append(
                query_scale
                * (
                    grad_query
                    - query
                    * query_live
                    * jnp.sum(query * grad_query, axis=1, keepdims=True)
                )
            )
            grads[1].append(
                key_scale
                * (grad_key - key * key_live * jnp.sum(key * grad_key, axis=1, keepdims=True))
            )
            grads[2].append(rate * solved)
            grad_rates = grad_rates + jnp.where(lanes == h, grad_rate, 0.0)
        grad_act = jnp.concatenate(grads[0] + grads[1] + grads[2], axis=1)
        grad_conv = grad_act * conv_sig * (1.0 + conv * (1.0 - conv_sig))
        grad_proj = taps[0:1] * grad_conv
        conv_grad_ref[0:1] += jnp.sum(
            grad_conv * window[PAD : PAD + CHUNK], axis=0, keepdims=True
        )
        for tap in range(1, KW):
            masked = grad_conv * tap_mask(aux, tap)
            conv_grad_ref[tap : tap + 1] += jnp.sum(
                masked * window[PAD - tap : PAD - tap + CHUNK], axis=0, keepdims=True
            )
            masked_ref[tap - 1, CHUNK : CHUNK + PAD] = masked_ref[tap - 1, 0:PAD]
            masked_ref[tap - 1, 0:CHUNK] = masked
            grad_proj = grad_proj + taps[tap : tap + 1] * masked_ref[tap - 1, tap : tap + CHUNK]
        grad_proj_ref[rows] = grad_proj.astype(jnp.bfloat16)
        grad_logit_ref[rows] = (grad_rates * rate_sig * (1.0 - rate_sig) * valid).astype(
            jnp.bfloat16
        )
        return 0

    lax.fori_loop(0, chunks, chunk, 0)


def in_vmem(count):
    return [pl.BlockSpec(memory_space=pltpu.VMEM)] * count


def run_forward(n1, qkv, beta, taps, aux, docs, gain):
    row_len, heads = n1.shape[0], qkv.shape[1] // (3 * DK)
    chunks, width, f32 = row_len // CHUNK, heads * DK, jnp.float32
    shapes = (
        ((row_len, 3 * width), jnp.bfloat16),
        ((row_len, beta.shape[0]), f32),
        ((row_len, width), f32),
        ((row_len, width), jnp.bfloat16),
        ((heads, chunks, CHUNK, CHUNK), f32),
        ((heads, chunks, DK, DK), f32),
        ((heads, chunks, CHUNK, DK), f32),
    )
    return pl.pallas_call(
        functools.partial(forward_kernel, heads),
        out_shape=[jax.ShapeDtypeStruct(*shape) for shape in shapes],
        in_specs=in_vmem(7),
        out_specs=in_vmem(len(shapes)),
        scratch_shapes=[
            pltpu.VMEM((PAD + CHUNK, 3 * width), f32),
            pltpu.VMEM((heads, DK, DK), f32),
        ],
        compiler_params=pltpu.CompilerParams(vmem_limit_bytes=48 * 1024 * 1024),
        name="mixer_forward",
    )(n1, qkv, beta, taps, aux, docs, gain)


def run_backward(grad, o_full, saved, taps, aux, docs, gain):
    row_len, heads = grad.shape[0], o_full.shape[1] // DK
    width, f32 = heads * DK, jnp.float32
    logit = saved[1]
    shapes = (
        ((row_len, 3 * width), jnp.bfloat16),
        (logit.shape, jnp.bfloat16),
        ((KW, 3 * width), f32),
        ((1, DK), f32),
    )
    return pl.pallas_call(
        functools.partial(backward_kernel, heads),
        out_shape=[jax.ShapeDtypeStruct(*shape) for shape in shapes],
        in_specs=in_vmem(12),
        out_specs=in_vmem(len(shapes)),
        scratch_shapes=[
            pltpu.VMEM((PAD + CHUNK, 3 * width), f32),
            pltpu.VMEM((KW - 1, CHUNK + PAD, 3 * width), f32),
            pltpu.VMEM((heads, DK, DK), f32),
        ],
        compiler_params=pltpu.CompilerParams(vmem_limit_bytes=48 * 1024 * 1024),
        name="mixer_backward",
    )(grad, o_full, *saved, taps, aux, docs, gain)


def row_aux(docs):
    f32 = jnp.float32
    chunks = docs.reshape(-1, CHUNK)
    prior = jnp.concatenate([jnp.full((1,), -1, jnp.int32), chunks[:-1, -1]])
    padded = jnp.concatenate([jnp.full((KW - 1,), -1, jnp.int32), docs])
    columns = [
        docs,
        docs < DOCS,
        (chunks == prior[:, None]).reshape(-1),
        (chunks == chunks[:, -1:]).reshape(-1),
    ] + [padded[KW - 1 - tap : KW - 1 - tap + docs.shape[0]] == docs for tap in range(1, KW)]
    columns = [column.astype(f32) for column in columns]
    columns += [jnp.zeros_like(columns[0])] * (8 - len(columns))
    return jnp.stack(columns, axis=1), chunks.astype(f32)


def swap_copy(source, target, send, recv, where):
    return pltpu.make_async_remote_copy(
        src_ref=source,
        dst_ref=target,
        send_sem=send,
        recv_sem=recv,
        device_id=where,
        device_id_type=pl.DeviceIdType.MESH,
    )


def greet(partners):
    barrier = pltpu.get_barrier_semaphore()
    for partner in partners:
        pl.semaphore_signal(
            barrier, inc=1, device_id=partner, device_id_type=pl.DeviceIdType.MESH
        )
    pl.semaphore_wait(barrier, len(partners))


def around(axis):
    count, place = lax.axis_size(axis), lax.axis_index(axis)
    return [lax.rem(place + by, count) for by in range(1, count)]


def small_sums_kernel(
    part_ref, out_ref, rows_ref, all_ref, send_row, recv_row, send_seq, recv_seq, send_tp, recv_tp
):
    row, seq, tp = (lax.axis_index(axis) for axis in ("row", "seq", "tp"))
    row_others, seq_others, tp_others = around("row"), around("seq"), around("tp")
    greet(
        [{"row": other} for other in row_others]
        + [{"seq": other} for other in seq_others]
        + [{"tp": other} for other in tp_others]
    )
    rows_ref[row] = part_ref[...]
    copies = [
        swap_copy(part_ref, rows_ref.at[row], send_row.at[i], recv_row.at[i], {"row": other})
        for i, other in enumerate(row_others)
    ]
    for copy in copies:
        copy.start()
    for copy in copies:
        copy.wait()
    total = rows_ref[0]
    for i in range(1, rows_ref.shape[0]):
        total = total + rows_ref[i]
    all_ref[tp, seq] = total
    copies = [
        swap_copy(
            all_ref.at[tp, seq], all_ref.at[tp, seq], send_seq.at[i], recv_seq.at[i], {"seq": other}
        )
        for i, other in enumerate(seq_others)
    ]
    for copy in copies:
        copy.start()
    for copy in copies:
        copy.wait()
    copies = [
        swap_copy(all_ref.at[tp], all_ref.at[tp], send_tp.at[i], recv_tp.at[i], {"tp": other})
        for i, other in enumerate(tp_others)
    ]
    for copy in copies:
        copy.start()
    for copy in copies:
        copy.wait()
    out_ref[...] = all_ref[...]


def run_small_sums(part):
    rows, seqs, tps = (lax.axis_size(axis) for axis in ("row", "seq", "tp"))
    dma = pltpu.SemaphoreType.DMA
    shape = (tps, seqs) + part.shape
    return pl.pallas_call(
        small_sums_kernel,
        out_shape=jax.ShapeDtypeStruct(shape, part.dtype),
        in_specs=in_vmem(1),
        out_specs=pl.BlockSpec(memory_space=pltpu.VMEM),
        scratch_shapes=[
            pltpu.VMEM((rows,) + part.shape, part.dtype),
            pltpu.VMEM(shape, part.dtype),
            dma((rows - 1,)),
            dma((rows - 1,)),
            dma((seqs - 1,)),
            dma((seqs - 1,)),
            dma((tps - 1,)),
            dma((tps - 1,)),
        ],
        compiler_params=pltpu.CompilerParams(collective_id=0, has_side_effects=True),
        name="small_sums",
    )(part)


def exchanged(parts, axis):
    count, place = lax.axis_size(axis), lax.axis_index(axis)
    came = [lax.dynamic_index_in_dim(parts, place, 0, keepdims=False)]
    for by in range(1, count):
        part = lax.dynamic_index_in_dim(parts, (place + by) % count, 0, keepdims=False)
        came.append(lax.ppermute(part, axis, [(i, (i + by) % count) for i in range(count)]))
    came = jnp.stack(came)
    order = (place - jnp.arange(count)) % count
    return jnp.concatenate(
        [lax.dynamic_slice_in_dim(came, order[j], 1, axis=0) for j in range(count)], axis=0
    )


def spread(shard, pieces, axis):
    rows, width = shard.shape
    return exchanged(shard.reshape(rows, pieces, width // pieces).transpose(1, 0, 2), axis)


def gathered(shard):
    pieces = lax.axis_size("seq")
    parts = spread(shard, pieces, "seq")
    whole = lax.all_gather(parts, "row", axis=0, tiled=True)
    return whole.reshape(-1, whole.shape[-1])


def returned(part):
    pieces = lax.axis_size("seq")
    rows = part.shape[0] // (pieces * lax.axis_size("row"))
    own = lax.psum_scatter(part, "row", scatter_dimension=0, tiled=True)
    return exchanged(own.reshape(pieces, rows, -1), "seq")


def token_gather(own):
    return lax.all_gather(own, ("seq", "tp"), axis=0, tiled=True)


def token_sum(term):
    return lax.psum_scatter(
        term.astype(jnp.bfloat16), ("seq", "tp"), scatter_dimension=0, tiled=True
    ).astype(jnp.float32)


def both_cores(own):
    cores = lax.axis_size("tp")
    if cores == 1:
        return own
    other = lax.ppermute(own, "tp", [(0, 1), (1, 0)])
    first = lax.axis_index("tp") == 0
    return jnp.concatenate([jnp.where(first, own, other), jnp.where(first, other, own)], axis=0)


def shifted(rows, by):
    if by == 0:
        return rows
    pad = jnp.zeros((abs(by),) + rows.shape[1:], rows.dtype)
    if by > 0:
        return jnp.concatenate([pad, rows[:-by]], axis=0)
    return jnp.concatenate([rows[-by:], pad], axis=0)


def local_heads(
    block_input,
    grad_out,
    doc_lengths,
    attn_gain,
    mlp_gain,
    out_gain,
    conv_weight,
    qkv_weight,
    beta_weight,
    o_weight,
    gate_up_weight,
    down_weight,
):
    tok_rows, model_width = block_input.shape[1:]
    pieces, cores = lax.axis_size("seq"), lax.axis_size("tp")
    piece, core = lax.axis_index("seq"), lax.axis_index("tp")
    row_len = pieces * tok_rows
    own_rows = tok_rows // cores
    shard_rows = qkv_weight.shape[1]
    half_width = qkv_weight.shape[2]
    width = half_width // pieces
    heads = width // DK
    units = gate_up_weight.shape[2] // pieces
    f32, b16 = jnp.float32, jnp.bfloat16

    qkv_parts = qkv_weight.reshape(3, shard_rows, pieces, width).transpose(1, 2, 0, 3)
    qkv_full = gathered(qkv_parts.reshape(shard_rows, -1))
    beta_full = lax.all_gather(beta_weight.T, ("row", "seq"), axis=1, tiled=True)
    beta_full = lax.dynamic_slice_in_dim(beta_full, piece * heads, heads, axis=0)
    beta_full = jnp.pad(beta_full, ((0, 16 - heads), (0, 0)))
    o_full = gathered(o_weight.T)
    gate_up_parts = gate_up_weight.reshape(2, shard_rows, pieces, units).transpose(1, 2, 0, 3)
    gate_up_full = gathered(gate_up_parts.reshape(shard_rows, -1))
    down_full = gathered(down_weight.T)

    ends = jnp.cumsum(doc_lengths[0])
    places = jnp.arange(row_len, dtype=jnp.int32)
    docs = jnp.sum((places[:, None] >= ends[None, :]).astype(jnp.int32), axis=1)
    aux, doc_rows = row_aux(docs)
    gain_row = out_gain[None]
    taps = lax.dynamic_slice_in_dim(conv_weight, piece * width, width, axis=2)
    taps = taps.transpose(1, 0, 2).reshape(KW, 3 * width)

    x_rows = lax.dynamic_slice_in_dim(block_input[0], core * own_rows, own_rows, axis=0)
    x_rows = x_rows.astype(f32)
    g_rows = lax.dynamic_slice_in_dim(grad_out[0], core * own_rows, own_rows, axis=0)
    scale_one = norm_scale(x_rows)
    normed_one = token_gather((x_rows * scale_one * attn_gain).astype(b16))
    g_full = token_gather(g_rows)
    proj, logit, mixed, normed_mix, inverse, states, written = run_forward(
        normed_one, qkv_full, beta_full, taps, aux, doc_rows, gain_row
    )
    o_term = jnp.einsum("te,de->td", normed_mix, o_full, preferred_element_type=f32)
    resid = x_rows + token_sum(o_term)
    scale_two = norm_scale(resid)
    normed_two = token_gather((resid * scale_two * mlp_gain).astype(b16))
    gate_up = jnp.dot(normed_two, gate_up_full, preferred_element_type=f32)
    gate, up = gate_up[:, :units], gate_up[:, units:]
    gate_sig = jax.nn.sigmoid(gate)
    gate_act = gate * gate_sig
    hidden = (gate_act * up).astype(b16)
    grad_hidden = jnp.dot(g_full, down_full, preferred_element_type=f32)
    grad_gate = grad_hidden * up * gate_sig * (1.0 + gate * (1.0 - gate_sig))
    grad_up = grad_hidden * gate_act
    grad_gate_up = jnp.concatenate([grad_gate, grad_up], axis=1).astype(b16)
    two_term = jnp.einsum("tf,df->td", grad_gate_up, gate_up_full, preferred_element_type=f32)
    grad_two = token_sum(two_term)
    mlp_gain_part = jnp.sum(grad_two * resid * scale_two, axis=0)
    grad_resid = g_rows.astype(f32) + norm_back(resid, scale_two, mlp_gain, grad_two)
    grad_attn = token_gather(grad_resid.astype(b16))
    down_term = jnp.einsum("tf,df->td", hidden, down_full, preferred_element_type=f32)
    result = both_cores((resid + token_sum(down_term)).astype(b16))
    down_part = jnp.einsum("td,tf->df", g_full, hidden, preferred_element_type=f32)
    gate_up_part = jnp.einsum("td,tf->df", normed_two, grad_gate_up, preferred_element_type=f32)
    o_part = jnp.einsum("td,te->de", grad_attn, normed_mix, preferred_element_type=f32)
    grad_proj, grad_logit, conv_part, out_gain_part = run_backward(
        grad_attn,
        o_full,
        (proj, logit, mixed, inverse, states, written),
        taps,
        aux,
        doc_rows,
        gain_row,
    )
    one_term = jnp.einsum("te,de->td", grad_proj, qkv_full, preferred_element_type=f32)
    one_term = one_term + jnp.einsum("th,hd->td", grad_logit, beta_full, preferred_element_type=f32)
    grad_one = token_sum(one_term)
    attn_gain_part = jnp.sum(grad_one * x_rows * scale_one, axis=0)
    input_grad = both_cores(
        (grad_resid + norm_back(x_rows, scale_one, attn_gain, grad_one)).astype(b16)
    )
    qkv_part = jnp.einsum("td,te->de", normed_one, grad_proj, preferred_element_type=f32)
    beta_part = jnp.einsum("td,th->hd", normed_one, grad_logit, preferred_element_type=f32)
    packed = jnp.concatenate(
        [
            conv_part.reshape(-1, 128),
            attn_gain_part.reshape(-1, 128),
            mlp_gain_part.reshape(-1, 128),
            beta_part[:heads].reshape(-1, 128),
            jnp.pad(out_gain_part, ((0, 7), (0, 0))),
        ],
        axis=0,
    )
    small = run_small_sums(packed)
    at = KW * 3 * width // 128
    span = model_width // 128
    conv_grad = small[:, :, :at].reshape(cores, pieces, KW, 3, width)
    conv_grad = conv_grad.transpose(3, 2, 0, 1, 4).reshape(3, KW, model_width)
    sums = jnp.sum(small[:, :, at:], axis=(0, 1))
    attn_gain_grad = sums[:span].reshape(-1)
    mlp_gain_grad = sums[span : 2 * span].reshape(-1)
    out_gain_grad = sums[(2 + heads) * span]
    beta_sum = lax.dynamic_index_in_dim(small, core, 0, keepdims=False)
    beta_sum = beta_sum[:, at + 2 * span : at + (2 + heads) * span]
    beta_sum = beta_sum.reshape(pieces * heads, model_width)
    beta_sum = lax.dynamic_slice_in_dim(
        beta_sum, (lax.axis_index("row") * pieces + piece) * shard_rows, shard_rows, axis=1
    ).T
    down_sum = returned(down_part.astype(b16))
    gate_up_sum = returned(gate_up_part.astype(b16)).reshape(pieces, shard_rows, 2, units)
    o_sum = returned(o_part.astype(b16))
    qkv_sum = returned(qkv_part.astype(b16)).reshape(pieces, shard_rows, 3, width)
    return (
        result[None],
        input_grad[None],
        attn_gain_grad,
        mlp_gain_grad,
        out_gain_grad,
        conv_grad,
        qkv_sum.transpose(2, 1, 0, 3).reshape(3, shard_rows, -1).astype(f32),
        beta_sum,
        o_sum.transpose(0, 2, 1).reshape(-1, shard_rows).astype(f32),
        gate_up_sum.transpose(2, 1, 0, 3).reshape(2, shard_rows, -1).astype(f32),
        down_sum.transpose(0, 2, 1).reshape(-1, shard_rows).astype(f32),
    )


def splits_heads(mesh, heads=16, units=5632):
    return (
        mesh.shape["tp"] == 2
        and heads % (mesh.shape["seq"] * 2) == 0
        and units % (mesh.shape["seq"] * 2) == 0
    )


def solution(mesh):
    in_specs = (
        P("row", "seq", None),
        P("row", "seq", None),
        P("row", None),
        P(),
        P(),
        P(),
        P(None, None, "tp"),
        P(None, ("row", "seq"), "tp"),
        P(("row", "seq"), "tp"),
        P("tp", ("row", "seq")),
        P(None, ("row", "seq"), "tp"),
        P("tp", ("row", "seq")),
    )
    out_specs = (
        P("row", "seq", None),
        P("row", "seq", None),
        P(),
        P(),
        P(),
        P(),
        P(None, ("row", "seq"), "tp"),
        P(("row", "seq"), "tp"),
        P("tp", ("row", "seq")),
        P(None, ("row", "seq"), "tp"),
        P("tp", ("row", "seq")),
    )
    local = local_heads if splits_heads(mesh) else local_pieces
    return jax.shard_map(local, mesh=mesh, in_specs=in_specs, out_specs=out_specs, check_vma=False)
```

```python
import functools

import jax
import jax.numpy as jnp
from jax import lax
from jax.experimental import pallas as pl
from jax.experimental.pallas import tpu as pltpu
from jax.sharding import PartitionSpec as P

DK = 128
KW = 4
GROUP = 64
DOCS = 8


eps = 1e-06
mix_floor = 0.01
precise = lax.Precision.HIGHEST


def from_behind(shard, axis, by):
    devices = lax.axis_size(axis)
    pairs = [(i, i + by) for i in range(devices) if 0 <= i + by < devices]
    return lax.ppermute(shard, axis, pairs)


def prefix(shard, axis, combine, identity, reverse):
    devices, place = (lax.axis_size(axis), lax.axis_index(axis))
    everything = jax.tree.map(
        lambda part, kind: lax.all_gather(part.astype(kind), axis),
        shard,
        (jnp.bfloat16, jnp.bfloat16),
    )
    start = jax.tree.map(
        lambda part, zero: jnp.broadcast_to(jnp.asarray(zero, part.dtype), part.shape),
        shard,
        identity,
    )

    def step(k, before):
        at = devices - 1 - k if reverse else k
        reached = at > place if reverse else at < place
        new = combine(
            before, jax.tree.map(lambda part, own: part[at].astype(own.dtype), everything, shard)
        )
        return jax.tree.map(lambda a, b: jnp.where(reached, a, b), new, before)

    return lax.fori_loop(0, devices, step, start)


def norm_scale(values):
    return lax.rsqrt(jnp.mean(values * values, axis=-1, keepdims=True) + eps)


def norm_back(values, scale, gain, grad):
    weighted = gain * grad
    return scale * weighted - values * scale**3 * jnp.mean(
        weighted * values, axis=-1, keepdims=True
    )


def batch_mul(left, right):
    return jnp.einsum("hij,hjk->hik", left, right, precision=precise)


def batch_mul_t(left, right):
    return jnp.einsum("hji,hjk->hik", left, right, precision=precise)


def compose(earlier, later):
    return (batch_mul(later[0], earlier[0]), batch_mul(later[0], earlier[1]) + later[1])


def over_heads(function, shared):
    return jax.vmap(jax.vmap(function), in_axes=shared)


def tp_total(term):
    return lax.psum(term.astype(jnp.bfloat16), "tp").astype(jnp.float32)


def group_parts(key_rows, value_rows, rates, same_doc, carry_mask):
    size = key_rows.shape[0]
    strict = jnp.tril(jnp.ones((size, size), jnp.float32), -1) * same_doc
    inner = jnp.dot(key_rows, key_rows.T, precision=precise)
    system = jnp.eye(size, dtype=jnp.float32) + rates[:, None] * inner * strict
    right_side = jnp.concatenate(
        [rates[:, None] * value_rows, (rates * carry_mask)[:, None] * key_rows], axis=1
    )
    solved = jax.scipy.linalg.solve_triangular(system, right_side, lower=True)
    base_rows = solved[:, : value_rows.shape[1]]
    wy_rows = solved[:, value_rows.shape[1] :]
    tail_keys = same_doc[size - 1][:, None] * key_rows
    identity_mat = jnp.eye(key_rows.shape[1], dtype=jnp.float32)
    transition = carry_mask[size - 1] * identity_mat - jnp.dot(
        tail_keys.T, wy_rows, precision=precise
    )
    contribution = jnp.dot(tail_keys.T, base_rows, precision=precise)
    return (transition, contribution, base_rows, wy_rows)


def group_output(queries, key_rows, same_doc, carry_mask, base_rows, wy_rows, state_in):
    size = key_rows.shape[0]
    lower = jnp.tril(jnp.ones((size, size), jnp.float32)) * same_doc
    written = base_rows - jnp.dot(wy_rows, state_in, precision=precise)
    scores = jnp.dot(queries, key_rows.T, precision=precise) * lower
    carried = carry_mask[:, None] * jnp.dot(queries, state_in, precision=precise)
    return carried + jnp.dot(scores, written, precision=precise)


def group_full(queries, key_rows, value_rows, rates, same_doc, carry_mask, state_in):
    transition, contribution, base_rows, wy_rows = group_parts(
        key_rows, value_rows, rates, same_doc, carry_mask
    )
    outputs = group_output(queries, key_rows, same_doc, carry_mask, base_rows, wy_rows, state_in)
    return (outputs, jnp.dot(transition, state_in, precision=precise) + contribution)


def state_pull(queries, key_rows, same_doc, carry_mask, wy_rows, grad_rows):
    size = key_rows.shape[0]
    lower = jnp.tril(jnp.ones((size, size), jnp.float32)) * same_doc
    scores = jnp.dot(queries, key_rows.T, precision=precise) * lower
    pulled = jnp.dot(scores.T, grad_rows, precision=precise)
    direct = jnp.dot((carry_mask[:, None] * queries).T, grad_rows, precision=precise)
    return direct - jnp.dot(wy_rows.T, pulled, precision=precise)


def group_grads(
    queries, key_rows, value_rows, rates, same_doc, carry_mask, state_in, grad_rows, grad_end
):

    def group_local(query_in, key_in, value_in, rate_in):
        return group_full(query_in, key_in, value_in, rate_in, same_doc, carry_mask, state_in)

    outputs, pullback = jax.vjp(group_local, queries, key_rows, value_rows, rates)
    return pullback((grad_rows, grad_end))


def local_pieces(
    block_input,
    grad_out,
    doc_lengths,
    attn_gain,
    mlp_gain,
    out_gain,
    conv_weight,
    qkv_weight,
    beta_weight,
    o_weight,
    gate_up_weight,
    down_weight,
):
    tok_rows = block_input.shape[1]
    model_width = block_input.shape[2]
    blocks = tok_rows // GROUP
    unit_floor = DK / 16.0
    x_rows = block_input[0].astype(jnp.float32)
    grad_rows_out = grad_out[0]
    qkv_full, beta_full, o_full, gate_up_full, down_full = (
        lax.all_gather(qkv_weight, ("row", "seq"), axis=1, tiled=True),
        lax.all_gather(beta_weight, ("row", "seq"), axis=0, tiled=True),
        lax.all_gather(o_weight, ("row", "seq"), axis=1, tiled=True),
        lax.all_gather(gate_up_weight, ("row", "seq"), axis=1, tiled=True),
        lax.all_gather(down_weight, ("row", "seq"), axis=1, tiled=True),
    )
    local_width = qkv_full.shape[2]
    head_count = local_width // DK
    lead_mask = (lax.axis_index("tp") == 0).astype(jnp.float32)
    ends = jnp.cumsum(doc_lengths[0])
    places = (
        lax.axis_index("seq") * tok_rows + jnp.arange(tok_rows + KW - 1, dtype=jnp.int32) - (KW - 1)
    )
    doc_ids = jnp.sum((places[:, None] >= ends[None, :]).astype(jnp.int32), axis=1)
    doc_ids = jnp.where(places < 0, -1, doc_ids)
    own_docs = doc_ids[KW - 1 :]
    prior_docs = doc_ids[KW - 2 : KW - 2 + tok_rows]
    valid = (own_docs < DOCS).astype(jnp.float32)
    fresh = (own_docs != prior_docs).astype(jnp.int32)
    tap_masks = [
        (doc_ids[KW - 1 - tap : KW - 1 - tap + tok_rows] == own_docs).astype(jnp.float32)
        for tap in range(KW)
    ]
    own_blocks = own_docs.reshape(blocks, GROUP)
    same_doc = (own_blocks[:, :, None] == own_blocks[:, None, :]).astype(jnp.float32)
    carry_mask = (jnp.cumsum(fresh.reshape(blocks, GROUP), axis=1) == 0).astype(jnp.float32)

    def to_blocks(array):
        return array.reshape(blocks, GROUP, head_count, -1).transpose(2, 0, 1, 3)

    def from_blocks(array):
        return array.transpose(1, 2, 0, 3).reshape(tok_rows, head_count, -1)

    scale_one = norm_scale(x_rows)
    normed_one = (x_rows * scale_one * attn_gain).astype(jnp.bfloat16)
    proj_low = jnp.einsum(
        "td,cde->cte", normed_one, qkv_full, preferred_element_type=jnp.float32
    ).astype(jnp.bfloat16)
    logit = jnp.dot(normed_one, beta_full, preferred_element_type=jnp.float32)
    rim_rows = from_behind(proj_low[:, tok_rows - (KW - 1) :, :], "seq", 1)
    extended = jnp.concatenate([rim_rows, proj_low], axis=1).astype(jnp.float32)
    conv_out = jnp.zeros((3, tok_rows, local_width), jnp.float32)
    for tap in range(KW):
        window = extended[:, KW - 1 - tap : KW - 1 - tap + tok_rows]
        conv_out = (
            conv_out + conv_weight[:, tap][:, None, :] * window * tap_masks[tap][None, :, None]
        )
    conv_sig = jax.nn.sigmoid(conv_out)
    activated = conv_out * conv_sig
    query_raw = activated[0].reshape(tok_rows, head_count, DK)
    key_raw = activated[1].reshape(tok_rows, head_count, DK)
    query_sq = jnp.sum(query_raw * query_raw, axis=-1, keepdims=True)
    key_sq = jnp.sum(key_raw * key_raw, axis=-1, keepdims=True)
    query_scale = lax.rsqrt(jnp.maximum(query_sq, unit_floor))
    key_scale = lax.rsqrt(jnp.maximum(key_sq, unit_floor))
    query_live = (query_sq > unit_floor).astype(jnp.float32)
    key_live = (key_sq > unit_floor).astype(jnp.float32)
    query_blocks = to_blocks(query_raw * query_scale)
    key_blocks = to_blocks(key_raw * key_scale)
    value_blocks = to_blocks(activated[2].reshape(tok_rows, head_count, DK))
    rate_sig = jax.nn.sigmoid(logit)
    rate_blocks = (rate_sig * valid[:, None]).reshape(blocks, GROUP, head_count).transpose(2, 0, 1)
    transition, contribution, base_rows, wy_rows = over_heads(group_parts, (0, 0, 0, None, None))(
        key_blocks, value_blocks, rate_blocks, same_doc, carry_mask
    )
    identity_mat = jnp.broadcast_to(jnp.eye(DK, dtype=jnp.float32), (head_count, DK, DK))
    zero_state = jnp.zeros((head_count, DK, DK), jnp.float32)
    transition_steps = jnp.moveaxis(transition, 1, 0)

    def chain(running, pair):
        product, partial_state = running
        step_trans, step_contrib = pair
        advanced = (
            batch_mul(step_trans, product),
            batch_mul(step_trans, partial_state) + step_contrib,
        )
        return (advanced, (product, partial_state))

    (dev_trans, dev_state), (products, partials) = lax.scan(
        chain, (identity_mat, zero_state), (transition_steps, jnp.moveaxis(contribution, 1, 0))
    )
    incoming = prefix((dev_trans, dev_state), "seq", compose, (identity_mat, zero_state), False)[1]
    group_starts = partials + jnp.einsum("nhij,hjk->nhik", products, incoming, precision=precise)
    start_blocks = jnp.moveaxis(group_starts, 0, 1)
    mix_blocks = over_heads(group_output, (0, 0, None, None, 0, 0, 0))(
        query_blocks, key_blocks, same_doc, carry_mask, base_rows, wy_rows, start_blocks
    )
    mixed = from_blocks(mix_blocks) * valid[:, None, None]
    mix_sq = jnp.mean(mixed * mixed, axis=-1, keepdims=True)
    mix_scale = lax.rsqrt(jnp.maximum(mix_sq, mix_floor))
    mix_live = (mix_sq > mix_floor).astype(jnp.float32)
    normed_mix = (mixed * mix_scale * out_gain).astype(jnp.bfloat16).reshape(tok_rows, local_width)
    o_term = jnp.dot(normed_mix, o_full, preferred_element_type=jnp.float32)
    resid = x_rows + tp_total(o_term)
    scale_two = norm_scale(resid)
    normed_local = (resid * scale_two * mlp_gain).astype(jnp.bfloat16)
    gate_up = jnp.einsum(
        "td,cdf->ctf", normed_local, gate_up_full, preferred_element_type=jnp.float32
    )
    gate_sig = jax.nn.sigmoid(gate_up[0])
    gate_act = gate_up[0] * gate_sig
    hidden = (gate_act * gate_up[1]).astype(jnp.bfloat16)
    down_term = jnp.dot(hidden, down_full, preferred_element_type=jnp.float32)
    mlp_out = tp_total(down_term)
    result = (resid + mlp_out).astype(jnp.bfloat16)
    grad_hidden = jnp.einsum(
        "td,fd->tf", grad_rows_out, down_full, preferred_element_type=jnp.float32
    )
    grad_gate = grad_hidden * gate_up[1] * gate_sig * (1.0 + gate_up[0] * (1.0 - gate_sig))
    grad_up = grad_hidden * gate_act
    grad_gate_up = jnp.stack([grad_gate, grad_up]).astype(jnp.bfloat16)
    down_part = jnp.einsum("tf,td->fd", hidden, grad_rows_out, preferred_element_type=jnp.float32)
    gate_up_part = jnp.einsum(
        "td,ctf->cdf", normed_local, grad_gate_up, preferred_element_type=jnp.float32
    )
    two_term = jnp.einsum(
        "ctf,cdf->td", grad_gate_up, gate_up_full, preferred_element_type=jnp.float32
    )
    grad_two = tp_total(two_term)
    mlp_gain_part = jnp.sum(grad_two * resid * scale_two, axis=0)
    grad_resid = grad_rows_out.astype(jnp.float32) + norm_back(resid, scale_two, mlp_gain, grad_two)
    grad_attn_local = grad_resid.astype(jnp.bfloat16)
    o_part = jnp.einsum(
        "te,td->ed", normed_mix, grad_attn_local, preferred_element_type=jnp.float32
    )
    grad_normed = jnp.einsum(
        "td,ed->te", grad_attn_local, o_full, preferred_element_type=jnp.float32
    ).reshape(tok_rows, head_count, DK)
    out_gain_part = jnp.sum(grad_normed * mixed * mix_scale, axis=(0, 1))
    weighted_mix = out_gain * grad_normed
    grad_mixed = (
        mix_scale * weighted_mix
        - mixed * mix_scale**3 * mix_live * jnp.mean(weighted_mix * mixed, axis=-1, keepdims=True)
    ) * valid[:, None, None]
    grad_blocks = to_blocks(grad_mixed)
    pulls = over_heads(state_pull, (0, 0, None, None, 0, 0))(
        query_blocks, key_blocks, same_doc, carry_mask, wy_rows, grad_blocks
    )

    def back_chain(running, pair):
        grad_end, product = running
        step_trans, step_pull = pair
        advanced = (step_pull + batch_mul_t(step_trans, grad_end), batch_mul_t(step_trans, product))
        return (advanced, (grad_end, product))

    (dev_pull, dev_back), (grad_ends, back_products) = lax.scan(
        back_chain,
        (zero_state, identity_mat),
        (transition_steps, jnp.moveaxis(pulls, 1, 0)),
        reverse=True,
    )
    outgoing = prefix((dev_back, dev_pull), "seq", compose, (identity_mat, zero_state), True)[1]
    end_grads = grad_ends + jnp.einsum("nhij,hjk->nhik", back_products, outgoing, precision=precise)
    grad_query, grad_key, grad_value, grad_rate = over_heads(
        group_grads, (0, 0, 0, 0, None, None, 0, 0, 0)
    )(
        query_blocks,
        key_blocks,
        value_blocks,
        rate_blocks,
        same_doc,
        carry_mask,
        start_blocks,
        grad_blocks,
        jnp.moveaxis(end_grads, 0, 1),
    )
    grad_query = from_blocks(grad_query)
    grad_key = from_blocks(grad_key)
    grad_query_raw = query_scale * grad_query - query_raw * query_scale**3 * query_live * jnp.sum(
        query_raw * grad_query, axis=-1, keepdims=True
    )
    grad_key_raw = key_scale * grad_key - key_raw * key_scale**3 * key_live * jnp.sum(
        key_raw * grad_key, axis=-1, keepdims=True
    )
    grad_activated = jnp.stack(
        [
            grad_query_raw.reshape(tok_rows, local_width),
            grad_key_raw.reshape(tok_rows, local_width),
            from_blocks(grad_value).reshape(tok_rows, local_width),
        ]
    )
    grad_conv = grad_activated * conv_sig * (1.0 + conv_out * (1.0 - conv_sig))
    grad_extended = jnp.zeros((3, tok_rows + KW - 1, local_width), jnp.float32)
    tap_grads = []
    for tap in range(KW):
        masked = grad_conv * tap_masks[tap][None, :, None]
        window = extended[:, KW - 1 - tap : KW - 1 - tap + tok_rows]
        tap_grads.append(jnp.sum(masked * window, axis=1))
        grad_extended = grad_extended + jnp.pad(
            conv_weight[:, tap][:, None, :] * masked, ((0, 0), (KW - 1 - tap, tap), (0, 0))
        )
    conv_part = jnp.stack(tap_grads, axis=1)
    rim_back = from_behind(grad_extended[:, : KW - 1], "seq", -1)
    grad_proj = jnp.concatenate(
        [grad_extended[:, KW - 1 : tok_rows], grad_extended[:, tok_rows:] + rim_back], axis=1
    ).astype(jnp.bfloat16)
    rate_grad = grad_rate.transpose(1, 2, 0).reshape(tok_rows, head_count)
    grad_logit = (rate_grad * valid[:, None] * rate_sig * (1.0 - rate_sig)).astype(jnp.bfloat16)
    qkv_part = jnp.einsum("td,cte->cde", normed_one, grad_proj, preferred_element_type=jnp.float32)
    beta_part = jnp.einsum("td,th->dh", normed_one, grad_logit, preferred_element_type=jnp.float32)
    grad_one_part = jnp.einsum(
        "cte,cde->td", grad_proj, qkv_full, preferred_element_type=jnp.float32
    ) + jnp.einsum("th,dh->td", grad_logit, beta_full, preferred_element_type=jnp.float32)
    grad_one = tp_total(grad_one_part)
    attn_gain_part = jnp.sum(grad_one * x_rows * scale_one, axis=0)
    input_local = (grad_resid + norm_back(x_rows, scale_one, attn_gain, grad_one)).astype(
        jnp.bfloat16
    )
    conv_whole = lax.dynamic_update_slice(
        jnp.zeros((3, KW, model_width), jnp.float32),
        conv_part,
        (0, 0, lax.axis_index("tp") * local_width),
    )
    attn_gain_grad, mlp_gain_grad, out_gain_grad, conv_grad = lax.psum(
        (attn_gain_part * lead_mask, mlp_gain_part * lead_mask, out_gain_part, conv_whole),
        ("row", "seq", "tp"),
    )
    qkv_sum, beta_sum, o_sum, gate_up_sum, down_sum = (
        lax.psum_scatter(
            qkv_part.astype(jnp.bfloat16), ("row", "seq"), scatter_dimension=1, tiled=True
        ).astype(jnp.float32),
        lax.psum_scatter(
            beta_part.astype(jnp.bfloat16), ("row", "seq"), scatter_dimension=0, tiled=True
        ).astype(jnp.float32),
        lax.psum_scatter(
            o_part.astype(jnp.bfloat16), ("row", "seq"), scatter_dimension=1, tiled=True
        ).astype(jnp.float32),
        lax.psum_scatter(
            gate_up_part.astype(jnp.bfloat16), ("row", "seq"), scatter_dimension=1, tiled=True
        ).astype(jnp.float32),
        lax.psum_scatter(
            down_part.astype(jnp.bfloat16), ("row", "seq"), scatter_dimension=1, tiled=True
        ).astype(jnp.float32),
    )
    return (
        result[None],
        input_local[None],
        attn_gain_grad,
        mlp_gain_grad,
        out_gain_grad,
        conv_grad,
        qkv_sum,
        beta_sum,
        o_sum,
        gate_up_sum,
        down_sum,
    )


CHUNK = 128
PAD = 8


def mul(left, right, dims, precision=None):
    return lax.dot_general(
        left, right, ((dims[:1], dims[1:]), ((), ())), precision=precision, preferred_element_type=jnp.float32
    )


def fine(left, right, dims=(1, 0)):
    return mul(left, right, dims, precise)


def plain(left, right, dims=(1, 0)):
    return mul(left.astype(jnp.bfloat16), right.astype(jnp.bfloat16), dims)


def chunk_masks(doc_col, doc_row):
    same = doc_col == doc_row
    down = lax.broadcasted_iota(jnp.int32, (CHUNK, CHUNK), 0)
    along = lax.broadcasted_iota(jnp.int32, (CHUNK, CHUNK), 1)
    lower = jnp.where(same & (down >= along), 1.0, 0.0)
    strict = jnp.where(same & (down > along), 1.0, 0.0)
    return lower, strict, down, along


def lower_inverse(systems, down, along):
    at_one = (down // 2 == along // 2) & (down != along)
    unit = jnp.where(down == along, 1.0, 0.0)
    inverses = [unit - jnp.where(at_one, system, 0.0) for system in systems]
    half = 2
    while half < CHUNK:
        joins = (down // (2 * half) == along // (2 * half)) & (down // half != along // half)
        inner = [
            fine(jnp.where(joins, system, 0.0), inverse)
            for system, inverse in zip(systems, inverses)
        ]
        inverses = [inverse - fine(inverse, part) for inverse, part in zip(inverses, inner)]
        half *= 2
    return inverses


def tap_mask(aux, tap):
    return 1.0 if tap == 0 else aux[:, 3 + tap : 4 + tap]


def convolved(window, taps, aux):
    total = 0.0
    for tap in range(KW):
        total = total + (
            taps[tap : tap + 1] * window[PAD - tap : PAD - tap + CHUNK] * tap_mask(aux, tap)
        )
    return total


def sigmoid(values):
    return 1.0 / (1.0 + jnp.exp(-values))


def unit_scale(values):
    total = jnp.sum(values * values, axis=1, keepdims=True)
    floor = DK / 16.0
    return lax.rsqrt(jnp.maximum(total, floor)), jnp.where(total > floor, 1.0, 0.0)


def mix_norm(mixed):
    mean = jnp.mean(mixed * mixed, axis=1, keepdims=True)
    return lax.rsqrt(jnp.maximum(mean, mix_floor)), jnp.where(mean > mix_floor, 1.0, 0.0)


def forward_kernel(
    heads,
    n1_ref,
    qkv_ref,
    beta_ref,
    taps_ref,
    aux_ref,
    docs_ref,
    gain_ref,
    proj_ref,
    logit_ref,
    mixed_ref,
    normed_ref,
    inverse_ref,
    states_ref,
    written_ref,
    window_ref,
    state_ref,
):
    width = heads * DK
    window_ref[0:PAD] = jnp.zeros((PAD, 3 * width), jnp.float32)
    state_ref[...] = jnp.zeros_like(state_ref)

    def chunk(n, _):
        rows = pl.ds(pl.multiple_of(n * CHUNK, CHUNK), CHUNK)
        n1 = n1_ref[rows]
        proj = mul(n1, qkv_ref[...], (1, 0)).astype(jnp.bfloat16)
        proj_ref[rows] = proj
        window_ref[PAD : PAD + CHUNK] = proj.astype(jnp.float32)
        logit = mul(n1, beta_ref[...], (1, 1))
        logit_ref[rows] = logit
        aux = aux_ref[rows]
        conv = convolved(window_ref[...], taps_ref[...], aux)
        act = conv * sigmoid(conv)
        window_ref[0:PAD] = window_ref[CHUNK : CHUNK + PAD]
        valid, carry, tail = aux[:, 1:2], aux[:, 2:3], aux[:, 3:4]
        carry_last = carry[CHUNK - 1 :]
        lower, strict, down, along = chunk_masks(aux[:, 0:1], docs_ref[pl.ds(n, 1)])
        rate_all = sigmoid(logit) * valid
        parts = []
        for h in range(heads):
            query = act[:, h * DK : (h + 1) * DK]
            key = act[:, width + h * DK : width + (h + 1) * DK]
            value = act[:, 2 * width + h * DK : 2 * width + (h + 1) * DK]
            query = query * unit_scale(query)[0]
            key = key * unit_scale(key)[0]
            rate = rate_all[:, h : h + 1]
            system = rate * fine(key, key, (1, 1)) * strict
            parts.append((query, key, value, rate, system))
        inverses = lower_inverse([part[4] for part in parts], down, along)
        for h, (query, key, value, rate, _) in enumerate(parts):
            inverse = inverses[h]
            state = state_ref[h]
            carried_key = carry * key
            right = rate * (value - fine(carried_key, state))
            written = fine(inverse, right)
            scores = plain(query, key, (1, 1)) * lower
            mixed = carry * plain(query, state) + plain(scores, written)
            mixed = mixed * valid
            states_ref[h, n] = state
            written_ref[h, n] = written
            inverse_ref[h, n] = inverse
            state_ref[h] = carry_last * state + fine(tail * key, written, (0, 0))
            columns = pl.ds(h * DK, DK)
            mixed_ref[rows, columns] = mixed
            normed_ref[rows, columns] = (
                mixed * mix_norm(mixed)[0] * gain_ref[...]
            ).astype(jnp.bfloat16)
        return 0

    lax.fori_loop(0, n1_ref.shape[0] // CHUNK, chunk, 0)


def backward_kernel(
    heads,
    grad_ref,
    o_ref,
    proj_ref,
    logit_ref,
    mixed_ref,
    inverse_ref,
    states_ref,
    written_ref,
    taps_ref,
    aux_ref,
    docs_ref,
    gain_ref,
    grad_proj_ref,
    grad_logit_ref,
    conv_grad_ref,
    gain_grad_ref,
    window_ref,
    masked_ref,
    state_ref,
):
    width = heads * DK
    chunks = grad_ref.shape[0] // CHUNK
    state_ref[...] = jnp.zeros_like(state_ref)
    masked_ref[...] = jnp.zeros_like(masked_ref)
    conv_grad_ref[...] = jnp.zeros_like(conv_grad_ref)
    gain_grad_ref[...] = jnp.zeros_like(gain_grad_ref)

    def chunk(step, _):
        n = chunks - 1 - step
        rows = pl.ds(pl.multiple_of(n * CHUNK, CHUNK), CHUNK)
        before = jnp.maximum(n - 1, 0)
        aux = aux_ref[rows]
        grad_normed = mul(grad_ref[rows], o_ref[...], (1, 0))
        prior = proj_ref[pl.ds(pl.multiple_of(before * CHUNK + CHUNK - 16, 16), 16)]
        window_ref[0:PAD] = prior.astype(jnp.float32)[16 - PAD :]
        window_ref[PAD : PAD + CHUNK] = proj_ref[rows].astype(jnp.float32)
        window = window_ref[...]
        taps = taps_ref[...]
        conv = convolved(window, taps, aux)
        conv_sig = sigmoid(conv)
        act = conv * conv_sig
        valid, carry, tail = aux[:, 1:2], aux[:, 2:3], aux[:, 3:4]
        carry_last = carry[CHUNK - 1 :]
        lower, strict, down, along = chunk_masks(aux[:, 0:1], docs_ref[pl.ds(n, 1)])
        rate_sig = sigmoid(logit_ref[rows])
        rate_all = rate_sig * valid
        lanes = lax.broadcasted_iota(jnp.int32, rate_all.shape, 1)
        grad_rates = jnp.zeros_like(rate_all)
        grads = [[], [], []]
        for h in range(heads):
            columns = pl.ds(h * DK, DK)
            mixed = mixed_ref[rows, columns]
            mix_scale, mix_live = mix_norm(mixed)
            grad_out = grad_normed[:, h * DK : (h + 1) * DK]
            scaled = mixed * mix_scale
            gain_grad_ref[...] += jnp.sum(grad_out * scaled, axis=0, keepdims=True)
            weighted = gain_ref[...] * grad_out
            grad_mix = (
                mix_scale * weighted
                - scaled
                * (mix_scale * mix_scale * mix_live)
                * jnp.mean(weighted * mixed, axis=1, keepdims=True)
            ) * valid
            query_raw = act[:, h * DK : (h + 1) * DK]
            key_raw = act[:, width + h * DK : width + (h + 1) * DK]
            value = act[:, 2 * width + h * DK : 2 * width + (h + 1) * DK]
            query_scale, query_live = unit_scale(query_raw)
            key_scale, key_live = unit_scale(key_raw)
            query = query_raw * query_scale
            key = key_raw * key_scale
            rate = rate_all[:, h : h + 1]
            inverse = inverse_ref[h, n]
            state = states_ref[h, n]
            written = written_ref[h, n]
            grad_state = state_ref[h]
            tail_key = tail * key
            carried_key = carry * key
            scores = plain(query, key, (1, 1)) * lower
            pulled = plain(scores, grad_mix, (0, 0)) + fine(tail_key, grad_state)
            solved = fine(inverse, pulled, (0, 0))
            state_ref[h] = (
                carry_last * grad_state
                + plain(carry * query, grad_mix, (0, 0))
                - fine(rate * carried_key, solved, (0, 0))
            )
            grad_scores = plain(grad_mix, written, (1, 1)) * lower
            grad_query = carry * plain(grad_mix, state, (1, 1)) + plain(grad_scores, key)
            guess_error = value - plain(carried_key, state)
            gram = plain(key, key, (1, 1)) * strict
            grad_system = plain(solved, written, (1, 1)) * strict
            grad_rate = jnp.sum(solved * guess_error, axis=1, keepdims=True) - jnp.sum(
                grad_system * gram, axis=1, keepdims=True
            )
            grad_gram = rate * grad_system
            grad_key = (
                plain(grad_scores, query, (0, 0))
                + tail * plain(written, grad_state, (1, 1))
                - rate * carry * plain(solved, state, (1, 1))
                - plain(grad_gram, key)
                - plain(grad_gram, key, (0, 0))
            )
            grads[0].append(
                query_scale
                * (
                    grad_query
                    - query
                    * query_live
                    * jnp.sum(query * grad_query, axis=1, keepdims=True)
                )
            )
            grads[1].append(
                key_scale
                * (grad_key - key * key_live * jnp.sum(key * grad_key, axis=1, keepdims=True))
            )
            grads[2].append(rate * solved)
            grad_rates = grad_rates + jnp.where(lanes == h, grad_rate, 0.0)
        grad_act = jnp.concatenate(grads[0] + grads[1] + grads[2], axis=1)
        grad_conv = grad_act * conv_sig * (1.0 + conv * (1.0 - conv_sig))
        grad_proj = taps[0:1] * grad_conv
        conv_grad_ref[0:1] += jnp.sum(
            grad_conv * window[PAD : PAD + CHUNK], axis=0, keepdims=True
        )
        for tap in range(1, KW):
            masked = grad_conv * tap_mask(aux, tap)
            conv_grad_ref[tap : tap + 1] += jnp.sum(
                masked * window[PAD - tap : PAD - tap + CHUNK], axis=0, keepdims=True
            )
            masked_ref[tap - 1, CHUNK : CHUNK + PAD] = masked_ref[tap - 1, 0:PAD]
            masked_ref[tap - 1, 0:CHUNK] = masked
            grad_proj = grad_proj + taps[tap : tap + 1] * masked_ref[tap - 1, tap : tap + CHUNK]
        grad_proj_ref[rows] = grad_proj.astype(jnp.bfloat16)
        grad_logit_ref[rows] = (grad_rates * rate_sig * (1.0 - rate_sig) * valid).astype(
            jnp.bfloat16
        )
        return 0

    lax.fori_loop(0, chunks, chunk, 0)


def in_vmem(count):
    return [pl.BlockSpec(memory_space=pltpu.VMEM)] * count


def run_forward(n1, qkv, beta, taps, aux, docs, gain):
    row_len, heads = n1.shape[0], qkv.shape[1] // (3 * DK)
    chunks, width, f32 = row_len // CHUNK, heads * DK, jnp.float32
    shapes = (
        ((row_len, 3 * width), jnp.bfloat16),
        ((row_len, beta.shape[0]), f32),
        ((row_len, width), f32),
        ((row_len, width), jnp.bfloat16),
        ((heads, chunks, CHUNK, CHUNK), f32),
        ((heads, chunks, DK, DK), f32),
        ((heads, chunks, CHUNK, DK), f32),
    )
    return pl.pallas_call(
        functools.partial(forward_kernel, heads),
        out_shape=[jax.ShapeDtypeStruct(*shape) for shape in shapes],
        in_specs=in_vmem(7),
        out_specs=in_vmem(len(shapes)),
        scratch_shapes=[
            pltpu.VMEM((PAD + CHUNK, 3 * width), f32),
            pltpu.VMEM((heads, DK, DK), f32),
        ],
        compiler_params=pltpu.CompilerParams(vmem_limit_bytes=48 * 1024 * 1024),
        name="mixer_forward",
    )(n1, qkv, beta, taps, aux, docs, gain)


def run_backward(grad, o_full, saved, taps, aux, docs, gain):
    row_len, heads = grad.shape[0], o_full.shape[1] // DK
    width, f32 = heads * DK, jnp.float32
    logit = saved[1]
    shapes = (
        ((row_len, 3 * width), jnp.bfloat16),
        (logit.shape, jnp.bfloat16),
        ((KW, 3 * width), f32),
        ((1, DK), f32),
    )
    return pl.pallas_call(
        functools.partial(backward_kernel, heads),
        out_shape=[jax.ShapeDtypeStruct(*shape) for shape in shapes],
        in_specs=in_vmem(12),
        out_specs=in_vmem(len(shapes)),
        scratch_shapes=[
            pltpu.VMEM((PAD + CHUNK, 3 * width), f32),
            pltpu.VMEM((KW - 1, CHUNK + PAD, 3 * width), f32),
            pltpu.VMEM((heads, DK, DK), f32),
        ],
        compiler_params=pltpu.CompilerParams(vmem_limit_bytes=48 * 1024 * 1024),
        name="mixer_backward",
    )(grad, o_full, *saved, taps, aux, docs, gain)


def row_aux(docs):
    f32 = jnp.float32
    chunks = docs.reshape(-1, CHUNK)
    prior = jnp.concatenate([jnp.full((1,), -1, jnp.int32), chunks[:-1, -1]])
    padded = jnp.concatenate([jnp.full((KW - 1,), -1, jnp.int32), docs])
    columns = [
        docs,
        docs < DOCS,
        (chunks == prior[:, None]).reshape(-1),
        (chunks == chunks[:, -1:]).reshape(-1),
    ] + [padded[KW - 1 - tap : KW - 1 - tap + docs.shape[0]] == docs for tap in range(1, KW)]
    columns = [column.astype(f32) for column in columns]
    columns += [jnp.zeros_like(columns[0])] * (8 - len(columns))
    return jnp.stack(columns, axis=1), chunks.astype(f32)


def remote(source, target, send, recv, where):
    return pltpu.make_async_remote_copy(
        src_ref=source,
        dst_ref=target,
        send_sem=send,
        recv_sem=recv,
        device_id=where,
        device_id_type=pl.DeviceIdType.MESH,
    )


def greet(partners):
    barrier = pltpu.get_barrier_semaphore()
    for partner, there in partners:

        @pl.when(there)
        def _(partner=partner):
            pl.semaphore_signal(
                barrier, inc=1, device_id=partner, device_id_type=pl.DeviceIdType.MESH
            )

    pl.semaphore_wait(barrier, sum(there.astype(jnp.int32) for _, there in partners))


def around(axis):
    count, place = lax.axis_size(axis), lax.axis_index(axis)
    return [lax.rem(place + by, count) for by in range(1, count)]


def line_partners():
    count, place, core = lax.axis_size("seq"), lax.axis_index("seq"), lax.axis_index("tp")
    return [
        ({"seq": jnp.minimum(place + 1, count - 1)}, place < count - 1),
        ({"seq": jnp.maximum(place - 1, 0)}, place > 0),
        ({"tp": 1 - core}, core >= 0),
    ]


class Line:
    def __init__(self):
        self.count, self.place = lax.axis_size("seq"), lax.axis_index("seq")
        self.core = lax.axis_index("tp")
        self.other = 1 - self.core
        self.right = {"seq": jnp.minimum(self.place + 1, self.count - 1)}
        self.left = {"seq": jnp.maximum(self.place - 1, 0)}
        self.across = {"tp": self.other}


class Gather:
    sems = 5

    def __init__(self, line, slots, sems):
        self.line, self.slots, self.sems = line, slots, sems

    def copy(self, kind, seq):
        line = self.line
        send = {"right": 0, "left": 1, "across": 2}[kind]
        recv = 4 if kind == "across" else 3
        slot = self.slots.at[seq, line.core]
        where = {"right": line.right, "left": line.left, "across": line.across}[kind]
        return remote(slot, slot, self.sems.at[send, seq], self.sems.at[recv, seq], where)

    def forward(self, seq, right, left):
        line = self.line
        if right:

            @pl.when(line.place < line.count - 1)
            def _():
                self.copy("right", seq).start()

        if left:

            @pl.when(line.place > 0)
            def _():
                self.copy("left", seq).start()

        self.copy("across", seq).start()

    def phase(self, by):
        line = self.line
        if by == 0:
            self.forward(line.place, True, True)
            return

        @pl.when(line.place - by >= 0)
        def _():
            self.copy("right", line.place - by).wait_recv()
            self.forward(line.place - by, True, False)

        @pl.when(line.place + by < line.count)
        def _():
            self.copy("left", line.place + by).wait_recv()
            self.forward(line.place + by, False, True)

    def finish(self):
        line = self.line
        for seq in range(line.count):

            @pl.when((line.place >= seq) & (line.place < line.count - 1))
            def _():
                self.copy("right", seq).wait_send()

            @pl.when((line.place <= seq) & (line.place > 0))
            def _():
                self.copy("left", seq).wait_send()

            self.copy("across", seq).wait()


class Scatter:
    sems = 5

    def __init__(self, line, blocks, came, across, sems):
        self.line, self.blocks, self.came, self.across, self.sems = line, blocks, came, across, sems

    def over(self, seq):
        line = self.line
        return remote(
            self.blocks.at[seq, line.other],
            self.across.at[seq],
            self.sems.at[0, seq],
            self.sems.at[1, seq],
            line.across,
        )

    def along(self, kind, seq):
        line = self.line
        way = {"right": 0, "left": 1}[kind]
        return remote(
            self.blocks.at[seq, line.core],
            self.came.at[way, seq],
            self.sems.at[2, seq],
            self.sems.at[3 + way, seq],
            line.right if way == 0 else line.left,
        )

    def offer(self, seq):
        self.over(seq).start()

    def chip_sum(self, seq):
        self.over(seq).wait_recv()
        return self.blocks[seq, self.line.core].astype(jnp.float32) + self.across[seq].astype(
            jnp.float32
        )

    def pass_on(self, kind, seq):
        line = self.line
        first = line.place == (0 if kind == "right" else line.count - 1)
        way = {"right": 0, "left": 1}[kind]
        total = self.chip_sum(seq)

        @pl.when(first)
        def _():
            self.blocks[seq, line.core] = total.astype(jnp.bfloat16)

        @pl.when(jnp.logical_not(first))
        def _():
            self.along(kind, seq).wait_recv()
            self.blocks[seq, line.core] = (
                total + self.came[way, seq].astype(jnp.float32)
            ).astype(jnp.bfloat16)

        self.along(kind, seq).start()

    def target(self, k):
        line = self.line
        return jnp.where(line.place < line.count // 2, line.count - 1 - k, k)

    def near(self, k):
        line = self.line
        low = line.place < line.count // 2

        @pl.when(low & (line.count - 1 - k > line.place))
        def _():
            self.pass_on("right", line.count - 1 - k)

        @pl.when(jnp.logical_not(low) & (k < line.place))
        def _():
            self.pass_on("left", k)

    def far(self, k):
        line = self.line
        low = line.place < line.count // 2

        @pl.when(low & (k < line.place))
        def _():
            self.pass_on("left", k)

        @pl.when(jnp.logical_not(low) & (line.count - 1 - k > line.place))
        def _():
            self.pass_on("right", line.count - 1 - k)

    def wait_own(self):
        line = self.line

        @pl.when(line.place > 0)
        def _():
            self.along("right", line.place).wait_recv()

        @pl.when(line.place < line.count - 1)
        def _():
            self.along("left", line.place).wait_recv()

        self.over(line.place).wait_recv()

    def own_rows(self, rows):
        line = self.line
        f32 = jnp.float32
        total = self.blocks[line.place, line.core, rows].astype(f32)
        total = total + self.across[line.place, rows].astype(f32)
        from_left = self.came[0, line.place, rows].astype(f32)
        from_right = self.came[1, line.place, rows].astype(f32)
        total = total + jnp.where(line.place > 0, from_left, 0.0)
        return total + jnp.where(line.place < line.count - 1, from_right, 0.0)

    def finish(self):
        line = self.line
        for seq in range(line.count):
            self.over(seq).wait_send()

            @pl.when(line.place != seq)
            def _():
                self.along("right", seq).wait_send()


def product_rows(left_ref, right_ref, blocks, seq, tile=512):
    cores, rows, width = blocks.shape[1:]
    left = left_ref[pl.ds(pl.multiple_of(seq * cores * rows, cores * rows), cores * rows)]

    def columns(t, _):
        span = pl.ds(pl.multiple_of(t * tile, tile), tile)
        part = mul(left, right_ref[span], (1, 1)).astype(jnp.bfloat16)
        for core in range(cores):
            blocks[seq, core, :, span] = part[core * rows : (core + 1) * rows]
        return 0

    lax.fori_loop(0, width // tile, columns, 0)


STEP = 32


def over_rows(count, body):
    def step(i, _):
        body(pl.ds(pl.multiple_of(i * STEP, STEP), STEP), i)
        return 0

    lax.fori_loop(0, count // STEP, step, 0)


def own_span(core, rows, inner):
    return pl.ds(pl.multiple_of(core * rows + inner.start, STEP), inner.size)


def resid_kernel(
    mix_ref, o_ref, x_ref, g_ref, gain_ref, resid_ref, n2_ref, g_full_ref,
    blocks, came, across, sum_sems, n2_sems, g_sems,
):
    line = Line()
    greet(line_partners())
    rows = n2_ref.shape[2]
    total = Scatter(line, blocks, came, across, sum_sems)
    n2 = Gather(line, n2_ref, n2_sems)
    grads = Gather(line, g_full_ref, g_sems)
    g_full_ref[line.place, line.core] = g_ref[
        pl.ds(pl.multiple_of(line.core * rows, rows), rows)
    ]
    for k in range(line.count):
        seq = total.target(k)
        product_rows(mix_ref, o_ref, blocks, seq)
        total.offer(seq)
    total.near(0)
    grads.phase(0)
    for k in range(1, line.count):
        total.near(k)
        grads.phase(k)
    for k in range(line.count):
        total.far(k)
    total.wait_own()

    def normed(span, i):
        x_span = pl.ds(pl.multiple_of(line.core * rows + i * STEP, STEP), STEP)
        resid = x_ref[x_span].astype(jnp.float32) + total.own_rows(span)
        resid_ref[span] = resid
        n2_ref[line.place, line.core, span] = (
            resid * norm_scale(resid) * gain_ref[...]
        ).astype(jnp.bfloat16)

    over_rows(rows, normed)
    for k in range(line.count):
        n2.phase(k)
    total.finish()
    n2.finish()
    grads.finish()


def dma_sems(*shape):
    return pltpu.SemaphoreType.DMA(shape)


def line_call(kernel, collective_id, name, outs, scratch, args, limit=56):
    return pl.pallas_call(
        kernel,
        out_shape=[jax.ShapeDtypeStruct(*out) for out in outs],
        in_specs=in_vmem(len(args)),
        out_specs=in_vmem(len(outs)),
        scratch_shapes=scratch,
        compiler_params=pltpu.CompilerParams(
            collective_id=collective_id,
            has_side_effects=True,
            vmem_limit_bytes=limit * 1024 * 1024,
        ),
        name=name,
    )(*args)


def scatter_scratch(seqs, cores, rows, width):
    b16 = jnp.bfloat16
    return [
        pltpu.VMEM((seqs, cores, rows, width), b16),
        pltpu.VMEM((2, seqs, rows, width), b16),
        pltpu.VMEM((seqs, rows, width), b16),
    ]


def run_resid(mix, o_full, x, g, gain):
    seqs, cores, (piece, width) = lax.axis_size("seq"), lax.axis_size("tp"), x.shape
    rows, b16 = piece // cores, jnp.bfloat16
    outs = (
        ((rows, width), jnp.float32),
        ((seqs, cores, rows, width), b16),
        ((seqs, cores, rows, width), b16),
    )
    scratch = scatter_scratch(seqs, cores, rows, width) + [dma_sems(5, seqs)] * 3
    resid, n2, g_full = line_call(
        resid_kernel, 1, "resid_norm", outs, scratch, (mix, o_full, x, g, gain)
    )
    return resid, n2.reshape(-1, width), g_full.reshape(-1, width)


def grad_resid_kernel(
    dgu_ref, gate_up_ref, hidden_ref, down_ref, resid_ref, g_ref, gain_ref,
    grad_resid_ref, grad_attn_ref, gain_grad_ref, result_ref,
    blocks, came, across, out_blocks, out_came, out_across,
    sum_sems, out_sems, attn_sems, swap_sems,
):
    line = Line()
    greet(line_partners())
    rows = resid_ref.shape[0]
    total = Scatter(line, blocks, came, across, sum_sems)
    result = Scatter(line, out_blocks, out_came, out_across, out_sems)
    attn = Gather(line, grad_attn_ref, attn_sems)
    for k in range(line.count):
        seq = total.target(k)
        product_rows(dgu_ref, gate_up_ref, blocks, seq)
        total.offer(seq)
        total.near(k)
    for k in range(line.count):
        total.far(k)
        product_rows(hidden_ref, down_ref, out_blocks, total.target(k))
    total.wait_own()
    gain_grad_ref[...] = jnp.zeros_like(gain_grad_ref)

    def back(span, i):
        own_span = pl.ds(pl.multiple_of(line.core * rows + i * STEP, STEP), STEP)
        resid = resid_ref[span]
        grad_two = total.own_rows(span)
        scale = norm_scale(resid)
        gain_grad_ref[...] += jnp.sum(grad_two * resid * scale, axis=0, keepdims=True)
        grad = g_ref[own_span].astype(jnp.float32) + norm_back(
            resid, scale, gain_ref[...], grad_two
        )
        grad_resid_ref[span] = grad
        grad_attn_ref[line.place, line.core, span] = grad.astype(jnp.bfloat16)

    over_rows(rows, back)
    attn.phase(0)
    for k in range(line.count):
        result.offer(result.target(k))
    for k in range(1, line.count):
        result.near(k - 1)
        attn.phase(k)
    for k in range(line.count):
        result.far(k)
    result.wait_own()

    def finish(span, i):
        own_span = pl.ds(pl.multiple_of(line.core * rows + i * STEP, STEP), STEP)
        result_ref[own_span] = (resid_ref[span] + result.own_rows(span)).astype(jnp.bfloat16)

    over_rows(rows, finish)
    swap = own_swap(line, result_ref, rows, swap_sems)
    swap.start()
    total.finish()
    result.finish()
    attn.finish()
    swap.wait()


def own_swap(line, ref, rows, sems):
    own = ref.at[pl.ds(pl.multiple_of(line.core * rows, rows), rows)]
    return remote(own, own, sems.at[0], sems.at[1], line.across)


def run_grad_resid(grad_gate_up, gate_up, hidden, down, resid, g, gain):
    seqs, cores, (piece, width) = lax.axis_size("seq"), lax.axis_size("tp"), g.shape
    rows, b16, f32 = piece // cores, jnp.bfloat16, jnp.float32
    outs = (
        ((rows, width), f32),
        ((seqs, cores, rows, width), b16),
        ((1, width), f32),
        ((piece, width), b16),
    )
    scratch = scatter_scratch(seqs, cores, rows, width) * 2
    scratch = scratch + [dma_sems(5, seqs)] * 3 + [dma_sems(2)]
    grad_resid, grad_attn, gain_grad, result = line_call(
        grad_resid_kernel, 2, "grad_resid", outs, scratch,
        (grad_gate_up, gate_up, hidden, down, resid, g, gain),
    )
    return grad_resid, grad_attn.reshape(-1, width), gain_grad, result


def input_grad_kernel(
    grad_proj_ref, qkv_ref, grad_logit_ref, beta_ref, x_ref, grad_resid_ref, gain_ref,
    input_grad_ref, gain_grad_ref,
    blocks, came, across, sum_sems, swap_sems,
):
    line = Line()
    greet(line_partners())
    rows = grad_resid_ref.shape[0]
    total = Scatter(line, blocks, came, across, sum_sems)

    def product(seq, tile=512):
        cores, _, width = blocks.shape[1:]
        at = pl.ds(pl.multiple_of(seq * cores * rows, cores * rows), cores * rows)
        left, logit = grad_proj_ref[at], grad_logit_ref[at]

        def columns(t, _):
            span = pl.ds(pl.multiple_of(t * tile, tile), tile)
            part = mul(left, qkv_ref[span], (1, 1)) + mul(logit, beta_ref[:, span], (1, 0))
            part = part.astype(jnp.bfloat16)
            for core in range(cores):
                blocks[seq, core, :, span] = part[core * rows : (core + 1) * rows]
            return 0

        lax.fori_loop(0, width // tile, columns, 0)

    for k in range(line.count):
        seq = total.target(k)
        product(seq)
        total.offer(seq)
        total.near(k)
    for k in range(line.count):
        total.far(k)
    total.wait_own()
    gain_grad_ref[...] = jnp.zeros_like(gain_grad_ref)

    def back(span, i):
        own_span = pl.ds(pl.multiple_of(line.core * rows + i * STEP, STEP), STEP)
        x = x_ref[own_span].astype(jnp.float32)
        grad_one = total.own_rows(span)
        scale = norm_scale(x)
        gain_grad_ref[...] += jnp.sum(grad_one * x * scale, axis=0, keepdims=True)
        input_grad_ref[own_span] = (
            grad_resid_ref[span] + norm_back(x, scale, gain_ref[...], grad_one)
        ).astype(jnp.bfloat16)

    over_rows(rows, back)
    swap = own_swap(line, input_grad_ref, rows, swap_sems)
    swap.start()
    total.finish()
    swap.wait()


def run_input_grad(grad_proj, qkv, grad_logit, beta, x, grad_resid, gain):
    seqs, cores, (piece, width) = lax.axis_size("seq"), lax.axis_size("tp"), x.shape
    rows, b16, f32 = piece // cores, jnp.bfloat16, jnp.float32
    outs = (((piece, width), b16), ((1, width), f32))
    scratch = scatter_scratch(seqs, cores, rows, width) + [dma_sems(5, seqs), dma_sems(2)]
    return line_call(
        input_grad_kernel, 3, "input_grad", outs, scratch,
        (grad_proj, qkv, grad_logit, beta, x, grad_resid, gain),
    )


def normed_kernel(
    x_ref, gain_ref, parts_ref, beta_ref, n1_ref, qkv_ref, beta_full_ref,
    n1_sems, send_line, recv_line, send_row, recv_row,
    beta_send_line, beta_recv_line, beta_send_row, beta_recv_row,
):
    line = Line()
    row = lax.axis_index("row")
    seq_others, row_others = around("seq"), around("row")
    greet(
        [({"seq": other}, other >= 0) for other in seq_others]
        + [({"row": other}, other >= 0) for other in row_others]
        + [(line.across, line.core >= 0)]
    )
    moves = (
        (parts_ref, qkv_ref, send_line, recv_line, send_row, recv_row),
        (beta_ref, beta_full_ref, beta_send_line, beta_recv_line, beta_send_row, beta_recv_row),
    )

    def spread(move, i):
        source, target, send, recv = move[:4]
        return remote(
            source.at[seq_others[i]],
            target.at[row, line.place],
            send.at[i],
            recv.at[i],
            {"seq": seq_others[i]},
        )

    def share(move, i, j):
        target, send, recv = move[1], move[4], move[5]
        came_from = lax.rem(line.place + line.count - i, line.count)
        slot = target.at[row, came_from]
        return remote(slot, slot, send.at[i, j], recv.at[i, j], {"row": row_others[j]})

    for move in moves:
        for i in range(len(seq_others)):
            spread(move, i).start()
    for move in moves:
        move[1][row, line.place] = move[0][line.place]
        for j in range(len(row_others)):
            share(move, 0, j).start()
    rows = n1_ref.shape[2]
    n1 = Gather(line, n1_ref, n1_sems)

    def normed(span, i):
        x_span = pl.ds(pl.multiple_of(line.core * rows + i * STEP, STEP), STEP)
        x = x_ref[x_span].astype(jnp.float32)
        n1_ref[line.place, line.core, span] = (x * norm_scale(x) * gain_ref[...]).astype(
            jnp.bfloat16
        )

    over_rows(rows, normed)
    n1.phase(0)
    for k in range(1, line.count):
        for move in moves:
            spread(move, k - 1).wait_recv()
            for j in range(len(row_others)):
                share(move, k, j).start()
        n1.phase(k)
    for move in moves:
        for i in range(len(seq_others)):
            spread(move, i).wait_send()
        for i in range(line.count):
            for j in range(len(row_others)):
                share(move, i, j).wait()
    n1.finish()


def run_normed(x, gain, parts, beta):
    rows_axis, seqs, cores = (lax.axis_size(axis) for axis in ("row", "seq", "tp"))
    piece, width = x.shape
    b16 = jnp.bfloat16
    outs = (
        ((seqs, cores, piece // cores, width), b16),
        ((rows_axis,) + parts.shape, b16),
        ((rows_axis,) + beta.shape, b16),
    )
    moves = [
        dma_sems(seqs - 1),
        dma_sems(seqs - 1),
        dma_sems(seqs, rows_axis - 1),
        dma_sems(seqs, rows_axis - 1),
    ]
    n1, qkv, beta_full = line_call(
        normed_kernel, 4, "norm_gather", outs, [dma_sems(5, seqs)] + moves * 2,
        (x, gain, parts, beta),
    )
    return n1.reshape(-1, width), qkv.reshape(-1, qkv.shape[-1]), beta_full


def small_sums_kernel(
    part_ref, out_ref, rows_ref, all_ref, send_row, recv_row, send_seq, recv_seq, send_tp, recv_tp
):
    row, seq, tp = (lax.axis_index(axis) for axis in ("row", "seq", "tp"))
    row_others, seq_others, tp_others = around("row"), around("seq"), around("tp")
    greet(
        [({"row": other}, other >= 0) for other in row_others]
        + [({"seq": other}, other >= 0) for other in seq_others]
        + [({"tp": other}, other >= 0) for other in tp_others]
    )
    rows_ref[row] = part_ref[...]
    copies = [
        remote(part_ref, rows_ref.at[row], send_row.at[i], recv_row.at[i], {"row": other})
        for i, other in enumerate(row_others)
    ]
    for copy in copies:
        copy.start()
    for copy in copies:
        copy.wait()
    total = rows_ref[0]
    for i in range(1, rows_ref.shape[0]):
        total = total + rows_ref[i]
    all_ref[tp, seq] = total
    copies = [
        remote(
            all_ref.at[tp, seq], all_ref.at[tp, seq], send_seq.at[i], recv_seq.at[i], {"seq": other}
        )
        for i, other in enumerate(seq_others)
    ]
    for copy in copies:
        copy.start()
    for copy in copies:
        copy.wait()
    copies = [
        remote(all_ref.at[tp], all_ref.at[tp], send_tp.at[i], recv_tp.at[i], {"tp": other})
        for i, other in enumerate(tp_others)
    ]
    for copy in copies:
        copy.start()
    for copy in copies:
        copy.wait()
    out_ref[...] = all_ref[...]


def run_small_sums(part):
    rows, seqs, tps = (lax.axis_size(axis) for axis in ("row", "seq", "tp"))
    dma = pltpu.SemaphoreType.DMA
    shape = (tps, seqs) + part.shape
    return pl.pallas_call(
        small_sums_kernel,
        out_shape=jax.ShapeDtypeStruct(shape, part.dtype),
        in_specs=in_vmem(1),
        out_specs=pl.BlockSpec(memory_space=pltpu.VMEM),
        scratch_shapes=[
            pltpu.VMEM((rows,) + part.shape, part.dtype),
            pltpu.VMEM(shape, part.dtype),
            dma((rows - 1,)),
            dma((rows - 1,)),
            dma((seqs - 1,)),
            dma((seqs - 1,)),
            dma((tps - 1,)),
            dma((tps - 1,)),
        ],
        compiler_params=pltpu.CompilerParams(collective_id=0, has_side_effects=True),
        name="small_sums",
    )(part)


def exchanged(parts, axis):
    count, place = lax.axis_size(axis), lax.axis_index(axis)
    came = [lax.dynamic_index_in_dim(parts, place, 0, keepdims=False)]
    for by in range(1, count):
        part = lax.dynamic_index_in_dim(parts, (place + by) % count, 0, keepdims=False)
        came.append(lax.ppermute(part, axis, [(i, (i + by) % count) for i in range(count)]))
    came = jnp.stack(came)
    order = (place - jnp.arange(count)) % count
    return jnp.concatenate(
        [lax.dynamic_slice_in_dim(came, order[j], 1, axis=0) for j in range(count)], axis=0
    )


def spread(shard, pieces, axis):
    rows, width = shard.shape
    return exchanged(shard.reshape(rows, pieces, width // pieces).transpose(1, 0, 2), axis)


def gathered(shard):
    pieces = lax.axis_size("seq")
    parts = spread(shard, pieces, "seq")
    whole = lax.all_gather(parts, "row", axis=0, tiled=True)
    return whole.reshape(-1, whole.shape[-1])


def returned(part):
    pieces = lax.axis_size("seq")
    rows = part.shape[0] // (pieces * lax.axis_size("row"))
    own = lax.psum_scatter(part, "row", scatter_dimension=0, tiled=True)
    return exchanged(own.reshape(pieces, rows, -1), "seq")


def local_heads(
    block_input,
    grad_out,
    doc_lengths,
    attn_gain,
    mlp_gain,
    out_gain,
    conv_weight,
    qkv_weight,
    beta_weight,
    o_weight,
    gate_up_weight,
    down_weight,
):
    tok_rows, model_width = block_input.shape[1:]
    pieces, cores = lax.axis_size("seq"), lax.axis_size("tp")
    piece, core = lax.axis_index("seq"), lax.axis_index("tp")
    row_len = pieces * tok_rows
    shard_rows = qkv_weight.shape[1]
    half_width = qkv_weight.shape[2]
    width = half_width // pieces
    heads = width // DK
    units = gate_up_weight.shape[2] // pieces
    f32, b16 = jnp.float32, jnp.bfloat16

    x_piece, g_piece = block_input[0], grad_out[0]
    qkv_parts = qkv_weight.reshape(3, shard_rows, pieces, width).transpose(2, 1, 0, 3)
    beta_parts = jnp.pad(
        beta_weight.T.reshape(pieces, heads, shard_rows), ((0, 0), (0, 16 - heads), (0, 0))
    )
    normed_one, qkv_full, beta_full = run_normed(
        x_piece, attn_gain[None], qkv_parts.reshape(pieces, shard_rows, -1), beta_parts
    )
    beta_full = beta_full.reshape(-1, 16, shard_rows).transpose(1, 0, 2).reshape(16, -1)
    o_full = gathered(o_weight.T)
    gate_up_parts = gate_up_weight.reshape(2, shard_rows, pieces, units).transpose(1, 2, 0, 3)
    gate_up_full = gathered(gate_up_parts.reshape(shard_rows, -1))
    down_full = gathered(down_weight.T)

    ends = jnp.cumsum(doc_lengths[0])
    places = jnp.arange(row_len, dtype=jnp.int32)
    docs = jnp.sum((places[:, None] >= ends[None, :]).astype(jnp.int32), axis=1)
    aux, doc_rows = row_aux(docs)
    gain_row = out_gain[None]
    taps = lax.dynamic_slice_in_dim(conv_weight, piece * width, width, axis=2)
    taps = taps.transpose(1, 0, 2).reshape(KW, 3 * width)

    proj, logit, mixed, normed_mix, inverse, states, written = run_forward(
        normed_one, qkv_full, beta_full, taps, aux, doc_rows, gain_row
    )
    resid, normed_two, g_full = run_resid(normed_mix, o_full, x_piece, g_piece, mlp_gain[None])
    gate_up = jnp.dot(normed_two, gate_up_full, preferred_element_type=f32)
    gate, up = gate_up[:, :units], gate_up[:, units:]
    gate_sig = jax.nn.sigmoid(gate)
    gate_act = gate * gate_sig
    hidden = (gate_act * up).astype(b16)
    grad_hidden = jnp.dot(g_full, down_full, preferred_element_type=f32)
    grad_gate = grad_hidden * up * gate_sig * (1.0 + gate * (1.0 - gate_sig))
    grad_up = grad_hidden * gate_act
    grad_gate_up = jnp.concatenate([grad_gate, grad_up], axis=1).astype(b16)
    grad_resid, grad_attn, mlp_gain_part, result = run_grad_resid(
        grad_gate_up, gate_up_full, hidden, down_full, resid, g_piece, mlp_gain[None]
    )
    down_part = jnp.einsum("td,tf->df", g_full, hidden, preferred_element_type=f32)
    gate_up_part = jnp.einsum("td,tf->df", normed_two, grad_gate_up, preferred_element_type=f32)
    o_part = jnp.einsum("td,te->de", grad_attn, normed_mix, preferred_element_type=f32)
    grad_proj, grad_logit, conv_part, out_gain_part = run_backward(
        grad_attn,
        o_full,
        (proj, logit, mixed, inverse, states, written),
        taps,
        aux,
        doc_rows,
        gain_row,
    )
    input_grad, attn_gain_part = run_input_grad(
        grad_proj, qkv_full, grad_logit, beta_full, x_piece, grad_resid, attn_gain[None]
    )
    qkv_part = jnp.einsum("td,te->de", normed_one, grad_proj, preferred_element_type=f32)
    beta_part = jnp.einsum("td,th->hd", normed_one, grad_logit, preferred_element_type=f32)
    packed = jnp.concatenate(
        [
            conv_part.reshape(-1, 128),
            attn_gain_part.reshape(-1, 128),
            mlp_gain_part.reshape(-1, 128),
            beta_part[:heads].reshape(-1, 128),
            jnp.pad(out_gain_part, ((0, 7), (0, 0))),
        ],
        axis=0,
    )
    small = run_small_sums(packed)
    at = KW * 3 * width // 128
    span = model_width // 128
    conv_grad = small[:, :, :at].reshape(cores, pieces, KW, 3, width)
    conv_grad = conv_grad.transpose(3, 2, 0, 1, 4).reshape(3, KW, model_width)
    sums = jnp.sum(small[:, :, at:], axis=(0, 1))
    attn_gain_grad = sums[:span].reshape(-1)
    mlp_gain_grad = sums[span : 2 * span].reshape(-1)
    out_gain_grad = sums[(2 + heads) * span]
    beta_sum = lax.dynamic_index_in_dim(small, core, 0, keepdims=False)
    beta_sum = beta_sum[:, at + 2 * span : at + (2 + heads) * span]
    beta_sum = beta_sum.reshape(pieces * heads, model_width)
    beta_sum = lax.dynamic_slice_in_dim(
        beta_sum, (lax.axis_index("row") * pieces + piece) * shard_rows, shard_rows, axis=1
    ).T
    down_sum = returned(down_part.astype(b16))
    gate_up_sum = returned(gate_up_part.astype(b16)).reshape(pieces, shard_rows, 2, units)
    o_sum = returned(o_part.astype(b16))
    qkv_sum = returned(qkv_part.astype(b16)).reshape(pieces, shard_rows, 3, width)
    return (
        result[None],
        input_grad[None],
        attn_gain_grad,
        mlp_gain_grad,
        out_gain_grad,
        conv_grad,
        qkv_sum.transpose(2, 1, 0, 3).reshape(3, shard_rows, -1).astype(f32),
        beta_sum,
        o_sum.transpose(0, 2, 1).reshape(-1, shard_rows).astype(f32),
        gate_up_sum.transpose(2, 1, 0, 3).reshape(2, shard_rows, -1).astype(f32),
        down_sum.transpose(0, 2, 1).reshape(-1, shard_rows).astype(f32),
    )


def splits_heads(mesh, heads=16, units=5632):
    return (
        mesh.shape["tp"] == 2
        and heads % (mesh.shape["seq"] * 2) == 0
        and units % (mesh.shape["seq"] * 2) == 0
    )


def solution(mesh):
    in_specs = (
        P("row", "seq", None),
        P("row", "seq", None),
        P("row", None),
        P(),
        P(),
        P(),
        P(None, None, "tp"),
        P(None, ("row", "seq"), "tp"),
        P(("row", "seq"), "tp"),
        P("tp", ("row", "seq")),
        P(None, ("row", "seq"), "tp"),
        P("tp", ("row", "seq")),
    )
    out_specs = (
        P("row", "seq", None),
        P("row", "seq", None),
        P(),
        P(),
        P(),
        P(),
        P(None, ("row", "seq"), "tp"),
        P(("row", "seq"), "tp"),
        P("tp", ("row", "seq")),
        P(None, ("row", "seq"), "tp"),
        P("tp", ("row", "seq")),
    )
    local = local_heads if splits_heads(mesh) else local_pieces
    return jax.shard_map(local, mesh=mesh, in_specs=in_specs, out_specs=out_specs, check_vma=False)
```

```python
import functools

import jax
import jax.numpy as jnp
from jax import lax
from jax.experimental import pallas as pl
from jax.experimental.pallas import tpu as pltpu
from jax.sharding import PartitionSpec as P

DK = 128
KW = 4
GROUP = 64
DOCS = 8


eps = 1e-06
mix_floor = 0.01
precise = lax.Precision.HIGHEST


def from_behind(shard, axis, by):
    devices = lax.axis_size(axis)
    pairs = [(i, i + by) for i in range(devices) if 0 <= i + by < devices]
    return lax.ppermute(shard, axis, pairs)


def prefix(shard, axis, combine, identity, reverse):
    devices, place = (lax.axis_size(axis), lax.axis_index(axis))
    everything = jax.tree.map(
        lambda part, kind: lax.all_gather(part.astype(kind), axis),
        shard,
        (jnp.bfloat16, jnp.bfloat16),
    )
    start = jax.tree.map(
        lambda part, zero: jnp.broadcast_to(jnp.asarray(zero, part.dtype), part.shape),
        shard,
        identity,
    )

    def step(k, before):
        at = devices - 1 - k if reverse else k
        reached = at > place if reverse else at < place
        new = combine(
            before, jax.tree.map(lambda part, own: part[at].astype(own.dtype), everything, shard)
        )
        return jax.tree.map(lambda a, b: jnp.where(reached, a, b), new, before)

    return lax.fori_loop(0, devices, step, start)


def norm_scale(values):
    return lax.rsqrt(jnp.mean(values * values, axis=-1, keepdims=True) + eps)


def norm_back(values, scale, gain, grad):
    weighted = gain * grad
    return scale * weighted - values * scale**3 * jnp.mean(
        weighted * values, axis=-1, keepdims=True
    )


def batch_mul(left, right):
    return jnp.einsum("hij,hjk->hik", left, right, precision=precise)


def batch_mul_t(left, right):
    return jnp.einsum("hji,hjk->hik", left, right, precision=precise)


def compose(earlier, later):
    return (batch_mul(later[0], earlier[0]), batch_mul(later[0], earlier[1]) + later[1])


def over_heads(function, shared):
    return jax.vmap(jax.vmap(function), in_axes=shared)


def tp_total(term):
    return lax.psum(term.astype(jnp.bfloat16), "tp").astype(jnp.float32)


def group_parts(key_rows, value_rows, rates, same_doc, carry_mask):
    size = key_rows.shape[0]
    strict = jnp.tril(jnp.ones((size, size), jnp.float32), -1) * same_doc
    inner = jnp.dot(key_rows, key_rows.T, precision=precise)
    system = jnp.eye(size, dtype=jnp.float32) + rates[:, None] * inner * strict
    right_side = jnp.concatenate(
        [rates[:, None] * value_rows, (rates * carry_mask)[:, None] * key_rows], axis=1
    )
    solved = jax.scipy.linalg.solve_triangular(system, right_side, lower=True)
    base_rows = solved[:, : value_rows.shape[1]]
    wy_rows = solved[:, value_rows.shape[1] :]
    tail_keys = same_doc[size - 1][:, None] * key_rows
    identity_mat = jnp.eye(key_rows.shape[1], dtype=jnp.float32)
    transition = carry_mask[size - 1] * identity_mat - jnp.dot(
        tail_keys.T, wy_rows, precision=precise
    )
    contribution = jnp.dot(tail_keys.T, base_rows, precision=precise)
    return (transition, contribution, base_rows, wy_rows)


def group_output(queries, key_rows, same_doc, carry_mask, base_rows, wy_rows, state_in):
    size = key_rows.shape[0]
    lower = jnp.tril(jnp.ones((size, size), jnp.float32)) * same_doc
    written = base_rows - jnp.dot(wy_rows, state_in, precision=precise)
    scores = jnp.dot(queries, key_rows.T, precision=precise) * lower
    carried = carry_mask[:, None] * jnp.dot(queries, state_in, precision=precise)
    return carried + jnp.dot(scores, written, precision=precise)


def group_full(queries, key_rows, value_rows, rates, same_doc, carry_mask, state_in):
    transition, contribution, base_rows, wy_rows = group_parts(
        key_rows, value_rows, rates, same_doc, carry_mask
    )
    outputs = group_output(queries, key_rows, same_doc, carry_mask, base_rows, wy_rows, state_in)
    return (outputs, jnp.dot(transition, state_in, precision=precise) + contribution)


def state_pull(queries, key_rows, same_doc, carry_mask, wy_rows, grad_rows):
    size = key_rows.shape[0]
    lower = jnp.tril(jnp.ones((size, size), jnp.float32)) * same_doc
    scores = jnp.dot(queries, key_rows.T, precision=precise) * lower
    pulled = jnp.dot(scores.T, grad_rows, precision=precise)
    direct = jnp.dot((carry_mask[:, None] * queries).T, grad_rows, precision=precise)
    return direct - jnp.dot(wy_rows.T, pulled, precision=precise)


def group_grads(
    queries, key_rows, value_rows, rates, same_doc, carry_mask, state_in, grad_rows, grad_end
):

    def group_local(query_in, key_in, value_in, rate_in):
        return group_full(query_in, key_in, value_in, rate_in, same_doc, carry_mask, state_in)

    outputs, pullback = jax.vjp(group_local, queries, key_rows, value_rows, rates)
    return pullback((grad_rows, grad_end))


def local_pieces(
    block_input,
    grad_out,
    doc_lengths,
    attn_gain,
    mlp_gain,
    out_gain,
    conv_weight,
    qkv_weight,
    beta_weight,
    o_weight,
    gate_up_weight,
    down_weight,
):
    tok_rows = block_input.shape[1]
    model_width = block_input.shape[2]
    blocks = tok_rows // GROUP
    unit_floor = DK / 16.0
    x_rows = block_input[0].astype(jnp.float32)
    grad_rows_out = grad_out[0]
    qkv_full, beta_full, o_full, gate_up_full, down_full = (
        lax.all_gather(qkv_weight, ("row", "seq"), axis=1, tiled=True),
        lax.all_gather(beta_weight, ("row", "seq"), axis=0, tiled=True),
        lax.all_gather(o_weight, ("row", "seq"), axis=1, tiled=True),
        lax.all_gather(gate_up_weight, ("row", "seq"), axis=1, tiled=True),
        lax.all_gather(down_weight, ("row", "seq"), axis=1, tiled=True),
    )
    local_width = qkv_full.shape[2]
    head_count = local_width // DK
    lead_mask = (lax.axis_index("tp") == 0).astype(jnp.float32)
    ends = jnp.cumsum(doc_lengths[0])
    places = (
        lax.axis_index("seq") * tok_rows + jnp.arange(tok_rows + KW - 1, dtype=jnp.int32) - (KW - 1)
    )
    doc_ids = jnp.sum((places[:, None] >= ends[None, :]).astype(jnp.int32), axis=1)
    doc_ids = jnp.where(places < 0, -1, doc_ids)
    own_docs = doc_ids[KW - 1 :]
    prior_docs = doc_ids[KW - 2 : KW - 2 + tok_rows]
    valid = (own_docs < DOCS).astype(jnp.float32)
    fresh = (own_docs != prior_docs).astype(jnp.int32)
    tap_masks = [
        (doc_ids[KW - 1 - tap : KW - 1 - tap + tok_rows] == own_docs).astype(jnp.float32)
        for tap in range(KW)
    ]
    own_blocks = own_docs.reshape(blocks, GROUP)
    same_doc = (own_blocks[:, :, None] == own_blocks[:, None, :]).astype(jnp.float32)
    carry_mask = (jnp.cumsum(fresh.reshape(blocks, GROUP), axis=1) == 0).astype(jnp.float32)

    def to_blocks(array):
        return array.reshape(blocks, GROUP, head_count, -1).transpose(2, 0, 1, 3)

    def from_blocks(array):
        return array.transpose(1, 2, 0, 3).reshape(tok_rows, head_count, -1)

    scale_one = norm_scale(x_rows)
    normed_one = (x_rows * scale_one * attn_gain).astype(jnp.bfloat16)
    proj_low = jnp.einsum(
        "td,cde->cte", normed_one, qkv_full, preferred_element_type=jnp.float32
    ).astype(jnp.bfloat16)
    logit = jnp.dot(normed_one, beta_full, preferred_element_type=jnp.float32)
    rim_rows = from_behind(proj_low[:, tok_rows - (KW - 1) :, :], "seq", 1)
    extended = jnp.concatenate([rim_rows, proj_low], axis=1).astype(jnp.float32)
    conv_out = jnp.zeros((3, tok_rows, local_width), jnp.float32)
    for tap in range(KW):
        window = extended[:, KW - 1 - tap : KW - 1 - tap + tok_rows]
        conv_out = (
            conv_out + conv_weight[:, tap][:, None, :] * window * tap_masks[tap][None, :, None]
        )
    conv_sig = jax.nn.sigmoid(conv_out)
    activated = conv_out * conv_sig
    query_raw = activated[0].reshape(tok_rows, head_count, DK)
    key_raw = activated[1].reshape(tok_rows, head_count, DK)
    query_sq = jnp.sum(query_raw * query_raw, axis=-1, keepdims=True)
    key_sq = jnp.sum(key_raw * key_raw, axis=-1, keepdims=True)
    query_scale = lax.rsqrt(jnp.maximum(query_sq, unit_floor))
    key_scale = lax.rsqrt(jnp.maximum(key_sq, unit_floor))
    query_live = (query_sq > unit_floor).astype(jnp.float32)
    key_live = (key_sq > unit_floor).astype(jnp.float32)
    query_blocks = to_blocks(query_raw * query_scale)
    key_blocks = to_blocks(key_raw * key_scale)
    value_blocks = to_blocks(activated[2].reshape(tok_rows, head_count, DK))
    rate_sig = jax.nn.sigmoid(logit)
    rate_blocks = (rate_sig * valid[:, None]).reshape(blocks, GROUP, head_count).transpose(2, 0, 1)
    transition, contribution, base_rows, wy_rows = over_heads(group_parts, (0, 0, 0, None, None))(
        key_blocks, value_blocks, rate_blocks, same_doc, carry_mask
    )
    identity_mat = jnp.broadcast_to(jnp.eye(DK, dtype=jnp.float32), (head_count, DK, DK))
    zero_state = jnp.zeros((head_count, DK, DK), jnp.float32)
    transition_steps = jnp.moveaxis(transition, 1, 0)

    def chain(running, pair):
        product, partial_state = running
        step_trans, step_contrib = pair
        advanced = (
            batch_mul(step_trans, product),
            batch_mul(step_trans, partial_state) + step_contrib,
        )
        return (advanced, (product, partial_state))

    (dev_trans, dev_state), (products, partials) = lax.scan(
        chain, (identity_mat, zero_state), (transition_steps, jnp.moveaxis(contribution, 1, 0))
    )
    incoming = prefix((dev_trans, dev_state), "seq", compose, (identity_mat, zero_state), False)[1]
    group_starts = partials + jnp.einsum("nhij,hjk->nhik", products, incoming, precision=precise)
    start_blocks = jnp.moveaxis(group_starts, 0, 1)
    mix_blocks = over_heads(group_output, (0, 0, None, None, 0, 0, 0))(
        query_blocks, key_blocks, same_doc, carry_mask, base_rows, wy_rows, start_blocks
    )
    mixed = from_blocks(mix_blocks) * valid[:, None, None]
    mix_sq = jnp.mean(mixed * mixed, axis=-1, keepdims=True)
    mix_scale = lax.rsqrt(jnp.maximum(mix_sq, mix_floor))
    mix_live = (mix_sq > mix_floor).astype(jnp.float32)
    normed_mix = (mixed * mix_scale * out_gain).astype(jnp.bfloat16).reshape(tok_rows, local_width)
    o_term = jnp.dot(normed_mix, o_full, preferred_element_type=jnp.float32)
    resid = x_rows + tp_total(o_term)
    scale_two = norm_scale(resid)
    normed_local = (resid * scale_two * mlp_gain).astype(jnp.bfloat16)
    gate_up = jnp.einsum(
        "td,cdf->ctf", normed_local, gate_up_full, preferred_element_type=jnp.float32
    )
    gate_sig = jax.nn.sigmoid(gate_up[0])
    gate_act = gate_up[0] * gate_sig
    hidden = (gate_act * gate_up[1]).astype(jnp.bfloat16)
    down_term = jnp.dot(hidden, down_full, preferred_element_type=jnp.float32)
    mlp_out = tp_total(down_term)
    result = (resid + mlp_out).astype(jnp.bfloat16)
    grad_hidden = jnp.einsum(
        "td,fd->tf", grad_rows_out, down_full, preferred_element_type=jnp.float32
    )
    grad_gate = grad_hidden * gate_up[1] * gate_sig * (1.0 + gate_up[0] * (1.0 - gate_sig))
    grad_up = grad_hidden * gate_act
    grad_gate_up = jnp.stack([grad_gate, grad_up]).astype(jnp.bfloat16)
    down_part = jnp.einsum("tf,td->fd", hidden, grad_rows_out, preferred_element_type=jnp.float32)
    gate_up_part = jnp.einsum(
        "td,ctf->cdf", normed_local, grad_gate_up, preferred_element_type=jnp.float32
    )
    two_term = jnp.einsum(
        "ctf,cdf->td", grad_gate_up, gate_up_full, preferred_element_type=jnp.float32
    )
    grad_two = tp_total(two_term)
    mlp_gain_part = jnp.sum(grad_two * resid * scale_two, axis=0)
    grad_resid = grad_rows_out.astype(jnp.float32) + norm_back(resid, scale_two, mlp_gain, grad_two)
    grad_attn_local = grad_resid.astype(jnp.bfloat16)
    o_part = jnp.einsum(
        "te,td->ed", normed_mix, grad_attn_local, preferred_element_type=jnp.float32
    )
    grad_normed = jnp.einsum(
        "td,ed->te", grad_attn_local, o_full, preferred_element_type=jnp.float32
    ).reshape(tok_rows, head_count, DK)
    out_gain_part = jnp.sum(grad_normed * mixed * mix_scale, axis=(0, 1))
    weighted_mix = out_gain * grad_normed
    grad_mixed = (
        mix_scale * weighted_mix
        - mixed * mix_scale**3 * mix_live * jnp.mean(weighted_mix * mixed, axis=-1, keepdims=True)
    ) * valid[:, None, None]
    grad_blocks = to_blocks(grad_mixed)
    pulls = over_heads(state_pull, (0, 0, None, None, 0, 0))(
        query_blocks, key_blocks, same_doc, carry_mask, wy_rows, grad_blocks
    )

    def back_chain(running, pair):
        grad_end, product = running
        step_trans, step_pull = pair
        advanced = (step_pull + batch_mul_t(step_trans, grad_end), batch_mul_t(step_trans, product))
        return (advanced, (grad_end, product))

    (dev_pull, dev_back), (grad_ends, back_products) = lax.scan(
        back_chain,
        (zero_state, identity_mat),
        (transition_steps, jnp.moveaxis(pulls, 1, 0)),
        reverse=True,
    )
    outgoing = prefix((dev_back, dev_pull), "seq", compose, (identity_mat, zero_state), True)[1]
    end_grads = grad_ends + jnp.einsum("nhij,hjk->nhik", back_products, outgoing, precision=precise)
    grad_query, grad_key, grad_value, grad_rate = over_heads(
        group_grads, (0, 0, 0, 0, None, None, 0, 0, 0)
    )(
        query_blocks,
        key_blocks,
        value_blocks,
        rate_blocks,
        same_doc,
        carry_mask,
        start_blocks,
        grad_blocks,
        jnp.moveaxis(end_grads, 0, 1),
    )
    grad_query = from_blocks(grad_query)
    grad_key = from_blocks(grad_key)
    grad_query_raw = query_scale * grad_query - query_raw * query_scale**3 * query_live * jnp.sum(
        query_raw * grad_query, axis=-1, keepdims=True
    )
    grad_key_raw = key_scale * grad_key - key_raw * key_scale**3 * key_live * jnp.sum(
        key_raw * grad_key, axis=-1, keepdims=True
    )
    grad_activated = jnp.stack(
        [
            grad_query_raw.reshape(tok_rows, local_width),
            grad_key_raw.reshape(tok_rows, local_width),
            from_blocks(grad_value).reshape(tok_rows, local_width),
        ]
    )
    grad_conv = grad_activated * conv_sig * (1.0 + conv_out * (1.0 - conv_sig))
    grad_extended = jnp.zeros((3, tok_rows + KW - 1, local_width), jnp.float32)
    tap_grads = []
    for tap in range(KW):
        masked = grad_conv * tap_masks[tap][None, :, None]
        window = extended[:, KW - 1 - tap : KW - 1 - tap + tok_rows]
        tap_grads.append(jnp.sum(masked * window, axis=1))
        grad_extended = grad_extended + jnp.pad(
            conv_weight[:, tap][:, None, :] * masked, ((0, 0), (KW - 1 - tap, tap), (0, 0))
        )
    conv_part = jnp.stack(tap_grads, axis=1)
    rim_back = from_behind(grad_extended[:, : KW - 1], "seq", -1)
    grad_proj = jnp.concatenate(
        [grad_extended[:, KW - 1 : tok_rows], grad_extended[:, tok_rows:] + rim_back], axis=1
    ).astype(jnp.bfloat16)
    rate_grad = grad_rate.transpose(1, 2, 0).reshape(tok_rows, head_count)
    grad_logit = (rate_grad * valid[:, None] * rate_sig * (1.0 - rate_sig)).astype(jnp.bfloat16)
    qkv_part = jnp.einsum("td,cte->cde", normed_one, grad_proj, preferred_element_type=jnp.float32)
    beta_part = jnp.einsum("td,th->dh", normed_one, grad_logit, preferred_element_type=jnp.float32)
    grad_one_part = jnp.einsum(
        "cte,cde->td", grad_proj, qkv_full, preferred_element_type=jnp.float32
    ) + jnp.einsum("th,dh->td", grad_logit, beta_full, preferred_element_type=jnp.float32)
    grad_one = tp_total(grad_one_part)
    attn_gain_part = jnp.sum(grad_one * x_rows * scale_one, axis=0)
    input_local = (grad_resid + norm_back(x_rows, scale_one, attn_gain, grad_one)).astype(
        jnp.bfloat16
    )
    conv_whole = lax.dynamic_update_slice(
        jnp.zeros((3, KW, model_width), jnp.float32),
        conv_part,
        (0, 0, lax.axis_index("tp") * local_width),
    )
    attn_gain_grad, mlp_gain_grad, out_gain_grad, conv_grad = lax.psum(
        (attn_gain_part * lead_mask, mlp_gain_part * lead_mask, out_gain_part, conv_whole),
        ("row", "seq", "tp"),
    )
    qkv_sum, beta_sum, o_sum, gate_up_sum, down_sum = (
        lax.psum_scatter(
            qkv_part.astype(jnp.bfloat16), ("row", "seq"), scatter_dimension=1, tiled=True
        ).astype(jnp.float32),
        lax.psum_scatter(
            beta_part.astype(jnp.bfloat16), ("row", "seq"), scatter_dimension=0, tiled=True
        ).astype(jnp.float32),
        lax.psum_scatter(
            o_part.astype(jnp.bfloat16), ("row", "seq"), scatter_dimension=1, tiled=True
        ).astype(jnp.float32),
        lax.psum_scatter(
            gate_up_part.astype(jnp.bfloat16), ("row", "seq"), scatter_dimension=1, tiled=True
        ).astype(jnp.float32),
        lax.psum_scatter(
            down_part.astype(jnp.bfloat16), ("row", "seq"), scatter_dimension=1, tiled=True
        ).astype(jnp.float32),
    )
    return (
        result[None],
        input_local[None],
        attn_gain_grad,
        mlp_gain_grad,
        out_gain_grad,
        conv_grad,
        qkv_sum,
        beta_sum,
        o_sum,
        gate_up_sum,
        down_sum,
    )


CHUNK = 128
PAD = 8


def mul(left, right, dims, precision=None):
    return lax.dot_general(
        left, right, ((dims[:1], dims[1:]), ((), ())), precision=precision, preferred_element_type=jnp.float32
    )


def fine(left, right, dims=(1, 0)):
    return mul(left, right, dims, precise)


def plain(left, right, dims=(1, 0)):
    return mul(left.astype(jnp.bfloat16), right.astype(jnp.bfloat16), dims)


def chunk_masks(doc_col, doc_row):
    same = doc_col == doc_row
    down = lax.broadcasted_iota(jnp.int32, (CHUNK, CHUNK), 0)
    along = lax.broadcasted_iota(jnp.int32, (CHUNK, CHUNK), 1)
    lower = jnp.where(same & (down >= along), 1.0, 0.0)
    strict = jnp.where(same & (down > along), 1.0, 0.0)
    return lower, strict, down, along


def lower_inverse(systems, down, along):
    at_one = (down // 2 == along // 2) & (down != along)
    unit = jnp.where(down == along, 1.0, 0.0)
    inverses = [unit - jnp.where(at_one, system, 0.0) for system in systems]
    half = 2
    while half < CHUNK:
        joins = (down // (2 * half) == along // (2 * half)) & (down // half != along // half)
        inner = [
            fine(jnp.where(joins, system, 0.0), inverse)
            for system, inverse in zip(systems, inverses)
        ]
        inverses = [inverse - fine(inverse, part) for inverse, part in zip(inverses, inner)]
        half *= 2
    return inverses


def tap_mask(aux, tap):
    return 1.0 if tap == 0 else aux[:, 3 + tap : 4 + tap]


def convolved(window, taps, aux):
    total = 0.0
    for tap in range(KW):
        total = total + (
            taps[tap : tap + 1] * window[PAD - tap : PAD - tap + CHUNK] * tap_mask(aux, tap)
        )
    return total


def sigmoid(values):
    return 1.0 / (1.0 + jnp.exp(-values))


def unit_scale(values):
    total = jnp.sum(values * values, axis=1, keepdims=True)
    floor = DK / 16.0
    return lax.rsqrt(jnp.maximum(total, floor)), jnp.where(total > floor, 1.0, 0.0)


def mix_norm(mixed):
    mean = jnp.mean(mixed * mixed, axis=1, keepdims=True)
    return lax.rsqrt(jnp.maximum(mean, mix_floor)), jnp.where(mean > mix_floor, 1.0, 0.0)


def forward_kernel(
    heads,
    n1_ref,
    qkv_ref,
    beta_ref,
    taps_ref,
    aux_ref,
    docs_ref,
    gain_ref,
    o_weight_ref,
    gate_ref,
    up_ref,
    down_ref,
    proj_ref,
    logit_ref,
    mixed_ref,
    normed_ref,
    inverse_ref,
    states_ref,
    written_ref,
    o_ref,
    gate_out,
    up_out,
    down_out,
    window_ref,
    state_ref,
    own_sems,
    *sems,
):
    width = heads * DK
    line = Line()
    greet(exchange_partners(line))
    row = lax.axis_index("row")

    def rows_of(ref, count):
        return lambda seq: ref.at[pl.ds(pl.multiple_of(seq * count, count), count)]

    units = down_out.shape[1]
    whole = Exchange(line, rows_of(o_weight_ref, width), o_ref, sems[:4])
    moves = [
        Exchange(line, lambda seq: gate_ref.at[seq], gate_out, sems[4:6]),
        Exchange(line, lambda seq: up_ref.at[seq], up_out, sems[6:8]),
        Exchange(line, rows_of(down_ref, units), down_out, sems[8:10]),
    ]
    whole.start()
    own = [
        pltpu.make_async_copy(whole.source(line.place), o_ref.at[row, line.place], own_sems.at[0])
    ]
    for i, move in enumerate(moves):
        own.append(
            pltpu.make_async_copy(
                move.source(line.place), move.target.at[line.place], own_sems.at[i + 1]
            )
        )
    for copy in own:
        copy.start()
    for move in moves:
        move.start()
    own[0].wait()
    whole.share_own()
    window_ref[0:PAD] = jnp.zeros((PAD, 3 * width), jnp.float32)
    state_ref[...] = jnp.zeros_like(state_ref)

    def chunk(n, _):
        rows = pl.ds(pl.multiple_of(n * CHUNK, CHUNK), CHUNK)
        n1 = n1_ref[rows]
        proj = jnp.concatenate(
            [mul(n1, qkv_ref[:, :, c].reshape(-1, width), (1, 0)) for c in range(3)], axis=1
        ).astype(jnp.bfloat16)
        proj_ref[rows] = proj
        window_ref[PAD : PAD + CHUNK] = proj.astype(jnp.float32)
        logit = mul(n1, beta_ref[...], (1, 1))
        logit_ref[rows] = logit
        aux = aux_ref[rows]
        conv = convolved(window_ref[...], taps_ref[...], aux)
        act = conv * sigmoid(conv)
        window_ref[0:PAD] = window_ref[CHUNK : CHUNK + PAD]
        valid, carry, tail = aux[:, 1:2], aux[:, 2:3], aux[:, 3:4]
        carry_last = carry[CHUNK - 1 :]
        lower, strict, down, along = chunk_masks(aux[:, 0:1], docs_ref[pl.ds(n, 1)])
        rate_all = sigmoid(logit) * valid
        parts = []
        for h in range(heads):
            query = act[:, h * DK : (h + 1) * DK]
            key = act[:, width + h * DK : width + (h + 1) * DK]
            value = act[:, 2 * width + h * DK : 2 * width + (h + 1) * DK]
            query = query * unit_scale(query)[0]
            key = key * unit_scale(key)[0]
            rate = rate_all[:, h : h + 1]
            system = rate * fine(key, key, (1, 1)) * strict
            parts.append((query, key, value, rate, system))
        inverses = lower_inverse([part[4] for part in parts], down, along)
        for h, (query, key, value, rate, _) in enumerate(parts):
            inverse = inverses[h]
            state = state_ref[h]
            carried_key = carry * key
            right = rate * (value - fine(carried_key, state))
            written = fine(inverse, right)
            scores = plain(query, key, (1, 1)) * lower
            mixed = carry * plain(query, state) + plain(scores, written)
            mixed = mixed * valid
            states_ref[h, n] = state
            written_ref[h, n] = written
            inverse_ref[h, n] = inverse
            state_ref[h] = carry_last * state + fine(tail * key, written, (0, 0))
            columns = pl.ds(h * DK, DK)
            mixed_ref[rows, columns] = mixed
            normed_ref[rows, columns] = (
                mixed * mix_norm(mixed)[0] * gain_ref[...]
            ).astype(jnp.bfloat16)
        return 0

    chunks = n1_ref.shape[0] // CHUNK
    middle = chunks // 2
    lax.fori_loop(0, middle, chunk, 0)
    for i in range(1, line.count):
        whole.share_came(i)
    lax.fori_loop(middle, chunks, chunk, 0)
    for copy in own[1:]:
        copy.wait()
    whole.finish()
    for move in moves:
        move.finish()


def backward_kernel(
    heads,
    grad_ref,
    o_ref,
    proj_ref,
    logit_ref,
    mixed_ref,
    inverse_ref,
    states_ref,
    written_ref,
    taps_ref,
    aux_ref,
    docs_ref,
    gain_ref,
    down_sum_ref,
    gate_sum_ref,
    up_sum_ref,
    o_part_ref,
    grad_proj_ref,
    grad_logit_ref,
    conv_grad_ref,
    gain_grad_ref,
    down_came_ref,
    gate_came_ref,
    up_came_ref,
    o_came_ref,
    window_ref,
    masked_ref,
    state_ref,
    o_rows,
    *sems,
):
    width = heads * DK
    greet(along_axis("seq") + along_axis("row"))
    moves = moves_of(
        Swap,
        "seq",
        (down_sum_ref, gate_sum_ref, up_sum_ref),
        (down_came_ref, gate_came_ref, up_came_ref),
        sems[:7],
    ) + moves_of(Swap, "row", (o_part_ref,), (o_came_ref,), sems[7:])
    for move in moves:
        move.start()
    side_by_side(o_ref, o_rows)
    chunks = grad_ref.shape[0] // CHUNK
    state_ref[...] = jnp.zeros_like(state_ref)
    masked_ref[...] = jnp.zeros_like(masked_ref)
    conv_grad_ref[...] = jnp.zeros_like(conv_grad_ref)
    gain_grad_ref[...] = jnp.zeros_like(gain_grad_ref)

    def chunk(step, _):
        n = chunks - 1 - step
        rows = pl.ds(pl.multiple_of(n * CHUNK, CHUNK), CHUNK)
        before = jnp.maximum(n - 1, 0)
        aux = aux_ref[rows]
        grad_normed = mul(grad_ref[rows], o_rows[...], (1, 1))
        prior = proj_ref[pl.ds(pl.multiple_of(before * CHUNK + CHUNK - 16, 16), 16)]
        window_ref[0:PAD] = prior.astype(jnp.float32)[16 - PAD :]
        window_ref[PAD : PAD + CHUNK] = proj_ref[rows].astype(jnp.float32)
        window = window_ref[...]
        taps = taps_ref[...]
        conv = convolved(window, taps, aux)
        conv_sig = sigmoid(conv)
        act = conv * conv_sig
        valid, carry, tail = aux[:, 1:2], aux[:, 2:3], aux[:, 3:4]
        carry_last = carry[CHUNK - 1 :]
        lower, strict, down, along = chunk_masks(aux[:, 0:1], docs_ref[pl.ds(n, 1)])
        rate_sig = sigmoid(logit_ref[rows])
        rate_all = rate_sig * valid
        lanes = lax.broadcasted_iota(jnp.int32, rate_all.shape, 1)
        grad_rates = jnp.zeros_like(rate_all)
        grads = [[], [], []]
        for h in range(heads):
            columns = pl.ds(h * DK, DK)
            mixed = mixed_ref[rows, columns]
            mix_scale, mix_live = mix_norm(mixed)
            grad_out = grad_normed[:, h * DK : (h + 1) * DK]
            scaled = mixed * mix_scale
            gain_grad_ref[...] += jnp.sum(grad_out * scaled, axis=0, keepdims=True)
            weighted = gain_ref[...] * grad_out
            grad_mix = (
                mix_scale * weighted
                - scaled
                * (mix_scale * mix_scale * mix_live)
                * jnp.mean(weighted * mixed, axis=1, keepdims=True)
            ) * valid
            query_raw = act[:, h * DK : (h + 1) * DK]
            key_raw = act[:, width + h * DK : width + (h + 1) * DK]
            value = act[:, 2 * width + h * DK : 2 * width + (h + 1) * DK]
            query_scale, query_live = unit_scale(query_raw)
            key_scale, key_live = unit_scale(key_raw)
            query = query_raw * query_scale
            key = key_raw * key_scale
            rate = rate_all[:, h : h + 1]
            inverse = inverse_ref[h, n]
            state = states_ref[h, n]
            written = written_ref[h, n]
            grad_state = state_ref[h]
            tail_key = tail * key
            carried_key = carry * key
            scores = plain(query, key, (1, 1)) * lower
            pulled = plain(scores, grad_mix, (0, 0)) + fine(tail_key, grad_state)
            solved = fine(inverse, pulled, (0, 0))
            state_ref[h] = (
                carry_last * grad_state
                + plain(carry * query, grad_mix, (0, 0))
                - fine(rate * carried_key, solved, (0, 0))
            )
            grad_scores = plain(grad_mix, written, (1, 1)) * lower
            grad_query = carry * plain(grad_mix, state, (1, 1)) + plain(grad_scores, key)
            guess_error = value - plain(carried_key, state)
            gram = plain(key, key, (1, 1)) * strict
            grad_system = plain(solved, written, (1, 1)) * strict
            grad_rate = jnp.sum(solved * guess_error, axis=1, keepdims=True) - jnp.sum(
                grad_system * gram, axis=1, keepdims=True
            )
            grad_gram = rate * grad_system
            grad_key = (
                plain(grad_scores, query, (0, 0))
                + tail * plain(written, grad_state, (1, 1))
                - rate * carry * plain(solved, state, (1, 1))
                - plain(grad_gram, key)
                - plain(grad_gram, key, (0, 0))
            )
            grads[0].append(
                query_scale
                * (
                    grad_query
                    - query
                    * query_live
                    * jnp.sum(query * grad_query, axis=1, keepdims=True)
                )
            )
            grads[1].append(
                key_scale
                * (grad_key - key * key_live * jnp.sum(key * grad_key, axis=1, keepdims=True))
            )
            grads[2].append(rate * solved)
            grad_rates = grad_rates + jnp.where(lanes == h, grad_rate, 0.0)
        grad_act = jnp.concatenate(grads[0] + grads[1] + grads[2], axis=1)
        grad_conv = grad_act * conv_sig * (1.0 + conv * (1.0 - conv_sig))
        grad_proj = taps[0:1] * grad_conv
        conv_grad_ref[0:1] += jnp.sum(
            grad_conv * window[PAD : PAD + CHUNK], axis=0, keepdims=True
        )
        for tap in range(1, KW):
            masked = grad_conv * tap_mask(aux, tap)
            conv_grad_ref[tap : tap + 1] += jnp.sum(
                masked * window[PAD - tap : PAD - tap + CHUNK], axis=0, keepdims=True
            )
            masked_ref[tap - 1, CHUNK : CHUNK + PAD] = masked_ref[tap - 1, 0:PAD]
            masked_ref[tap - 1, 0:CHUNK] = masked
            grad_proj = grad_proj + taps[tap : tap + 1] * masked_ref[tap - 1, tap : tap + CHUNK]
        grad_proj_ref[rows] = grad_proj.astype(jnp.bfloat16)
        grad_logit_ref[rows] = (grad_rates * rate_sig * (1.0 - rate_sig) * valid).astype(
            jnp.bfloat16
        )
        return 0

    lax.fori_loop(0, chunks, chunk, 0)
    for move in moves:
        move.finish()


def in_vmem(count):
    return [pl.BlockSpec(memory_space=pltpu.VMEM)] * count


def run_forward(n1, qkv, beta, taps, aux, docs, gain, o_weight, gate, up, down):
    row_len, heads = n1.shape[0], qkv.shape[-1] // DK
    rows_axis, seqs = qkv.shape[:2]
    chunks, width, f32 = row_len // CHUNK, heads * DK, jnp.float32
    shapes = (
        ((row_len, 3 * width), jnp.bfloat16),
        ((row_len, beta.shape[0]), f32),
        ((row_len, width), f32),
        ((row_len, width), jnp.bfloat16),
        ((heads, chunks, CHUNK, CHUNK), f32),
        ((heads, chunks, DK, DK), f32),
        ((heads, chunks, CHUNK, DK), f32),
        ((rows_axis, seqs, width, o_weight.shape[1]), jnp.bfloat16),
        (gate.shape, jnp.bfloat16),
        (up.shape, jnp.bfloat16),
        ((seqs, down.shape[0] // seqs, down.shape[1]), jnp.bfloat16),
    )
    hbm = [pl.BlockSpec(memory_space=pl.ANY)]
    return pl.pallas_call(
        functools.partial(forward_kernel, heads),
        out_shape=[jax.ShapeDtypeStruct(*shape) for shape in shapes],
        in_specs=in_vmem(7) + hbm * 4,
        out_specs=in_vmem(7) + hbm * 4,
        scratch_shapes=[
            pltpu.VMEM((PAD + CHUNK, 3 * width), f32),
            pltpu.VMEM((heads, DK, DK), f32),
            dma_sems(4),
        ]
        + exchange_sems()
        + [dma_sems(seqs - 1)] * 6,
        compiler_params=pltpu.CompilerParams(
            collective_id=5, has_side_effects=True, vmem_limit_bytes=48 * 1024 * 1024
        ),
        name="mixer_forward",
    )(n1, qkv, beta, taps, aux, docs, gain, o_weight, gate, up, down)


def run_backward(grad, o_full, saved, taps, aux, docs, gain, sums, o_part):
    row_len, heads = grad.shape[0], o_full.shape[2] // DK
    width, f32 = heads * DK, jnp.float32
    logit = saved[1]
    shapes = (
        ((row_len, 3 * width), jnp.bfloat16),
        (logit.shape, jnp.bfloat16),
        ((KW, 3 * width), f32),
        ((1, DK), f32),
    )
    far = [pl.BlockSpec(memory_space=pl.ANY)] * (len(sums) + 1)
    far_shapes = tuple((array.shape, array.dtype) for array in (*sums, o_part))
    return pl.pallas_call(
        functools.partial(backward_kernel, heads),
        out_shape=[jax.ShapeDtypeStruct(*shape) for shape in shapes + far_shapes],
        in_specs=in_vmem(12) + far,
        out_specs=in_vmem(len(shapes)) + far,
        scratch_shapes=[
            pltpu.VMEM((PAD + CHUNK, 3 * width), f32),
            pltpu.VMEM((KW - 1, CHUNK + PAD, 3 * width), f32),
            pltpu.VMEM((heads, DK, DK), f32),
            pltpu.VMEM((width, grad.shape[1]), jnp.bfloat16),
        ]
        + pair_sems("seq", len(sums))
        + pair_sems("row", 1),
        compiler_params=pltpu.CompilerParams(
            collective_id=6, has_side_effects=True, vmem_limit_bytes=48 * 1024 * 1024
        ),
        name="mixer_backward",
    )(grad, o_full, *saved, taps, aux, docs, gain, *sums, o_part)


def row_aux(docs):
    f32 = jnp.float32
    chunks = docs.reshape(-1, CHUNK)
    prior = jnp.concatenate([jnp.full((1,), -1, jnp.int32), chunks[:-1, -1]])
    padded = jnp.concatenate([jnp.full((KW - 1,), -1, jnp.int32), docs])
    columns = [
        docs,
        docs < DOCS,
        (chunks == prior[:, None]).reshape(-1),
        (chunks == chunks[:, -1:]).reshape(-1),
    ] + [padded[KW - 1 - tap : KW - 1 - tap + docs.shape[0]] == docs for tap in range(1, KW)]
    columns = [column.astype(f32) for column in columns]
    columns += [jnp.zeros_like(columns[0])] * (8 - len(columns))
    return jnp.stack(columns, axis=1), chunks.astype(f32)


def remote(source, target, send, recv, where):
    return pltpu.make_async_remote_copy(
        src_ref=source,
        dst_ref=target,
        send_sem=send,
        recv_sem=recv,
        device_id=where,
        device_id_type=pl.DeviceIdType.MESH,
    )


def greet(partners):
    barrier = pltpu.get_barrier_semaphore()
    for partner, there in partners:

        @pl.when(there)
        def _(partner=partner):
            pl.semaphore_signal(
                barrier, inc=1, device_id=partner, device_id_type=pl.DeviceIdType.MESH
            )

    pl.semaphore_wait(barrier, sum(there.astype(jnp.int32) for _, there in partners))


def around(axis):
    count, place = lax.axis_size(axis), lax.axis_index(axis)
    return [lax.rem(place + by, count) for by in range(1, count)]


def line_partners():
    count, place, core = lax.axis_size("seq"), lax.axis_index("seq"), lax.axis_index("tp")
    return [
        ({"seq": jnp.minimum(place + 1, count - 1)}, place < count - 1),
        ({"seq": jnp.maximum(place - 1, 0)}, place > 0),
        ({"tp": 1 - core}, core >= 0),
    ]


class Line:
    def __init__(self):
        self.count, self.place = lax.axis_size("seq"), lax.axis_index("seq")
        self.core = lax.axis_index("tp")
        self.other = 1 - self.core
        self.right = {"seq": jnp.minimum(self.place + 1, self.count - 1)}
        self.left = {"seq": jnp.maximum(self.place - 1, 0)}
        self.across = {"tp": self.other}


class Gather:
    def __init__(self, line, slots, sems):
        self.line, self.slots, self.sems = line, slots, sems
        self.parts = sems.shape[2]
        self.rows = slots.shape[2] // self.parts

    def span(self, part):
        return pl.ds(part * self.rows, self.rows)

    def copy(self, kind, seq, part):
        line = self.line
        send = {"right": 0, "left": 1, "across": 2}[kind]
        recv = 4 if kind == "across" else 3
        slot = self.slots.at[seq, line.core, self.span(part)]
        where = {"right": line.right, "left": line.left, "across": line.across}[kind]
        return remote(
            slot, slot, self.sems.at[send, seq, part], self.sems.at[recv, seq, part], where
        )

    def forward(self, seq, part, right, left):
        line = self.line
        if right:

            @pl.when(line.place < line.count - 1)
            def _():
                self.copy("right", seq, part).start()

        if left:

            @pl.when(line.place > 0)
            def _():
                self.copy("left", seq, part).start()

        self.copy("across", seq, part).start()

    def phase(self, by, part):
        line = self.line
        if by == 0:
            self.forward(line.place, part, True, True)
            return

        @pl.when(line.place - by >= 0)
        def _():
            self.copy("right", line.place - by, part).wait_recv()
            self.forward(line.place - by, part, True, False)

        @pl.when(line.place + by < line.count)
        def _():
            self.copy("left", line.place + by, part).wait_recv()
            self.forward(line.place + by, part, False, True)

    def phases(self, by):
        for part in range(self.parts):
            self.phase(by, part)

    def finish(self):
        line = self.line
        for seq in range(line.count):
            for part in range(self.parts):

                @pl.when((line.place >= seq) & (line.place < line.count - 1))
                def _():
                    self.copy("right", seq, part).wait_send()

                @pl.when((line.place <= seq) & (line.place > 0))
                def _():
                    self.copy("left", seq, part).wait_send()

                self.copy("across", seq, part).wait()


class Scatter:
    def __init__(self, line, blocks, came, across, sems):
        self.line, self.blocks, self.came, self.across, self.sems = line, blocks, came, across, sems
        self.parts = sems.shape[2]
        self.rows = blocks.shape[2] // self.parts

    def span(self, part):
        return pl.ds(part * self.rows, self.rows)

    def over(self, seq, part):
        line, span = self.line, self.span(part)
        return remote(
            self.blocks.at[seq, line.other, span],
            self.across.at[seq, span],
            self.sems.at[0, seq, part],
            self.sems.at[1, seq, part],
            line.across,
        )

    def along(self, kind, seq, part):
        line, span = self.line, self.span(part)
        way = {"right": 0, "left": 1}[kind]
        return remote(
            self.blocks.at[seq, line.core, span],
            self.came.at[way, seq, span],
            self.sems.at[2, seq, part],
            self.sems.at[3 + way, seq, part],
            line.right if way == 0 else line.left,
        )

    def nears(self, k):
        for part in range(self.parts):
            self.near(k, part)

    def fars(self, k):
        for part in range(self.parts):
            self.far(k, part)

    def product(self, left_ref, right_ref, part, order=1, tile=512, right_tile=None):
        seqs, cores, _, width = self.blocks.shape
        span = self.span(part)
        left = left_ref[:, span].reshape(seqs * cores * self.rows, -1)

        def columns(t, _):
            across = pl.ds(pl.multiple_of(t * tile, tile), tile)
            if right_tile is not None:
                total = right_tile(left, t, across)
            elif order == 1:
                total = mul(left, right_ref[across], (1, 1))
            else:
                total = mul(left, right_ref[:, across], (1, 0))
            self.blocks[:, :, span, across] = total.astype(jnp.bfloat16).reshape(
                seqs, cores, self.rows, tile
            )
            return 0

        lax.fori_loop(0, width // tile, columns, 0)
        for k in range(seqs):
            self.over(self.target(k), part).start()

    def pass_on(self, kind, seq, part):
        line, span = self.line, self.span(part)
        f32 = jnp.float32
        first = line.place == (0 if kind == "right" else line.count - 1)
        way = {"right": 0, "left": 1}[kind]
        self.over(seq, part).wait_recv()
        total = self.blocks[seq, line.core, span].astype(f32)
        total = total + self.across[seq, span].astype(f32)

        @pl.when(first)
        def _():
            self.blocks[seq, line.core, span] = total.astype(jnp.bfloat16)

        @pl.when(jnp.logical_not(first))
        def _():
            self.along(kind, seq, part).wait_recv()
            self.blocks[seq, line.core, span] = (
                total + self.came[way, seq, span].astype(f32)
            ).astype(jnp.bfloat16)

        self.along(kind, seq, part).start()

    def target(self, k):
        line = self.line
        return jnp.where(line.place < line.count // 2, line.count - 1 - k, k)

    def near(self, k, part):
        line = self.line
        low = line.place < line.count // 2

        @pl.when(low & (line.count - 1 - k > line.place))
        def _():
            self.pass_on("right", line.count - 1 - k, part)

        @pl.when(jnp.logical_not(low) & (k < line.place))
        def _():
            self.pass_on("left", k, part)

    def far(self, k, part):
        line = self.line
        low = line.place < line.count // 2

        @pl.when(low & (k < line.place))
        def _():
            self.pass_on("left", k, part)

        @pl.when(jnp.logical_not(low) & (line.count - 1 - k > line.place))
        def _():
            self.pass_on("right", line.count - 1 - k, part)

    def wait_own(self, part):
        line = self.line

        @pl.when(line.place > 0)
        def _():
            self.along("right", line.place, part).wait_recv()

        @pl.when(line.place < line.count - 1)
        def _():
            self.along("left", line.place, part).wait_recv()

        self.over(line.place, part).wait_recv()

    def own_rows(self, rows):
        line = self.line
        f32 = jnp.float32
        total = self.blocks[line.place, line.core, rows].astype(f32)
        total = total + self.across[line.place, rows].astype(f32)
        from_left = self.came[0, line.place, rows].astype(f32)
        from_right = self.came[1, line.place, rows].astype(f32)
        total = total + jnp.where(line.place > 0, from_left, 0.0)
        return total + jnp.where(line.place < line.count - 1, from_right, 0.0)

    def finish(self):
        line = self.line
        for seq in range(line.count):
            for part in range(self.parts):
                self.over(seq, part).wait_send()

                @pl.when(line.place != seq)
                def _():
                    self.along("right", seq, part).wait_send()


class Exchange:
    def __init__(self, line, source, target, sems):
        self.line, self.source, self.target = line, source, target
        self.send, self.recv = sems[:2]
        self.shared = len(sems) > 2
        if self.shared:
            self.send_row, self.recv_row = sems[2:]
        self.row = lax.axis_index("row")
        self.seq_others, self.row_others = around("seq"), around("row")

    def spread(self, i):
        other = self.seq_others[i]
        return remote(
            self.source(other),
            self.target.at[self.row, self.line.place]
            if self.shared
            else self.target.at[self.line.place],
            self.send.at[i],
            self.recv.at[i],
            {"seq": other},
        )

    def share(self, i, j):
        line = self.line
        came_from = lax.rem(line.place + line.count - i, line.count)
        slot = self.target.at[self.row, came_from]
        return remote(
            slot, slot, self.send_row.at[i, j], self.recv_row.at[i, j], {"row": self.row_others[j]}
        )

    def start(self):
        for i in range(len(self.seq_others)):
            self.spread(i).start()

    def share_own(self):
        for j in range(len(self.row_others)):
            self.share(0, j).start()

    def share_came(self, i):
        self.spread(i - 1).wait_recv()
        for j in range(len(self.row_others)):
            self.share(i, j).start()

    def finish(self):
        for i in range(len(self.seq_others)):
            self.spread(i).wait_send()
            if not self.shared:
                self.spread(i).wait_recv()
        for i in range(len(self.seq_others) + 1 if self.shared else 0):
            for j in range(len(self.row_others)):
                self.share(i, j).wait()


class Share:
    def __init__(self, axis, source, target, sems, own_sem):
        self.axis, self.source, self.target = axis, source, target
        self.send, self.recv = sems
        self.others = around(axis)
        self.own = pltpu.make_async_copy(source, target.at[lax.axis_index(axis)], own_sem)

    def copy(self, i):
        return remote(
            self.source,
            self.target.at[lax.axis_index(self.axis)],
            self.send.at[i],
            self.recv.at[i],
            {self.axis: self.others[i]},
        )

    def start(self):
        for i in range(len(self.others)):
            self.copy(i).start()
        self.own.start()

    def finish(self):
        for i in range(len(self.others)):
            self.copy(i).wait()
        self.own.wait()


class Swap:
    def __init__(self, axis, source, target, sems, own_sem):
        self.axis, self.source, self.target = axis, source, target
        self.send, self.recv = sems
        self.others = around(axis)
        place = lax.axis_index(axis)
        self.own = pltpu.make_async_copy(source.at[place], target.at[place], own_sem)

    def copy(self, i):
        return remote(
            self.source.at[self.others[i]],
            self.target.at[lax.axis_index(self.axis)],
            self.send.at[i],
            self.recv.at[i],
            {self.axis: self.others[i]},
        )

    def start(self):
        for i in range(len(self.others)):
            self.copy(i).start()
        self.own.start()

    def finish(self):
        for i in range(len(self.others)):
            self.copy(i).wait()
        self.own.wait()


def pair_sems(axis, count):
    return [dma_sems(lax.axis_size(axis) - 1)] * (2 * count) + [dma_sems(count)]


def moves_of(kind, axis, sources, targets, sems):
    return [
        kind(axis, source, target, sems[2 * i : 2 * i + 2], sems[-1].at[i])
        for i, (source, target) in enumerate(zip(sources, targets))
    ]


def along_axis(axis):
    return [({axis: other}, other >= 0) for other in around(axis)]


def exchange_sems():
    seqs, rows = lax.axis_size("seq"), lax.axis_size("row")
    return [
        dma_sems(seqs - 1),
        dma_sems(seqs - 1),
        dma_sems(seqs, rows - 1),
        dma_sems(seqs, rows - 1),
    ]


def exchange_partners(line):
    return [({"seq": other}, other >= 0) for other in around("seq")] + [
        ({"row": other}, other >= 0) for other in around("row")
    ]


STEP = 32


def over_rows(total, part, body):
    def step(i, _):
        body(pl.ds(pl.multiple_of(part * total.rows + i * STEP, STEP), STEP))
        return 0

    lax.fori_loop(0, total.rows // STEP, step, 0)


def resid_kernel(
    mix_ref, o_ref, x_ref, g_ref, gain_ref, gate_ref, up_ref, down_ref,
    resid_ref, n2_ref, g_full_ref, gate_full_ref, up_full_ref, down_full_ref,
    blocks, came, across, o_rows, sum_sems, n2_sems, g_sems, *sems,
):
    line = Line()
    greet(line_partners() + along_axis("row"))
    shares = moves_of(
        Share,
        "row",
        (gate_ref, up_ref, down_ref),
        (gate_full_ref, up_full_ref, down_full_ref),
        sems,
    )
    for share in shares:
        share.start()
    rows = n2_ref.shape[2]
    total = Scatter(line, blocks, came, across, sum_sems)
    n2 = Gather(line, n2_ref, n2_sems)
    grads = Gather(line, g_full_ref, g_sems)
    g_full_ref[line.place, line.core] = g_ref[
        pl.ds(pl.multiple_of(line.core * rows, rows), rows)
    ]
    grads.phases(0)
    side_by_side(o_ref, o_rows)
    for part in range(total.parts):
        total.product(mix_ref, o_rows, part, order=0)
    for k in range(1, line.count):
        grads.phases(k)
        total.nears(k - 1)
    for k in range(line.count - 1):
        total.fars(k)

    def normed(span):
        x_span = pl.ds(pl.multiple_of(line.core * rows + span.start, STEP), STEP)
        resid = x_ref[x_span].astype(jnp.float32) + total.own_rows(span)
        resid_ref[span] = resid
        n2_ref[line.place, line.core, span] = (
            resid * norm_scale(resid) * gain_ref[...]
        ).astype(jnp.bfloat16)

    for part in range(total.parts):
        total.wait_own(part)
        over_rows(total, part, normed)
        n2.phase(0, part)
    for k in range(1, line.count):
        n2.phases(k)
    total.finish()
    n2.finish()
    grads.finish()
    for share in shares:
        share.finish()


def side_by_side(blocks_ref, out_ref):
    outer, inner, _, width = blocks_ref.shape
    for i in range(outer):
        for j in range(inner):
            out_ref[:, (i * inner + j) * width : (i * inner + j + 1) * width] = blocks_ref[i, j]


def dma_sems(*shape):
    return pltpu.SemaphoreType.DMA(shape)


def line_call(kernel, collective_id, name, outs, scratch, args, limit=56, far_args=(), far_outs=()):
    far = pl.BlockSpec(memory_space=pl.ANY)
    return pl.pallas_call(
        kernel,
        out_shape=[jax.ShapeDtypeStruct(*out) for out in (*outs, *far_outs)],
        in_specs=in_vmem(len(args)) + [far] * len(far_args),
        out_specs=in_vmem(len(outs)) + [far] * len(far_outs),
        scratch_shapes=scratch,
        compiler_params=pltpu.CompilerParams(
            collective_id=collective_id,
            has_side_effects=True,
            vmem_limit_bytes=limit * 1024 * 1024,
        ),
        name=name,
    )(*args, *far_args)


def scatter_scratch(seqs, cores, rows, width):
    b16 = jnp.bfloat16
    return [
        pltpu.VMEM((seqs, cores, rows, width), b16),
        pltpu.VMEM((2, seqs, rows, width), b16),
        pltpu.VMEM((seqs, rows, width), b16),
    ]


PARTS = 2


def run_resid(mix, o_full, x, g, gain, weights):
    seqs, cores, (piece, width) = lax.axis_size("seq"), lax.axis_size("tp"), x.shape
    rows, b16 = piece // cores, jnp.bfloat16
    outs = (
        ((rows, width), jnp.float32),
        ((seqs, cores, rows, width), b16),
        ((seqs, cores, rows, width), b16),
    )
    scratch = scatter_scratch(seqs, cores, rows, width)
    scratch = scratch + [pltpu.VMEM((o_full.shape[2], width), b16)] + [dma_sems(5, seqs, PARTS)] * 3
    scratch = scratch + pair_sems("row", len(weights))
    mix = mix.reshape(seqs * cores, rows, -1)
    resid, n2, g_full, *full = line_call(
        resid_kernel, 1, "resid_norm", outs, scratch, (mix, o_full, x, g, gain),
        far_args=weights,
        far_outs=[((lax.axis_size("row"),) + weight.shape, b16) for weight in weights],
    )
    return resid, n2.reshape(-1, width), g_full.reshape(-1, width), full


def grad_resid_kernel(
    grad_gate_ref, grad_up_ref, gate_ref, up_ref, hidden_ref, down_ref, resid_ref, g_ref, gain_ref,
    down_part_ref, gate_part_ref, up_part_ref,
    grad_resid_ref, grad_attn_ref, gain_grad_ref, result_ref,
    down_came_ref, gate_came_ref, up_came_ref,
    blocks, came, across, out_blocks, out_came, out_across, down_rows,
    sum_sems, out_sems, attn_sems, swap_sems, *sems,
):
    line = Line()
    greet(line_partners() + along_axis("row"))
    parts = moves_of(
        Swap,
        "row",
        (down_part_ref, gate_part_ref, up_part_ref),
        (down_came_ref, gate_came_ref, up_came_ref),
        sems,
    )
    for move in parts:
        move.start()
    rows = resid_ref.shape[0]
    total = Scatter(line, blocks, came, across, sum_sems)
    result = Scatter(line, out_blocks, out_came, out_across, out_sems)
    attn = Gather(line, grad_attn_ref, attn_sems)
    units = gate_ref.shape[1]
    for part in range(total.parts):
        left_up = grad_up_ref[:, total.span(part)].reshape(-1, units)

        def right_tile(left, t, columns, left_up=left_up):
            return mul(left, gate_ref[columns], (1, 1)) + mul(left_up, up_ref[columns], (1, 1))

        total.product(grad_gate_ref, None, part, right_tile=right_tile)
    side_by_side(down_ref, down_rows)
    total.nears(0)
    for part in range(result.parts):
        result.product(hidden_ref, down_rows, part, order=0)
    for k in range(1, line.count - 1):
        total.nears(k)
    for k in range(line.count - 1):
        total.fars(k)
    gain_grad_ref[...] = jnp.zeros_like(gain_grad_ref)

    def back(span):
        own_span = pl.ds(pl.multiple_of(line.core * rows + span.start, STEP), STEP)
        resid = resid_ref[span]
        grad_two = total.own_rows(span)
        scale = norm_scale(resid)
        gain_grad_ref[...] += jnp.sum(grad_two * resid * scale, axis=0, keepdims=True)
        grad = g_ref[own_span].astype(jnp.float32) + norm_back(
            resid, scale, gain_ref[...], grad_two
        )
        grad_resid_ref[span] = grad
        grad_attn_ref[line.place, line.core, span] = grad.astype(jnp.bfloat16)

    for part in range(total.parts):
        total.wait_own(part)
        over_rows(total, part, back)
        attn.phase(0, part)
    for k in range(1, line.count):
        attn.phases(k)
        result.nears(k - 1)
    for k in range(line.count - 1):
        result.fars(k)

    def finish(span):
        own_span = pl.ds(pl.multiple_of(line.core * rows + span.start, STEP), STEP)
        result_ref[own_span] = (resid_ref[span] + result.own_rows(span)).astype(jnp.bfloat16)

    for part in range(result.parts):
        result.wait_own(part)
        over_rows(result, part, finish)
    swap = own_swap(line, result_ref, rows, swap_sems)
    swap.start()
    total.finish()
    result.finish()
    attn.finish()
    swap.wait()
    for move in parts:
        move.finish()


def own_swap(line, ref, rows, sems):
    own = ref.at[pl.ds(pl.multiple_of(line.core * rows, rows), rows)]
    return remote(own, own, sems.at[0], sems.at[1], line.across)


def run_grad_resid(grad_gate, grad_up, gate, up, hidden, down, resid, g, gain, parts):
    seqs, cores, (piece, width) = lax.axis_size("seq"), lax.axis_size("tp"), g.shape
    rows, b16, f32 = piece // cores, jnp.bfloat16, jnp.float32
    outs = (
        ((rows, width), f32),
        ((seqs, cores, rows, width), b16),
        ((1, width), f32),
        ((piece, width), b16),
    )
    scratch = scatter_scratch(seqs, cores, rows, width) * 2
    scratch = scratch + [pltpu.VMEM((down.shape[2], width), b16)]
    scratch = scratch + [dma_sems(5, seqs, PARTS)] * 3 + [dma_sems(2)]
    scratch = scratch + pair_sems("row", len(parts))
    grad_gate, grad_up, hidden = (
        array.reshape(seqs * cores, rows, -1) for array in (grad_gate, grad_up, hidden)
    )
    grad_resid, grad_attn, gain_grad, result, *came = line_call(
        grad_resid_kernel, 2, "grad_resid", outs, scratch,
        (grad_gate, grad_up, gate, up, hidden, down, resid, g, gain),
        far_args=parts,
        far_outs=[(part.shape, b16) for part in parts],
    )
    return grad_resid, grad_attn.reshape(-1, width), gain_grad, result, came


def input_grad_kernel(
    grad_proj_ref, qkv_ref, grad_logit_ref, beta_ref, x_ref, grad_resid_ref, gain_ref, qkv_part_ref,
    o_sum_ref,
    input_grad_ref, gain_grad_ref, qkv_came_ref,
    o_came_ref,
    blocks, came, across, qkv_rows, qkv_sum, sum_sems, swap_sems, *sems,
):
    line = Line()
    greet(along_axis("seq") + along_axis("row") + along_axis("tp"))
    (o_move,) = moves_of(Swap, "seq", (o_sum_ref,), (o_came_ref,), sems[:3])
    (rows_move,) = moves_of(Swap, "row", (qkv_part_ref,), (qkv_rows,), sems[3:6])
    (qkv_move,) = moves_of(Swap, "seq", (qkv_sum,), (qkv_came_ref,), sems[6:9])
    rows_move.start()
    o_move.start()
    rows = grad_resid_ref.shape[0]
    total = Scatter(line, blocks, came, across, sum_sems)

    width = qkv_ref.shape[-1]

    for part in range(total.parts):
        logit = grad_logit_ref[:, total.span(part)].reshape(-1, grad_logit_ref.shape[-1])

        def right_tile(left, t, across, logit=logit):
            block = qkv_ref[t]
            out = mul(logit, beta_ref[:, across], (1, 0))
            for c in range(3):
                out = out + mul(
                    left[:, c * width : (c + 1) * width], block[:, c].reshape(-1, width), (1, 1)
                )
            return out

        tile = qkv_ref.shape[1] * qkv_ref.shape[3]
        total.product(grad_proj_ref, None, part, tile=tile, right_tile=right_tile)
    for k in range(line.count - 1):
        total.nears(k)
    for k in range(line.count - 1):
        total.fars(k)
    rows_move.finish()
    for i in range(qkv_rows.shape[1]):
        piece = qkv_rows[0, i].astype(jnp.float32)
        for j in range(1, qkv_rows.shape[0]):
            piece = piece + qkv_rows[j, i].astype(jnp.float32)
        qkv_sum[i] = piece.astype(jnp.bfloat16)
    qkv_move.start()
    gain_grad_ref[...] = jnp.zeros_like(gain_grad_ref)

    def back(span):
        own_span = pl.ds(pl.multiple_of(line.core * rows + span.start, STEP), STEP)
        x = x_ref[own_span].astype(jnp.float32)
        grad_one = total.own_rows(span)
        scale = norm_scale(x)
        gain_grad_ref[...] += jnp.sum(grad_one * x * scale, axis=0, keepdims=True)
        input_grad_ref[own_span] = (
            grad_resid_ref[span] + norm_back(x, scale, gain_ref[...], grad_one)
        ).astype(jnp.bfloat16)

    for part in range(total.parts):
        total.wait_own(part)
        over_rows(total, part, back)
    swap = own_swap(line, input_grad_ref, rows, swap_sems)
    swap.start()
    total.finish()
    swap.wait()
    o_move.finish()
    qkv_move.finish()


def run_input_grad(grad_proj, qkv, grad_logit, beta, x, grad_resid, gain, qkv_part, o_sum):
    seqs, cores, (piece, width) = lax.axis_size("seq"), lax.axis_size("tp"), x.shape
    rows, b16, f32 = piece // cores, jnp.bfloat16, jnp.float32
    outs = (((piece, width), b16), ((1, width), f32), (qkv_part.shape[1:], b16))
    scratch = scatter_scratch(seqs, cores, rows, width)
    scratch = scratch + [pltpu.VMEM(qkv_part.shape, b16), pltpu.VMEM(qkv_part.shape[1:], b16)]
    scratch = scratch + [dma_sems(5, seqs, PARTS), dma_sems(2)]
    scratch = scratch + pair_sems("seq", 1) + pair_sems("row", 1) + pair_sems("seq", 1)
    grad_proj = grad_proj.reshape(seqs * cores, rows, -1)
    grad_logit = grad_logit.reshape(seqs * cores, rows, -1)
    return line_call(
        input_grad_kernel, 3, "input_grad", outs, scratch,
        (grad_proj, qkv, grad_logit, beta, x, grad_resid, gain, qkv_part),
        far_args=(o_sum,),
        far_outs=((o_sum.shape, b16),),
    )


def normed_kernel(
    x_ref, gain_ref, weight_ref, beta_ref, n1_ref, qkv_ref, beta_full_ref, n1_sems, own_sems, *sems
):
    line = Line()
    row = lax.axis_index("row")
    greet(exchange_partners(line) + [(line.across, line.core >= 0)])
    width = qkv_ref.shape[-1]

    def columns(seq):
        return weight_ref.at[:, :, pl.ds(pl.multiple_of(seq * width, width), width)]

    moves = [
        Exchange(line, columns, qkv_ref, sems[:4]),
        Exchange(line, lambda seq: beta_ref.at[seq], beta_full_ref, sems[4:]),
    ]
    for move in moves:
        move.start()
    own = [
        pltpu.make_async_copy(
            move.source(line.place), move.target.at[row, line.place], own_sems.at[i]
        )
        for i, move in enumerate(moves)
    ]
    for copy in own:
        copy.start()
    rows = n1_ref.shape[2]
    n1 = Gather(line, n1_ref, n1_sems)

    def normed(span):
        x_span = pl.ds(pl.multiple_of(line.core * rows + span.start, STEP), STEP)
        x = x_ref[x_span].astype(jnp.float32)
        n1_ref[line.place, line.core, span] = (x * norm_scale(x) * gain_ref[...]).astype(
            jnp.bfloat16
        )

    for part in range(n1.parts):
        over_rows(n1, part, normed)
        n1.phase(0, part)
    for copy in own:
        copy.wait()
    for move in moves:
        move.share_own()
    for k in range(1, line.count):
        for move in moves:
            move.share_came(k)
        n1.phases(k)
    for move in moves:
        move.finish()
    n1.finish()


def run_normed(x, gain, weight, beta):
    rows_axis, seqs, cores = (lax.axis_size(axis) for axis in ("row", "seq", "tp"))
    piece, width = x.shape
    b16 = jnp.bfloat16
    outs = (
        ((seqs, cores, piece // cores, width), b16),
        ((rows_axis, seqs) + weight.shape[:2] + (weight.shape[2] // seqs,), b16),
        ((rows_axis,) + beta.shape, b16),
    )
    n1, qkv, beta_full = line_call(
        normed_kernel, 4, "norm_gather", outs,
        [dma_sems(5, seqs, PARTS), dma_sems(2)] + exchange_sems() * 2,
        (x, gain, weight, beta),
    )
    return n1.reshape(-1, width), qkv, beta_full


def mlp_kernel(
    n2_ref, g_ref, gate_ref, up_ref, down_ref, hidden_ref, grad_gate_ref, grad_up_ref, down_rows
):
    @pl.when(pl.program_id(0) == 0)
    def _():
        side_by_side(down_ref, down_rows)

    n2 = n2_ref[...]
    gate = mul(n2, gate_ref[...], (1, 0))
    up = mul(n2, up_ref[...], (1, 0))
    grad_hidden = mul(g_ref[...], down_rows[...], (1, 1))
    sig = sigmoid(gate)
    act = gate * sig
    hidden_ref[...] = (act * up).astype(jnp.bfloat16)
    grad_up_ref[...] = (grad_hidden * act).astype(jnp.bfloat16)
    grad_gate_ref[...] = (grad_hidden * up * sig * (1.0 + gate * (1.0 - sig))).astype(jnp.bfloat16)


def run_mlp(n2, g, gate, up, down, block=128):
    row_len, width = n2.shape
    units = gate.shape[1]
    tokens = pl.BlockSpec((block, width), lambda i: (i, 0))
    out = pl.BlockSpec((block, units), lambda i: (i, 0))
    whole = pl.BlockSpec(memory_space=pltpu.VMEM)
    shape = jax.ShapeDtypeStruct((row_len, units), jnp.bfloat16)
    return pl.pallas_call(
        mlp_kernel,
        grid=(row_len // block,),
        out_shape=[shape] * 3,
        in_specs=[tokens, tokens, whole, whole, whole],
        out_specs=[out] * 3,
        scratch_shapes=[pltpu.VMEM((units, width), jnp.bfloat16)],
        compiler_params=pltpu.CompilerParams(vmem_limit_bytes=48 * 1024 * 1024),
        name="mlp",
    )(n2, g, gate, up, down)


def small_sums_kernel(
    part_ref, out_ref, rows_ref, all_ref, send_row, recv_row, send_seq, recv_seq, send_tp, recv_tp
):
    row, seq, tp = (lax.axis_index(axis) for axis in ("row", "seq", "tp"))
    row_others, seq_others, tp_others = around("row"), around("seq"), around("tp")
    greet(
        [({"row": other}, other >= 0) for other in row_others]
        + [({"seq": other}, other >= 0) for other in seq_others]
        + [({"tp": other}, other >= 0) for other in tp_others]
    )
    rows_ref[row] = part_ref[...]
    copies = [
        remote(part_ref, rows_ref.at[row], send_row.at[i], recv_row.at[i], {"row": other})
        for i, other in enumerate(row_others)
    ]
    for copy in copies:
        copy.start()
    for copy in copies:
        copy.wait()
    total = rows_ref[0]
    for i in range(1, rows_ref.shape[0]):
        total = total + rows_ref[i]
    all_ref[tp, seq] = total
    copies = [
        remote(
            all_ref.at[tp, seq], all_ref.at[tp, seq], send_seq.at[i], recv_seq.at[i], {"seq": other}
        )
        for i, other in enumerate(seq_others)
    ]
    for copy in copies:
        copy.start()
    for copy in copies:
        copy.wait()
    copies = [
        remote(all_ref.at[tp], all_ref.at[tp], send_tp.at[i], recv_tp.at[i], {"tp": other})
        for i, other in enumerate(tp_others)
    ]
    for copy in copies:
        copy.start()
    for copy in copies:
        copy.wait()
    out_ref[...] = all_ref[...]


def run_small_sums(part):
    rows, seqs, tps = (lax.axis_size(axis) for axis in ("row", "seq", "tp"))
    dma = pltpu.SemaphoreType.DMA
    shape = (tps, seqs) + part.shape
    return pl.pallas_call(
        small_sums_kernel,
        out_shape=jax.ShapeDtypeStruct(shape, part.dtype),
        in_specs=in_vmem(1),
        out_specs=pl.BlockSpec(memory_space=pltpu.VMEM),
        scratch_shapes=[
            pltpu.VMEM((rows,) + part.shape, part.dtype),
            pltpu.VMEM(shape, part.dtype),
            dma((rows - 1,)),
            dma((rows - 1,)),
            dma((seqs - 1,)),
            dma((seqs - 1,)),
            dma((tps - 1,)),
            dma((tps - 1,)),
        ],
        compiler_params=pltpu.CompilerParams(collective_id=0, has_side_effects=True),
        name="small_sums",
    )(part)


def local_heads(
    block_input,
    grad_out,
    doc_lengths,
    attn_gain,
    mlp_gain,
    out_gain,
    conv_weight,
    qkv_weight,
    beta_weight,
    o_weight,
    gate_up_weight,
    down_weight,
):
    tok_rows, model_width = block_input.shape[1:]
    pieces, cores = lax.axis_size("seq"), lax.axis_size("tp")
    piece, core = lax.axis_index("seq"), lax.axis_index("tp")
    row_len = pieces * tok_rows
    shard_rows = qkv_weight.shape[1]
    half_width = qkv_weight.shape[2]
    width = half_width // pieces
    heads = width // DK
    units = gate_up_weight.shape[2] // pieces
    f32, b16 = jnp.float32, jnp.bfloat16

    x_piece, g_piece = block_input[0], grad_out[0]
    beta_parts = jnp.pad(
        beta_weight.T.reshape(pieces, heads, shard_rows), ((0, 0), (0, 16 - heads), (0, 0))
    )
    normed_one, qkv_full, beta_full = run_normed(
        x_piece, attn_gain[None], qkv_weight, beta_parts
    )
    beta_full = beta_full.reshape(-1, 16, shard_rows).transpose(1, 0, 2).reshape(16, -1)
    gate_up_parts = gate_up_weight.reshape(2, shard_rows, pieces, units).transpose(0, 2, 1, 3)

    ends = jnp.cumsum(doc_lengths[0])
    places = jnp.arange(row_len, dtype=jnp.int32)
    docs = jnp.sum((places[:, None] >= ends[None, :]).astype(jnp.int32), axis=1)
    aux, doc_rows = row_aux(docs)
    gain_row = out_gain[None]
    taps = lax.dynamic_slice_in_dim(conv_weight, piece * width, width, axis=2)
    taps = taps.transpose(1, 0, 2).reshape(KW, 3 * width)

    (
        proj, logit, mixed, normed_mix, inverse, states, written,
        o_full, gate_came, up_came, down_came,
    ) = run_forward(
        normed_one, qkv_full, beta_full, taps, aux, doc_rows, gain_row,
        o_weight, gate_up_parts[0], gate_up_parts[1], down_weight,
    )
    resid, normed_two, g_full, (gate_full, up_full, down_full) = run_resid(
        normed_mix, o_full, x_piece, g_piece, mlp_gain[None], (gate_came, up_came, down_came)
    )
    gate_full = gate_full.reshape(model_width, units)
    up_full = up_full.reshape(model_width, units)
    hidden, grad_gate, grad_up = run_mlp(normed_two, g_full, gate_full, up_full, down_full)
    down_part = jnp.einsum("td,tf->df", g_full, hidden, preferred_element_type=f32).astype(b16)
    gate_part = jnp.einsum("td,tf->df", normed_two, grad_gate, preferred_element_type=f32).astype(b16)
    up_part = jnp.einsum("td,tf->df", normed_two, grad_up, preferred_element_type=f32).astype(b16)
    rows_axis = lax.axis_size("row")

    def by_row(part):
        return part.reshape(rows_axis, pieces, shard_rows, -1)

    def summed(came):
        return jnp.sum(came.astype(f32), axis=0).astype(b16)

    grad_resid, grad_attn, mlp_gain_part, result, came = run_grad_resid(
        grad_gate, grad_up, gate_full, up_full, hidden, down_full, resid, g_piece, mlp_gain[None],
        (by_row(down_part), by_row(gate_part), by_row(up_part)),
    )
    o_part = jnp.einsum("td,te->de", grad_attn, normed_mix, preferred_element_type=f32)
    (
        grad_proj, grad_logit, conv_part, out_gain_part, down_sum, gate_sum, up_sum, o_came,
    ) = run_backward(
        grad_attn,
        o_full,
        (proj, logit, mixed, inverse, states, written),
        taps,
        aux,
        doc_rows,
        gain_row,
        [summed(array) for array in came],
        by_row(o_part.astype(b16)),
    )
    qkv_part = jnp.einsum("td,te->de", normed_one, grad_proj, preferred_element_type=f32)
    input_grad, attn_gain_part, qkv_sum, o_sum = run_input_grad(
        grad_proj, qkv_full, grad_logit, beta_full, x_piece, grad_resid, attn_gain[None],
        by_row(qkv_part.astype(b16)), summed(o_came),
    )
    beta_part = jnp.einsum("td,th->hd", normed_one, grad_logit, preferred_element_type=f32)
    packed = jnp.concatenate(
        [
            conv_part.reshape(-1, 128),
            attn_gain_part.reshape(-1, 128),
            mlp_gain_part.reshape(-1, 128),
            beta_part[:heads].reshape(-1, 128),
            jnp.pad(out_gain_part, ((0, 7), (0, 0))),
        ],
        axis=0,
    )
    small = run_small_sums(packed)
    at = KW * 3 * width // 128
    span = model_width // 128
    conv_grad = small[:, :, :at].reshape(cores, pieces, KW, 3, width)
    conv_grad = conv_grad.transpose(3, 2, 0, 1, 4).reshape(3, KW, model_width)
    sums = jnp.sum(small[:, :, at:], axis=(0, 1))
    attn_gain_grad = sums[:span].reshape(-1)
    mlp_gain_grad = sums[span : 2 * span].reshape(-1)
    out_gain_grad = sums[(2 + heads) * span]
    beta_sum = lax.dynamic_index_in_dim(small, core, 0, keepdims=False)
    beta_sum = beta_sum[:, at + 2 * span : at + (2 + heads) * span]
    beta_sum = beta_sum.reshape(pieces * heads, model_width)
    beta_sum = lax.dynamic_slice_in_dim(
        beta_sum, (lax.axis_index("row") * pieces + piece) * shard_rows, shard_rows, axis=1
    ).T
    qkv_sum = qkv_sum.reshape(pieces, shard_rows, 3, width)
    return (
        result[None],
        input_grad[None],
        attn_gain_grad,
        mlp_gain_grad,
        out_gain_grad,
        conv_grad,
        qkv_sum.transpose(2, 1, 0, 3).reshape(3, shard_rows, -1).astype(f32),
        beta_sum,
        o_sum.transpose(0, 2, 1).reshape(-1, shard_rows).astype(f32),
        jnp.stack([gate_sum, up_sum]).transpose(0, 2, 1, 3).reshape(2, shard_rows, -1).astype(f32),
        down_sum.transpose(0, 2, 1).reshape(-1, shard_rows).astype(f32),
    )


def splits_heads(mesh, heads=16, units=5632):
    return (
        mesh.shape["tp"] == 2
        and heads % (mesh.shape["seq"] * 2) == 0
        and units % (mesh.shape["seq"] * 2) == 0
    )


def solution(mesh):
    in_specs = (
        P("row", "seq", None),
        P("row", "seq", None),
        P("row", None),
        P(),
        P(),
        P(),
        P(None, None, "tp"),
        P(None, ("row", "seq"), "tp"),
        P(("row", "seq"), "tp"),
        P("tp", ("row", "seq")),
        P(None, ("row", "seq"), "tp"),
        P("tp", ("row", "seq")),
    )
    out_specs = (
        P("row", "seq", None),
        P("row", "seq", None),
        P(),
        P(),
        P(),
        P(),
        P(None, ("row", "seq"), "tp"),
        P(("row", "seq"), "tp"),
        P("tp", ("row", "seq")),
        P(None, ("row", "seq"), "tp"),
        P("tp", ("row", "seq")),
    )
    local = local_heads if splits_heads(mesh) else local_pieces
    return jax.shard_map(local, mesh=mesh, in_specs=in_specs, out_specs=out_specs, check_vma=False)
```

```python
import functools

import jax
import jax.numpy as jnp
from jax import lax
from jax.experimental import pallas as pl
from jax.experimental.pallas import tpu as pltpu
from jax.sharding import PartitionSpec as P

DK = 128
KW = 4
GROUP = 64
DOCS = 8


eps = 1e-06
mix_floor = 0.01
precise = lax.Precision.HIGHEST


def from_behind(shard, axis, by):
    devices = lax.axis_size(axis)
    pairs = [(i, i + by) for i in range(devices) if 0 <= i + by < devices]
    return lax.ppermute(shard, axis, pairs)


def prefix(shard, axis, combine, identity, reverse):
    devices, place = (lax.axis_size(axis), lax.axis_index(axis))
    everything = jax.tree.map(
        lambda part, kind: lax.all_gather(part.astype(kind), axis),
        shard,
        (jnp.bfloat16, jnp.bfloat16),
    )
    start = jax.tree.map(
        lambda part, zero: jnp.broadcast_to(jnp.asarray(zero, part.dtype), part.shape),
        shard,
        identity,
    )

    def step(k, before):
        at = devices - 1 - k if reverse else k
        reached = at > place if reverse else at < place
        new = combine(
            before, jax.tree.map(lambda part, own: part[at].astype(own.dtype), everything, shard)
        )
        return jax.tree.map(lambda a, b: jnp.where(reached, a, b), new, before)

    return lax.fori_loop(0, devices, step, start)


def norm_scale(values):
    return lax.rsqrt(jnp.mean(values * values, axis=-1, keepdims=True) + eps)


def norm_back(values, scale, gain, grad):
    weighted = gain * grad
    return scale * weighted - values * scale**3 * jnp.mean(
        weighted * values, axis=-1, keepdims=True
    )


def batch_mul(left, right):
    return jnp.einsum("hij,hjk->hik", left, right, precision=precise)


def batch_mul_t(left, right):
    return jnp.einsum("hji,hjk->hik", left, right, precision=precise)


def compose(earlier, later):
    return (batch_mul(later[0], earlier[0]), batch_mul(later[0], earlier[1]) + later[1])


def over_heads(function, shared):
    return jax.vmap(jax.vmap(function), in_axes=shared)


def tp_total(term):
    return lax.psum(term.astype(jnp.bfloat16), "tp").astype(jnp.float32)


def group_parts(key_rows, value_rows, rates, same_doc, carry_mask):
    size = key_rows.shape[0]
    strict = jnp.tril(jnp.ones((size, size), jnp.float32), -1) * same_doc
    inner = jnp.dot(key_rows, key_rows.T, precision=precise)
    system = jnp.eye(size, dtype=jnp.float32) + rates[:, None] * inner * strict
    right_side = jnp.concatenate(
        [rates[:, None] * value_rows, (rates * carry_mask)[:, None] * key_rows], axis=1
    )
    solved = jax.scipy.linalg.solve_triangular(system, right_side, lower=True)
    base_rows = solved[:, : value_rows.shape[1]]
    wy_rows = solved[:, value_rows.shape[1] :]
    tail_keys = same_doc[size - 1][:, None] * key_rows
    identity_mat = jnp.eye(key_rows.shape[1], dtype=jnp.float32)
    transition = carry_mask[size - 1] * identity_mat - jnp.dot(
        tail_keys.T, wy_rows, precision=precise
    )
    contribution = jnp.dot(tail_keys.T, base_rows, precision=precise)
    return (transition, contribution, base_rows, wy_rows)


def group_output(queries, key_rows, same_doc, carry_mask, base_rows, wy_rows, state_in):
    size = key_rows.shape[0]
    lower = jnp.tril(jnp.ones((size, size), jnp.float32)) * same_doc
    written = base_rows - jnp.dot(wy_rows, state_in, precision=precise)
    scores = jnp.dot(queries, key_rows.T, precision=precise) * lower
    carried = carry_mask[:, None] * jnp.dot(queries, state_in, precision=precise)
    return carried + jnp.dot(scores, written, precision=precise)


def group_full(queries, key_rows, value_rows, rates, same_doc, carry_mask, state_in):
    transition, contribution, base_rows, wy_rows = group_parts(
        key_rows, value_rows, rates, same_doc, carry_mask
    )
    outputs = group_output(queries, key_rows, same_doc, carry_mask, base_rows, wy_rows, state_in)
    return (outputs, jnp.dot(transition, state_in, precision=precise) + contribution)


def state_pull(queries, key_rows, same_doc, carry_mask, wy_rows, grad_rows):
    size = key_rows.shape[0]
    lower = jnp.tril(jnp.ones((size, size), jnp.float32)) * same_doc
    scores = jnp.dot(queries, key_rows.T, precision=precise) * lower
    pulled = jnp.dot(scores.T, grad_rows, precision=precise)
    direct = jnp.dot((carry_mask[:, None] * queries).T, grad_rows, precision=precise)
    return direct - jnp.dot(wy_rows.T, pulled, precision=precise)


def group_grads(
    queries, key_rows, value_rows, rates, same_doc, carry_mask, state_in, grad_rows, grad_end
):

    def group_local(query_in, key_in, value_in, rate_in):
        return group_full(query_in, key_in, value_in, rate_in, same_doc, carry_mask, state_in)

    outputs, pullback = jax.vjp(group_local, queries, key_rows, value_rows, rates)
    return pullback((grad_rows, grad_end))


def local_pieces(
    block_input,
    grad_out,
    doc_lengths,
    attn_gain,
    mlp_gain,
    out_gain,
    conv_weight,
    qkv_weight,
    beta_weight,
    o_weight,
    gate_up_weight,
    down_weight,
):
    tok_rows = block_input.shape[1]
    model_width = block_input.shape[2]
    blocks = tok_rows // GROUP
    unit_floor = DK / 16.0
    x_rows = block_input[0].astype(jnp.float32)
    grad_rows_out = grad_out[0]
    qkv_full, beta_full, o_full, gate_up_full, down_full = (
        lax.all_gather(qkv_weight, ("row", "seq"), axis=1, tiled=True),
        lax.all_gather(beta_weight, ("row", "seq"), axis=0, tiled=True),
        lax.all_gather(o_weight, ("row", "seq"), axis=1, tiled=True),
        lax.all_gather(gate_up_weight, ("row", "seq"), axis=1, tiled=True),
        lax.all_gather(down_weight, ("row", "seq"), axis=1, tiled=True),
    )
    local_width = qkv_full.shape[2]
    head_count = local_width // DK
    lead_mask = (lax.axis_index("tp") == 0).astype(jnp.float32)
    ends = jnp.cumsum(doc_lengths[0])
    places = (
        lax.axis_index("seq") * tok_rows + jnp.arange(tok_rows + KW - 1, dtype=jnp.int32) - (KW - 1)
    )
    doc_ids = jnp.sum((places[:, None] >= ends[None, :]).astype(jnp.int32), axis=1)
    doc_ids = jnp.where(places < 0, -1, doc_ids)
    own_docs = doc_ids[KW - 1 :]
    prior_docs = doc_ids[KW - 2 : KW - 2 + tok_rows]
    valid = (own_docs < DOCS).astype(jnp.float32)
    fresh = (own_docs != prior_docs).astype(jnp.int32)
    tap_masks = [
        (doc_ids[KW - 1 - tap : KW - 1 - tap + tok_rows] == own_docs).astype(jnp.float32)
        for tap in range(KW)
    ]
    own_blocks = own_docs.reshape(blocks, GROUP)
    same_doc = (own_blocks[:, :, None] == own_blocks[:, None, :]).astype(jnp.float32)
    carry_mask = (jnp.cumsum(fresh.reshape(blocks, GROUP), axis=1) == 0).astype(jnp.float32)

    def to_blocks(array):
        return array.reshape(blocks, GROUP, head_count, -1).transpose(2, 0, 1, 3)

    def from_blocks(array):
        return array.transpose(1, 2, 0, 3).reshape(tok_rows, head_count, -1)

    scale_one = norm_scale(x_rows)
    normed_one = (x_rows * scale_one * attn_gain).astype(jnp.bfloat16)
    proj_low = jnp.einsum(
        "td,cde->cte", normed_one, qkv_full, preferred_element_type=jnp.float32
    ).astype(jnp.bfloat16)
    logit = jnp.dot(normed_one, beta_full, preferred_element_type=jnp.float32)
    rim_rows = from_behind(proj_low[:, tok_rows - (KW - 1) :, :], "seq", 1)
    extended = jnp.concatenate([rim_rows, proj_low], axis=1).astype(jnp.float32)
    conv_out = jnp.zeros((3, tok_rows, local_width), jnp.float32)
    for tap in range(KW):
        window = extended[:, KW - 1 - tap : KW - 1 - tap + tok_rows]
        conv_out = (
            conv_out + conv_weight[:, tap][:, None, :] * window * tap_masks[tap][None, :, None]
        )
    conv_sig = jax.nn.sigmoid(conv_out)
    activated = conv_out * conv_sig
    query_raw = activated[0].reshape(tok_rows, head_count, DK)
    key_raw = activated[1].reshape(tok_rows, head_count, DK)
    query_sq = jnp.sum(query_raw * query_raw, axis=-1, keepdims=True)
    key_sq = jnp.sum(key_raw * key_raw, axis=-1, keepdims=True)
    query_scale = lax.rsqrt(jnp.maximum(query_sq, unit_floor))
    key_scale = lax.rsqrt(jnp.maximum(key_sq, unit_floor))
    query_live = (query_sq > unit_floor).astype(jnp.float32)
    key_live = (key_sq > unit_floor).astype(jnp.float32)
    query_blocks = to_blocks(query_raw * query_scale)
    key_blocks = to_blocks(key_raw * key_scale)
    value_blocks = to_blocks(activated[2].reshape(tok_rows, head_count, DK))
    rate_sig = jax.nn.sigmoid(logit)
    rate_blocks = (rate_sig * valid[:, None]).reshape(blocks, GROUP, head_count).transpose(2, 0, 1)
    transition, contribution, base_rows, wy_rows = over_heads(group_parts, (0, 0, 0, None, None))(
        key_blocks, value_blocks, rate_blocks, same_doc, carry_mask
    )
    identity_mat = jnp.broadcast_to(jnp.eye(DK, dtype=jnp.float32), (head_count, DK, DK))
    zero_state = jnp.zeros((head_count, DK, DK), jnp.float32)
    transition_steps = jnp.moveaxis(transition, 1, 0)

    def chain(running, pair):
        product, partial_state = running
        step_trans, step_contrib = pair
        advanced = (
            batch_mul(step_trans, product),
            batch_mul(step_trans, partial_state) + step_contrib,
        )
        return (advanced, (product, partial_state))

    (dev_trans, dev_state), (products, partials) = lax.scan(
        chain, (identity_mat, zero_state), (transition_steps, jnp.moveaxis(contribution, 1, 0))
    )
    incoming = prefix((dev_trans, dev_state), "seq", compose, (identity_mat, zero_state), False)[1]
    group_starts = partials + jnp.einsum("nhij,hjk->nhik", products, incoming, precision=precise)
    start_blocks = jnp.moveaxis(group_starts, 0, 1)
    mix_blocks = over_heads(group_output, (0, 0, None, None, 0, 0, 0))(
        query_blocks, key_blocks, same_doc, carry_mask, base_rows, wy_rows, start_blocks
    )
    mixed = from_blocks(mix_blocks) * valid[:, None, None]
    mix_sq = jnp.mean(mixed * mixed, axis=-1, keepdims=True)
    mix_scale = lax.rsqrt(jnp.maximum(mix_sq, mix_floor))
    mix_live = (mix_sq > mix_floor).astype(jnp.float32)
    normed_mix = (mixed * mix_scale * out_gain).astype(jnp.bfloat16).reshape(tok_rows, local_width)
    o_term = jnp.dot(normed_mix, o_full, preferred_element_type=jnp.float32)
    resid = x_rows + tp_total(o_term)
    scale_two = norm_scale(resid)
    normed_local = (resid * scale_two * mlp_gain).astype(jnp.bfloat16)
    gate_up = jnp.einsum(
        "td,cdf->ctf", normed_local, gate_up_full, preferred_element_type=jnp.float32
    )
    gate_sig = jax.nn.sigmoid(gate_up[0])
    gate_act = gate_up[0] * gate_sig
    hidden = (gate_act * gate_up[1]).astype(jnp.bfloat16)
    down_term = jnp.dot(hidden, down_full, preferred_element_type=jnp.float32)
    mlp_out = tp_total(down_term)
    result = (resid + mlp_out).astype(jnp.bfloat16)
    grad_hidden = jnp.einsum(
        "td,fd->tf", grad_rows_out, down_full, preferred_element_type=jnp.float32
    )
    grad_gate = grad_hidden * gate_up[1] * gate_sig * (1.0 + gate_up[0] * (1.0 - gate_sig))
    grad_up = grad_hidden * gate_act
    grad_gate_up = jnp.stack([grad_gate, grad_up]).astype(jnp.bfloat16)
    down_part = jnp.einsum("tf,td->fd", hidden, grad_rows_out, preferred_element_type=jnp.float32)
    gate_up_part = jnp.einsum(
        "td,ctf->cdf", normed_local, grad_gate_up, preferred_element_type=jnp.float32
    )
    two_term = jnp.einsum(
        "ctf,cdf->td", grad_gate_up, gate_up_full, preferred_element_type=jnp.float32
    )
    grad_two = tp_total(two_term)
    mlp_gain_part = jnp.sum(grad_two * resid * scale_two, axis=0)
    grad_resid = grad_rows_out.astype(jnp.float32) + norm_back(resid, scale_two, mlp_gain, grad_two)
    grad_attn_local = grad_resid.astype(jnp.bfloat16)
    o_part = jnp.einsum(
        "te,td->ed", normed_mix, grad_attn_local, preferred_element_type=jnp.float32
    )
    grad_normed = jnp.einsum(
        "td,ed->te", grad_attn_local, o_full, preferred_element_type=jnp.float32
    ).reshape(tok_rows, head_count, DK)
    out_gain_part = jnp.sum(grad_normed * mixed * mix_scale, axis=(0, 1))
    weighted_mix = out_gain * grad_normed
    grad_mixed = (
        mix_scale * weighted_mix
        - mixed * mix_scale**3 * mix_live * jnp.mean(weighted_mix * mixed, axis=-1, keepdims=True)
    ) * valid[:, None, None]
    grad_blocks = to_blocks(grad_mixed)
    pulls = over_heads(state_pull, (0, 0, None, None, 0, 0))(
        query_blocks, key_blocks, same_doc, carry_mask, wy_rows, grad_blocks
    )

    def back_chain(running, pair):
        grad_end, product = running
        step_trans, step_pull = pair
        advanced = (step_pull + batch_mul_t(step_trans, grad_end), batch_mul_t(step_trans, product))
        return (advanced, (grad_end, product))

    (dev_pull, dev_back), (grad_ends, back_products) = lax.scan(
        back_chain,
        (zero_state, identity_mat),
        (transition_steps, jnp.moveaxis(pulls, 1, 0)),
        reverse=True,
    )
    outgoing = prefix((dev_back, dev_pull), "seq", compose, (identity_mat, zero_state), True)[1]
    end_grads = grad_ends + jnp.einsum("nhij,hjk->nhik", back_products, outgoing, precision=precise)
    grad_query, grad_key, grad_value, grad_rate = over_heads(
        group_grads, (0, 0, 0, 0, None, None, 0, 0, 0)
    )(
        query_blocks,
        key_blocks,
        value_blocks,
        rate_blocks,
        same_doc,
        carry_mask,
        start_blocks,
        grad_blocks,
        jnp.moveaxis(end_grads, 0, 1),
    )
    grad_query = from_blocks(grad_query)
    grad_key = from_blocks(grad_key)
    grad_query_raw = query_scale * grad_query - query_raw * query_scale**3 * query_live * jnp.sum(
        query_raw * grad_query, axis=-1, keepdims=True
    )
    grad_key_raw = key_scale * grad_key - key_raw * key_scale**3 * key_live * jnp.sum(
        key_raw * grad_key, axis=-1, keepdims=True
    )
    grad_activated = jnp.stack(
        [
            grad_query_raw.reshape(tok_rows, local_width),
            grad_key_raw.reshape(tok_rows, local_width),
            from_blocks(grad_value).reshape(tok_rows, local_width),
        ]
    )
    grad_conv = grad_activated * conv_sig * (1.0 + conv_out * (1.0 - conv_sig))
    grad_extended = jnp.zeros((3, tok_rows + KW - 1, local_width), jnp.float32)
    tap_grads = []
    for tap in range(KW):
        masked = grad_conv * tap_masks[tap][None, :, None]
        window = extended[:, KW - 1 - tap : KW - 1 - tap + tok_rows]
        tap_grads.append(jnp.sum(masked * window, axis=1))
        grad_extended = grad_extended + jnp.pad(
            conv_weight[:, tap][:, None, :] * masked, ((0, 0), (KW - 1 - tap, tap), (0, 0))
        )
    conv_part = jnp.stack(tap_grads, axis=1)
    rim_back = from_behind(grad_extended[:, : KW - 1], "seq", -1)
    grad_proj = jnp.concatenate(
        [grad_extended[:, KW - 1 : tok_rows], grad_extended[:, tok_rows:] + rim_back], axis=1
    ).astype(jnp.bfloat16)
    rate_grad = grad_rate.transpose(1, 2, 0).reshape(tok_rows, head_count)
    grad_logit = (rate_grad * valid[:, None] * rate_sig * (1.0 - rate_sig)).astype(jnp.bfloat16)
    qkv_part = jnp.einsum("td,cte->cde", normed_one, grad_proj, preferred_element_type=jnp.float32)
    beta_part = jnp.einsum("td,th->dh", normed_one, grad_logit, preferred_element_type=jnp.float32)
    grad_one_part = jnp.einsum(
        "cte,cde->td", grad_proj, qkv_full, preferred_element_type=jnp.float32
    ) + jnp.einsum("th,dh->td", grad_logit, beta_full, preferred_element_type=jnp.float32)
    grad_one = tp_total(grad_one_part)
    attn_gain_part = jnp.sum(grad_one * x_rows * scale_one, axis=0)
    input_local = (grad_resid + norm_back(x_rows, scale_one, attn_gain, grad_one)).astype(
        jnp.bfloat16
    )
    conv_whole = lax.dynamic_update_slice(
        jnp.zeros((3, KW, model_width), jnp.float32),
        conv_part,
        (0, 0, lax.axis_index("tp") * local_width),
    )
    attn_gain_grad, mlp_gain_grad, out_gain_grad, conv_grad = lax.psum(
        (attn_gain_part * lead_mask, mlp_gain_part * lead_mask, out_gain_part, conv_whole),
        ("row", "seq", "tp"),
    )
    qkv_sum, beta_sum, o_sum, gate_up_sum, down_sum = (
        lax.psum_scatter(
            qkv_part.astype(jnp.bfloat16), ("row", "seq"), scatter_dimension=1, tiled=True
        ).astype(jnp.float32),
        lax.psum_scatter(
            beta_part.astype(jnp.bfloat16), ("row", "seq"), scatter_dimension=0, tiled=True
        ).astype(jnp.float32),
        lax.psum_scatter(
            o_part.astype(jnp.bfloat16), ("row", "seq"), scatter_dimension=1, tiled=True
        ).astype(jnp.float32),
        lax.psum_scatter(
            gate_up_part.astype(jnp.bfloat16), ("row", "seq"), scatter_dimension=1, tiled=True
        ).astype(jnp.float32),
        lax.psum_scatter(
            down_part.astype(jnp.bfloat16), ("row", "seq"), scatter_dimension=1, tiled=True
        ).astype(jnp.float32),
    )
    return (
        result[None],
        input_local[None],
        attn_gain_grad,
        mlp_gain_grad,
        out_gain_grad,
        conv_grad,
        qkv_sum,
        beta_sum,
        o_sum,
        gate_up_sum,
        down_sum,
    )


CHUNK = 128
PAD = 8


def mul(left, right, dims, precision=None):
    return lax.dot_general(
        left, right, ((dims[:1], dims[1:]), ((), ())), precision=precision, preferred_element_type=jnp.float32
    )


def fine(left, right, dims=(1, 0)):
    return mul(left, right, dims, precise)


def plain(left, right, dims=(1, 0)):
    return mul(left.astype(jnp.bfloat16), right.astype(jnp.bfloat16), dims)


def chunk_masks(doc_col, doc_row):
    same = doc_col == doc_row
    down = lax.broadcasted_iota(jnp.int32, (CHUNK, CHUNK), 0)
    along = lax.broadcasted_iota(jnp.int32, (CHUNK, CHUNK), 1)
    lower = jnp.where(same & (down >= along), 1.0, 0.0)
    strict = jnp.where(same & (down > along), 1.0, 0.0)
    return lower, strict, down, along


def lower_inverse(systems, down, along):
    at_one = (down // 2 == along // 2) & (down != along)
    unit = jnp.where(down == along, 1.0, 0.0)
    inverses = [unit - jnp.where(at_one, system, 0.0) for system in systems]
    half = 2
    while half < CHUNK:
        joins = (down // (2 * half) == along // (2 * half)) & (down // half != along // half)
        inner = [
            fine(jnp.where(joins, system, 0.0), inverse)
            for system, inverse in zip(systems, inverses)
        ]
        inverses = [inverse - fine(inverse, part) for inverse, part in zip(inverses, inner)]
        half *= 2
    return inverses


def tap_mask(aux, tap):
    return 1.0 if tap == 0 else aux[:, 3 + tap : 4 + tap]


def convolved(window, taps, aux):
    total = 0.0
    for tap in range(KW):
        total = total + (
            taps[tap : tap + 1] * window[PAD - tap : PAD - tap + CHUNK] * tap_mask(aux, tap)
        )
    return total


def sigmoid(values):
    return 1.0 / (1.0 + jnp.exp(-values))


def unit_scale(values):
    total = jnp.sum(values * values, axis=1, keepdims=True)
    floor = DK / 16.0
    return lax.rsqrt(jnp.maximum(total, floor)), jnp.where(total > floor, 1.0, 0.0)


def mix_norm(mixed):
    mean = jnp.mean(mixed * mixed, axis=1, keepdims=True)
    return lax.rsqrt(jnp.maximum(mean, mix_floor)), jnp.where(mean > mix_floor, 1.0, 0.0)


def forward_kernel(
    heads,
    n1_ref,
    qkv_ref,
    beta_ref,
    taps_ref,
    aux_ref,
    docs_ref,
    gain_ref,
    o_weight_ref,
    gate_ref,
    up_ref,
    down_ref,
    proj_ref,
    logit_ref,
    mixed_ref,
    normed_ref,
    inverse_ref,
    states_ref,
    written_ref,
    o_ref,
    gate_out,
    up_out,
    down_out,
    window_ref,
    state_ref,
    own_sems,
    *sems,
):
    width = heads * DK
    line = Line()
    greet(exchange_partners(line))
    row = lax.axis_index("row")

    def rows_of(ref, count):
        return lambda seq: ref.at[pl.ds(pl.multiple_of(seq * count, count), count)]

    units = down_out.shape[1]
    whole = Exchange(line, rows_of(o_weight_ref, width), o_ref, sems[:4])
    gates = Exchange(line, lambda seq: gate_ref.at[seq], gate_out, sems[4:8])
    moves = [
        Exchange(line, lambda seq: up_ref.at[seq], up_out, sems[8:10]),
        Exchange(line, rows_of(down_ref, units), down_out, sems[10:12]),
    ]
    own = []
    for i, move in enumerate((whole, gates)):
        target = move.target.at[row, line.place]
        own.append(pltpu.make_async_copy(move.source(line.place), target, own_sems.at[i]))
    for i, move in enumerate(moves):
        target = move.target.at[line.place]
        own.append(pltpu.make_async_copy(move.source(line.place), target, own_sems.at[i + 2]))
    for move in (whole, gates, *moves):
        move.start()
    for copy in own:
        copy.start()
    for i, move in enumerate((whole, gates)):
        own[i].wait()
        move.share_own()
    window_ref[0:PAD] = jnp.zeros((PAD, 3 * width), jnp.float32)
    state_ref[...] = jnp.zeros_like(state_ref)

    def chunk(n, _):
        rows = pl.ds(pl.multiple_of(n * CHUNK, CHUNK), CHUNK)
        n1 = n1_ref[rows]
        proj = jnp.concatenate(
            [mul(n1, qkv_ref[:, :, c].reshape(-1, width), (1, 0)) for c in range(3)], axis=1
        ).astype(jnp.bfloat16)
        proj_ref[rows] = proj
        window_ref[PAD : PAD + CHUNK] = proj.astype(jnp.float32)
        logit = mul(n1, beta_ref[...], (1, 1))
        logit_ref[rows] = logit
        aux = aux_ref[rows]
        conv = convolved(window_ref[...], taps_ref[...], aux)
        act = conv * sigmoid(conv)
        window_ref[0:PAD] = window_ref[CHUNK : CHUNK + PAD]
        valid, carry, tail = aux[:, 1:2], aux[:, 2:3], aux[:, 3:4]
        carry_last = carry[CHUNK - 1 :]
        lower, strict, down, along = chunk_masks(aux[:, 0:1], docs_ref[pl.ds(n, 1)])
        rate_all = sigmoid(logit) * valid
        parts = []
        for h in range(heads):
            query = act[:, h * DK : (h + 1) * DK]
            key = act[:, width + h * DK : width + (h + 1) * DK]
            value = act[:, 2 * width + h * DK : 2 * width + (h + 1) * DK]
            query = query * unit_scale(query)[0]
            key = key * unit_scale(key)[0]
            rate = rate_all[:, h : h + 1]
            system = rate * fine(key, key, (1, 1)) * strict
            parts.append((query, key, value, rate, system))
        inverses = lower_inverse([part[4] for part in parts], down, along)
        for h, (query, key, value, rate, _) in enumerate(parts):
            inverse = inverses[h]
            state = state_ref[h]
            carried_key = carry * key
            right = rate * (value - fine(carried_key, state))
            written = fine(inverse, right)
            scores = plain(query, key, (1, 1)) * lower
            mixed = carry * plain(query, state) + plain(scores, written)
            mixed = mixed * valid
            states_ref[h, n] = state
            written_ref[h, n] = written
            inverse_ref[h, n] = inverse
            state_ref[h] = carry_last * state + fine(tail * key, written, (0, 0))
            columns = pl.ds(h * DK, DK)
            mixed_ref[rows, columns] = mixed
            normed_ref[rows, columns] = (
                mixed * mix_norm(mixed)[0] * gain_ref[...]
            ).astype(jnp.bfloat16)
        return 0

    chunks = n1_ref.shape[0] // CHUNK
    early, late = chunks // 4, 3 * chunks // 4
    lax.fori_loop(0, early, chunk, 0)
    for i in range(1, line.count):
        whole.share_came(i)
    lax.fori_loop(early, late, chunk, 0)
    for i in range(1, line.count):
        gates.share_came(i)
    lax.fori_loop(late, chunks, chunk, 0)
    for copy in own[2:]:
        copy.wait()
    for move in (whole, gates, *moves):
        move.finish()


def backward_kernel(
    heads,
    grad_ref,
    o_ref,
    proj_ref,
    logit_ref,
    mixed_ref,
    inverse_ref,
    states_ref,
    written_ref,
    taps_ref,
    aux_ref,
    docs_ref,
    gain_ref,
    normed_mix_ref,
    n1_ref,
    qkv_ref,
    beta_ref,
    attn_gain_ref,
    mlp_grad_ref,
    sum_ref,
    grad_proj_ref,
    grad_logit_ref,
    small_ref,
    qkv_part_ref,
    down_came_ref,
    gate_came_ref,
    up_came_ref,
    o_came_ref,
    window_ref,
    masked_ref,
    state_ref,
    o_rows,
    o_part_ref,
    conv_grad_ref,
    gain_grad_ref,
    *sems,
):
    width = heads * DK
    greet(along_axis("seq") + along_axis("row"))
    moves = moves_of(
        Swap,
        "seq",
        [sum_ref.at[m] for m in range(3)],
        (down_came_ref, gate_came_ref, up_came_ref),
        sems[:7],
    )
    for move in moves:
        move.start()
    rows_axis, seqs, shard, _ = o_part_ref.shape
    span = seqs * shard

    def o_rows_of(r, _):
        columns = pl.ds(pl.multiple_of(r * span, span), span)
        part = mul(grad_ref[:, columns], normed_mix_ref[...], (0, 0))
        o_part_ref[r] = part.astype(jnp.bfloat16).reshape(seqs, shard, -1)
        return 0

    lax.fori_loop(0, rows_axis, o_rows_of, 0)
    o_moves = moves_of(Swap, "row", (o_part_ref,), (o_came_ref,), sems[7:])
    for move in o_moves:
        move.start()
    side_by_side(o_ref, o_rows)
    chunks = grad_ref.shape[0] // CHUNK
    state_ref[...] = jnp.zeros_like(state_ref)
    masked_ref[...] = jnp.zeros_like(masked_ref)
    conv_grad_ref[...] = jnp.zeros_like(conv_grad_ref)
    gain_grad_ref[...] = jnp.zeros_like(gain_grad_ref)

    def chunk(step, _):
        n = chunks - 1 - step
        rows = pl.ds(pl.multiple_of(n * CHUNK, CHUNK), CHUNK)
        before = jnp.maximum(n - 1, 0)
        aux = aux_ref[rows]
        grad_normed = mul(grad_ref[rows], o_rows[...], (1, 1))
        prior = proj_ref[pl.ds(pl.multiple_of(before * CHUNK + CHUNK - 16, 16), 16)]
        window_ref[0:PAD] = prior.astype(jnp.float32)[16 - PAD :]
        window_ref[PAD : PAD + CHUNK] = proj_ref[rows].astype(jnp.float32)
        window = window_ref[...]
        taps = taps_ref[...]
        conv = convolved(window, taps, aux)
        conv_sig = sigmoid(conv)
        act = conv * conv_sig
        valid, carry, tail = aux[:, 1:2], aux[:, 2:3], aux[:, 3:4]
        carry_last = carry[CHUNK - 1 :]
        lower, strict, down, along = chunk_masks(aux[:, 0:1], docs_ref[pl.ds(n, 1)])
        rate_sig = sigmoid(logit_ref[rows])
        rate_all = rate_sig * valid
        lanes = lax.broadcasted_iota(jnp.int32, rate_all.shape, 1)
        grad_rates = jnp.zeros_like(rate_all)
        grads = [[], [], []]
        for h in range(heads):
            columns = pl.ds(h * DK, DK)
            mixed = mixed_ref[rows, columns]
            mix_scale, mix_live = mix_norm(mixed)
            grad_out = grad_normed[:, h * DK : (h + 1) * DK]
            scaled = mixed * mix_scale
            gain_grad_ref[...] += jnp.sum(grad_out * scaled, axis=0, keepdims=True)
            weighted = gain_ref[...] * grad_out
            grad_mix = (
                mix_scale * weighted
                - scaled
                * (mix_scale * mix_scale * mix_live)
                * jnp.mean(weighted * mixed, axis=1, keepdims=True)
            ) * valid
            query_raw = act[:, h * DK : (h + 1) * DK]
            key_raw = act[:, width + h * DK : width + (h + 1) * DK]
            value = act[:, 2 * width + h * DK : 2 * width + (h + 1) * DK]
            query_scale, query_live = unit_scale(query_raw)
            key_scale, key_live = unit_scale(key_raw)
            query = query_raw * query_scale
            key = key_raw * key_scale
            rate = rate_all[:, h : h + 1]
            inverse = inverse_ref[h, n]
            state = states_ref[h, n]
            written = written_ref[h, n]
            grad_state = state_ref[h]
            tail_key = tail * key
            carried_key = carry * key
            scores = plain(query, key, (1, 1)) * lower
            pulled = plain(scores, grad_mix, (0, 0)) + fine(tail_key, grad_state)
            solved = fine(inverse, pulled, (0, 0))
            state_ref[h] = (
                carry_last * grad_state
                + plain(carry * query, grad_mix, (0, 0))
                - fine(rate * carried_key, solved, (0, 0))
            )
            grad_scores = plain(grad_mix, written, (1, 1)) * lower
            grad_query = carry * plain(grad_mix, state, (1, 1)) + plain(grad_scores, key)
            guess_error = value - plain(carried_key, state)
            gram = plain(key, key, (1, 1)) * strict
            grad_system = plain(solved, written, (1, 1)) * strict
            grad_rate = jnp.sum(solved * guess_error, axis=1, keepdims=True) - jnp.sum(
                grad_system * gram, axis=1, keepdims=True
            )
            grad_gram = rate * grad_system
            grad_key = (
                plain(grad_scores, query, (0, 0))
                + tail * plain(written, grad_state, (1, 1))
                - rate * carry * plain(solved, state, (1, 1))
                - plain(grad_gram, key)
                - plain(grad_gram, key, (0, 0))
            )
            grads[0].append(
                query_scale
                * (
                    grad_query
                    - query
                    * query_live
                    * jnp.sum(query * grad_query, axis=1, keepdims=True)
                )
            )
            grads[1].append(
                key_scale
                * (grad_key - key * key_live * jnp.sum(key * grad_key, axis=1, keepdims=True))
            )
            grads[2].append(rate * solved)
            grad_rates = grad_rates + jnp.where(lanes == h, grad_rate, 0.0)
        grad_act = jnp.concatenate(grads[0] + grads[1] + grads[2], axis=1)
        grad_conv = grad_act * conv_sig * (1.0 + conv * (1.0 - conv_sig))
        grad_proj = taps[0:1] * grad_conv
        conv_grad_ref[0:1] += jnp.sum(
            grad_conv * window[PAD : PAD + CHUNK], axis=0, keepdims=True
        )
        for tap in range(1, KW):
            masked = grad_conv * tap_mask(aux, tap)
            conv_grad_ref[tap : tap + 1] += jnp.sum(
                masked * window[PAD - tap : PAD - tap + CHUNK], axis=0, keepdims=True
            )
            masked_ref[tap - 1, CHUNK : CHUNK + PAD] = masked_ref[tap - 1, 0:PAD]
            masked_ref[tap - 1, 0:CHUNK] = masked
            grad_proj = grad_proj + taps[tap : tap + 1] * masked_ref[tap - 1, tap : tap + CHUNK]
        grad_proj_ref[rows] = grad_proj.astype(jnp.bfloat16)
        grad_logit_ref[rows] = (grad_rates * rate_sig * (1.0 - rate_sig) * valid).astype(
            jnp.bfloat16
        )
        return 0

    lax.fori_loop(0, chunks, chunk, 0)

    def qkv_rows_of(r, _):
        columns = pl.ds(pl.multiple_of(r * span, span), span)
        n1 = n1_ref[:, columns]
        part = mul(n1, grad_proj_ref[...], (0, 0))
        qkv_part_ref[r] = part.astype(jnp.bfloat16).reshape(seqs, shard, -1)
        weights = qkv_ref[r]
        total = 0.0
        for c in range(3):
            weight = weights[:, c].reshape(span, width).astype(jnp.float32)
            total = total + weight * part[:, c * width : (c + 1) * width]
        total = fine(jnp.ones((8, width), jnp.float32), total, (1, 1))[0:1]
        beta_part = mul(grad_logit_ref[...], n1, (0, 0))
        total = total + jnp.sum(
            beta_part * beta_ref[:, columns].astype(jnp.float32), axis=0, keepdims=True
        )
        small_ref[0:1, columns] = total / attn_gain_ref[:, columns]
        small_ref[2 : 2 + heads, columns] = beta_part[:heads]
        return 0

    lax.fori_loop(0, rows_axis, qkv_rows_of, 0)
    small_ref[1:2] = mlp_grad_ref[...]
    at = 2 + heads
    for tap in range(KW):
        lanes = pl.ds((tap % 2) * 3 * width, 3 * width)
        small_ref[at + tap // 2 : at + tap // 2 + 1, lanes] = conv_grad_ref[tap : tap + 1]
    small_ref[at : at + 1, 6 * width : 6 * width + DK] = gain_grad_ref[...]
    for move in moves + o_moves:
        move.finish()


def in_vmem(count):
    return [pl.BlockSpec(memory_space=pltpu.VMEM)] * count


def run_forward(n1, qkv, beta, taps, aux, docs, gain, o_weight, gate, up, down):
    row_len, heads = n1.shape[0], qkv.shape[-1] // DK
    rows_axis, seqs = qkv.shape[:2]
    chunks, width, f32 = row_len // CHUNK, heads * DK, jnp.float32
    shapes = (
        ((row_len, 3 * width), jnp.bfloat16),
        ((row_len, beta.shape[0]), f32),
        ((row_len, width), f32),
        ((row_len, width), jnp.bfloat16),
        ((heads, chunks, CHUNK, CHUNK), f32),
        ((heads, chunks, DK, DK), f32),
        ((heads, chunks, CHUNK, DK), f32),
        ((rows_axis, seqs, width, o_weight.shape[1]), jnp.bfloat16),
        ((rows_axis,) + gate.shape, jnp.bfloat16),
        (up.shape, jnp.bfloat16),
        ((seqs, down.shape[0] // seqs, down.shape[1]), jnp.bfloat16),
    )
    hbm = [pl.BlockSpec(memory_space=pl.ANY)]
    return pl.pallas_call(
        functools.partial(forward_kernel, heads),
        out_shape=[jax.ShapeDtypeStruct(*shape) for shape in shapes],
        in_specs=in_vmem(7) + hbm * 4,
        out_specs=in_vmem(7) + hbm * 4,
        scratch_shapes=[
            pltpu.VMEM((PAD + CHUNK, 3 * width), f32),
            pltpu.VMEM((heads, DK, DK), f32),
            dma_sems(4),
        ]
        + exchange_sems() * 2
        + [dma_sems(seqs - 1)] * 4,
        compiler_params=pltpu.CompilerParams(
            collective_id=5, has_side_effects=True, vmem_limit_bytes=48 * 1024 * 1024
        ),
        name="mixer_forward",
    )(n1, qkv, beta, taps, aux, docs, gain, o_weight, gate, up, down)


def run_backward(grad, o_full, saved, taps, aux, docs, gain, extra, sums):
    row_len, heads = grad.shape[0], o_full.shape[2] // DK
    model_width = grad.shape[1]
    rows_axis, seqs, _, shard = o_full.shape
    b16 = jnp.bfloat16
    width, f32 = heads * DK, jnp.float32
    logit = saved[1]
    shapes = (
        ((row_len, 3 * width), jnp.bfloat16),
        (logit.shape, jnp.bfloat16),
        ((4 + heads, model_width), f32),
        ((rows_axis, seqs, shard, 3 * width), b16),
    )
    o_shape = (rows_axis, seqs, shard, width)
    far = [pl.BlockSpec(memory_space=pl.ANY)]
    far_shapes = ((sums.shape[1:], b16),) * 3 + ((o_shape, b16),)
    return pl.pallas_call(
        functools.partial(backward_kernel, heads),
        out_shape=[jax.ShapeDtypeStruct(*shape) for shape in shapes + far_shapes],
        in_specs=in_vmem(12 + len(extra)) + far,
        out_specs=in_vmem(len(shapes)) + far * len(far_shapes),
        scratch_shapes=[
            pltpu.VMEM((PAD + CHUNK, 3 * width), f32),
            pltpu.VMEM((KW - 1, CHUNK + PAD, 3 * width), f32),
            pltpu.VMEM((heads, DK, DK), f32),
            pltpu.VMEM((width, model_width), b16),
            pltpu.VMEM(o_shape, b16),
            pltpu.VMEM((KW, 3 * width), f32),
            pltpu.VMEM((1, DK), f32),
        ]
        + pair_sems("seq", 3)
        + pair_sems("row", 1),
        compiler_params=pltpu.CompilerParams(
            collective_id=6, has_side_effects=True, vmem_limit_bytes=48 * 1024 * 1024
        ),
        name="mixer_backward",
    )(grad, o_full, *saved, taps, aux, docs, gain, *extra, sums)


def row_aux(docs):
    f32 = jnp.float32
    chunks = docs.reshape(-1, CHUNK)
    prior = jnp.concatenate([jnp.full((1,), -1, jnp.int32), chunks[:-1, -1]])
    padded = jnp.concatenate([jnp.full((KW - 1,), -1, jnp.int32), docs])
    columns = [
        docs,
        docs < DOCS,
        (chunks == prior[:, None]).reshape(-1),
        (chunks == chunks[:, -1:]).reshape(-1),
    ] + [padded[KW - 1 - tap : KW - 1 - tap + docs.shape[0]] == docs for tap in range(1, KW)]
    columns = [column.astype(f32) for column in columns]
    columns += [jnp.zeros_like(columns[0])] * (8 - len(columns))
    return jnp.stack(columns, axis=1), chunks.astype(f32)


def remote(source, target, send, recv, where):
    return pltpu.make_async_remote_copy(
        src_ref=source,
        dst_ref=target,
        send_sem=send,
        recv_sem=recv,
        device_id=where,
        device_id_type=pl.DeviceIdType.MESH,
    )


def greet(partners):
    barrier = pltpu.get_barrier_semaphore()
    for partner, there in partners:

        @pl.when(there)
        def _(partner=partner):
            pl.semaphore_signal(
                barrier, inc=1, device_id=partner, device_id_type=pl.DeviceIdType.MESH
            )

    pl.semaphore_wait(barrier, sum(there.astype(jnp.int32) for _, there in partners))


def around(axis):
    count, place = lax.axis_size(axis), lax.axis_index(axis)
    return [lax.rem(place + by, count) for by in range(1, count)]


def line_partners():
    count, place, core = lax.axis_size("seq"), lax.axis_index("seq"), lax.axis_index("tp")
    return [
        ({"seq": jnp.minimum(place + 1, count - 1)}, place < count - 1),
        ({"seq": jnp.maximum(place - 1, 0)}, place > 0),
        ({"tp": 1 - core}, core >= 0),
    ]


class Line:
    def __init__(self):
        self.count, self.place = lax.axis_size("seq"), lax.axis_index("seq")
        self.core = lax.axis_index("tp")
        self.other = 1 - self.core
        self.right = {"seq": jnp.minimum(self.place + 1, self.count - 1)}
        self.left = {"seq": jnp.maximum(self.place - 1, 0)}
        self.across = {"tp": self.other}


class Gather:
    def __init__(self, line, slots, sems):
        self.line, self.slots, self.sems = line, slots, sems
        self.parts = sems.shape[2]
        self.rows = slots.shape[2] // self.parts

    def span(self, part):
        return pl.ds(part * self.rows, self.rows)

    def copy(self, kind, seq, part):
        line = self.line
        send = {"right": 0, "left": 1, "across": 2}[kind]
        recv = 4 if kind == "across" else 3
        slot = self.slots.at[seq, line.core, self.span(part)]
        where = {"right": line.right, "left": line.left, "across": line.across}[kind]
        return remote(
            slot, slot, self.sems.at[send, seq, part], self.sems.at[recv, seq, part], where
        )

    def forward(self, seq, part, right, left):
        line = self.line
        if right:

            @pl.when(line.place < line.count - 1)
            def _():
                self.copy("right", seq, part).start()

        if left:

            @pl.when(line.place > 0)
            def _():
                self.copy("left", seq, part).start()

        self.copy("across", seq, part).start()

    def phase(self, by, part):
        line = self.line
        if by == 0:
            self.forward(line.place, part, True, True)
            return

        @pl.when(line.place - by >= 0)
        def _():
            self.copy("right", line.place - by, part).wait_recv()
            self.forward(line.place - by, part, True, False)

        @pl.when(line.place + by < line.count)
        def _():
            self.copy("left", line.place + by, part).wait_recv()
            self.forward(line.place + by, part, False, True)

    def phases(self, by):
        for part in range(self.parts):
            self.phase(by, part)

    def finish(self):
        line = self.line
        for seq in range(line.count):
            for part in range(self.parts):

                @pl.when((line.place >= seq) & (line.place < line.count - 1))
                def _():
                    self.copy("right", seq, part).wait_send()

                @pl.when((line.place <= seq) & (line.place > 0))
                def _():
                    self.copy("left", seq, part).wait_send()

                self.copy("across", seq, part).wait()


class Scatter:
    def __init__(self, line, blocks, came, across, sems):
        self.line, self.blocks, self.came, self.across, self.sems = line, blocks, came, across, sems
        self.parts = sems.shape[2]
        self.rows = blocks.shape[2] // self.parts

    def span(self, part):
        return pl.ds(part * self.rows, self.rows)

    def over(self, seq, part):
        line, span = self.line, self.span(part)
        return remote(
            self.blocks.at[seq, line.other, span],
            self.across.at[seq, span],
            self.sems.at[0, seq, part],
            self.sems.at[1, seq, part],
            line.across,
        )

    def along(self, kind, seq, part):
        line, span = self.line, self.span(part)
        way = {"right": 0, "left": 1}[kind]
        slot = seq if way == 0 else jnp.where(seq == line.place - 1, line.count, seq)
        return remote(
            self.blocks.at[seq, line.core, span],
            self.came.at[slot, span],
            self.sems.at[2, seq, part],
            self.sems.at[3 + way, seq, part],
            line.right if way == 0 else line.left,
        )

    def nears(self, k):
        for part in range(self.parts):
            self.near(k, part)

    def fars(self, k):
        for part in range(self.parts):
            self.far(k, part)

    def product(self, left_ref, right_ref, part, order=1, tile=512, right_tile=None):
        seqs, cores, _, width = self.blocks.shape
        span = self.span(part)
        left = left_ref[:, span].reshape(seqs * cores * self.rows, -1)

        def columns(t, _):
            across = pl.ds(pl.multiple_of(t * tile, tile), tile)
            if right_tile is not None:
                total = right_tile(left, t, across)
            elif order == 1:
                total = mul(left, right_ref[across], (1, 1))
            else:
                total = mul(left, right_ref[:, across], (1, 0))
            self.blocks[:, :, span, across] = total.astype(jnp.bfloat16).reshape(
                seqs, cores, self.rows, tile
            )
            return 0

        lax.fori_loop(0, width // tile, columns, 0)
        self.offer(part)

    def offer(self, part):
        for k in range(self.blocks.shape[0]):
            self.over(self.target(k), part).start()

    def pass_on(self, kind, seq, part):
        line, span = self.line, self.span(part)
        f32 = jnp.float32
        first = line.place == (0 if kind == "right" else line.count - 1)
        way = {"right": 0, "left": 1}[kind]
        self.over(seq, part).wait_recv()
        total = self.blocks[seq, line.core, span].astype(f32)
        total = total + self.across[seq, span].astype(f32)

        @pl.when(first)
        def _():
            self.blocks[seq, line.core, span] = total.astype(jnp.bfloat16)

        @pl.when(jnp.logical_not(first))
        def _():
            self.along(kind, seq, part).wait_recv()
            self.blocks[seq, line.core, span] = (
                total + self.came[seq, span].astype(f32)
            ).astype(jnp.bfloat16)

        self.along(kind, seq, part).start()

    def target(self, k):
        line = self.line
        return jnp.where(line.place < line.count // 2, line.count - 1 - k, k)

    def edge(self):
        return (self.line.place == 0) | (self.line.place == self.line.count - 1)

    def near(self, k, part):
        line = self.line
        low = line.place < line.count // 2

        @pl.when(low & (line.count - 1 - k > line.place))
        def _():
            self.pass_on("right", line.count - 1 - k, part)

        @pl.when(jnp.logical_not(low) & (k < line.place))
        def _():
            self.pass_on("left", k, part)

    def far(self, k, part):
        line = self.line
        low = line.place < line.count // 2

        @pl.when(low & (k < line.place))
        def _():
            self.pass_on("left", k, part)

        @pl.when(jnp.logical_not(low) & (line.count - 1 - k > line.place))
        def _():
            self.pass_on("right", line.count - 1 - k, part)

    def start_edges(self, part):
        @pl.when(self.edge())
        def _():
            for k in range(self.line.count - 1):
                self.near(k, part)

    def relay(self, k, part):
        @pl.when(jnp.logical_not(self.edge()))
        def _():
            self.near(k, part)

    def relay_back(self, part):
        @pl.when(jnp.logical_not(self.edge()))
        def _():
            for k in range(self.line.count - 1):
                self.far(k, part)

    def wait_own(self, part):
        line = self.line

        @pl.when(line.place > 0)
        def _():
            self.along("right", line.place, part).wait_recv()

        @pl.when(line.place < line.count - 1)
        def _():
            self.along("left", line.place, part).wait_recv()

        self.over(line.place, part).wait_recv()

    def own_rows(self, rows):
        line = self.line
        f32 = jnp.float32
        total = self.blocks[line.place, line.core, rows].astype(f32)
        total = total + self.across[line.place, rows].astype(f32)
        from_left = self.came[line.place, rows].astype(f32)
        from_right = self.came[line.count, rows].astype(f32)
        total = total + jnp.where(line.place > 0, from_left, 0.0)
        return total + jnp.where(line.place < line.count - 1, from_right, 0.0)

    def finish(self):
        line = self.line
        for seq in range(line.count):
            for part in range(self.parts):
                self.over(seq, part).wait_send()

                @pl.when(line.place != seq)
                def _():
                    self.along("right", seq, part).wait_send()


class Exchange:
    def __init__(self, line, source, target, sems):
        self.line, self.source, self.target = line, source, target
        self.send, self.recv = sems[:2]
        self.shared = len(sems) > 2
        if self.shared:
            self.send_row, self.recv_row = sems[2:]
        self.row = lax.axis_index("row")
        self.seq_others, self.row_others = around("seq"), around("row")

    def spread(self, i):
        other = self.seq_others[i]
        return remote(
            self.source(other),
            self.target.at[self.row, self.line.place]
            if self.shared
            else self.target.at[self.line.place],
            self.send.at[i],
            self.recv.at[i],
            {"seq": other},
        )

    def share(self, i, j):
        line = self.line
        came_from = lax.rem(line.place + line.count - i, line.count)
        slot = self.target.at[self.row, came_from]
        return remote(
            slot, slot, self.send_row.at[i, j], self.recv_row.at[i, j], {"row": self.row_others[j]}
        )

    def start(self):
        for i in range(len(self.seq_others)):
            self.spread(i).start()

    def share_own(self):
        for j in range(len(self.row_others)):
            self.share(0, j).start()

    def share_came(self, i):
        self.spread(i - 1).wait_recv()
        for j in range(len(self.row_others)):
            self.share(i, j).start()

    def finish(self):
        for i in range(len(self.seq_others)):
            self.spread(i).wait_send()
            if not self.shared:
                self.spread(i).wait_recv()
        for i in range(len(self.seq_others) + 1 if self.shared else 0):
            for j in range(len(self.row_others)):
                self.share(i, j).wait()


class Share:
    def __init__(self, axis, source, target, sems, own_sem):
        self.axis, self.source, self.target = axis, source, target
        self.send, self.recv = sems
        self.others = around(axis)
        self.own = pltpu.make_async_copy(source, target.at[lax.axis_index(axis)], own_sem)

    def copy(self, i):
        return remote(
            self.source,
            self.target.at[lax.axis_index(self.axis)],
            self.send.at[i],
            self.recv.at[i],
            {self.axis: self.others[i]},
        )

    def start(self):
        for i in range(len(self.others)):
            self.copy(i).start()
        self.own.start()

    def finish(self):
        for i in range(len(self.others)):
            self.copy(i).wait()
        self.own.wait()


class Swap:
    def __init__(self, axis, source, target, sems, own_sem):
        self.axis, self.source, self.target = axis, source, target
        self.send, self.recv = sems
        self.others = around(axis)
        place = lax.axis_index(axis)
        self.own = pltpu.make_async_copy(source.at[place], target.at[place], own_sem)

    def copy(self, i):
        return remote(
            self.source.at[self.others[i]],
            self.target.at[lax.axis_index(self.axis)],
            self.send.at[i],
            self.recv.at[i],
            {self.axis: self.others[i]},
        )

    def start(self):
        for i in range(len(self.others)):
            self.copy(i).start()
        self.own.start()

    def finish(self):
        for i in range(len(self.others)):
            self.copy(i).wait()
        self.own.wait()


class RowSum:
    def __init__(self, blocks, halves, came, sems):
        self.blocks, self.halves, self.came = blocks, halves, came
        self.row = lax.axis_index("row")
        even_x, even_y = lax.rem(self.row, 2) == 0, self.row < 2
        x_step, y_step = jnp.where(even_x, 1, -1), jnp.where(even_y, 2, -2)
        self.near = (self.row + x_step, self.row + y_step)
        self.far = self.row + x_step + y_step
        self.half = blocks.shape[2] // 2
        self.send_half, self.recv_half, self.send, self.recv = sems

    def rows(self, i):
        return pl.ds(i * self.half, self.half)

    def half_copy(self, i, m):
        return remote(
            self.blocks.at[self.far, m, self.rows(i)],
            self.halves.at[i, m],
            self.send_half.at[i, m],
            self.recv_half.at[i, m],
            {"row": self.near[i]},
        )

    def copy(self, i, j, m):
        return remote(
            self.blocks.at[self.near[i], m, self.rows(j)],
            self.came.at[i, m, self.rows(j)],
            self.send.at[i, j, m],
            self.recv.at[i, j, m],
            {"row": self.near[i]},
        )

    def start_far(self, m):
        for i in range(2):
            self.half_copy(i, m).start()

    def start_near(self, i, m):
        self.copy(i, i, m).start()

    def add_half(self, i, m):
        j = 1 - i
        self.half_copy(j, m).wait_recv()
        rows = self.rows(j)
        total = self.blocks[self.near[i], m, rows].astype(jnp.float32)
        total = total + self.halves[j, m].astype(jnp.float32)
        self.blocks[self.near[i], m, rows] = total.astype(jnp.bfloat16)
        self.copy(i, j, m).start()

    def total(self, m):
        for i in range(2):
            for j in range(2):
                self.copy(i, j, m).wait_recv()
        total = self.blocks[self.row, m].astype(jnp.float32)
        for i in range(2):
            total = total + self.came[i, m].astype(jnp.float32)
        return total

    def finish(self):
        for m in range(self.blocks.shape[1]):
            for i in range(2):
                self.half_copy(i, m).wait_send()
                for j in range(2):
                    self.copy(i, j, m).wait_send()


def row_sum_scratch(shape):
    b16 = jnp.bfloat16
    _, count, rows, width = shape
    return [
        pltpu.VMEM(shape, b16),
        pltpu.VMEM((2, count, rows // 2, width), b16),
        pltpu.VMEM((2, count, rows, width), b16),
    ], [dma_sems(2, count), dma_sems(2, count), dma_sems(2, 2, count), dma_sems(2, 2, count)]


def pair_sems(axis, count):
    return [dma_sems(lax.axis_size(axis) - 1)] * (2 * count) + [dma_sems(count)]


def moves_of(kind, axis, sources, targets, sems):
    return [
        kind(axis, source, target, sems[2 * i : 2 * i + 2], sems[-1].at[i])
        for i, (source, target) in enumerate(zip(sources, targets))
    ]


def along_axis(axis):
    return [({axis: other}, other >= 0) for other in around(axis)]


def exchange_sems():
    seqs, rows = lax.axis_size("seq"), lax.axis_size("row")
    return [
        dma_sems(seqs - 1),
        dma_sems(seqs - 1),
        dma_sems(seqs, rows - 1),
        dma_sems(seqs, rows - 1),
    ]


def exchange_partners(line):
    return [({"seq": other}, other >= 0) for other in around("seq")] + [
        ({"row": other}, other >= 0) for other in around("row")
    ]


STEP = 32


def over_rows(total, part, body):
    def step(i, _):
        body(pl.ds(pl.multiple_of(part * total.rows + i * STEP, STEP), STEP))
        return 0

    lax.fori_loop(0, total.rows // STEP, step, 0)


def resid_kernel(
    mix_ref, o_ref, x_ref, g_ref, gain_ref, up_ref, down_ref,
    resid_ref, n2_ref, g_full_ref, up_full_ref, down_full_ref,
    blocks, came, across, o_rows, sum_sems, n2_sems, g_sems, *sems,
):
    line = Line()
    greet(line_partners() + along_axis("row"))
    shares = moves_of(
        Share,
        "row",
        (up_ref, down_ref),
        (up_full_ref, down_full_ref),
        sems,
    )
    for share in shares:
        share.start()
    rows = n2_ref.shape[2]
    total = Scatter(line, blocks, came, across, sum_sems)
    n2 = Gather(line, n2_ref, n2_sems)
    grads = Gather(line, g_full_ref, g_sems)
    g_full_ref[line.place, line.core] = g_ref[
        pl.ds(pl.multiple_of(line.core * rows, rows), rows)
    ]
    grads.phases(0)
    side_by_side(o_ref, o_rows)
    for part in range(total.parts):
        total.product(mix_ref, o_rows, part, order=0)
    for k in range(1, line.count):
        grads.phases(k)
        total.nears(k - 1)
    for k in range(line.count - 1):
        total.fars(k)

    def normed(span):
        x_span = pl.ds(pl.multiple_of(line.core * rows + span.start, STEP), STEP)
        resid = x_ref[x_span].astype(jnp.float32) + total.own_rows(span)
        resid_ref[span] = resid
        n2_ref[line.place, line.core, span] = (
            resid * norm_scale(resid) * gain_ref[...]
        ).astype(jnp.bfloat16)

    for part in range(total.parts):
        total.wait_own(part)
        over_rows(total, part, normed)
        n2.phase(0, part)
    for k in range(1, line.count):
        n2.phases(k)
    total.finish()
    n2.finish()
    grads.finish()
    for share in shares:
        share.finish()


def side_by_side(blocks_ref, out_ref):
    outer, inner, _, width = blocks_ref.shape
    for i in range(outer):
        for j in range(inner):
            out_ref[:, (i * inner + j) * width : (i * inner + j + 1) * width] = blocks_ref[i, j]


def dma_sems(*shape):
    return pltpu.SemaphoreType.DMA(shape)


def line_call(kernel, collective_id, name, outs, scratch, args, limit=56, far_args=(), far_outs=()):
    far = pl.BlockSpec(memory_space=pl.ANY)
    return pl.pallas_call(
        kernel,
        out_shape=[jax.ShapeDtypeStruct(*out) for out in (*outs, *far_outs)],
        in_specs=in_vmem(len(args)) + [far] * len(far_args),
        out_specs=in_vmem(len(outs)) + [far] * len(far_outs),
        scratch_shapes=scratch,
        compiler_params=pltpu.CompilerParams(
            collective_id=collective_id,
            has_side_effects=True,
            vmem_limit_bytes=limit * 1024 * 1024,
        ),
        name=name,
    )(*args, *far_args)


def scatter_scratch(seqs, cores, rows, width):
    b16 = jnp.bfloat16
    return [
        pltpu.VMEM((seqs, cores, rows, width), b16),
        pltpu.VMEM((seqs + 1, rows, width), b16),
        pltpu.VMEM((seqs, rows, width), b16),
    ]


PARTS = 2


def run_resid(mix, o_full, x, g, gain, weights):
    seqs, cores, (piece, width) = lax.axis_size("seq"), lax.axis_size("tp"), x.shape
    rows, b16 = piece // cores, jnp.bfloat16
    outs = (
        ((rows, width), jnp.float32),
        ((seqs, cores, rows, width), b16),
        ((seqs, cores, rows, width), b16),
    )
    scratch = scatter_scratch(seqs, cores, rows, width)
    scratch = scratch + [pltpu.VMEM((o_full.shape[2], width), b16)] + [dma_sems(5, seqs, PARTS)] * 3
    scratch = scratch + pair_sems("row", len(weights))
    mix = mix.reshape(seqs * cores, rows, -1)
    resid, n2, g_full, *full = line_call(
        resid_kernel, 1, "resid_norm", outs, scratch, (mix, o_full, x, g, gain),
        far_args=weights,
        far_outs=[((lax.axis_size("row"),) + weight.shape, b16) for weight in weights],
    )
    return resid, n2.reshape(-1, width), g_full.reshape(-1, width), full


def grad_resid_kernel(
    grad_gate_ref, grad_up_ref, hidden_ref, down_ref, resid_ref, g_ref, gain_ref,
    gate_ref, up_ref, n2_ref, g_full_ref,
    grad_resid_ref, grad_attn_ref, gain_grad_ref, result_ref,
    sum_ref,
    blocks, came, across, out_blocks, out_came, out_across, weights, tokens, parts, halves, parts_came,
    sum_sems, out_sems, attn_sems, swap_sems, weight_sems, token_sems, own_sems, *sems,
):
    line = Line()
    greet(line_partners() + along_axis("row"))
    rows = resid_ref.shape[0]
    total = Scatter(line, blocks, came, across, sum_sems)
    result = Scatter(line, out_blocks, out_came, out_across, out_sems)
    attn = Gather(line, grad_attn_ref, attn_sems)
    sums = RowSum(parts, halves, parts_came, sems)
    units = hidden_ref.shape[2]
    tile = weights.shape[2]
    tiles = blocks.shape[3] // tile
    steps = total.parts * tiles

    def weight_copies(step):
        slot = step % 2
        span = pl.ds((step % tiles) * tile, tile)
        return [
            pltpu.make_async_copy(ref.at[span], weights.at[slot, i], weight_sems.at[slot, i])
            for i, ref in enumerate((gate_ref, up_ref))
        ]

    orders = (sums.far, sums.near[0], sums.near[1], sums.row)
    block_width = tokens.shape[3]

    def token_copies(step):
        slot = step % 2
        columns = pl.ds(pl.multiple_of(orders[step] * block_width, block_width), block_width)
        return [
            pltpu.make_async_copy(ref.at[:, columns], tokens.at[slot, i], token_sems.at[slot, i])
            for i, ref in enumerate((g_full_ref, n2_ref))
        ]

    for copy in weight_copies(0) + token_copies(0):
        copy.start()

    def product(part):
        span = total.span(part)
        left_gate = grad_gate_ref[:, span].reshape(-1, units)
        left_up = grad_up_ref[:, span].reshape(-1, units)
        for t in range(tiles):
            step = part * tiles + t
            if step + 1 < steps:
                for copy in weight_copies(step + 1):
                    copy.start()
            for copy in weight_copies(step):
                copy.wait()
            slot = step % 2
            out = mul(left_gate, weights[slot, 0], (1, 1)) + mul(left_up, weights[slot, 1], (1, 1))
            out = out.astype(jnp.bfloat16).reshape(blocks.shape[:2] + (total.rows, tile))
            blocks[:, :, span, t * tile : (t + 1) * tile] = out
        total.offer(part)
        total.start_edges(part)

    def weight_grads(step):
        if step + 1 < len(orders):
            for copy in token_copies(step + 1):
                copy.start()
        for copy in token_copies(step):
            copy.wait()
        slot, to = step % 2, orders[step]
        for m, (i, ref) in enumerate(((0, hidden_ref), (1, grad_gate_ref), (1, grad_up_ref))):
            part = mul(tokens[slot, i], ref[...].reshape(-1, units), (0, 0))
            parts[to, m] = part.astype(jnp.bfloat16)
            if step == 0:
                sums.start_far(m)
            elif step < 3:
                sums.start_near(step - 1, m)

    for part in range(total.parts):
        product(part)
    weight_grads(0)
    total.relay(0, 0)
    total.relay(1, 0)
    weight_grads(1)
    total.relay_back(0)
    weight_grads(2)
    total.relay(0, 1)
    total.relay(1, 1)
    weight_grads(3)
    total.relay_back(1)
    gain_grad_ref[...] = jnp.zeros_like(gain_grad_ref)

    def back(span):
        own_span = pl.ds(pl.multiple_of(line.core * rows + span.start, STEP), STEP)
        resid = resid_ref[span]
        grad_two = total.own_rows(span)
        scale = norm_scale(resid)
        gain_grad_ref[...] += jnp.sum(grad_two * resid * scale, axis=0, keepdims=True)
        grad = g_ref[own_span].astype(jnp.float32) + norm_back(
            resid, scale, gain_ref[...], grad_two
        )
        grad_resid_ref[span] = grad
        grad_attn_ref[line.place, line.core, span] = grad.astype(jnp.bfloat16)

    for part in range(total.parts):
        total.wait_own(part)
        over_rows(total, part, back)
        attn.phase(0, part)
    for part in range(result.parts):
        result.product(hidden_ref, down_ref, part, order=0)
    for m in range(parts.shape[1]):
        for i in range(2):
            sums.add_half(i, m)
    for k in range(1, line.count):
        attn.phases(k)
        result.nears(k - 1)
    for k in range(line.count - 1):
        result.fars(k)

    def finish(span):
        own_span = pl.ds(pl.multiple_of(line.core * rows + span.start, STEP), STEP)
        result_ref[own_span] = (resid_ref[span] + result.own_rows(span)).astype(jnp.bfloat16)

    for part in range(result.parts):
        result.wait_own(part)
        over_rows(result, part, finish)
    swap = own_swap(line, result_ref, rows, swap_sems)
    swap.start()
    own = []
    for m in range(parts.shape[1]):
        parts[sums.row, m] = sums.total(m).astype(jnp.bfloat16)
        own.append(
            pltpu.make_async_copy(parts.at[sums.row, m], sum_ref.at[m], own_sems.at[m])
        )
        own[m].start()
    total.finish()
    result.finish()
    attn.finish()
    swap.wait()
    sums.finish()
    for copy in own:
        copy.wait()


def own_swap(line, ref, rows, sems):
    own = ref.at[pl.ds(pl.multiple_of(line.core * rows, rows), rows)]
    return remote(own, own, sems.at[0], sems.at[1], line.across)


def run_grad_resid(grad_gate, grad_up, gate, up, hidden, down, resid, g, gain, n2, g_full):
    seqs, cores, (piece, width) = lax.axis_size("seq"), lax.axis_size("tp"), g.shape
    rows_axis = lax.axis_size("row")
    rows, b16, f32 = piece // cores, jnp.bfloat16, jnp.float32
    units, span = gate.shape[1], width // rows_axis
    outs = (
        ((rows, width), f32),
        ((seqs, cores, rows, width), b16),
        ((1, width), f32),
        ((piece, width), b16),
    )
    sum_buffers, sum_sems = row_sum_scratch((rows_axis, 3, span, units))
    scratch = scatter_scratch(seqs, cores, rows, width) * 2
    scratch = scratch + [
        pltpu.VMEM((2, 2, span, units), b16),
        pltpu.VMEM((2, 2, n2.shape[0], span), b16),
    ]
    scratch = scratch + sum_buffers + [dma_sems(5, seqs, PARTS)] * 3
    scratch = scratch + [dma_sems(2), dma_sems(2, 2), dma_sems(2, 2), dma_sems(3)] + sum_sems
    grad_gate, grad_up, hidden = (
        array.reshape(seqs * cores, rows, -1) for array in (grad_gate, grad_up, hidden)
    )
    grad_resid, grad_attn, gain_grad, result, sums = line_call(
        grad_resid_kernel, 2, "grad_resid", outs, scratch,
        (grad_gate, grad_up, hidden, down, resid, g, gain),
        limit=60,
        far_args=(gate, up, n2, g_full),
        far_outs=(((3, span, units), b16),),
    )
    return grad_resid, grad_attn.reshape(-1, width), gain_grad, result, sums


def input_grad_kernel(
    grad_proj_ref, qkv_ref, grad_logit_ref, beta_ref, x_ref, grad_resid_ref, gain_ref, qkv_part_ref,
    small_ref, o_sum_ref,
    input_grad_ref, qkv_came_ref, small_all_ref,
    o_came_ref,
    blocks, came, across, qkv_rows, qkv_sum, small_rows, sum_sems, swap_sems, *sems,
):
    line = Line()
    greet(along_axis("seq") + along_axis("row") + along_axis("tp"))
    (o_move,) = moves_of(Swap, "seq", (o_sum_ref,), (o_came_ref,), sems[:3])
    (rows_move,) = moves_of(Swap, "row", (qkv_part_ref,), (qkv_rows,), sems[3:6])
    (qkv_move,) = moves_of(Swap, "seq", (qkv_sum,), (qkv_came_ref,), sems[6:9])
    (small_row,) = moves_of(Share, "row", (small_ref,), (small_rows,), sems[9:12])
    own_small = small_all_ref.at[line.core, line.place]
    small_seq = [
        remote(own_small, own_small, sems[12].at[i], sems[13].at[i], {"seq": other})
        for i, other in enumerate(around("seq"))
    ]
    core_small = small_all_ref.at[line.core]
    small_core = remote(core_small, core_small, sems[14].at[0], sems[14].at[1], line.across)
    small_row.start()
    rows_move.start()
    o_move.start()
    rows = grad_resid_ref.shape[0]
    total = Scatter(line, blocks, came, across, sum_sems)

    width = qkv_ref.shape[-1]

    for part in range(total.parts):
        logit = grad_logit_ref[:, total.span(part)].reshape(-1, grad_logit_ref.shape[-1])

        def right_tile(left, t, across, logit=logit):
            block = qkv_ref[t]
            out = mul(logit, beta_ref[:, across], (1, 0))
            for c in range(3):
                out = out + mul(
                    left[:, c * width : (c + 1) * width], block[:, c].reshape(-1, width), (1, 1)
                )
            return out

        tile = qkv_ref.shape[1] * qkv_ref.shape[3]
        total.product(grad_proj_ref, None, part, tile=tile, right_tile=right_tile)
    small_row.finish()
    small = small_rows[0]
    for i in range(1, small_rows.shape[0]):
        small = small + small_rows[i]
    small_all_ref[line.core, line.place] = small
    for copy in small_seq:
        copy.start()
    for k in range(line.count - 1):
        total.nears(k)
    for copy in small_seq:
        copy.wait()
    small_core.start()
    for k in range(line.count - 1):
        total.fars(k)
    rows_move.finish()
    for i in range(qkv_rows.shape[1]):
        piece = qkv_rows[0, i].astype(jnp.float32)
        for j in range(1, qkv_rows.shape[0]):
            piece = piece + qkv_rows[j, i].astype(jnp.float32)
        qkv_sum[i] = piece.astype(jnp.bfloat16)
    qkv_move.start()

    def back(span):
        own_span = pl.ds(pl.multiple_of(line.core * rows + span.start, STEP), STEP)
        x = x_ref[own_span].astype(jnp.float32)
        grad_one = total.own_rows(span)
        scale = norm_scale(x)
        input_grad_ref[own_span] = (
            grad_resid_ref[span] + norm_back(x, scale, gain_ref[...], grad_one)
        ).astype(jnp.bfloat16)

    for part in range(total.parts):
        total.wait_own(part)
        over_rows(total, part, back)
    swap = own_swap(line, input_grad_ref, rows, swap_sems)
    swap.start()
    total.finish()
    swap.wait()
    small_core.wait()
    o_move.finish()
    qkv_move.finish()


def run_input_grad(grad_proj, qkv, grad_logit, beta, x, grad_resid, gain, qkv_part, small, o_sum):
    seqs, cores, (piece, width) = lax.axis_size("seq"), lax.axis_size("tp"), x.shape
    rows, b16, f32 = piece // cores, jnp.bfloat16, jnp.float32
    outs = (
        ((piece, width), b16),
        (qkv_part.shape[1:], b16),
        ((cores, seqs) + small.shape, f32),
    )
    scratch = scatter_scratch(seqs, cores, rows, width)
    scratch = scratch + [pltpu.VMEM(qkv_part.shape, b16), pltpu.VMEM(qkv_part.shape[1:], b16)]
    scratch = scratch + [pltpu.VMEM((lax.axis_size("row"),) + small.shape, f32)]
    scratch = scratch + [dma_sems(5, seqs, PARTS), dma_sems(2)]
    scratch = scratch + pair_sems("seq", 1) + pair_sems("row", 1) + pair_sems("seq", 1)
    scratch = scratch + pair_sems("row", 1) + [dma_sems(seqs - 1)] * 2 + [dma_sems(2)]
    grad_proj = grad_proj.reshape(seqs * cores, rows, -1)
    grad_logit = grad_logit.reshape(seqs * cores, rows, -1)
    return line_call(
        input_grad_kernel, 3, "input_grad", outs, scratch,
        (grad_proj, qkv, grad_logit, beta, x, grad_resid, gain, qkv_part, small),
        far_args=(o_sum,),
        far_outs=((o_sum.shape, b16),),
    )


def normed_kernel(
    x_ref, gain_ref, weight_ref, beta_ref, n1_ref, qkv_ref, beta_full_ref, n1_sems, own_sems, *sems
):
    line = Line()
    row = lax.axis_index("row")
    greet(exchange_partners(line) + [(line.across, line.core >= 0)])
    width = qkv_ref.shape[-1]

    def columns(seq):
        return weight_ref.at[:, :, pl.ds(pl.multiple_of(seq * width, width), width)]

    moves = [
        Exchange(line, columns, qkv_ref, sems[:4]),
        Exchange(line, lambda seq: beta_ref.at[seq], beta_full_ref, sems[4:]),
    ]
    for move in moves:
        move.start()
    own = [
        pltpu.make_async_copy(
            move.source(line.place), move.target.at[row, line.place], own_sems.at[i]
        )
        for i, move in enumerate(moves)
    ]
    for copy in own:
        copy.start()
    rows = n1_ref.shape[2]
    n1 = Gather(line, n1_ref, n1_sems)

    def normed(span):
        x_span = pl.ds(pl.multiple_of(line.core * rows + span.start, STEP), STEP)
        x = x_ref[x_span].astype(jnp.float32)
        n1_ref[line.place, line.core, span] = (x * norm_scale(x) * gain_ref[...]).astype(
            jnp.bfloat16
        )

    for part in range(n1.parts):
        over_rows(n1, part, normed)
        n1.phase(0, part)
    for copy in own:
        copy.wait()
    for move in moves:
        move.share_own()
    for k in range(1, line.count):
        for move in moves:
            move.share_came(k)
        n1.phases(k)
    for move in moves:
        move.finish()
    n1.finish()


def run_normed(x, gain, weight, beta):
    rows_axis, seqs, cores = (lax.axis_size(axis) for axis in ("row", "seq", "tp"))
    piece, width = x.shape
    b16 = jnp.bfloat16
    outs = (
        ((seqs, cores, piece // cores, width), b16),
        ((rows_axis, seqs) + weight.shape[:2] + (weight.shape[2] // seqs,), b16),
        ((rows_axis,) + beta.shape, b16),
    )
    n1, qkv, beta_full = line_call(
        normed_kernel, 4, "norm_gather", outs,
        [dma_sems(5, seqs, PARTS), dma_sems(2)] + exchange_sems() * 2,
        (x, gain, weight, beta),
    )
    return n1.reshape(-1, width), qkv, beta_full


def mlp_kernel(
    n2_ref, g_ref, gate_ref, up_ref, down_ref, hidden_ref, grad_gate_ref, grad_up_ref, down_rows
):
    @pl.when(pl.program_id(0) == 0)
    def _():
        side_by_side(down_ref, down_rows)

    n2 = n2_ref[...]
    gate = mul(n2, gate_ref[...], (1, 0))
    up = mul(n2, up_ref[...], (1, 0))
    grad_hidden = mul(g_ref[...], down_rows[...], (1, 1))
    sig = sigmoid(gate)
    act = gate * sig
    hidden_ref[...] = (act * up).astype(jnp.bfloat16)
    grad_up_ref[...] = (grad_hidden * act).astype(jnp.bfloat16)
    grad_gate_ref[...] = (grad_hidden * up * sig * (1.0 + gate * (1.0 - sig))).astype(jnp.bfloat16)


def run_mlp(n2, g, gate, up, down, block=256):
    row_len, width = n2.shape
    units = gate.shape[1]
    tokens = pl.BlockSpec((block, width), lambda i: (i, 0))
    out = pl.BlockSpec((block, units), lambda i: (i, 0))
    whole = pl.BlockSpec(memory_space=pltpu.VMEM)
    shape = jax.ShapeDtypeStruct((row_len, units), jnp.bfloat16)
    return pl.pallas_call(
        mlp_kernel,
        grid=(row_len // block,),
        out_shape=[shape] * 3 + [jax.ShapeDtypeStruct((units, width), jnp.bfloat16)],
        in_specs=[tokens, tokens, whole, whole, whole],
        out_specs=[out] * 3 + [whole],
        compiler_params=pltpu.CompilerParams(vmem_limit_bytes=48 * 1024 * 1024),
        name="mlp",
    )(n2, g, gate, up, down)


def finish_kernel(
    small_ref, qkv_ref, o_ref, gate_ref, up_ref, down_ref,
    attn_gain_ref, mlp_gain_ref, out_gain_ref, conv_ref, qkv_out, o_out, gate_up_out, down_out,
):
    f32 = jnp.float32
    cores, seqs, _, _ = small_ref.shape
    _, shard, width3 = qkv_ref.shape
    width, units = width3 // 3, gate_ref.shape[2]
    at = 2 + width // DK
    for ref, rows, lanes in (
        (attn_gain_ref, slice(0, 1), slice(None)),
        (mlp_gain_ref, slice(1, 2), slice(None)),
        (out_gain_ref, slice(at, at + 1), slice(2 * width3, 2 * width3 + DK)),
    ):
        total = small_ref[0, 0, rows, lanes]
        for i in range(1, cores * seqs):
            total = total + small_ref[i // seqs, i % seqs, rows, lanes]
        ref[...] = total
    down = lax.broadcasted_iota(jnp.int32, (shard, shard), 0)
    along = lax.broadcasted_iota(jnp.int32, (shard, shard), 1)
    unit = jnp.where(down == along, 1.0, 0.0).astype(jnp.bfloat16)
    for core in range(cores):
        for seq in range(seqs):
            for c in range(3):
                for tap in range(KW):
                    row, lane = at + tap // 2, (tap % 2) * width3 + c * width
                    to = (core * seqs + seq) * width
                    conv_ref[c, tap : tap + 1, to : to + width] = small_ref[
                        core, seq, row : row + 1, lane : lane + width
                    ]
    for seq in range(seqs):
        for c in range(3):
            qkv_out[c, :, seq * width : (seq + 1) * width] = qkv_ref[
                seq, :, c * width : (c + 1) * width
            ].astype(f32)
        o_out[seq * width : (seq + 1) * width] = mul(o_ref[seq], unit, (0, 0))
        down_out[seq * units : (seq + 1) * units] = mul(down_ref[seq], unit, (0, 0))
    for i, ref in enumerate((gate_ref, up_ref)):
        gate_up_out[i] = jnp.concatenate([ref[seq].astype(f32) for seq in range(seqs)], axis=1)


def run_finish(small, qkv, o, gate, up, down):
    f32 = jnp.float32
    cores, seqs, _, model_width = small.shape
    _, shard, width3 = qkv.shape
    units = gate.shape[2]
    shapes = (
        (1, model_width),
        (1, model_width),
        (1, DK),
        (3, KW, model_width),
        (3, shard, seqs * width3 // 3),
        (seqs * width3 // 3, shard),
        (2, shard, seqs * units),
        (seqs * units, shard),
    )
    return pl.pallas_call(
        finish_kernel,
        out_shape=[jax.ShapeDtypeStruct(shape, f32) for shape in shapes],
        in_specs=in_vmem(6),
        out_specs=in_vmem(len(shapes)),
        compiler_params=pltpu.CompilerParams(vmem_limit_bytes=48 * 1024 * 1024),
        name="finish",
    )(small, qkv, o, gate, up, down)


def local_heads(
    block_input,
    grad_out,
    doc_lengths,
    attn_gain,
    mlp_gain,
    out_gain,
    conv_weight,
    qkv_weight,
    beta_weight,
    o_weight,
    gate_up_weight,
    down_weight,
):
    tok_rows, model_width = block_input.shape[1:]
    pieces, cores = lax.axis_size("seq"), lax.axis_size("tp")
    piece, core = lax.axis_index("seq"), lax.axis_index("tp")
    row_len = pieces * tok_rows
    shard_rows = qkv_weight.shape[1]
    width = qkv_weight.shape[2] // pieces
    heads = width // DK
    units = gate_up_weight.shape[2] // pieces
    f32, b16 = jnp.float32, jnp.bfloat16

    x_piece, g_piece = block_input[0], grad_out[0]
    beta_parts = jnp.pad(
        beta_weight.T.reshape(pieces, heads, shard_rows), ((0, 0), (0, 16 - heads), (0, 0))
    )
    normed_one, qkv_full, beta_full = run_normed(
        x_piece, attn_gain[None], qkv_weight, beta_parts
    )
    beta_full = beta_full.reshape(-1, 16, shard_rows).transpose(1, 0, 2).reshape(16, -1)
    gate_up_parts = gate_up_weight.reshape(2, shard_rows, pieces, units).transpose(0, 2, 1, 3)

    ends = jnp.cumsum(doc_lengths[0])
    places = jnp.arange(row_len, dtype=jnp.int32)
    docs = jnp.sum((places[:, None] >= ends[None, :]).astype(jnp.int32), axis=1)
    aux, doc_rows = row_aux(docs)
    gain_row = out_gain[None]
    taps = lax.dynamic_slice_in_dim(conv_weight, piece * width, width, axis=2)
    taps = taps.transpose(1, 0, 2).reshape(KW, 3 * width)

    (
        proj, logit, mixed, normed_mix, inverse, states, written,
        o_full, gate_full, up_came, down_came,
    ) = run_forward(
        normed_one, qkv_full, beta_full, taps, aux, doc_rows, gain_row,
        o_weight, gate_up_parts[0], gate_up_parts[1], down_weight,
    )
    resid, normed_two, g_full, (up_full, down_full) = run_resid(
        normed_mix, o_full, x_piece, g_piece, mlp_gain[None], (up_came, down_came)
    )
    gate_full = gate_full.reshape(model_width, units)
    up_full = up_full.reshape(model_width, units)
    hidden, grad_gate, grad_up, down_rows = run_mlp(
        normed_two, g_full, gate_full, up_full, down_full
    )

    def summed(came):
        return jnp.sum(came.astype(f32), axis=0).astype(b16)

    grad_resid, grad_attn, mlp_gain_part, result, sums = run_grad_resid(
        grad_gate, grad_up, gate_full, up_full, hidden, down_rows, resid, g_piece, mlp_gain[None],
        normed_two, g_full,
    )
    grad_proj, grad_logit, small, qkv_part, down_sum, gate_sum, up_sum, o_came = run_backward(
        grad_attn,
        o_full,
        (proj, logit, mixed, inverse, states, written),
        taps,
        aux,
        doc_rows,
        gain_row,
        (normed_mix, normed_one, qkv_full, beta_full, attn_gain[None], mlp_gain_part),
        sums.reshape(3, pieces, shard_rows, units),
    )
    input_grad, qkv_sum, small, o_sum = run_input_grad(
        grad_proj, qkv_full, grad_logit, beta_full, x_piece, grad_resid, attn_gain[None],
        qkv_part, small, summed(o_came),
    )
    attn_gain_grad, mlp_gain_grad, out_gain_grad, conv_grad, qkv_grad, o_grad, gate_up_grad, down_grad = (
        run_finish(small, qkv_sum, o_sum, gate_sum, up_sum, down_sum)
    )
    beta_sum = lax.dynamic_index_in_dim(small[:, :, 2 : 2 + heads], core, 0, keepdims=False)
    beta_sum = lax.dynamic_slice_in_dim(
        beta_sum.reshape(pieces * heads, model_width),
        (lax.axis_index("row") * pieces + piece) * shard_rows,
        shard_rows,
        axis=1,
    ).T
    return (
        result[None],
        input_grad[None],
        attn_gain_grad[0],
        mlp_gain_grad[0],
        out_gain_grad[0],
        conv_grad,
        qkv_grad,
        beta_sum,
        o_grad,
        gate_up_grad,
        down_grad,
    )


def splits_heads(mesh, heads=16, units=5632):
    return (
        mesh.shape["tp"] == 2
        and heads % (mesh.shape["seq"] * 2) == 0
        and units % (mesh.shape["seq"] * 2) == 0
    )


def solution(mesh):
    in_specs = (
        P("row", "seq", None),
        P("row", "seq", None),
        P("row", None),
        P(),
        P(),
        P(),
        P(None, None, "tp"),
        P(None, ("row", "seq"), "tp"),
        P(("row", "seq"), "tp"),
        P("tp", ("row", "seq")),
        P(None, ("row", "seq"), "tp"),
        P("tp", ("row", "seq")),
    )
    out_specs = (
        P("row", "seq", None),
        P("row", "seq", None),
        P(),
        P(),
        P(),
        P(),
        P(None, ("row", "seq"), "tp"),
        P(("row", "seq"), "tp"),
        P("tp", ("row", "seq")),
        P(None, ("row", "seq"), "tp"),
        P("tp", ("row", "seq")),
    )
    local = local_heads if splits_heads(mesh) else local_pieces
    return jax.shard_map(local, mesh=mesh, in_specs=in_specs, out_specs=out_specs, check_vma=False)
```

```python
import functools

import jax
import jax.numpy as jnp
from jax import lax
from jax.experimental import pallas as pl
from jax.experimental.pallas import tpu as pltpu
from jax.sharding import PartitionSpec as P

DK = 128
KW = 4
GROUP = 64
DOCS = 8


eps = 1e-06
mix_floor = 0.01
precise = lax.Precision.HIGHEST


def from_behind(shard, axis, by):
    devices = lax.axis_size(axis)
    pairs = [(i, i + by) for i in range(devices) if 0 <= i + by < devices]
    return lax.ppermute(shard, axis, pairs)


def prefix(shard, axis, combine, identity, reverse):
    devices, place = (lax.axis_size(axis), lax.axis_index(axis))
    everything = jax.tree.map(
        lambda part, kind: lax.all_gather(part.astype(kind), axis),
        shard,
        (jnp.bfloat16, jnp.bfloat16),
    )
    start = jax.tree.map(
        lambda part, zero: jnp.broadcast_to(jnp.asarray(zero, part.dtype), part.shape),
        shard,
        identity,
    )

    def step(k, before):
        at = devices - 1 - k if reverse else k
        reached = at > place if reverse else at < place
        new = combine(
            before, jax.tree.map(lambda part, own: part[at].astype(own.dtype), everything, shard)
        )
        return jax.tree.map(lambda a, b: jnp.where(reached, a, b), new, before)

    return lax.fori_loop(0, devices, step, start)


def norm_scale(values):
    return lax.rsqrt(jnp.mean(values * values, axis=-1, keepdims=True) + eps)


def norm_back(values, scale, gain, grad):
    weighted = gain * grad
    return scale * weighted - values * scale**3 * jnp.mean(
        weighted * values, axis=-1, keepdims=True
    )


def batch_mul(left, right):
    return jnp.einsum("hij,hjk->hik", left, right, precision=precise)


def batch_mul_t(left, right):
    return jnp.einsum("hji,hjk->hik", left, right, precision=precise)


def compose(earlier, later):
    return (batch_mul(later[0], earlier[0]), batch_mul(later[0], earlier[1]) + later[1])


def over_heads(function, shared):
    return jax.vmap(jax.vmap(function), in_axes=shared)


def tp_total(term):
    return lax.psum(term.astype(jnp.bfloat16), "tp").astype(jnp.float32)


def group_parts(key_rows, value_rows, rates, same_doc, carry_mask):
    size = key_rows.shape[0]
    strict = jnp.tril(jnp.ones((size, size), jnp.float32), -1) * same_doc
    inner = jnp.dot(key_rows, key_rows.T, precision=precise)
    system = jnp.eye(size, dtype=jnp.float32) + rates[:, None] * inner * strict
    right_side = jnp.concatenate(
        [rates[:, None] * value_rows, (rates * carry_mask)[:, None] * key_rows], axis=1
    )
    solved = jax.scipy.linalg.solve_triangular(system, right_side, lower=True)
    base_rows = solved[:, : value_rows.shape[1]]
    wy_rows = solved[:, value_rows.shape[1] :]
    tail_keys = same_doc[size - 1][:, None] * key_rows
    identity_mat = jnp.eye(key_rows.shape[1], dtype=jnp.float32)
    transition = carry_mask[size - 1] * identity_mat - jnp.dot(
        tail_keys.T, wy_rows, precision=precise
    )
    contribution = jnp.dot(tail_keys.T, base_rows, precision=precise)
    return (transition, contribution, base_rows, wy_rows)


def group_output(queries, key_rows, same_doc, carry_mask, base_rows, wy_rows, state_in):
    size = key_rows.shape[0]
    lower = jnp.tril(jnp.ones((size, size), jnp.float32)) * same_doc
    written = base_rows - jnp.dot(wy_rows, state_in, precision=precise)
    scores = jnp.dot(queries, key_rows.T, precision=precise) * lower
    carried = carry_mask[:, None] * jnp.dot(queries, state_in, precision=precise)
    return carried + jnp.dot(scores, written, precision=precise)


def group_full(queries, key_rows, value_rows, rates, same_doc, carry_mask, state_in):
    transition, contribution, base_rows, wy_rows = group_parts(
        key_rows, value_rows, rates, same_doc, carry_mask
    )
    outputs = group_output(queries, key_rows, same_doc, carry_mask, base_rows, wy_rows, state_in)
    return (outputs, jnp.dot(transition, state_in, precision=precise) + contribution)


def state_pull(queries, key_rows, same_doc, carry_mask, wy_rows, grad_rows):
    size = key_rows.shape[0]
    lower = jnp.tril(jnp.ones((size, size), jnp.float32)) * same_doc
    scores = jnp.dot(queries, key_rows.T, precision=precise) * lower
    pulled = jnp.dot(scores.T, grad_rows, precision=precise)
    direct = jnp.dot((carry_mask[:, None] * queries).T, grad_rows, precision=precise)
    return direct - jnp.dot(wy_rows.T, pulled, precision=precise)


def group_grads(
    queries, key_rows, value_rows, rates, same_doc, carry_mask, state_in, grad_rows, grad_end
):

    def group_local(query_in, key_in, value_in, rate_in):
        return group_full(query_in, key_in, value_in, rate_in, same_doc, carry_mask, state_in)

    outputs, pullback = jax.vjp(group_local, queries, key_rows, value_rows, rates)
    return pullback((grad_rows, grad_end))


def local_pieces(
    block_input,
    grad_out,
    doc_lengths,
    attn_gain,
    mlp_gain,
    out_gain,
    conv_weight,
    qkv_weight,
    beta_weight,
    o_weight,
    gate_up_weight,
    down_weight,
):
    tok_rows = block_input.shape[1]
    model_width = block_input.shape[2]
    blocks = tok_rows // GROUP
    unit_floor = DK / 16.0
    x_rows = block_input[0].astype(jnp.float32)
    grad_rows_out = grad_out[0]
    qkv_full, beta_full, o_full, gate_up_full, down_full = (
        lax.all_gather(qkv_weight, ("row", "seq"), axis=1, tiled=True),
        lax.all_gather(beta_weight, ("row", "seq"), axis=0, tiled=True),
        lax.all_gather(o_weight, ("row", "seq"), axis=1, tiled=True),
        lax.all_gather(gate_up_weight, ("row", "seq"), axis=1, tiled=True),
        lax.all_gather(down_weight, ("row", "seq"), axis=1, tiled=True),
    )
    local_width = qkv_full.shape[2]
    head_count = local_width // DK
    lead_mask = (lax.axis_index("tp") == 0).astype(jnp.float32)
    ends = jnp.cumsum(doc_lengths[0])
    places = (
        lax.axis_index("seq") * tok_rows + jnp.arange(tok_rows + KW - 1, dtype=jnp.int32) - (KW - 1)
    )
    doc_ids = jnp.sum((places[:, None] >= ends[None, :]).astype(jnp.int32), axis=1)
    doc_ids = jnp.where(places < 0, -1, doc_ids)
    own_docs = doc_ids[KW - 1 :]
    prior_docs = doc_ids[KW - 2 : KW - 2 + tok_rows]
    valid = (own_docs < DOCS).astype(jnp.float32)
    fresh = (own_docs != prior_docs).astype(jnp.int32)
    tap_masks = [
        (doc_ids[KW - 1 - tap : KW - 1 - tap + tok_rows] == own_docs).astype(jnp.float32)
        for tap in range(KW)
    ]
    own_blocks = own_docs.reshape(blocks, GROUP)
    same_doc = (own_blocks[:, :, None] == own_blocks[:, None, :]).astype(jnp.float32)
    carry_mask = (jnp.cumsum(fresh.reshape(blocks, GROUP), axis=1) == 0).astype(jnp.float32)

    def to_blocks(array):
        return array.reshape(blocks, GROUP, head_count, -1).transpose(2, 0, 1, 3)

    def from_blocks(array):
        return array.transpose(1, 2, 0, 3).reshape(tok_rows, head_count, -1)

    scale_one = norm_scale(x_rows)
    normed_one = (x_rows * scale_one * attn_gain).astype(jnp.bfloat16)
    proj_low = jnp.einsum(
        "td,cde->cte", normed_one, qkv_full, preferred_element_type=jnp.float32
    ).astype(jnp.bfloat16)
    logit = jnp.dot(normed_one, beta_full, preferred_element_type=jnp.float32)
    rim_rows = from_behind(proj_low[:, tok_rows - (KW - 1) :, :], "seq", 1)
    extended = jnp.concatenate([rim_rows, proj_low], axis=1).astype(jnp.float32)
    conv_out = jnp.zeros((3, tok_rows, local_width), jnp.float32)
    for tap in range(KW):
        window = extended[:, KW - 1 - tap : KW - 1 - tap + tok_rows]
        conv_out = (
            conv_out + conv_weight[:, tap][:, None, :] * window * tap_masks[tap][None, :, None]
        )
    conv_sig = jax.nn.sigmoid(conv_out)
    activated = conv_out * conv_sig
    query_raw = activated[0].reshape(tok_rows, head_count, DK)
    key_raw = activated[1].reshape(tok_rows, head_count, DK)
    query_sq = jnp.sum(query_raw * query_raw, axis=-1, keepdims=True)
    key_sq = jnp.sum(key_raw * key_raw, axis=-1, keepdims=True)
    query_scale = lax.rsqrt(jnp.maximum(query_sq, unit_floor))
    key_scale = lax.rsqrt(jnp.maximum(key_sq, unit_floor))
    query_live = (query_sq > unit_floor).astype(jnp.float32)
    key_live = (key_sq > unit_floor).astype(jnp.float32)
    query_blocks = to_blocks(query_raw * query_scale)
    key_blocks = to_blocks(key_raw * key_scale)
    value_blocks = to_blocks(activated[2].reshape(tok_rows, head_count, DK))
    rate_sig = jax.nn.sigmoid(logit)
    rate_blocks = (rate_sig * valid[:, None]).reshape(blocks, GROUP, head_count).transpose(2, 0, 1)
    transition, contribution, base_rows, wy_rows = over_heads(group_parts, (0, 0, 0, None, None))(
        key_blocks, value_blocks, rate_blocks, same_doc, carry_mask
    )
    identity_mat = jnp.broadcast_to(jnp.eye(DK, dtype=jnp.float32), (head_count, DK, DK))
    zero_state = jnp.zeros((head_count, DK, DK), jnp.float32)
    transition_steps = jnp.moveaxis(transition, 1, 0)

    def chain(running, pair):
        product, partial_state = running
        step_trans, step_contrib = pair
        advanced = (
            batch_mul(step_trans, product),
            batch_mul(step_trans, partial_state) + step_contrib,
        )
        return (advanced, (product, partial_state))

    (dev_trans, dev_state), (products, partials) = lax.scan(
        chain, (identity_mat, zero_state), (transition_steps, jnp.moveaxis(contribution, 1, 0))
    )
    incoming = prefix((dev_trans, dev_state), "seq", compose, (identity_mat, zero_state), False)[1]
    group_starts = partials + jnp.einsum("nhij,hjk->nhik", products, incoming, precision=precise)
    start_blocks = jnp.moveaxis(group_starts, 0, 1)
    mix_blocks = over_heads(group_output, (0, 0, None, None, 0, 0, 0))(
        query_blocks, key_blocks, same_doc, carry_mask, base_rows, wy_rows, start_blocks
    )
    mixed = from_blocks(mix_blocks) * valid[:, None, None]
    mix_sq = jnp.mean(mixed * mixed, axis=-1, keepdims=True)
    mix_scale = lax.rsqrt(jnp.maximum(mix_sq, mix_floor))
    mix_live = (mix_sq > mix_floor).astype(jnp.float32)
    normed_mix = (mixed * mix_scale * out_gain).astype(jnp.bfloat16).reshape(tok_rows, local_width)
    o_term = jnp.dot(normed_mix, o_full, preferred_element_type=jnp.float32)
    resid = x_rows + tp_total(o_term)
    scale_two = norm_scale(resid)
    normed_local = (resid * scale_two * mlp_gain).astype(jnp.bfloat16)
    gate_up = jnp.einsum(
        "td,cdf->ctf", normed_local, gate_up_full, preferred_element_type=jnp.float32
    )
    gate_sig = jax.nn.sigmoid(gate_up[0])
    gate_act = gate_up[0] * gate_sig
    hidden = (gate_act * gate_up[1]).astype(jnp.bfloat16)
    down_term = jnp.dot(hidden, down_full, preferred_element_type=jnp.float32)
    mlp_out = tp_total(down_term)
    result = (resid + mlp_out).astype(jnp.bfloat16)
    grad_hidden = jnp.einsum(
        "td,fd->tf", grad_rows_out, down_full, preferred_element_type=jnp.float32
    )
    grad_gate = grad_hidden * gate_up[1] * gate_sig * (1.0 + gate_up[0] * (1.0 - gate_sig))
    grad_up = grad_hidden * gate_act
    grad_gate_up = jnp.stack([grad_gate, grad_up]).astype(jnp.bfloat16)
    down_part = jnp.einsum("tf,td->fd", hidden, grad_rows_out, preferred_element_type=jnp.float32)
    gate_up_part = jnp.einsum(
        "td,ctf->cdf", normed_local, grad_gate_up, preferred_element_type=jnp.float32
    )
    two_term = jnp.einsum(
        "ctf,cdf->td", grad_gate_up, gate_up_full, preferred_element_type=jnp.float32
    )
    grad_two = tp_total(two_term)
    mlp_gain_part = jnp.sum(grad_two * resid * scale_two, axis=0)
    grad_resid = grad_rows_out.astype(jnp.float32) + norm_back(resid, scale_two, mlp_gain, grad_two)
    grad_attn_local = grad_resid.astype(jnp.bfloat16)
    o_part = jnp.einsum(
        "te,td->ed", normed_mix, grad_attn_local, preferred_element_type=jnp.float32
    )
    grad_normed = jnp.einsum(
        "td,ed->te", grad_attn_local, o_full, preferred_element_type=jnp.float32
    ).reshape(tok_rows, head_count, DK)
    out_gain_part = jnp.sum(grad_normed * mixed * mix_scale, axis=(0, 1))
    weighted_mix = out_gain * grad_normed
    grad_mixed = (
        mix_scale * weighted_mix
        - mixed * mix_scale**3 * mix_live * jnp.mean(weighted_mix * mixed, axis=-1, keepdims=True)
    ) * valid[:, None, None]
    grad_blocks = to_blocks(grad_mixed)
    pulls = over_heads(state_pull, (0, 0, None, None, 0, 0))(
        query_blocks, key_blocks, same_doc, carry_mask, wy_rows, grad_blocks
    )

    def back_chain(running, pair):
        grad_end, product = running
        step_trans, step_pull = pair
        advanced = (step_pull + batch_mul_t(step_trans, grad_end), batch_mul_t(step_trans, product))
        return (advanced, (grad_end, product))

    (dev_pull, dev_back), (grad_ends, back_products) = lax.scan(
        back_chain,
        (zero_state, identity_mat),
        (transition_steps, jnp.moveaxis(pulls, 1, 0)),
        reverse=True,
    )
    outgoing = prefix((dev_back, dev_pull), "seq", compose, (identity_mat, zero_state), True)[1]
    end_grads = grad_ends + jnp.einsum("nhij,hjk->nhik", back_products, outgoing, precision=precise)
    grad_query, grad_key, grad_value, grad_rate = over_heads(
        group_grads, (0, 0, 0, 0, None, None, 0, 0, 0)
    )(
        query_blocks,
        key_blocks,
        value_blocks,
        rate_blocks,
        same_doc,
        carry_mask,
        start_blocks,
        grad_blocks,
        jnp.moveaxis(end_grads, 0, 1),
    )
    grad_query = from_blocks(grad_query)
    grad_key = from_blocks(grad_key)
    grad_query_raw = query_scale * grad_query - query_raw * query_scale**3 * query_live * jnp.sum(
        query_raw * grad_query, axis=-1, keepdims=True
    )
    grad_key_raw = key_scale * grad_key - key_raw * key_scale**3 * key_live * jnp.sum(
        key_raw * grad_key, axis=-1, keepdims=True
    )
    grad_activated = jnp.stack(
        [
            grad_query_raw.reshape(tok_rows, local_width),
            grad_key_raw.reshape(tok_rows, local_width),
            from_blocks(grad_value).reshape(tok_rows, local_width),
        ]
    )
    grad_conv = grad_activated * conv_sig * (1.0 + conv_out * (1.0 - conv_sig))
    grad_extended = jnp.zeros((3, tok_rows + KW - 1, local_width), jnp.float32)
    tap_grads = []
    for tap in range(KW):
        masked = grad_conv * tap_masks[tap][None, :, None]
        window = extended[:, KW - 1 - tap : KW - 1 - tap + tok_rows]
        tap_grads.append(jnp.sum(masked * window, axis=1))
        grad_extended = grad_extended + jnp.pad(
            conv_weight[:, tap][:, None, :] * masked, ((0, 0), (KW - 1 - tap, tap), (0, 0))
        )
    conv_part = jnp.stack(tap_grads, axis=1)
    rim_back = from_behind(grad_extended[:, : KW - 1], "seq", -1)
    grad_proj = jnp.concatenate(
        [grad_extended[:, KW - 1 : tok_rows], grad_extended[:, tok_rows:] + rim_back], axis=1
    ).astype(jnp.bfloat16)
    rate_grad = grad_rate.transpose(1, 2, 0).reshape(tok_rows, head_count)
    grad_logit = (rate_grad * valid[:, None] * rate_sig * (1.0 - rate_sig)).astype(jnp.bfloat16)
    qkv_part = jnp.einsum("td,cte->cde", normed_one, grad_proj, preferred_element_type=jnp.float32)
    beta_part = jnp.einsum("td,th->dh", normed_one, grad_logit, preferred_element_type=jnp.float32)
    grad_one_part = jnp.einsum(
        "cte,cde->td", grad_proj, qkv_full, preferred_element_type=jnp.float32
    ) + jnp.einsum("th,dh->td", grad_logit, beta_full, preferred_element_type=jnp.float32)
    grad_one = tp_total(grad_one_part)
    attn_gain_part = jnp.sum(grad_one * x_rows * scale_one, axis=0)
    input_local = (grad_resid + norm_back(x_rows, scale_one, attn_gain, grad_one)).astype(
        jnp.bfloat16
    )
    conv_whole = lax.dynamic_update_slice(
        jnp.zeros((3, KW, model_width), jnp.float32),
        conv_part,
        (0, 0, lax.axis_index("tp") * local_width),
    )
    attn_gain_grad, mlp_gain_grad, out_gain_grad, conv_grad = lax.psum(
        (attn_gain_part * lead_mask, mlp_gain_part * lead_mask, out_gain_part, conv_whole),
        ("row", "seq", "tp"),
    )
    qkv_sum, beta_sum, o_sum, gate_up_sum, down_sum = (
        lax.psum_scatter(
            qkv_part.astype(jnp.bfloat16), ("row", "seq"), scatter_dimension=1, tiled=True
        ).astype(jnp.float32),
        lax.psum_scatter(
            beta_part.astype(jnp.bfloat16), ("row", "seq"), scatter_dimension=0, tiled=True
        ).astype(jnp.float32),
        lax.psum_scatter(
            o_part.astype(jnp.bfloat16), ("row", "seq"), scatter_dimension=1, tiled=True
        ).astype(jnp.float32),
        lax.psum_scatter(
            gate_up_part.astype(jnp.bfloat16), ("row", "seq"), scatter_dimension=1, tiled=True
        ).astype(jnp.float32),
        lax.psum_scatter(
            down_part.astype(jnp.bfloat16), ("row", "seq"), scatter_dimension=1, tiled=True
        ).astype(jnp.float32),
    )
    return (
        result[None],
        input_local[None],
        attn_gain_grad,
        mlp_gain_grad,
        out_gain_grad,
        conv_grad,
        qkv_sum,
        beta_sum,
        o_sum,
        gate_up_sum,
        down_sum,
    )


CHUNK = 128
PAD = 8


def mul(left, right, dims):
    return lax.dot_general(
        left, right, ((dims[:1], dims[1:]), ((), ())), preferred_element_type=jnp.float32
    )


def fine(left, right, dims=(1, 0)):
    left_high, right_high = left.astype(jnp.bfloat16), right.astype(jnp.bfloat16)
    left_rest = (left - left_high.astype(jnp.float32)).astype(jnp.bfloat16)
    right_rest = (right - right_high.astype(jnp.float32)).astype(jnp.bfloat16)
    rest = mul(left_high, right_rest, dims) + mul(left_rest, right_high, dims)
    return mul(left_high, right_high, dims) + rest


def plain(left, right, dims=(1, 0)):
    return mul(left.astype(jnp.bfloat16), right.astype(jnp.bfloat16), dims)


def chunk_masks(doc_col, doc_row):
    same = doc_col == doc_row
    down = lax.broadcasted_iota(jnp.int32, (CHUNK, CHUNK), 0)
    along = lax.broadcasted_iota(jnp.int32, (CHUNK, CHUNK), 1)
    lower = jnp.where(same & (down >= along), 1.0, 0.0)
    strict = jnp.where(same & (down > along), 1.0, 0.0)
    return lower, strict, down, along


def lower_inverse(systems, down, along):
    at_one = (down // 2 == along // 2) & (down != along)
    unit = jnp.where(down == along, 1.0, 0.0)
    inverses = [unit - jnp.where(at_one, system, 0.0) for system in systems]
    half = 2
    while half < CHUNK:
        joins = (down // (2 * half) == along // (2 * half)) & (down // half != along // half)
        inner = [
            fine(jnp.where(joins, system, 0.0), inverse)
            for system, inverse in zip(systems, inverses)
        ]
        inverses = [inverse - fine(inverse, part) for inverse, part in zip(inverses, inner)]
        half *= 2
    return inverses


def tap_mask(aux, tap):
    return 1.0 if tap == 0 else aux[:, 3 + tap : 4 + tap]


def convolved(window, taps, aux):
    total = 0.0
    for tap in range(KW):
        total = total + (
            taps[tap : tap + 1] * window[PAD - tap : PAD - tap + CHUNK] * tap_mask(aux, tap)
        )
    return total


def sigmoid(values):
    return 1.0 / (1.0 + jnp.exp(-values))


def unit_scale(values):
    total = jnp.sum(values * values, axis=1, keepdims=True)
    floor = DK / 16.0
    return lax.rsqrt(jnp.maximum(total, floor)), jnp.where(total > floor, 1.0, 0.0)


def mix_norm(mixed):
    mean = jnp.mean(mixed * mixed, axis=1, keepdims=True)
    return lax.rsqrt(jnp.maximum(mean, mix_floor)), jnp.where(mean > mix_floor, 1.0, 0.0)


def forward_kernel(
    heads,
    staged,
    n1_ref,
    qkv_ref,
    beta_ref,
    taps_ref,
    aux_ref,
    docs_ref,
    gain_ref,
    x_ref,
    mlp_gain_ref,
    g_ref,
    o_weight_ref,
    gate_ref,
    up_ref,
    down_ref,
    proj_ref,
    logit_ref,
    mixed_ref,
    normed_ref,
    inverse_ref,
    states_ref,
    written_ref,
    o_ref,
    resid_ref,
    n2_ref,
    g_full_ref,
    gate_out,
    up_out,
    down_out,
    window_ref,
    state_ref,
    o_rows,
    n2_own,
    blocks,
    came,
    across,
    own_sems,
    sum_sems,
    n2_sems,
    g_sems,
    *sems,
):
    width = heads * DK
    line = Line()
    greet(exchange_partners(line) + along_axis("tp"))
    row = lax.axis_index("row")
    rows = n2_ref.shape[2]
    units = down_out.shape[2]

    def rows_of(ref, count):
        return lambda seq: ref.at[pl.ds(pl.multiple_of(seq * count, count), count)]

    o_move = Exchange(line, rows_of(o_weight_ref, width), o_ref, sems[:4])
    gate_move = Exchange(line, lambda seq: gate_ref.at[seq], gate_out, sems[4:8])
    up_move = Exchange(line, lambda seq: up_ref.at[seq], up_out, sems[8:12])
    down_move = Exchange(line, rows_of(down_ref, units), down_out, sems[12:16])
    moves = (o_move, gate_move, up_move, down_move)
    total = Scatter(line, blocks, came, across, sum_sems)
    n2 = Gather(line, n2_ref, n2_own, n2_sems)
    g_own = g_ref.at[pl.ds(pl.multiple_of(line.core * rows, rows), rows)]
    grads = Gather(line, g_full_ref, g_own, g_sems)
    own = []
    for i, move in enumerate(moves):
        target = move.target.at[row, line.place]
        own.append(pltpu.make_async_copy(move.source(line.place), target, own_sems.at[i]))
        own[i].start()
    o_move.start()
    gate_move.start()
    grads.phases(0)
    for i, move in enumerate(moves):
        own[i].wait()
        move.share_own()
    window_ref[0:PAD] = jnp.zeros((PAD, 3 * width), jnp.float32)
    state_ref[...] = jnp.zeros_like(state_ref)

    def prepare(n):
        rows = pl.ds(pl.multiple_of(n * CHUNK, CHUNK), CHUNK)
        n1 = n1_ref[rows]
        proj = jnp.concatenate(
            [mul(n1, qkv_ref[:, :, c].reshape(-1, width), (1, 0)) for c in range(3)], axis=1
        ).astype(jnp.bfloat16)
        proj_ref[rows] = proj
        window_ref[PAD : PAD + CHUNK] = proj.astype(jnp.float32)
        logit = mul(n1, beta_ref[...], (1, 1))
        logit_ref[rows] = logit
        aux = aux_ref[rows]
        conv = convolved(window_ref[...], taps_ref[...], aux)
        act = conv * sigmoid(conv)
        window_ref[0:PAD] = window_ref[CHUNK : CHUNK + PAD]
        valid, carry, tail = aux[:, 1:2], aux[:, 2:3], aux[:, 3:4]
        lower, strict, down, along = chunk_masks(aux[:, 0:1], docs_ref[pl.ds(n, 1)])
        rate_all = sigmoid(logit) * valid
        parts = []
        for h in range(heads):
            query = act[:, h * DK : (h + 1) * DK]
            key = act[:, width + h * DK : width + (h + 1) * DK]
            value = act[:, 2 * width + h * DK : 2 * width + (h + 1) * DK]
            query = query * unit_scale(query)[0]
            key = key * unit_scale(key)[0]
            rate = rate_all[:, h : h + 1]
            scores = plain(query, key, (1, 1)) * lower
            system = rate * fine(key, key, (1, 1)) * strict
            parts.append((query, key, value, rate, scores, system))
        return rows, valid, carry, tail, parts, down, along

    def advance(n, rows, valid, carry, tail, parts, inverses):
        carry_last = carry[CHUNK - 1 :]
        for h, (query, key, value, rate, scores, _) in enumerate(parts):
            inverse = inverses[h]
            state = state_ref[h]
            written = fine(inverse, rate * (value - fine(carry * key, state)))
            mixed = (carry * plain(query, state) + plain(scores, written)) * valid
            states_ref[h, n] = state
            written_ref[h, n] = written
            inverse_ref[h, n] = inverse
            state_ref[h] = carry_last * state + fine(tail * key, written, (0, 0))
            columns = pl.ds(h * DK, DK)
            mixed_ref[rows, columns] = mixed
            normed_ref[rows, columns] = (
                mixed * mix_norm(mixed)[0] * gain_ref[...]
            ).astype(jnp.bfloat16)

    chunks = n1_ref.shape[0] // CHUNK
    together = 4 if chunks % 4 == 0 else 1

    def several(m, _):
        ready = [prepare(together * m + i) for i in range(together)]
        down, along = ready[0][5:]
        inverses = lower_inverse([part[5] for one in ready for part in one[4]], down, along)
        for i, one in enumerate(ready):
            advance(together * m + i, *one[:5], inverses[i * heads : (i + 1) * heads])
        return 0

    def share_came(move):
        for i in range(1, line.count):
            move.share_came(i)

    half = chunks // together // 2
    staged.need(n1_ref, qkv_ref, beta_ref, taps_ref, aux_ref, docs_ref, gain_ref)
    lax.fori_loop(0, half, several, 0)
    share_came(o_move)
    grads.phases(1)
    up_move.start()
    lax.fori_loop(half, chunks // together, several, 0)
    staged.store(
        proj_ref, logit_ref, mixed_ref, normed_ref, inverse_ref, states_ref, written_ref
    )
    share_came(gate_move)
    down_move.start()
    o_move.finish()
    staged.store(o_ref)
    side_by_side(o_ref, o_rows)
    for part in range(total.parts):
        total.product(part_rows(normed_ref, total, part), o_rows, part, order=0)
        total.start_edges(part)
    grads.phases(2)
    total.relay(0, 0)
    total.relay(1, 0)
    share_came(up_move)
    total.relay_back(0)
    grads.phases(3)
    total.relay(0, 1)
    total.relay(1, 1)
    share_came(down_move)
    total.relay_back(1)
    staged.need(x_ref, mlp_gain_ref)

    def normed(span):
        x_span = pl.ds(pl.multiple_of(line.core * rows + span.start, STEP), STEP)
        resid = x_ref[x_span].astype(jnp.float32) + total.own_rows(span)
        resid_ref[span] = resid
        n2_own[span] = (resid * norm_scale(resid) * mlp_gain_ref[...]).astype(jnp.bfloat16)

    for part in range(total.parts):
        total.wait_own(part)
        over_rows(total, part, normed)
        n2.phase(0, part)
    staged.store(resid_ref)
    for k in range(1, line.count):
        n2.phases(k)
    total.finish()
    n2.finish()
    grads.finish()
    for move in moves[1:]:
        move.finish()


def part_rows(ref, total, part):
    seqs, cores, rows, _ = total.blocks.shape
    return jnp.concatenate(
        [ref[pl.ds(i * rows + part * total.rows, total.rows)] for i in range(seqs * cores)], axis=0
    )


def backward_kernel(
    heads,
    staged,
    grad_ref,
    o_ref,
    proj_ref,
    logit_ref,
    mixed_ref,
    inverse_ref,
    states_ref,
    written_ref,
    taps_ref,
    aux_ref,
    docs_ref,
    gain_ref,
    normed_mix_ref,
    n1_ref,
    qkv_ref,
    beta_ref,
    attn_gain_ref,
    mlp_grad_ref,
    x_ref,
    grad_resid_ref,
    sum_ref,
    input_grad_ref,
    small_all_ref,
    qkv_came_ref,
    o_came_ref,
    down_came_ref,
    gate_came_ref,
    up_came_ref,
    window_ref,
    masked_ref,
    state_ref,
    o_rows,
    conv_grad_ref,
    gain_grad_ref,
    grad_proj_ref,
    grad_logit_ref,
    small_ref,
    small_rows,
    qkv_sum,
    o_sum,
    blocks,
    came,
    across,
    qkv_parts,
    qkv_halves,
    qkv_rows_came,
    o_parts,
    o_halves,
    o_rows_came,
    sum_sems,
    swap_sems,
    *sems,
):
    width = heads * DK
    line = Line()
    greet(along_axis("seq") + along_axis("row") + along_axis("tp"))
    moves = moves_of(
        Swap,
        "seq",
        [sum_ref.at[m] for m in range(3)],
        (down_came_ref, gate_came_ref, up_came_ref),
        sems[:7],
    )
    for move in moves:
        move.start()
    (o_move,) = moves_of(Swap, "seq", (o_sum,), (o_came_ref,), sems[7:10])
    (qkv_move,) = moves_of(Swap, "seq", (qkv_sum,), (qkv_came_ref,), sems[10:13])
    (small_row,) = moves_of(Share, "row", (small_ref,), (small_rows,), sems[13:16])
    own_small = small_all_ref.at[line.core, line.place]
    small_seq = [
        remote(own_small, own_small, sems[16].at[i], sems[17].at[i], {"seq": other})
        for i, other in enumerate(around("seq"))
    ]
    core_small = small_all_ref.at[line.core]
    small_core = remote(core_small, core_small, sems[18].at[0], sems[18].at[1], line.across)
    o_sums = RowSum(o_parts, o_halves, o_rows_came, sems[19:23])
    qkv_sums = RowSum(qkv_parts, qkv_halves, qkv_rows_came, sems[23:27])
    total = Scatter(line, blocks, came, across, sum_sems)
    span = o_parts.shape[2]

    def own_columns(index):
        return pl.ds(pl.multiple_of(index * span, span), span)

    staged.need(grad_ref, normed_mix_ref)
    for step, index in enumerate(o_sums.order()):
        part = mul(grad_ref[:, own_columns(index)], normed_mix_ref[...], (0, 0))
        o_parts[index, 0] = part.astype(jnp.bfloat16)
        o_sums.start(step, 0)
    chunks = grad_ref.shape[0] // CHUNK
    staged.need(
        o_ref, proj_ref, logit_ref, mixed_ref, inverse_ref, states_ref, written_ref, taps_ref,
        aux_ref, docs_ref, gain_ref,
    )
    side_by_side(o_ref, o_rows)
    state_ref[...] = jnp.zeros_like(state_ref)
    masked_ref[...] = jnp.zeros_like(masked_ref)
    conv_grad_ref[...] = jnp.zeros_like(conv_grad_ref)
    gain_grad_ref[...] = jnp.zeros_like(gain_grad_ref)

    def chunk(step, _):
        n = chunks - 1 - step
        rows = pl.ds(pl.multiple_of(n * CHUNK, CHUNK), CHUNK)
        before = jnp.maximum(n - 1, 0)
        aux = aux_ref[rows]
        grad_normed = mul(grad_ref[rows], o_rows[...], (1, 1))
        prior = proj_ref[pl.ds(pl.multiple_of(before * CHUNK + CHUNK - 16, 16), 16)]
        window_ref[0:PAD] = prior.astype(jnp.float32)[16 - PAD :]
        window_ref[PAD : PAD + CHUNK] = proj_ref[rows].astype(jnp.float32)
        window = window_ref[...]
        taps = taps_ref[...]
        conv = convolved(window, taps, aux)
        conv_sig = sigmoid(conv)
        act = conv * conv_sig
        valid, carry, tail = aux[:, 1:2], aux[:, 2:3], aux[:, 3:4]
        carry_last = carry[CHUNK - 1 :]
        lower, strict, down, along = chunk_masks(aux[:, 0:1], docs_ref[pl.ds(n, 1)])
        rate_sig = sigmoid(logit_ref[rows])
        rate_all = rate_sig * valid
        lanes = lax.broadcasted_iota(jnp.int32, rate_all.shape, 1)
        grad_rates = jnp.zeros_like(rate_all)
        grads = [[], [], []]
        for h in range(heads):
            columns = pl.ds(h * DK, DK)
            mixed = mixed_ref[rows, columns]
            mix_scale, mix_live = mix_norm(mixed)
            grad_out = grad_normed[:, h * DK : (h + 1) * DK]
            scaled = mixed * mix_scale
            gain_grad_ref[...] += jnp.sum(grad_out * scaled, axis=0, keepdims=True)
            weighted = gain_ref[...] * grad_out
            grad_mix = (
                mix_scale * weighted
                - scaled
                * (mix_scale * mix_scale * mix_live)
                * jnp.mean(weighted * mixed, axis=1, keepdims=True)
            ) * valid
            query_raw = act[:, h * DK : (h + 1) * DK]
            key_raw = act[:, width + h * DK : width + (h + 1) * DK]
            value = act[:, 2 * width + h * DK : 2 * width + (h + 1) * DK]
            query_scale, query_live = unit_scale(query_raw)
            key_scale, key_live = unit_scale(key_raw)
            query = query_raw * query_scale
            key = key_raw * key_scale
            rate = rate_all[:, h : h + 1]
            inverse = inverse_ref[h, n]
            state = states_ref[h, n]
            written = written_ref[h, n]
            grad_state = state_ref[h]
            tail_key = tail * key
            carried_key = carry * key
            scores = plain(query, key, (1, 1)) * lower
            pulled = plain(scores, grad_mix, (0, 0)) + fine(tail_key, grad_state)
            solved = fine(inverse, pulled, (0, 0))
            state_ref[h] = (
                carry_last * grad_state
                + plain(carry * query, grad_mix, (0, 0))
                - fine(rate * carried_key, solved, (0, 0))
            )
            grad_scores = plain(grad_mix, written, (1, 1)) * lower
            grad_query = carry * plain(grad_mix, state, (1, 1)) + plain(grad_scores, key)
            guess_error = value - plain(carried_key, state)
            gram = plain(key, key, (1, 1)) * strict
            grad_system = plain(solved, written, (1, 1)) * strict
            grad_rate = jnp.sum(solved * guess_error, axis=1, keepdims=True) - jnp.sum(
                grad_system * gram, axis=1, keepdims=True
            )
            grad_gram = rate * grad_system
            grad_key = (
                plain(grad_scores, query, (0, 0))
                + tail * plain(written, grad_state, (1, 1))
                - rate * carry * plain(solved, state, (1, 1))
                - plain(grad_gram, key)
                - plain(grad_gram, key, (0, 0))
            )
            grads[0].append(
                query_scale
                * (
                    grad_query
                    - query
                    * query_live
                    * jnp.sum(query * grad_query, axis=1, keepdims=True)
                )
            )
            grads[1].append(
                key_scale
                * (grad_key - key * key_live * jnp.sum(key * grad_key, axis=1, keepdims=True))
            )
            grads[2].append(rate * solved)
            grad_rates = grad_rates + jnp.where(lanes == h, grad_rate, 0.0)
        grad_act = jnp.concatenate(grads[0] + grads[1] + grads[2], axis=1)
        grad_conv = grad_act * conv_sig * (1.0 + conv * (1.0 - conv_sig))
        grad_proj = taps[0:1] * grad_conv
        conv_grad_ref[0:1] += jnp.sum(
            grad_conv * window[PAD : PAD + CHUNK], axis=0, keepdims=True
        )
        for tap in range(1, KW):
            masked = grad_conv * tap_mask(aux, tap)
            conv_grad_ref[tap : tap + 1] += jnp.sum(
                masked * window[PAD - tap : PAD - tap + CHUNK], axis=0, keepdims=True
            )
            masked_ref[tap - 1, CHUNK : CHUNK + PAD] = masked_ref[tap - 1, 0:PAD]
            masked_ref[tap - 1, 0:CHUNK] = masked
            grad_proj = grad_proj + taps[tap : tap + 1] * masked_ref[tap - 1, tap : tap + CHUNK]
        grad_proj_ref[rows] = grad_proj.astype(jnp.bfloat16)
        grad_logit_ref[rows] = (grad_rates * rate_sig * (1.0 - rate_sig) * valid).astype(
            jnp.bfloat16
        )
        return 0

    early, late = chunks // 4, chunks // 2
    lax.fori_loop(0, early, chunk, 0)
    o_sums.add_halves(0)
    lax.fori_loop(early, late, chunk, 0)
    o_sum[...] = o_sums.total(0).astype(jnp.bfloat16).reshape(o_sum.shape)
    o_move.start()
    lax.fori_loop(late, chunks, chunk, 0)
    staged.need(
        n1_ref, qkv_ref, beta_ref, attn_gain_ref, mlp_grad_ref, x_ref, grad_resid_ref
    )

    def product(part):
        left = part_rows(grad_proj_ref, total, part)
        logit = part_rows(grad_logit_ref, total, part)

        def right_tile(left, t, across):
            weights = qkv_ref[t]
            out = mul(logit, beta_ref[:, across], (1, 0))
            for c in range(3):
                out = out + mul(
                    left[:, c * width : (c + 1) * width], weights[:, c].reshape(-1, width), (1, 1)
                )
            return out

        total.product(left, None, part, tile=span, right_tile=right_tile)
        total.start_edges(part)

    def qkv_grads(step):
        index = qkv_sums.order()[step]
        columns = own_columns(index)
        n1 = n1_ref[:, columns]
        part = mul(n1, grad_proj_ref[...], (0, 0))
        qkv_parts[index, 0] = part.astype(jnp.bfloat16)
        qkv_sums.start(step, 0)
        weights = qkv_ref[index]
        terms = 0.0
        for c in range(3):
            weight = weights[:, c].reshape(span, width).astype(jnp.float32)
            terms = terms + weight * part[:, c * width : (c + 1) * width]
        terms = fine(jnp.ones((8, width), jnp.float32), terms, (1, 1))[0:1]
        beta_part = mul(grad_logit_ref[...], n1, (0, 0))
        terms = terms + jnp.sum(
            beta_part * beta_ref[:, columns].astype(jnp.float32), axis=0, keepdims=True
        )
        small_ref[0:1, columns] = terms / attn_gain_ref[:, columns]
        small_ref[2 : 2 + heads, columns] = beta_part[:heads]

    product(0)
    qkv_grads(0)
    product(1)
    qkv_grads(1)
    total.relay(0, 0)
    total.relay(1, 0)
    qkv_grads(2)
    qkv_grads(3)
    small_ref[1:2] = mlp_grad_ref[...]
    at = 2 + heads
    for tap in range(KW):
        lanes = pl.ds((tap % 2) * 3 * width, 3 * width)
        small_ref[at + tap // 2 : at + tap // 2 + 1, lanes] = conv_grad_ref[tap : tap + 1]
    small_ref[at : at + 1, 6 * width : 6 * width + DK] = gain_grad_ref[...]
    small_row.start()
    total.relay_back(0)
    qkv_sums.add_halves(0)
    total.relay(0, 1)
    total.relay(1, 1)
    small_row.finish()
    small = small_rows[0]
    for i in range(1, small_rows.shape[0]):
        small = small + small_rows[i]
    small_all_ref[line.core, line.place] = small
    for copy in small_seq:
        copy.start()
    total.relay_back(1)
    qkv_sum[...] = qkv_sums.total(0).astype(jnp.bfloat16).reshape(qkv_sum.shape)
    qkv_move.start()
    rows = grad_resid_ref.shape[0]

    def back(inner):
        own_span = pl.ds(pl.multiple_of(line.core * rows + inner.start, STEP), STEP)
        x = x_ref[own_span].astype(jnp.float32)
        input_grad_ref[own_span] = (
            grad_resid_ref[inner]
            + norm_back(x, norm_scale(x), attn_gain_ref[...], total.own_rows(inner))
        ).astype(jnp.bfloat16)

    for part in range(total.parts):
        total.wait_own(part)
        over_rows(total, part, back)
    swap = own_swap(line, input_grad_ref, rows, swap_sems)
    swap.start()
    for copy in small_seq:
        copy.wait()
    small_core.start()
    total.finish()
    o_sums.finish()
    qkv_sums.finish()
    for move in moves + [o_move, qkv_move]:
        move.finish()
    swap.wait()
    small_core.wait()


def in_vmem(count):
    return [pl.BlockSpec(memory_space=pltpu.VMEM)] * count


def run_forward(n1, qkv, beta, taps, aux, docs, gain, x, g, mlp_gain, weights):
    row_len, heads = n1.shape[0], qkv.shape[-1] // DK
    rows_axis, seqs, _, shard, _ = qkv.shape
    cores, (piece, model_width) = lax.axis_size("tp"), x.shape
    rows = piece // cores
    chunks, width, f32, b16 = row_len // CHUNK, heads * DK, jnp.float32, jnp.bfloat16
    units = weights[3].shape[0] // seqs
    outs = (
        ((row_len, 3 * width), b16),
        ((row_len, beta.shape[0]), f32),
        ((row_len, width), f32),
        ((row_len, width), b16),
        ((heads, chunks, CHUNK, CHUNK), f32),
        ((heads, chunks, DK, DK), f32),
        ((heads, chunks, CHUNK, DK), f32),
        ((rows_axis, seqs, width, shard), b16),
        ((rows, model_width), f32),
    )
    scratch = [
        pltpu.VMEM((PAD + CHUNK, 3 * width), f32),
        pltpu.VMEM((heads, DK, DK), f32),
        pltpu.VMEM((width, model_width), b16),
        pltpu.VMEM((rows, model_width), b16),
    ]
    scratch = scratch + scatter_scratch(seqs, cores, rows, model_width) + [dma_sems(4)]
    scratch = scratch + [dma_sems(6, seqs, PARTS)] * 3 + exchange_sems() * 4
    *saved, o_full, resid, n2, g_full, gate, up, down = line_call(
        functools.partial(forward_kernel, heads), 5, "mixer_forward", outs, scratch,
        (n1, qkv, beta, taps, aux, docs, gain, x, mlp_gain),
        far_args=(g, *weights),
        far_outs=(
            ((seqs, cores, rows, model_width), b16),
            ((seqs, cores, rows, model_width), b16),
            ((rows_axis,) + weights[1].shape, b16),
            ((rows_axis,) + weights[2].shape, b16),
            ((rows_axis, seqs, units, shard), b16),
        ),
    )
    n2, g_full = n2.reshape(-1, model_width), g_full.reshape(-1, model_width)
    gate, up = gate.reshape(model_width, units), up.reshape(model_width, units)
    return saved, o_full, resid, n2, g_full, gate, up, down


def run_backward(grad, o_full, saved, taps, aux, docs, gain, extra, sums):
    row_len, heads = grad.shape[0], o_full.shape[2] // DK
    model_width = grad.shape[1]
    rows_axis, seqs, _, shard = o_full.shape
    cores = lax.axis_size("tp")
    width, f32, b16 = heads * DK, jnp.float32, jnp.bfloat16
    rows, span = row_len // (seqs * cores), model_width // rows_axis
    small = (4 + heads, model_width)
    outs = (((cores * rows, model_width), b16), ((cores, seqs) + small, f32))
    far_outs = (((seqs, shard, 3 * width), b16), ((seqs, shard, width), b16))
    qkv_buffers, qkv_sems = row_sum_scratch((rows_axis, 1, span, 3 * width))
    o_buffers, o_sems = row_sum_scratch((rows_axis, 1, span, width))
    scratch = [
        pltpu.VMEM((PAD + CHUNK, 3 * width), f32),
        pltpu.VMEM((KW - 1, CHUNK + PAD, 3 * width), f32),
        pltpu.VMEM((heads, DK, DK), f32),
        pltpu.VMEM((width, model_width), b16),
        pltpu.VMEM((KW, 3 * width), f32),
        pltpu.VMEM((1, DK), f32),
        pltpu.VMEM((row_len, 3 * width), b16),
        pltpu.VMEM(saved[1].shape, b16),
        pltpu.VMEM(small, f32),
        pltpu.VMEM((rows_axis,) + small, f32),
        pltpu.VMEM((seqs, shard, 3 * width), b16),
        pltpu.VMEM((seqs, shard, width), b16),
    ]
    scratch = scratch + scatter_scratch(seqs, cores, rows, model_width) + qkv_buffers + o_buffers
    scratch = scratch + [dma_sems(6, seqs, PARTS), dma_sems(2)]
    scratch = scratch + pair_sems("seq", 3) + pair_sems("seq", 1) * 2 + pair_sems("row", 1)
    scratch = scratch + [dma_sems(seqs - 1)] * 2 + [dma_sems(2)] + o_sems + qkv_sems
    return line_call(
        functools.partial(backward_kernel, heads), 6, "mixer_backward", outs, scratch,
        (grad, o_full, *saved, taps, aux, docs, gain, *extra),
        far_args=(sums,),
        far_outs=far_outs + ((sums.shape[1:], b16),) * 3,
    )


def row_aux(docs):
    f32 = jnp.float32
    chunks = docs.reshape(-1, CHUNK)
    prior = jnp.concatenate([jnp.full((1,), -1, jnp.int32), chunks[:-1, -1]])
    padded = jnp.concatenate([jnp.full((KW - 1,), -1, jnp.int32), docs])
    columns = [
        docs,
        docs < DOCS,
        (chunks == prior[:, None]).reshape(-1),
        (chunks == chunks[:, -1:]).reshape(-1),
    ] + [padded[KW - 1 - tap : KW - 1 - tap + docs.shape[0]] == docs for tap in range(1, KW)]
    columns = [column.astype(f32) for column in columns]
    columns += [jnp.zeros_like(columns[0])] * (8 - len(columns))
    return jnp.stack(columns, axis=1), chunks.astype(f32)


def remote(source, target, send, recv, where):
    return pltpu.make_async_remote_copy(
        src_ref=source,
        dst_ref=target,
        send_sem=send,
        recv_sem=recv,
        device_id=where,
        device_id_type=pl.DeviceIdType.MESH,
    )


def greet(partners):
    barrier = pltpu.get_barrier_semaphore()
    for partner, there in partners:

        @pl.when(there)
        def _(partner=partner):
            pl.semaphore_signal(
                barrier, inc=1, device_id=partner, device_id_type=pl.DeviceIdType.MESH
            )

    pl.semaphore_wait(barrier, sum(there.astype(jnp.int32) for _, there in partners))


def around(axis):
    count, place = lax.axis_size(axis), lax.axis_index(axis)
    return [lax.rem(place + by, count) for by in range(1, count)]


def line_partners():
    count, place, core = lax.axis_size("seq"), lax.axis_index("seq"), lax.axis_index("tp")
    return [
        ({"seq": jnp.minimum(place + 1, count - 1)}, place < count - 1),
        ({"seq": jnp.maximum(place - 1, 0)}, place > 0),
        ({"tp": 1 - core}, core >= 0),
    ]


class Line:
    def __init__(self):
        self.count, self.place = lax.axis_size("seq"), lax.axis_index("seq")
        self.core = lax.axis_index("tp")
        self.other = 1 - self.core
        self.right = {"seq": jnp.minimum(self.place + 1, self.count - 1)}
        self.left = {"seq": jnp.maximum(self.place - 1, 0)}
        self.across = {"tp": self.other}


class Gather:
    def __init__(self, line, slots, own, sems):
        self.line, self.slots, self.own, self.sems = line, slots, own, sems
        self.parts = sems.shape[2]
        self.rows = slots.shape[2] // self.parts

    def span(self, part):
        return pl.ds(part * self.rows, self.rows)

    def copy(self, kind, seq, part, own=False):
        line = self.line
        send = {"right": 0, "left": 1, "across": 2}[kind]
        recv = 4 if kind == "across" else 3
        slot = self.slots.at[seq, line.core, self.span(part)]
        where = {"right": line.right, "left": line.left, "across": line.across}[kind]
        source = self.own.at[self.span(part)] if own else slot
        return remote(
            source, slot, self.sems.at[send, seq, part], self.sems.at[recv, seq, part], where
        )

    def own_copy(self, part):
        line = self.line
        return pltpu.make_async_copy(
            self.own.at[self.span(part)],
            self.slots.at[line.place, line.core, self.span(part)],
            self.sems.at[5, 0, part],
        )

    def forward(self, seq, part, right, left, own=False):
        line = self.line
        if right:

            @pl.when(line.place < line.count - 1)
            def _():
                self.copy("right", seq, part, own).start()

        if left:

            @pl.when(line.place > 0)
            def _():
                self.copy("left", seq, part, own).start()

        self.copy("across", seq, part, own).start()

    def phase(self, by, part):
        line = self.line
        if by == 0:
            self.forward(line.place, part, True, True, own=True)
            self.own_copy(part).start()
            return

        @pl.when(line.place - by >= 0)
        def _():
            self.copy("right", line.place - by, part).wait_recv()
            self.forward(line.place - by, part, True, False)

        @pl.when(line.place + by < line.count)
        def _():
            self.copy("left", line.place + by, part).wait_recv()
            self.forward(line.place + by, part, False, True)

    def phases(self, by):
        for part in range(self.parts):
            self.phase(by, part)

    def finish(self):
        line = self.line
        for part in range(self.parts):
            self.own_copy(part).wait()
        for seq in range(line.count):
            for part in range(self.parts):

                @pl.when((line.place >= seq) & (line.place < line.count - 1))
                def _():
                    self.copy("right", seq, part).wait_send()

                @pl.when((line.place <= seq) & (line.place > 0))
                def _():
                    self.copy("left", seq, part).wait_send()

                self.copy("across", seq, part).wait()


class Scatter:
    def __init__(self, line, blocks, came, across, sems):
        self.line, self.blocks, self.came, self.across, self.sems = line, blocks, came, across, sems
        self.parts = sems.shape[2]
        self.rows = blocks.shape[2] // self.parts

    def span(self, part):
        return pl.ds(part * self.rows, self.rows)

    def over(self, seq, part):
        line, span = self.line, self.span(part)
        return remote(
            self.blocks.at[seq, line.other, span],
            self.across.at[seq, span],
            self.sems.at[0, seq, part],
            self.sems.at[1, seq, part],
            line.across,
        )

    def along(self, kind, seq, part):
        line, span = self.line, self.span(part)
        way = {"right": 0, "left": 1}[kind]
        slot = seq if way == 0 else jnp.where(seq == line.place - 1, line.count, seq)
        return remote(
            self.blocks.at[seq, line.core, span],
            self.came.at[slot, span],
            self.sems.at[2, seq, part],
            self.sems.at[3 + way, seq, part],
            line.right if way == 0 else line.left,
        )

    def nears(self, k):
        for part in range(self.parts):
            self.near(k, part)

    def fars(self, k):
        for part in range(self.parts):
            self.far(k, part)

    def product(self, left_ref, right_ref, part, order=1, tile=512, right_tile=None):
        seqs, cores, _, width = self.blocks.shape
        span = self.span(part)
        left = left_ref
        if len(left_ref.shape) == 3:
            left = left_ref[:, span].reshape(seqs * cores * self.rows, -1)

        def columns(t, _):
            across = pl.ds(pl.multiple_of(t * tile, tile), tile)
            if right_tile is not None:
                total = right_tile(left, t, across)
            elif order == 1:
                total = mul(left, right_ref[across], (1, 1))
            else:
                total = mul(left, right_ref[:, across], (1, 0))
            self.blocks[:, :, span, across] = total.astype(jnp.bfloat16).reshape(
                seqs, cores, self.rows, tile
            )
            return 0

        lax.fori_loop(0, width // tile, columns, 0)
        self.offer(part)

    def offer(self, part):
        for k in range(self.blocks.shape[0]):
            self.over(self.target(k), part).start()

    def pass_on(self, kind, seq, part):
        line, span = self.line, self.span(part)
        f32 = jnp.float32
        first = line.place == (0 if kind == "right" else line.count - 1)
        way = {"right": 0, "left": 1}[kind]
        self.over(seq, part).wait_recv()
        total = self.blocks[seq, line.core, span].astype(f32)
        total = total + self.across[seq, span].astype(f32)

        @pl.when(first)
        def _():
            self.blocks[seq, line.core, span] = total.astype(jnp.bfloat16)

        @pl.when(jnp.logical_not(first))
        def _():
            self.along(kind, seq, part).wait_recv()
            self.blocks[seq, line.core, span] = (
                total + self.came[seq, span].astype(f32)
            ).astype(jnp.bfloat16)

        self.along(kind, seq, part).start()

    def target(self, k):
        line = self.line
        return jnp.where(line.place < line.count // 2, line.count - 1 - k, k)

    def edge(self):
        return (self.line.place == 0) | (self.line.place == self.line.count - 1)

    def near(self, k, part):
        line = self.line
        low = line.place < line.count // 2

        @pl.when(low & (line.count - 1 - k > line.place))
        def _():
            self.pass_on("right", line.count - 1 - k, part)

        @pl.when(jnp.logical_not(low) & (k < line.place))
        def _():
            self.pass_on("left", k, part)

    def far(self, k, part):
        line = self.line
        low = line.place < line.count // 2

        @pl.when(low & (k < line.place))
        def _():
            self.pass_on("left", k, part)

        @pl.when(jnp.logical_not(low) & (line.count - 1 - k > line.place))
        def _():
            self.pass_on("right", line.count - 1 - k, part)

    def start_edges(self, part):
        @pl.when(self.edge())
        def _():
            for k in range(self.line.count - 1):
                self.near(k, part)

    def relay(self, k, part):
        @pl.when(jnp.logical_not(self.edge()))
        def _():
            self.near(k, part)

    def relay_back(self, part):
        @pl.when(jnp.logical_not(self.edge()))
        def _():
            for k in range(self.line.count - 1):
                self.far(k, part)

    def wait_own(self, part):
        line = self.line

        @pl.when(line.place > 0)
        def _():
            self.along("right", line.place, part).wait_recv()

        @pl.when(line.place < line.count - 1)
        def _():
            self.along("left", line.place, part).wait_recv()

        self.over(line.place, part).wait_recv()

    def own_rows(self, rows):
        line = self.line
        f32 = jnp.float32
        total = self.blocks[line.place, line.core, rows].astype(f32)
        total = total + self.across[line.place, rows].astype(f32)
        from_left = self.came[line.place, rows].astype(f32)
        from_right = self.came[line.count, rows].astype(f32)
        total = total + jnp.where(line.place > 0, from_left, 0.0)
        return total + jnp.where(line.place < line.count - 1, from_right, 0.0)

    def finish(self):
        line = self.line
        for seq in range(line.count):
            for part in range(self.parts):
                self.over(seq, part).wait_send()

                @pl.when(line.place != seq)
                def _():
                    self.along("right", seq, part).wait_send()


class Exchange:
    def __init__(self, line, source, target, sems):
        self.line, self.source, self.target = line, source, target
        self.send, self.recv, self.send_row, self.recv_row = sems
        self.row = lax.axis_index("row")
        self.seq_others, self.row_others = around("seq"), around("row")

    def spread(self, i):
        other = self.seq_others[i]
        return remote(
            self.source(other),
            self.target.at[self.row, self.line.place],
            self.send.at[i],
            self.recv.at[i],
            {"seq": other},
        )

    def share(self, i, j):
        line = self.line
        came_from = lax.rem(line.place + line.count - i, line.count)
        slot = self.target.at[self.row, came_from]
        return remote(
            slot, slot, self.send_row.at[i, j], self.recv_row.at[i, j], {"row": self.row_others[j]}
        )

    def start(self):
        for i in range(len(self.seq_others)):
            self.spread(i).start()

    def share_own(self):
        for j in range(len(self.row_others)):
            self.share(0, j).start()

    def share_came(self, i):
        self.spread(i - 1).wait_recv()
        for j in range(len(self.row_others)):
            self.share(i, j).start()

    def finish(self):
        for i in range(len(self.seq_others)):
            self.spread(i).wait_send()
        for i in range(len(self.seq_others) + 1):
            for j in range(len(self.row_others)):
                self.share(i, j).wait()


class Share:
    def __init__(self, axis, source, target, sems, own_sem):
        self.axis, self.source, self.target = axis, source, target
        self.send, self.recv = sems
        self.others = around(axis)
        self.own = pltpu.make_async_copy(source, target.at[lax.axis_index(axis)], own_sem)

    def copy(self, i):
        return remote(
            self.source,
            self.target.at[lax.axis_index(self.axis)],
            self.send.at[i],
            self.recv.at[i],
            {self.axis: self.others[i]},
        )

    def start(self):
        for i in range(len(self.others)):
            self.copy(i).start()
        self.own.start()

    def finish(self):
        for i in range(len(self.others)):
            self.copy(i).wait()
        self.own.wait()


class Swap:
    def __init__(self, axis, source, target, sems, own_sem):
        self.axis, self.source, self.target = axis, source, target
        self.send, self.recv = sems
        self.others = around(axis)
        place = lax.axis_index(axis)
        self.own = pltpu.make_async_copy(source.at[place], target.at[place], own_sem)

    def copy(self, i):
        return remote(
            self.source.at[self.others[i]],
            self.target.at[lax.axis_index(self.axis)],
            self.send.at[i],
            self.recv.at[i],
            {self.axis: self.others[i]},
        )

    def start(self):
        for i in range(len(self.others)):
            self.copy(i).start()
        self.own.start()

    def finish(self):
        for i in range(len(self.others)):
            self.copy(i).wait()
        self.own.wait()


class RowSum:
    def __init__(self, blocks, halves, came, sems):
        self.blocks, self.halves, self.came = blocks, halves, came
        self.row = lax.axis_index("row")
        even_x, even_y = lax.rem(self.row, 2) == 0, self.row < 2
        x_step, y_step = jnp.where(even_x, 1, -1), jnp.where(even_y, 2, -2)
        self.near = (self.row + x_step, self.row + y_step)
        self.far = self.row + x_step + y_step
        self.half = blocks.shape[2] // 2
        self.send_half, self.recv_half, self.send, self.recv = sems

    def rows(self, i):
        return pl.ds(i * self.half, self.half)

    def half_copy(self, i, m):
        return remote(
            self.blocks.at[self.far, m, self.rows(i)],
            self.halves.at[i, m],
            self.send_half.at[i, m],
            self.recv_half.at[i, m],
            {"row": self.near[i]},
        )

    def copy(self, i, j, m):
        return remote(
            self.blocks.at[self.near[i], m, self.rows(j)],
            self.came.at[i, m, self.rows(j)],
            self.send.at[i, j, m],
            self.recv.at[i, j, m],
            {"row": self.near[i]},
        )

    def start_far(self, m):
        for i in range(2):
            self.half_copy(i, m).start()

    def start_near(self, i, m):
        self.copy(i, i, m).start()

    def add_half(self, i, m):
        j = 1 - i
        self.half_copy(j, m).wait_recv()
        rows = self.rows(j)
        total = self.blocks[self.near[i], m, rows].astype(jnp.float32)
        total = total + self.halves[j, m].astype(jnp.float32)
        self.blocks[self.near[i], m, rows] = total.astype(jnp.bfloat16)
        self.copy(i, j, m).start()

    def start(self, step, m):
        if step == 0:
            self.start_far(m)
        elif step < 3:
            self.start_near(step - 1, m)

    def order(self):
        return (self.far, self.near[0], self.near[1], self.row)

    def add_halves(self, m):
        for i in range(2):
            self.add_half(i, m)

    def total(self, m):
        for i in range(2):
            for j in range(2):
                self.copy(i, j, m).wait_recv()
        total = self.blocks[self.row, m].astype(jnp.float32)
        for i in range(2):
            total = total + self.came[i, m].astype(jnp.float32)
        return total

    def finish(self):
        for m in range(self.blocks.shape[1]):
            for i in range(2):
                self.half_copy(i, m).wait_send()
                for j in range(2):
                    self.copy(i, j, m).wait_send()


def row_sum_scratch(shape):
    b16 = jnp.bfloat16
    _, count, rows, width = shape
    return [
        pltpu.VMEM(shape, b16),
        pltpu.VMEM((2, count, rows // 2, width), b16),
        pltpu.VMEM((2, count, rows, width), b16),
    ], [dma_sems(2, count), dma_sems(2, count), dma_sems(2, 2, count), dma_sems(2, 2, count)]


def pair_sems(axis, count):
    return [dma_sems(lax.axis_size(axis) - 1)] * (2 * count) + [dma_sems(count)]


def moves_of(kind, axis, sources, targets, sems):
    return [
        kind(axis, source, target, sems[2 * i : 2 * i + 2], sems[-1].at[i])
        for i, (source, target) in enumerate(zip(sources, targets))
    ]


def along_axis(axis):
    return [({axis: other}, other >= 0) for other in around(axis)]


def exchange_sems():
    seqs, rows = lax.axis_size("seq"), lax.axis_size("row")
    return [
        dma_sems(seqs - 1),
        dma_sems(seqs - 1),
        dma_sems(seqs, rows - 1),
        dma_sems(seqs, rows - 1),
    ]


def exchange_partners(line):
    return [({"seq": other}, other >= 0) for other in around("seq")] + [
        ({"row": other}, other >= 0) for other in around("row")
    ]


STEP = 32


def over_rows(total, part, body):
    def step(i, _):
        body(pl.ds(pl.multiple_of(part * total.rows + i * STEP, STEP), STEP))
        return 0

    lax.fori_loop(0, total.rows // STEP, step, 0)


def side_by_side(blocks_ref, out_ref):
    outer, inner, _, width = blocks_ref.shape
    for i in range(outer):
        for j in range(inner):
            out_ref[:, (i * inner + j) * width : (i * inner + j + 1) * width] = blocks_ref[i, j]


def dma_sems(*shape):
    return pltpu.SemaphoreType.DMA(shape)


class Staged:
    def __init__(self, inputs, outputs, in_sems, out_sems):
        self.loads = [
            (near, pltpu.make_async_copy(far, near, in_sems.at[i]))
            for i, (far, near) in enumerate(inputs)
        ]
        self.stores = [
            (near, pltpu.make_async_copy(near, far, out_sems.at[i]))
            for i, (far, near) in enumerate(outputs)
        ]
        self.stored = []
        for _, copy in self.loads:
            copy.start()

    def need(self, *refs):
        for ref in refs:
            (at,) = [i for i, (near, _) in enumerate(self.loads) if near is ref]
            self.loads.pop(at)[1].wait()

    def store(self, *refs):
        for ref in refs:
            (at,) = [i for i, (near, _) in enumerate(self.stores) if near is ref]
            copy = self.stores.pop(at)[1]
            copy.start()
            self.stored.append(copy)

    def finish(self):
        self.need(*[near for near, _ in self.loads])
        self.store(*[near for near, _ in self.stores])
        for copy in self.stored:
            copy.wait()


def line_call(kernel, collective_id, name, outs, scratch, args, limit=60, far_args=(), far_outs=()):
    counts = [len(args), len(far_args), len(outs), len(far_outs), len(args), len(outs)]

    def body(*refs):
        groups, at = [], 0
        for count in counts:
            groups.append(refs[at : at + count])
            at += count
        near_in, near_out, in_sems, out_sems, *rest = *groups[4:], *refs[at:]
        staged = Staged(
            list(zip(groups[0], near_in)), list(zip(groups[2], near_out)), in_sems, out_sems
        )
        kernel(staged, *near_in, *groups[1], *near_out, *groups[3], *rest)
        staged.finish()

    far = pl.BlockSpec(memory_space=pl.ANY)
    stages = [pltpu.VMEM(arg.shape, arg.dtype) for arg in args]
    stages += [pltpu.VMEM(*out) for out in outs]
    stages += [dma_sems(max(len(args), 1)), dma_sems(max(len(outs), 1))]
    return pl.pallas_call(
        body,
        out_shape=[jax.ShapeDtypeStruct(*out) for out in (*outs, *far_outs)],
        in_specs=[far] * (len(args) + len(far_args)),
        out_specs=[far] * (len(outs) + len(far_outs)),
        scratch_shapes=stages + scratch,
        compiler_params=pltpu.CompilerParams(
            collective_id=collective_id,
            has_side_effects=collective_id is not None,
            vmem_limit_bytes=limit * 1024 * 1024,
        ),
        name=name,
    )(*args, *far_args)


def scatter_scratch(seqs, cores, rows, width):
    b16 = jnp.bfloat16
    return [
        pltpu.VMEM((seqs, cores, rows, width), b16),
        pltpu.VMEM((seqs + 1, rows, width), b16),
        pltpu.VMEM((seqs, rows, width), b16),
    ]


PARTS = 2


def grad_resid_kernel(
    staged, grad_gate_ref, grad_up_ref, hidden_ref, down_ref, resid_ref, g_ref, gain_ref,
    gate_ref, up_ref, n2_ref, g_full_ref,
    grad_resid_ref, gain_grad_ref, result_ref,
    grad_attn_ref, sum_ref,
    attn_own, blocks, came, across, out_blocks, out_came, out_across, weights, tokens, parts, halves, parts_came,
    sum_sems, out_sems, attn_sems, swap_sems, weight_sems, token_sems, own_sems, *sems,
):
    line = Line()
    greet(line_partners() + along_axis("row"))
    rows = resid_ref.shape[0]
    total = Scatter(line, blocks, came, across, sum_sems)
    result = Scatter(line, out_blocks, out_came, out_across, out_sems)
    attn = Gather(line, grad_attn_ref, attn_own, attn_sems)
    sums = RowSum(parts, halves, parts_came, sems)
    units = hidden_ref.shape[2]
    tile = weights.shape[2]
    tiles = blocks.shape[3] // tile
    steps = total.parts * tiles

    def weight_copies(step):
        slot = step % 2
        span = pl.ds((step % tiles) * tile, tile)
        return [
            pltpu.make_async_copy(ref.at[span], weights.at[slot, i], weight_sems.at[slot, i])
            for i, ref in enumerate((gate_ref, up_ref))
        ]

    orders = sums.order()
    block_width = tokens.shape[3]

    def token_copies(step):
        slot = step % 2
        columns = pl.ds(pl.multiple_of(orders[step] * block_width, block_width), block_width)
        return [
            pltpu.make_async_copy(ref.at[:, columns], tokens.at[slot, i], token_sems.at[slot, i])
            for i, ref in enumerate((g_full_ref, n2_ref))
        ]

    for copy in weight_copies(0) + token_copies(0):
        copy.start()

    def product(part):
        span = total.span(part)
        left_gate = grad_gate_ref[:, span].reshape(-1, units)
        left_up = grad_up_ref[:, span].reshape(-1, units)
        for t in range(tiles):
            step = part * tiles + t
            if step + 1 < steps:
                for copy in weight_copies(step + 1):
                    copy.start()
            for copy in weight_copies(step):
                copy.wait()
            slot = step % 2
            out = mul(left_gate, weights[slot, 0], (1, 1)) + mul(left_up, weights[slot, 1], (1, 1))
            out = out.astype(jnp.bfloat16).reshape(blocks.shape[:2] + (total.rows, tile))
            blocks[:, :, span, t * tile : (t + 1) * tile] = out
        total.offer(part)
        total.start_edges(part)

    def weight_grads(step):
        if step + 1 < len(orders):
            for copy in token_copies(step + 1):
                copy.start()
        for copy in token_copies(step):
            copy.wait()
        slot, to = step % 2, orders[step]
        for m, (i, ref) in enumerate(((0, hidden_ref), (1, grad_gate_ref), (1, grad_up_ref))):
            part = mul(tokens[slot, i], ref[...].reshape(-1, units), (0, 0))
            parts[to, m] = part.astype(jnp.bfloat16)
            sums.start(step, m)

    staged.need(grad_gate_ref, grad_up_ref)
    for part in range(total.parts):
        product(part)
    staged.need(hidden_ref)
    weight_grads(0)
    total.relay(0, 0)
    total.relay(1, 0)
    weight_grads(1)
    total.relay_back(0)
    weight_grads(2)
    total.relay(0, 1)
    total.relay(1, 1)
    weight_grads(3)
    total.relay_back(1)
    staged.need(resid_ref, g_ref, gain_ref, down_ref)
    gain_grad_ref[...] = jnp.zeros_like(gain_grad_ref)

    def back(span):
        own_span = pl.ds(pl.multiple_of(line.core * rows + span.start, STEP), STEP)
        resid = resid_ref[span]
        grad_two = total.own_rows(span)
        scale = norm_scale(resid)
        gain_grad_ref[...] += jnp.sum(grad_two * resid * scale, axis=0, keepdims=True)
        grad = g_ref[own_span].astype(jnp.float32) + norm_back(
            resid, scale, gain_ref[...], grad_two
        )
        grad_resid_ref[span] = grad
        attn_own[span] = grad.astype(jnp.bfloat16)

    for part in range(total.parts):
        total.wait_own(part)
        over_rows(total, part, back)
        attn.phase(0, part)
    staged.store(grad_resid_ref, gain_grad_ref)
    for part in range(result.parts):
        result.product(hidden_ref, down_ref, part, order=0)
    for m in range(parts.shape[1]):
        sums.add_halves(m)
    for k in range(1, line.count):
        attn.phases(k)
        result.nears(k - 1)
    for k in range(line.count - 1):
        result.fars(k)

    def finish(span):
        own_span = pl.ds(pl.multiple_of(line.core * rows + span.start, STEP), STEP)
        result_ref[own_span] = (resid_ref[span] + result.own_rows(span)).astype(jnp.bfloat16)

    for part in range(result.parts):
        result.wait_own(part)
        over_rows(result, part, finish)
    swap = own_swap(line, result_ref, rows, swap_sems)
    swap.start()
    own = []
    for m in range(parts.shape[1]):
        parts[sums.row, m] = sums.total(m).astype(jnp.bfloat16)
        own.append(
            pltpu.make_async_copy(parts.at[sums.row, m], sum_ref.at[m], own_sems.at[m])
        )
        own[m].start()
    total.finish()
    result.finish()
    attn.finish()
    swap.wait()
    sums.finish()
    for copy in own:
        copy.wait()


def own_swap(line, ref, rows, sems):
    own = ref.at[pl.ds(pl.multiple_of(line.core * rows, rows), rows)]
    return remote(own, own, sems.at[0], sems.at[1], line.across)


def run_grad_resid(grad_gate, grad_up, gate, up, hidden, down, resid, g, gain, n2, g_full):
    seqs, cores, (piece, width) = lax.axis_size("seq"), lax.axis_size("tp"), g.shape
    rows_axis = lax.axis_size("row")
    rows, b16, f32 = piece // cores, jnp.bfloat16, jnp.float32
    units, span = gate.shape[1], width // rows_axis
    outs = (
        ((rows, width), f32),
        ((1, width), f32),
        ((piece, width), b16),
    )
    sum_buffers, sum_sems = row_sum_scratch((rows_axis, 3, span, units))
    scratch = [pltpu.VMEM((rows, width), b16)] + scatter_scratch(seqs, cores, rows, width) * 2
    scratch = scratch + [
        pltpu.VMEM((2, 2, span, units), b16),
        pltpu.VMEM((2, 2, n2.shape[0], span), b16),
    ]
    scratch = scratch + sum_buffers + [dma_sems(6, seqs, PARTS)] * 3
    scratch = scratch + [dma_sems(2), dma_sems(2, 2), dma_sems(2, 2), dma_sems(3)] + sum_sems
    grad_gate, grad_up, hidden = (
        array.reshape(seqs * cores, rows, -1) for array in (grad_gate, grad_up, hidden)
    )
    grad_resid, gain_grad, result, grad_attn, sums = line_call(
        grad_resid_kernel, 2, "grad_resid", outs, scratch,
        (grad_gate, grad_up, hidden, down, resid, g, gain),
        far_args=(gate, up, n2, g_full),
        far_outs=(((seqs, cores, rows, width), b16), ((3, span, units), b16)),
    )
    return grad_resid, grad_attn.reshape(-1, width), gain_grad, result, sums


def normed_kernel(
    staged, x_ref, gain_ref, weight_ref, beta_ref, n1_ref, qkv_ref, beta_full_ref, n1_own, n1_sems,
    own_sems, *sems,
):
    line = Line()
    row = lax.axis_index("row")
    greet(exchange_partners(line) + [(line.across, line.core >= 0)])
    width = qkv_ref.shape[-1]

    def columns(seq):
        return weight_ref.at[:, :, pl.ds(pl.multiple_of(seq * width, width), width)]

    moves = [
        Exchange(line, columns, qkv_ref, sems[:4]),
        Exchange(line, lambda seq: beta_ref.at[seq], beta_full_ref, sems[4:]),
    ]
    for move in moves:
        move.start()
    own = [
        pltpu.make_async_copy(
            move.source(line.place), move.target.at[row, line.place], own_sems.at[i]
        )
        for i, move in enumerate(moves)
    ]
    for copy in own:
        copy.start()
    rows = n1_ref.shape[2]
    n1 = Gather(line, n1_ref, n1_own, n1_sems)
    staged.need(x_ref, gain_ref)

    def normed(span):
        x_span = pl.ds(pl.multiple_of(line.core * rows + span.start, STEP), STEP)
        x = x_ref[x_span].astype(jnp.float32)
        n1_own[span] = (x * norm_scale(x) * gain_ref[...]).astype(jnp.bfloat16)

    for part in range(n1.parts):
        over_rows(n1, part, normed)
        n1.phase(0, part)
    for copy in own:
        copy.wait()
    for move in moves:
        move.share_own()
    for k in range(1, line.count):
        for move in moves:
            move.share_came(k)
        n1.phases(k)
    for move in moves:
        move.finish()
    n1.finish()


def run_normed(x, gain, weight, beta):
    rows_axis, seqs, cores = (lax.axis_size(axis) for axis in ("row", "seq", "tp"))
    piece, width = x.shape
    b16 = jnp.bfloat16
    outs = (
        ((seqs, cores, piece // cores, width), b16),
        ((rows_axis, seqs) + weight.shape[:2] + (weight.shape[2] // seqs,), b16),
        ((rows_axis,) + beta.shape, b16),
    )
    n1, qkv, beta_full = line_call(
        normed_kernel, 4, "norm_gather", (),
        [pltpu.VMEM((piece // cores, width), b16), dma_sems(6, seqs, PARTS), dma_sems(2)]
        + exchange_sems() * 2,
        (x, gain),
        far_args=(weight, beta),
        far_outs=outs,
    )
    return n1.reshape(-1, width), qkv, beta_full


def mlp_kernel(
    n2_ref, g_ref, gate_ref, up_ref, down_ref, hidden_ref, grad_gate_ref, grad_up_ref, down_rows
):
    @pl.when(pl.program_id(0) == 0)
    def _():
        side_by_side(down_ref, down_rows)

    n2 = n2_ref[...]
    gate = mul(n2, gate_ref[...], (1, 0))
    up = mul(n2, up_ref[...], (1, 0))
    grad_hidden = mul(g_ref[...], down_rows[...], (1, 1))
    sig = sigmoid(gate)
    act = gate * sig
    hidden_ref[...] = (act * up).astype(jnp.bfloat16)
    grad_up_ref[...] = (grad_hidden * act).astype(jnp.bfloat16)
    grad_gate_ref[...] = (grad_hidden * up * sig * (1.0 + gate * (1.0 - sig))).astype(jnp.bfloat16)


def run_mlp(n2, g, gate, up, down, block=256):
    row_len, width = n2.shape
    units = gate.shape[1]
    tokens = pl.BlockSpec((block, width), lambda i: (i, 0))
    out = pl.BlockSpec((block, units), lambda i: (i, 0))
    whole = pl.BlockSpec(memory_space=pltpu.VMEM)
    shape = jax.ShapeDtypeStruct((row_len, units), jnp.bfloat16)
    return pl.pallas_call(
        mlp_kernel,
        grid=(row_len // block,),
        out_shape=[shape] * 3 + [jax.ShapeDtypeStruct((units, width), jnp.bfloat16)],
        in_specs=[tokens, tokens, whole, whole, whole],
        out_specs=[out] * 3 + [whole],
        compiler_params=pltpu.CompilerParams(vmem_limit_bytes=48 * 1024 * 1024),
        name="mlp",
    )(n2, g, gate, up, down)


def finish_kernel(
    staged, small_ref, qkv_ref, o_ref, gate_ref, up_ref, down_ref,
    attn_gain_ref, mlp_gain_ref, out_gain_ref, conv_ref, qkv_out, o_out, gate_up_out, down_out,
):
    f32 = jnp.float32
    staged.need(small_ref, qkv_ref, o_ref, gate_ref, up_ref, down_ref)
    cores, seqs, _, _ = small_ref.shape
    _, shard, width3 = qkv_ref.shape
    width, units = width3 // 3, gate_ref.shape[2]
    at = 2 + width // DK
    for ref, rows, lanes in (
        (attn_gain_ref, slice(0, 1), slice(None)),
        (mlp_gain_ref, slice(1, 2), slice(None)),
        (out_gain_ref, slice(at, at + 1), slice(2 * width3, 2 * width3 + DK)),
    ):
        total = small_ref[0, 0, rows, lanes]
        for i in range(1, cores * seqs):
            total = total + small_ref[i // seqs, i % seqs, rows, lanes]
        ref[...] = total
    down = lax.broadcasted_iota(jnp.int32, (shard, shard), 0)
    along = lax.broadcasted_iota(jnp.int32, (shard, shard), 1)
    unit = jnp.where(down == along, 1.0, 0.0).astype(jnp.bfloat16)
    for core in range(cores):
        for seq in range(seqs):
            for c in range(3):
                for tap in range(KW):
                    row, lane = at + tap // 2, (tap % 2) * width3 + c * width
                    to = (core * seqs + seq) * width
                    conv_ref[c, tap : tap + 1, to : to + width] = small_ref[
                        core, seq, row : row + 1, lane : lane + width
                    ]
    for seq in range(seqs):
        for c in range(3):
            qkv_out[c, :, seq * width : (seq + 1) * width] = qkv_ref[
                seq, :, c * width : (c + 1) * width
            ].astype(f32)
        o_out[seq * width : (seq + 1) * width] = mul(o_ref[seq], unit, (0, 0))
        down_out[seq * units : (seq + 1) * units] = mul(down_ref[seq], unit, (0, 0))
    for i, ref in enumerate((gate_ref, up_ref)):
        gate_up_out[i] = jnp.concatenate([ref[seq].astype(f32) for seq in range(seqs)], axis=1)


def run_finish(small, qkv, o, gate, up, down):
    f32 = jnp.float32
    cores, seqs, _, model_width = small.shape
    _, shard, width3 = qkv.shape
    units = gate.shape[2]
    shapes = (
        (1, model_width),
        (1, model_width),
        (1, DK),
        (3, KW, model_width),
        (3, shard, seqs * width3 // 3),
        (seqs * width3 // 3, shard),
        (2, shard, seqs * units),
        (seqs * units, shard),
    )
    return line_call(
        finish_kernel, None, "finish", [(shape, f32) for shape in shapes], [],
        (small, qkv, o, gate, up, down),
    )


def local_heads(
    block_input,
    grad_out,
    doc_lengths,
    attn_gain,
    mlp_gain,
    out_gain,
    conv_weight,
    qkv_weight,
    beta_weight,
    o_weight,
    gate_up_weight,
    down_weight,
):
    tok_rows, model_width = block_input.shape[1:]
    pieces, cores = lax.axis_size("seq"), lax.axis_size("tp")
    piece, core = lax.axis_index("seq"), lax.axis_index("tp")
    row_len = pieces * tok_rows
    shard_rows = qkv_weight.shape[1]
    width = qkv_weight.shape[2] // pieces
    heads = width // DK
    units = gate_up_weight.shape[2] // pieces
    f32, b16 = jnp.float32, jnp.bfloat16

    x_piece, g_piece = block_input[0], grad_out[0]
    beta_parts = jnp.pad(
        beta_weight.T.reshape(pieces, heads, shard_rows), ((0, 0), (0, 16 - heads), (0, 0))
    )
    normed_one, qkv_full, beta_full = run_normed(
        x_piece, attn_gain[None], qkv_weight, beta_parts
    )
    beta_full = beta_full.reshape(-1, 16, shard_rows).transpose(1, 0, 2).reshape(16, -1)
    gate_up_parts = gate_up_weight.reshape(2, shard_rows, pieces, units).transpose(0, 2, 1, 3)

    ends = jnp.cumsum(doc_lengths[0])
    places = jnp.arange(row_len, dtype=jnp.int32)
    docs = jnp.sum((places[:, None] >= ends[None, :]).astype(jnp.int32), axis=1)
    aux, doc_rows = row_aux(docs)
    gain_row = out_gain[None]
    taps = lax.dynamic_slice_in_dim(conv_weight, piece * width, width, axis=2)
    taps = taps.transpose(1, 0, 2).reshape(KW, 3 * width)

    saved, o_full, resid, normed_two, g_full, gate_full, up_full, down_full = run_forward(
        normed_one, qkv_full, beta_full, taps, aux, doc_rows, gain_row,
        x_piece, g_piece, mlp_gain[None],
        (o_weight, gate_up_parts[0], gate_up_parts[1], down_weight),
    )
    proj, logit, mixed, normed_mix, inverse, states, written = saved
    hidden, grad_gate, grad_up, down_rows = run_mlp(
        normed_two, g_full, gate_full, up_full, down_full
    )

    grad_resid, grad_attn, mlp_gain_part, result, sums = run_grad_resid(
        grad_gate, grad_up, gate_full, up_full, hidden, down_rows, resid, g_piece, mlp_gain[None],
        normed_two, g_full,
    )
    input_grad, small, qkv_sum, o_sum, down_sum, gate_sum, up_sum = run_backward(
        grad_attn,
        o_full,
        (proj, logit, mixed, inverse, states, written),
        taps,
        aux,
        doc_rows,
        gain_row,
        (
            normed_mix, normed_one, qkv_full, beta_full, attn_gain[None], mlp_gain_part,
            x_piece, grad_resid,
        ),
        sums.reshape(3, pieces, shard_rows, units),
    )
    attn_gain_grad, mlp_gain_grad, out_gain_grad, conv_grad, qkv_grad, o_grad, gate_up_grad, down_grad = (
        run_finish(small, qkv_sum, o_sum, gate_sum, up_sum, down_sum)
    )
    beta_sum = lax.dynamic_index_in_dim(small[:, :, 2 : 2 + heads], core, 0, keepdims=False)
    beta_sum = lax.dynamic_slice_in_dim(
        beta_sum.reshape(pieces * heads, model_width),
        (lax.axis_index("row") * pieces + piece) * shard_rows,
        shard_rows,
        axis=1,
    ).T
    return (
        result[None],
        input_grad[None],
        attn_gain_grad[0],
        mlp_gain_grad[0],
        out_gain_grad[0],
        conv_grad,
        qkv_grad,
        beta_sum,
        o_grad,
        gate_up_grad,
        down_grad,
    )


def splits_heads(mesh, heads=16, units=5632):
    return (
        mesh.shape["tp"] == 2
        and heads % (mesh.shape["seq"] * 2) == 0
        and units % (mesh.shape["seq"] * 2) == 0
    )


def solution(mesh):
    in_specs = (
        P("row", "seq", None),
        P("row", "seq", None),
        P("row", None),
        P(),
        P(),
        P(),
        P(None, None, "tp"),
        P(None, ("row", "seq"), "tp"),
        P(("row", "seq"), "tp"),
        P("tp", ("row", "seq")),
        P(None, ("row", "seq"), "tp"),
        P("tp", ("row", "seq")),
    )
    out_specs = (
        P("row", "seq", None),
        P("row", "seq", None),
        P(),
        P(),
        P(),
        P(),
        P(None, ("row", "seq"), "tp"),
        P(("row", "seq"), "tp"),
        P("tp", ("row", "seq")),
        P(None, ("row", "seq"), "tp"),
        P("tp", ("row", "seq")),
    )
    local = local_heads if splits_heads(mesh) else local_pieces
    return jax.shard_map(local, mesh=mesh, in_specs=in_specs, out_specs=out_specs, check_vma=False)
```

```python
import functools

import jax
import jax.numpy as jnp
from jax import lax
from jax.experimental import pallas as pl
from jax.experimental.pallas import tpu as pltpu
from jax.sharding import PartitionSpec as P

DK = 128
KW = 4
GROUP = 64
DOCS = 8


eps = 1e-06
mix_floor = 0.01
precise = lax.Precision.HIGHEST


def from_behind(shard, axis, by):
    devices = lax.axis_size(axis)
    pairs = [(i, i + by) for i in range(devices) if 0 <= i + by < devices]
    return lax.ppermute(shard, axis, pairs)


def prefix(shard, axis, combine, identity, reverse):
    devices, place = (lax.axis_size(axis), lax.axis_index(axis))
    everything = jax.tree.map(
        lambda part, kind: lax.all_gather(part.astype(kind), axis),
        shard,
        (jnp.bfloat16, jnp.bfloat16),
    )
    start = jax.tree.map(
        lambda part, zero: jnp.broadcast_to(jnp.asarray(zero, part.dtype), part.shape),
        shard,
        identity,
    )

    def step(k, before):
        at = devices - 1 - k if reverse else k
        reached = at > place if reverse else at < place
        new = combine(
            before, jax.tree.map(lambda part, own: part[at].astype(own.dtype), everything, shard)
        )
        return jax.tree.map(lambda a, b: jnp.where(reached, a, b), new, before)

    return lax.fori_loop(0, devices, step, start)


def norm_scale(values):
    return lax.rsqrt(jnp.mean(values * values, axis=-1, keepdims=True) + eps)


def norm_back(values, scale, gain, grad):
    weighted = gain * grad
    return scale * weighted - values * scale**3 * jnp.mean(
        weighted * values, axis=-1, keepdims=True
    )


def batch_mul(left, right):
    return jnp.einsum("hij,hjk->hik", left, right, precision=precise)


def batch_mul_t(left, right):
    return jnp.einsum("hji,hjk->hik", left, right, precision=precise)


def compose(earlier, later):
    return (batch_mul(later[0], earlier[0]), batch_mul(later[0], earlier[1]) + later[1])


def over_heads(function, shared):
    return jax.vmap(jax.vmap(function), in_axes=shared)


def tp_total(term):
    return lax.psum(term.astype(jnp.bfloat16), "tp").astype(jnp.float32)


def group_parts(key_rows, value_rows, rates, same_doc, carry_mask):
    size = key_rows.shape[0]
    strict = jnp.tril(jnp.ones((size, size), jnp.float32), -1) * same_doc
    inner = jnp.dot(key_rows, key_rows.T, precision=precise)
    system = jnp.eye(size, dtype=jnp.float32) + rates[:, None] * inner * strict
    right_side = jnp.concatenate(
        [rates[:, None] * value_rows, (rates * carry_mask)[:, None] * key_rows], axis=1
    )
    solved = jax.scipy.linalg.solve_triangular(system, right_side, lower=True)
    base_rows = solved[:, : value_rows.shape[1]]
    wy_rows = solved[:, value_rows.shape[1] :]
    tail_keys = same_doc[size - 1][:, None] * key_rows
    identity_mat = jnp.eye(key_rows.shape[1], dtype=jnp.float32)
    transition = carry_mask[size - 1] * identity_mat - jnp.dot(
        tail_keys.T, wy_rows, precision=precise
    )
    contribution = jnp.dot(tail_keys.T, base_rows, precision=precise)
    return (transition, contribution, base_rows, wy_rows)


def group_output(queries, key_rows, same_doc, carry_mask, base_rows, wy_rows, state_in):
    size = key_rows.shape[0]
    lower = jnp.tril(jnp.ones((size, size), jnp.float32)) * same_doc
    written = base_rows - jnp.dot(wy_rows, state_in, precision=precise)
    scores = jnp.dot(queries, key_rows.T, precision=precise) * lower
    carried = carry_mask[:, None] * jnp.dot(queries, state_in, precision=precise)
    return carried + jnp.dot(scores, written, precision=precise)


def group_full(queries, key_rows, value_rows, rates, same_doc, carry_mask, state_in):
    transition, contribution, base_rows, wy_rows = group_parts(
        key_rows, value_rows, rates, same_doc, carry_mask
    )
    outputs = group_output(queries, key_rows, same_doc, carry_mask, base_rows, wy_rows, state_in)
    return (outputs, jnp.dot(transition, state_in, precision=precise) + contribution)


def state_pull(queries, key_rows, same_doc, carry_mask, wy_rows, grad_rows):
    size = key_rows.shape[0]
    lower = jnp.tril(jnp.ones((size, size), jnp.float32)) * same_doc
    scores = jnp.dot(queries, key_rows.T, precision=precise) * lower
    pulled = jnp.dot(scores.T, grad_rows, precision=precise)
    direct = jnp.dot((carry_mask[:, None] * queries).T, grad_rows, precision=precise)
    return direct - jnp.dot(wy_rows.T, pulled, precision=precise)


def group_grads(
    queries, key_rows, value_rows, rates, same_doc, carry_mask, state_in, grad_rows, grad_end
):

    def group_local(query_in, key_in, value_in, rate_in):
        return group_full(query_in, key_in, value_in, rate_in, same_doc, carry_mask, state_in)

    outputs, pullback = jax.vjp(group_local, queries, key_rows, value_rows, rates)
    return pullback((grad_rows, grad_end))


def local_pieces(
    block_input,
    grad_out,
    doc_lengths,
    attn_gain,
    mlp_gain,
    out_gain,
    conv_weight,
    qkv_weight,
    beta_weight,
    o_weight,
    gate_up_weight,
    down_weight,
):
    tok_rows = block_input.shape[1]
    model_width = block_input.shape[2]
    blocks = tok_rows // GROUP
    unit_floor = DK / 16.0
    x_rows = block_input[0].astype(jnp.float32)
    grad_rows_out = grad_out[0]
    qkv_full, beta_full, o_full, gate_up_full, down_full = (
        lax.all_gather(qkv_weight, ("row", "seq"), axis=1, tiled=True),
        lax.all_gather(beta_weight, ("row", "seq"), axis=0, tiled=True),
        lax.all_gather(o_weight, ("row", "seq"), axis=1, tiled=True),
        lax.all_gather(gate_up_weight, ("row", "seq"), axis=1, tiled=True),
        lax.all_gather(down_weight, ("row", "seq"), axis=1, tiled=True),
    )
    local_width = qkv_full.shape[2]
    head_count = local_width // DK
    lead_mask = (lax.axis_index("tp") == 0).astype(jnp.float32)
    ends = jnp.cumsum(doc_lengths[0])
    places = (
        lax.axis_index("seq") * tok_rows + jnp.arange(tok_rows + KW - 1, dtype=jnp.int32) - (KW - 1)
    )
    doc_ids = jnp.sum((places[:, None] >= ends[None, :]).astype(jnp.int32), axis=1)
    doc_ids = jnp.where(places < 0, -1, doc_ids)
    own_docs = doc_ids[KW - 1 :]
    prior_docs = doc_ids[KW - 2 : KW - 2 + tok_rows]
    valid = (own_docs < DOCS).astype(jnp.float32)
    fresh = (own_docs != prior_docs).astype(jnp.int32)
    tap_masks = [
        (doc_ids[KW - 1 - tap : KW - 1 - tap + tok_rows] == own_docs).astype(jnp.float32)
        for tap in range(KW)
    ]
    own_blocks = own_docs.reshape(blocks, GROUP)
    same_doc = (own_blocks[:, :, None] == own_blocks[:, None, :]).astype(jnp.float32)
    carry_mask = (jnp.cumsum(fresh.reshape(blocks, GROUP), axis=1) == 0).astype(jnp.float32)

    def to_blocks(array):
        return array.reshape(blocks, GROUP, head_count, -1).transpose(2, 0, 1, 3)

    def from_blocks(array):
        return array.transpose(1, 2, 0, 3).reshape(tok_rows, head_count, -1)

    scale_one = norm_scale(x_rows)
    normed_one = (x_rows * scale_one * attn_gain).astype(jnp.bfloat16)
    proj_low = jnp.einsum(
        "td,cde->cte", normed_one, qkv_full, preferred_element_type=jnp.float32
    ).astype(jnp.bfloat16)
    logit = jnp.dot(normed_one, beta_full, preferred_element_type=jnp.float32)
    rim_rows = from_behind(proj_low[:, tok_rows - (KW - 1) :, :], "seq", 1)
    extended = jnp.concatenate([rim_rows, proj_low], axis=1).astype(jnp.float32)
    conv_out = jnp.zeros((3, tok_rows, local_width), jnp.float32)
    for tap in range(KW):
        window = extended[:, KW - 1 - tap : KW - 1 - tap + tok_rows]
        conv_out = (
            conv_out + conv_weight[:, tap][:, None, :] * window * tap_masks[tap][None, :, None]
        )
    conv_sig = jax.nn.sigmoid(conv_out)
    activated = conv_out * conv_sig
    query_raw = activated[0].reshape(tok_rows, head_count, DK)
    key_raw = activated[1].reshape(tok_rows, head_count, DK)
    query_sq = jnp.sum(query_raw * query_raw, axis=-1, keepdims=True)
    key_sq = jnp.sum(key_raw * key_raw, axis=-1, keepdims=True)
    query_scale = lax.rsqrt(jnp.maximum(query_sq, unit_floor))
    key_scale = lax.rsqrt(jnp.maximum(key_sq, unit_floor))
    query_live = (query_sq > unit_floor).astype(jnp.float32)
    key_live = (key_sq > unit_floor).astype(jnp.float32)
    query_blocks = to_blocks(query_raw * query_scale)
    key_blocks = to_blocks(key_raw * key_scale)
    value_blocks = to_blocks(activated[2].reshape(tok_rows, head_count, DK))
    rate_sig = jax.nn.sigmoid(logit)
    rate_blocks = (rate_sig * valid[:, None]).reshape(blocks, GROUP, head_count).transpose(2, 0, 1)
    transition, contribution, base_rows, wy_rows = over_heads(group_parts, (0, 0, 0, None, None))(
        key_blocks, value_blocks, rate_blocks, same_doc, carry_mask
    )
    identity_mat = jnp.broadcast_to(jnp.eye(DK, dtype=jnp.float32), (head_count, DK, DK))
    zero_state = jnp.zeros((head_count, DK, DK), jnp.float32)
    transition_steps = jnp.moveaxis(transition, 1, 0)

    def chain(running, pair):
        product, partial_state = running
        step_trans, step_contrib = pair
        advanced = (
            batch_mul(step_trans, product),
            batch_mul(step_trans, partial_state) + step_contrib,
        )
        return (advanced, (product, partial_state))

    (dev_trans, dev_state), (products, partials) = lax.scan(
        chain, (identity_mat, zero_state), (transition_steps, jnp.moveaxis(contribution, 1, 0))
    )
    incoming = prefix((dev_trans, dev_state), "seq", compose, (identity_mat, zero_state), False)[1]
    group_starts = partials + jnp.einsum("nhij,hjk->nhik", products, incoming, precision=precise)
    start_blocks = jnp.moveaxis(group_starts, 0, 1)
    mix_blocks = over_heads(group_output, (0, 0, None, None, 0, 0, 0))(
        query_blocks, key_blocks, same_doc, carry_mask, base_rows, wy_rows, start_blocks
    )
    mixed = from_blocks(mix_blocks) * valid[:, None, None]
    mix_sq = jnp.mean(mixed * mixed, axis=-1, keepdims=True)
    mix_scale = lax.rsqrt(jnp.maximum(mix_sq, mix_floor))
    mix_live = (mix_sq > mix_floor).astype(jnp.float32)
    normed_mix = (mixed * mix_scale * out_gain).astype(jnp.bfloat16).reshape(tok_rows, local_width)
    o_term = jnp.dot(normed_mix, o_full, preferred_element_type=jnp.float32)
    resid = x_rows + tp_total(o_term)
    scale_two = norm_scale(resid)
    normed_local = (resid * scale_two * mlp_gain).astype(jnp.bfloat16)
    gate_up = jnp.einsum(
        "td,cdf->ctf", normed_local, gate_up_full, preferred_element_type=jnp.float32
    )
    gate_sig = jax.nn.sigmoid(gate_up[0])
    gate_act = gate_up[0] * gate_sig
    hidden = (gate_act * gate_up[1]).astype(jnp.bfloat16)
    down_term = jnp.dot(hidden, down_full, preferred_element_type=jnp.float32)
    mlp_out = tp_total(down_term)
    result = (resid + mlp_out).astype(jnp.bfloat16)
    grad_hidden = jnp.einsum(
        "td,fd->tf", grad_rows_out, down_full, preferred_element_type=jnp.float32
    )
    grad_gate = grad_hidden * gate_up[1] * gate_sig * (1.0 + gate_up[0] * (1.0 - gate_sig))
    grad_up = grad_hidden * gate_act
    grad_gate_up = jnp.stack([grad_gate, grad_up]).astype(jnp.bfloat16)
    down_part = jnp.einsum("tf,td->fd", hidden, grad_rows_out, preferred_element_type=jnp.float32)
    gate_up_part = jnp.einsum(
        "td,ctf->cdf", normed_local, grad_gate_up, preferred_element_type=jnp.float32
    )
    two_term = jnp.einsum(
        "ctf,cdf->td", grad_gate_up, gate_up_full, preferred_element_type=jnp.float32
    )
    grad_two = tp_total(two_term)
    mlp_gain_part = jnp.sum(grad_two * resid * scale_two, axis=0)
    grad_resid = grad_rows_out.astype(jnp.float32) + norm_back(resid, scale_two, mlp_gain, grad_two)
    grad_attn_local = grad_resid.astype(jnp.bfloat16)
    o_part = jnp.einsum(
        "te,td->ed", normed_mix, grad_attn_local, preferred_element_type=jnp.float32
    )
    grad_normed = jnp.einsum(
        "td,ed->te", grad_attn_local, o_full, preferred_element_type=jnp.float32
    ).reshape(tok_rows, head_count, DK)
    out_gain_part = jnp.sum(grad_normed * mixed * mix_scale, axis=(0, 1))
    weighted_mix = out_gain * grad_normed
    grad_mixed = (
        mix_scale * weighted_mix
        - mixed * mix_scale**3 * mix_live * jnp.mean(weighted_mix * mixed, axis=-1, keepdims=True)
    ) * valid[:, None, None]
    grad_blocks = to_blocks(grad_mixed)
    pulls = over_heads(state_pull, (0, 0, None, None, 0, 0))(
        query_blocks, key_blocks, same_doc, carry_mask, wy_rows, grad_blocks
    )

    def back_chain(running, pair):
        grad_end, product = running
        step_trans, step_pull = pair
        advanced = (step_pull + batch_mul_t(step_trans, grad_end), batch_mul_t(step_trans, product))
        return (advanced, (grad_end, product))

    (dev_pull, dev_back), (grad_ends, back_products) = lax.scan(
        back_chain,
        (zero_state, identity_mat),
        (transition_steps, jnp.moveaxis(pulls, 1, 0)),
        reverse=True,
    )
    outgoing = prefix((dev_back, dev_pull), "seq", compose, (identity_mat, zero_state), True)[1]
    end_grads = grad_ends + jnp.einsum("nhij,hjk->nhik", back_products, outgoing, precision=precise)
    grad_query, grad_key, grad_value, grad_rate = over_heads(
        group_grads, (0, 0, 0, 0, None, None, 0, 0, 0)
    )(
        query_blocks,
        key_blocks,
        value_blocks,
        rate_blocks,
        same_doc,
        carry_mask,
        start_blocks,
        grad_blocks,
        jnp.moveaxis(end_grads, 0, 1),
    )
    grad_query = from_blocks(grad_query)
    grad_key = from_blocks(grad_key)
    grad_query_raw = query_scale * grad_query - query_raw * query_scale**3 * query_live * jnp.sum(
        query_raw * grad_query, axis=-1, keepdims=True
    )
    grad_key_raw = key_scale * grad_key - key_raw * key_scale**3 * key_live * jnp.sum(
        key_raw * grad_key, axis=-1, keepdims=True
    )
    grad_activated = jnp.stack(
        [
            grad_query_raw.reshape(tok_rows, local_width),
            grad_key_raw.reshape(tok_rows, local_width),
            from_blocks(grad_value).reshape(tok_rows, local_width),
        ]
    )
    grad_conv = grad_activated * conv_sig * (1.0 + conv_out * (1.0 - conv_sig))
    grad_extended = jnp.zeros((3, tok_rows + KW - 1, local_width), jnp.float32)
    tap_grads = []
    for tap in range(KW):
        masked = grad_conv * tap_masks[tap][None, :, None]
        window = extended[:, KW - 1 - tap : KW - 1 - tap + tok_rows]
        tap_grads.append(jnp.sum(masked * window, axis=1))
        grad_extended = grad_extended + jnp.pad(
            conv_weight[:, tap][:, None, :] * masked, ((0, 0), (KW - 1 - tap, tap), (0, 0))
        )
    conv_part = jnp.stack(tap_grads, axis=1)
    rim_back = from_behind(grad_extended[:, : KW - 1], "seq", -1)
    grad_proj = jnp.concatenate(
        [grad_extended[:, KW - 1 : tok_rows], grad_extended[:, tok_rows:] + rim_back], axis=1
    ).astype(jnp.bfloat16)
    rate_grad = grad_rate.transpose(1, 2, 0).reshape(tok_rows, head_count)
    grad_logit = (rate_grad * valid[:, None] * rate_sig * (1.0 - rate_sig)).astype(jnp.bfloat16)
    qkv_part = jnp.einsum("td,cte->cde", normed_one, grad_proj, preferred_element_type=jnp.float32)
    beta_part = jnp.einsum("td,th->dh", normed_one, grad_logit, preferred_element_type=jnp.float32)
    grad_one_part = jnp.einsum(
        "cte,cde->td", grad_proj, qkv_full, preferred_element_type=jnp.float32
    ) + jnp.einsum("th,dh->td", grad_logit, beta_full, preferred_element_type=jnp.float32)
    grad_one = tp_total(grad_one_part)
    attn_gain_part = jnp.sum(grad_one * x_rows * scale_one, axis=0)
    input_local = (grad_resid + norm_back(x_rows, scale_one, attn_gain, grad_one)).astype(
        jnp.bfloat16
    )
    conv_whole = lax.dynamic_update_slice(
        jnp.zeros((3, KW, model_width), jnp.float32),
        conv_part,
        (0, 0, lax.axis_index("tp") * local_width),
    )
    attn_gain_grad, mlp_gain_grad, out_gain_grad, conv_grad = lax.psum(
        (attn_gain_part * lead_mask, mlp_gain_part * lead_mask, out_gain_part, conv_whole),
        ("row", "seq", "tp"),
    )
    qkv_sum, beta_sum, o_sum, gate_up_sum, down_sum = (
        lax.psum_scatter(
            qkv_part.astype(jnp.bfloat16), ("row", "seq"), scatter_dimension=1, tiled=True
        ).astype(jnp.float32),
        lax.psum_scatter(
            beta_part.astype(jnp.bfloat16), ("row", "seq"), scatter_dimension=0, tiled=True
        ).astype(jnp.float32),
        lax.psum_scatter(
            o_part.astype(jnp.bfloat16), ("row", "seq"), scatter_dimension=1, tiled=True
        ).astype(jnp.float32),
        lax.psum_scatter(
            gate_up_part.astype(jnp.bfloat16), ("row", "seq"), scatter_dimension=1, tiled=True
        ).astype(jnp.float32),
        lax.psum_scatter(
            down_part.astype(jnp.bfloat16), ("row", "seq"), scatter_dimension=1, tiled=True
        ).astype(jnp.float32),
    )
    return (
        result[None],
        input_local[None],
        attn_gain_grad,
        mlp_gain_grad,
        out_gain_grad,
        conv_grad,
        qkv_sum,
        beta_sum,
        o_sum,
        gate_up_sum,
        down_sum,
    )


CHUNK = 128
PAD = 8


def mul(left, right, dims):
    return lax.dot_general(
        left, right, ((dims[:1], dims[1:]), ((), ())), preferred_element_type=jnp.float32
    )


def fine(left, right, dims=(1, 0)):
    left_high, right_high = left.astype(jnp.bfloat16), right.astype(jnp.bfloat16)
    left_rest = (left - left_high.astype(jnp.float32)).astype(jnp.bfloat16)
    right_rest = (right - right_high.astype(jnp.float32)).astype(jnp.bfloat16)
    rest = mul(left_high, right_rest, dims) + mul(left_rest, right_high, dims)
    return mul(left_high, right_high, dims) + rest


def plain(left, right, dims=(1, 0)):
    return mul(left.astype(jnp.bfloat16), right.astype(jnp.bfloat16), dims)


def chunk_masks(doc_col, doc_row):
    same = doc_col == doc_row
    down = lax.broadcasted_iota(jnp.int32, (CHUNK, CHUNK), 0)
    along = lax.broadcasted_iota(jnp.int32, (CHUNK, CHUNK), 1)
    lower = jnp.where(same & (down >= along), 1.0, 0.0)
    strict = jnp.where(same & (down > along), 1.0, 0.0)
    return lower, strict, down, along


def lower_inverse(systems, down, along):
    at_one = (down // 2 == along // 2) & (down != along)
    unit = jnp.where(down == along, 1.0, 0.0)
    inverses = [unit - jnp.where(at_one, system, 0.0) for system in systems]
    half = 2
    while half < CHUNK:
        joins = (down // (2 * half) == along // (2 * half)) & (down // half != along // half)
        inner = [
            fine(jnp.where(joins, system, 0.0), inverse)
            for system, inverse in zip(systems, inverses)
        ]
        inverses = [inverse - fine(inverse, part) for inverse, part in zip(inverses, inner)]
        half *= 2
    return inverses


def tap_mask(aux, tap):
    return 1.0 if tap == 0 else aux[:, 3 + tap : 4 + tap]


def convolved(window, taps, aux):
    total = 0.0
    for tap in range(KW):
        total = total + (
            taps[tap : tap + 1] * window[PAD - tap : PAD - tap + CHUNK] * tap_mask(aux, tap)
        )
    return total


def sigmoid(values):
    return 1.0 / (1.0 + jnp.exp(-values))


def unit_scale(values):
    total = jnp.sum(values * values, axis=1, keepdims=True)
    floor = DK / 16.0
    return lax.rsqrt(jnp.maximum(total, floor)), jnp.where(total > floor, 1.0, 0.0)


def mix_norm(mixed):
    mean = jnp.mean(mixed * mixed, axis=1, keepdims=True)
    return lax.rsqrt(jnp.maximum(mean, mix_floor)), jnp.where(mean > mix_floor, 1.0, 0.0)


def forward_kernel(
    heads,
    staged,
    n1_ref,
    qkv_ref,
    beta_blocks_ref,
    taps_ref,
    aux_ref,
    docs_ref,
    gain_ref,
    x_ref,
    mlp_gain_ref,
    g_ref,
    o_weight_ref,
    gate_ref,
    up_ref,
    down_ref,
    proj_ref,
    logit_ref,
    mixed_ref,
    normed_ref,
    inverse_ref,
    states_ref,
    written_ref,
    o_ref,
    resid_ref,
    n2_ref,
    g_full_ref,
    gate_out,
    up_out,
    down_out,
    window_ref,
    state_ref,
    o_rows,
    n2_own,
    beta_ref,
    blocks,
    came,
    across,
    own_sems,
    sum_sems,
    n2_sems,
    g_sems,
    *sems,
):
    width = heads * DK
    line = Line()
    greet(exchange_partners(line) + along_axis("tp"))
    row = lax.axis_index("row")
    rows = n2_ref.shape[2]
    units = down_out.shape[2]

    def rows_of(ref, count):
        return lambda seq: ref.at[pl.ds(pl.multiple_of(seq * count, count), count)]

    o_move = Exchange(line, rows_of(o_weight_ref, width), o_ref, sems[:4])
    gate_move = Exchange(line, lambda seq: gate_ref.at[seq], gate_out, sems[4:8])
    up_move = Exchange(line, lambda seq: up_ref.at[seq], up_out, sems[8:12])
    down_move = Exchange(line, rows_of(down_ref, units), down_out, sems[12:16])
    moves = (o_move, gate_move, up_move, down_move)
    total = Scatter(line, blocks, came, across, sum_sems)
    n2 = Gather(line, n2_ref, n2_own, n2_sems)
    g_own = g_ref.at[pl.ds(pl.multiple_of(line.core * rows, rows), rows)]
    grads = Gather(line, g_full_ref, g_own, g_sems)
    own = []
    for i, move in enumerate(moves):
        target = move.target.at[row, line.place]
        own.append(pltpu.make_async_copy(move.source(line.place), target, own_sems.at[i]))
        own[i].start()
    o_move.start()
    gate_move.start()
    grads.phases(0)
    for move in moves:
        move.share_own()
    window_ref[0:PAD] = jnp.zeros((PAD, 3 * width), jnp.float32)
    state_ref[...] = jnp.zeros_like(state_ref)

    def prepare(n):
        rows = pl.ds(pl.multiple_of(n * CHUNK, CHUNK), CHUNK)
        n1 = n1_ref[rows]
        proj = jnp.concatenate(
            [mul(n1, qkv_ref[:, :, c].reshape(-1, width), (1, 0)) for c in range(3)], axis=1
        ).astype(jnp.bfloat16)
        proj_ref[rows] = proj
        window_ref[PAD : PAD + CHUNK] = proj.astype(jnp.float32)
        logit = mul(n1, beta_ref[...], (1, 1))
        logit_ref[rows] = logit
        aux = aux_ref[rows]
        conv = convolved(window_ref[...], taps_ref[...], aux)
        act = conv * sigmoid(conv)
        window_ref[0:PAD] = window_ref[CHUNK : CHUNK + PAD]
        valid, carry, tail = aux[:, 1:2], aux[:, 2:3], aux[:, 3:4]
        lower, strict, down, along = chunk_masks(aux[:, 0:1], docs_ref[pl.ds(n, 1)])
        rate_all = sigmoid(logit) * valid
        parts = []
        for h in range(heads):
            query = act[:, h * DK : (h + 1) * DK]
            key = act[:, width + h * DK : width + (h + 1) * DK]
            value = act[:, 2 * width + h * DK : 2 * width + (h + 1) * DK]
            query = query * unit_scale(query)[0]
            key = key * unit_scale(key)[0]
            rate = rate_all[:, h : h + 1]
            scores = plain(query, key, (1, 1)) * lower
            system = rate * fine(key, key, (1, 1)) * strict
            parts.append((query, key, value, rate, scores, system))
        return rows, valid, carry, tail, parts, down, along

    def advance(n, rows, valid, carry, tail, parts, inverses):
        carry_last = carry[CHUNK - 1 :]
        for h, (query, key, value, rate, scores, _) in enumerate(parts):
            inverse = inverses[h]
            state = state_ref[h]
            written = fine(inverse, rate * (value - fine(carry * key, state)))
            mixed = (carry * plain(query, state) + plain(scores, written)) * valid
            states_ref[h, n] = state
            written_ref[h, n] = written
            inverse_ref[h, n] = inverse
            state_ref[h] = carry_last * state + fine(tail * key, written, (0, 0))
            columns = pl.ds(h * DK, DK)
            mixed_ref[rows, columns] = mixed
            normed_ref[rows, columns] = (
                mixed * mix_norm(mixed)[0] * gain_ref[...]
            ).astype(jnp.bfloat16)

    chunks = n1_ref.shape[0] // CHUNK
    together = 4 if chunks % 4 == 0 else 1

    def several(m, _):
        ready = [prepare(together * m + i) for i in range(together)]
        down, along = ready[0][5:]
        inverses = lower_inverse([part[5] for one in ready for part in one[4]], down, along)
        for i, one in enumerate(ready):
            advance(together * m + i, *one[:5], inverses[i * heads : (i + 1) * heads])
        return 0

    def share_came(move):
        for i in range(1, line.count):
            move.share_came(i)

    half = chunks // together // 2
    staged.need(n1_ref, qkv_ref, beta_blocks_ref, taps_ref, aux_ref, docs_ref, gain_ref)
    side_by_side(beta_blocks_ref, beta_ref)
    lax.fori_loop(0, half, several, 0)
    share_came(o_move)
    grads.phases(1)
    up_move.start()
    lax.fori_loop(half, chunks // together, several, 0)
    staged.store(
        proj_ref, logit_ref, mixed_ref, normed_ref, inverse_ref, states_ref, written_ref
    )
    share_came(gate_move)
    down_move.start()
    own[0].wait()
    o_move.finish()
    staged.store(o_ref)
    side_by_side(o_ref, o_rows)
    for part in range(total.parts):
        total.product(part_rows(normed_ref, total, part), o_rows, part, order=0)
        total.start_edges(part)
    grads.phases(2)
    total.relay(0, 0)
    total.relay(1, 0)
    share_came(up_move)
    total.relay_back(0)
    grads.phases(3)
    total.relay(0, 1)
    total.relay(1, 1)
    share_came(down_move)
    total.relay_back(1)
    staged.need(x_ref, mlp_gain_ref)

    def normed(span):
        x_span = pl.ds(pl.multiple_of(line.core * rows + span.start, STEP), STEP)
        resid = x_ref[x_span].astype(jnp.float32) + total.own_rows(span)
        resid_ref[span] = resid
        n2_own[span] = (resid * norm_scale(resid) * mlp_gain_ref[...]).astype(jnp.bfloat16)

    for part in range(total.parts):
        total.wait_own(part)
        over_rows(total, part, normed)
        n2.phase(0, part)
    staged.store(resid_ref)
    for k in range(1, line.count):
        n2.phases(k)
    total.finish()
    n2.finish()
    grads.finish()
    for i, move in enumerate(moves[1:]):
        own[i + 1].wait()
        move.finish()


def part_rows(ref, total, part):
    seqs, cores, rows, _ = total.blocks.shape
    return jnp.concatenate(
        [ref[pl.ds(i * rows + part * total.rows, total.rows)] for i in range(seqs * cores)], axis=0
    )


def backward_kernel(
    heads,
    staged,
    grad_ref,
    o_ref,
    proj_ref,
    logit_ref,
    mixed_ref,
    inverse_ref,
    states_ref,
    written_ref,
    taps_ref,
    aux_ref,
    docs_ref,
    gain_ref,
    normed_mix_ref,
    n1_ref,
    qkv_ref,
    beta_blocks_ref,
    attn_gain_ref,
    mlp_grad_ref,
    x_ref,
    grad_resid_ref,
    sum_ref,
    input_grad_ref,
    small_all_ref,
    qkv_came_ref,
    o_came_ref,
    down_came_ref,
    gate_came_ref,
    up_came_ref,
    window_ref,
    masked_ref,
    state_ref,
    o_rows,
    beta_ref,
    conv_grad_ref,
    gain_grad_ref,
    grad_proj_ref,
    grad_logit_ref,
    small_ref,
    small_rows,
    qkv_sum,
    o_sum,
    blocks,
    came,
    across,
    qkv_parts,
    qkv_halves,
    qkv_rows_came,
    o_parts,
    o_halves,
    o_rows_came,
    sum_sems,
    swap_sems,
    *sems,
):
    width = heads * DK
    line = Line()
    greet(along_axis("seq") + along_axis("row") + along_axis("tp"))
    moves = moves_of(
        Swap,
        "seq",
        [sum_ref.at[m] for m in range(3)],
        (down_came_ref, gate_came_ref, up_came_ref),
        sems[:7],
    )
    for move in moves:
        move.start()
    (o_move,) = moves_of(Swap, "seq", (o_sum,), (o_came_ref,), sems[7:10])
    (qkv_move,) = moves_of(Swap, "seq", (qkv_sum,), (qkv_came_ref,), sems[10:13])
    (small_row,) = moves_of(Share, "row", (small_ref,), (small_rows,), sems[13:16])
    own_small = small_all_ref.at[line.core, line.place]
    small_seq = [
        remote(own_small, own_small, sems[16].at[i], sems[17].at[i], {"seq": other})
        for i, other in enumerate(around("seq"))
    ]
    core_small = small_all_ref.at[line.core]
    small_core = remote(core_small, core_small, sems[18].at[0], sems[18].at[1], line.across)
    o_sums = RowSum(o_parts, o_halves, o_rows_came, sems[19:23])
    qkv_sums = RowSum(qkv_parts, qkv_halves, qkv_rows_came, sems[23:27])
    total = Scatter(line, blocks, came, across, sum_sems)
    span = o_parts.shape[2]

    def own_columns(index):
        return pl.ds(pl.multiple_of(index * span, span), span)

    staged.need(grad_ref, normed_mix_ref)
    for step, index in enumerate(o_sums.order()):
        part = mul(grad_ref[:, own_columns(index)], normed_mix_ref[...], (0, 0))
        o_parts[index, 0] = part.astype(jnp.bfloat16)
        o_sums.start(step, 0)
    chunks = grad_ref.shape[0] // CHUNK
    staged.need(
        o_ref, proj_ref, logit_ref, mixed_ref, inverse_ref, states_ref, written_ref, taps_ref,
        aux_ref, docs_ref, gain_ref,
    )
    side_by_side(o_ref, o_rows)
    state_ref[...] = jnp.zeros_like(state_ref)
    masked_ref[...] = jnp.zeros_like(masked_ref)
    conv_grad_ref[...] = jnp.zeros_like(conv_grad_ref)
    gain_grad_ref[...] = jnp.zeros_like(gain_grad_ref)

    def chunk(step, _):
        n = chunks - 1 - step
        rows = pl.ds(pl.multiple_of(n * CHUNK, CHUNK), CHUNK)
        before = jnp.maximum(n - 1, 0)
        aux = aux_ref[rows]
        grad_normed = mul(grad_ref[rows], o_rows[...], (1, 1))
        prior = proj_ref[pl.ds(pl.multiple_of(before * CHUNK + CHUNK - 16, 16), 16)]
        window_ref[0:PAD] = prior.astype(jnp.float32)[16 - PAD :]
        window_ref[PAD : PAD + CHUNK] = proj_ref[rows].astype(jnp.float32)
        window = window_ref[...]
        taps = taps_ref[...]
        conv = convolved(window, taps, aux)
        conv_sig = sigmoid(conv)
        act = conv * conv_sig
        valid, carry, tail = aux[:, 1:2], aux[:, 2:3], aux[:, 3:4]
        carry_last = carry[CHUNK - 1 :]
        lower, strict, down, along = chunk_masks(aux[:, 0:1], docs_ref[pl.ds(n, 1)])
        rate_sig = sigmoid(logit_ref[rows])
        rate_all = rate_sig * valid
        lanes = lax.broadcasted_iota(jnp.int32, rate_all.shape, 1)
        grad_rates = jnp.zeros_like(rate_all)
        grads = [[], [], []]
        for h in range(heads):
            columns = pl.ds(h * DK, DK)
            mixed = mixed_ref[rows, columns]
            mix_scale, mix_live = mix_norm(mixed)
            grad_out = grad_normed[:, h * DK : (h + 1) * DK]
            scaled = mixed * mix_scale
            gain_grad_ref[...] += jnp.sum(grad_out * scaled, axis=0, keepdims=True)
            weighted = gain_ref[...] * grad_out
            grad_mix = (
                mix_scale * weighted
                - scaled
                * (mix_scale * mix_scale * mix_live)
                * jnp.mean(weighted * mixed, axis=1, keepdims=True)
            ) * valid
            query_raw = act[:, h * DK : (h + 1) * DK]
            key_raw = act[:, width + h * DK : width + (h + 1) * DK]
            value = act[:, 2 * width + h * DK : 2 * width + (h + 1) * DK]
            query_scale, query_live = unit_scale(query_raw)
            key_scale, key_live = unit_scale(key_raw)
            query = query_raw * query_scale
            key = key_raw * key_scale
            rate = rate_all[:, h : h + 1]
            inverse = inverse_ref[h, n]
            state = states_ref[h, n]
            written = written_ref[h, n]
            grad_state = state_ref[h]
            tail_key = tail * key
            carried_key = carry * key
            scores = plain(query, key, (1, 1)) * lower
            pulled = plain(scores, grad_mix, (0, 0)) + fine(tail_key, grad_state)
            solved = fine(inverse, pulled, (0, 0))
            state_ref[h] = (
                carry_last * grad_state
                + plain(carry * query, grad_mix, (0, 0))
                - fine(rate * carried_key, solved, (0, 0))
            )
            grad_scores = plain(grad_mix, written, (1, 1)) * lower
            grad_query = carry * plain(grad_mix, state, (1, 1)) + plain(grad_scores, key)
            guess_error = value - plain(carried_key, state)
            gram = plain(key, key, (1, 1)) * strict
            grad_system = plain(solved, written, (1, 1)) * strict
            grad_rate = jnp.sum(solved * guess_error, axis=1, keepdims=True) - jnp.sum(
                grad_system * gram, axis=1, keepdims=True
            )
            grad_gram = rate * grad_system
            grad_key = (
                plain(grad_scores, query, (0, 0))
                + tail * plain(written, grad_state, (1, 1))
                - rate * carry * plain(solved, state, (1, 1))
                - plain(grad_gram, key)
                - plain(grad_gram, key, (0, 0))
            )
            grads[0].append(
                query_scale
                * (
                    grad_query
                    - query
                    * query_live
                    * jnp.sum(query * grad_query, axis=1, keepdims=True)
                )
            )
            grads[1].append(
                key_scale
                * (grad_key - key * key_live * jnp.sum(key * grad_key, axis=1, keepdims=True))
            )
            grads[2].append(rate * solved)
            grad_rates = grad_rates + jnp.where(lanes == h, grad_rate, 0.0)
        grad_act = jnp.concatenate(grads[0] + grads[1] + grads[2], axis=1)
        grad_conv = grad_act * conv_sig * (1.0 + conv * (1.0 - conv_sig))
        grad_proj = taps[0:1] * grad_conv
        conv_grad_ref[0:1] += jnp.sum(
            grad_conv * window[PAD : PAD + CHUNK], axis=0, keepdims=True
        )
        for tap in range(1, KW):
            masked = grad_conv * tap_mask(aux, tap)
            conv_grad_ref[tap : tap + 1] += jnp.sum(
                masked * window[PAD - tap : PAD - tap + CHUNK], axis=0, keepdims=True
            )
            masked_ref[tap - 1, CHUNK : CHUNK + PAD] = masked_ref[tap - 1, 0:PAD]
            masked_ref[tap - 1, 0:CHUNK] = masked
            grad_proj = grad_proj + taps[tap : tap + 1] * masked_ref[tap - 1, tap : tap + CHUNK]
        grad_proj_ref[rows] = grad_proj.astype(jnp.bfloat16)
        grad_logit_ref[rows] = (grad_rates * rate_sig * (1.0 - rate_sig) * valid).astype(
            jnp.bfloat16
        )
        return 0

    early, late = chunks // 4, chunks // 2
    lax.fori_loop(0, early, chunk, 0)
    o_sums.add_halves(0)
    lax.fori_loop(early, late, chunk, 0)
    o_sum[...] = o_sums.total(0).astype(jnp.bfloat16).reshape(o_sum.shape)
    o_move.start()
    lax.fori_loop(late, chunks, chunk, 0)
    staged.need(
        n1_ref, qkv_ref, beta_blocks_ref, attn_gain_ref, mlp_grad_ref, x_ref, grad_resid_ref
    )
    side_by_side(beta_blocks_ref, beta_ref)

    def product(part):
        left = part_rows(grad_proj_ref, total, part)
        logit = part_rows(grad_logit_ref, total, part)

        def right_tile(left, t, across):
            weights = qkv_ref[t]
            out = mul(logit, beta_ref[:, across], (1, 0))
            for c in range(3):
                out = out + mul(
                    left[:, c * width : (c + 1) * width], weights[:, c].reshape(-1, width), (1, 1)
                )
            return out

        total.product(left, None, part, tile=span, right_tile=right_tile)
        total.start_edges(part)

    def qkv_grads(step):
        index = qkv_sums.order()[step]
        columns = own_columns(index)
        n1 = n1_ref[:, columns]
        part = mul(n1, grad_proj_ref[...], (0, 0))
        qkv_parts[index, 0] = part.astype(jnp.bfloat16)
        qkv_sums.start(step, 0)
        weights = qkv_ref[index]
        terms = 0.0
        for c in range(3):
            weight = weights[:, c].reshape(span, width).astype(jnp.float32)
            terms = terms + weight * part[:, c * width : (c + 1) * width]
        terms = fine(jnp.ones((8, width), jnp.float32), terms, (1, 1))[0:1]
        beta_part = mul(grad_logit_ref[...], n1, (0, 0))
        terms = terms + jnp.sum(
            beta_part * beta_ref[:, columns].astype(jnp.float32), axis=0, keepdims=True
        )
        small_ref[0:1, columns] = terms / attn_gain_ref[:, columns]
        small_ref[2 : 2 + heads, columns] = beta_part[:heads]

    product(0)
    qkv_grads(0)
    product(1)
    qkv_grads(1)
    total.relay(0, 0)
    total.relay(1, 0)
    qkv_grads(2)
    qkv_grads(3)
    small_ref[1:2] = mlp_grad_ref[...]
    at = 2 + heads
    for tap in range(KW):
        lanes = pl.ds((tap % 2) * 3 * width, 3 * width)
        small_ref[at + tap // 2 : at + tap // 2 + 1, lanes] = conv_grad_ref[tap : tap + 1]
    small_ref[at : at + 1, 6 * width : 6 * width + DK] = gain_grad_ref[...]
    small_row.start()
    total.relay_back(0)
    qkv_sums.add_halves(0)
    total.relay(0, 1)
    total.relay(1, 1)
    small_row.finish()
    small = small_rows[0]
    for i in range(1, small_rows.shape[0]):
        small = small + small_rows[i]
    small_all_ref[line.core, line.place] = small
    for copy in small_seq:
        copy.start()
    total.relay_back(1)
    qkv_sum[...] = qkv_sums.total(0).astype(jnp.bfloat16).reshape(qkv_sum.shape)
    qkv_move.start()
    rows = grad_resid_ref.shape[0]

    def back(inner):
        own_span = pl.ds(pl.multiple_of(line.core * rows + inner.start, STEP), STEP)
        x = x_ref[own_span].astype(jnp.float32)
        input_grad_ref[own_span] = (
            grad_resid_ref[inner]
            + norm_back(x, norm_scale(x), attn_gain_ref[...], total.own_rows(inner))
        ).astype(jnp.bfloat16)

    for part in range(total.parts):
        total.wait_own(part)
        over_rows(total, part, back)
    swap = own_swap(line, input_grad_ref, rows, swap_sems)
    swap.start()
    for copy in small_seq:
        copy.wait()
    small_core.start()
    total.finish()
    o_sums.finish()
    qkv_sums.finish()
    for move in moves + [o_move, qkv_move]:
        move.finish()
    swap.wait()
    small_core.wait()


def in_vmem(count):
    return [pl.BlockSpec(memory_space=pltpu.VMEM)] * count


def run_forward(n1, qkv, beta, taps, aux, docs, gain, x, g, mlp_gain, weights):
    row_len, heads = n1.shape[0], qkv.shape[-1] // DK
    rows_axis, seqs, _, shard, _ = qkv.shape
    cores, (piece, model_width) = lax.axis_size("tp"), x.shape
    rows = piece // cores
    chunks, width, f32, b16 = row_len // CHUNK, heads * DK, jnp.float32, jnp.bfloat16
    units = weights[3].shape[0] // seqs
    outs = (
        ((row_len, 3 * width), b16),
        ((row_len, beta.shape[2]), f32),
        ((row_len, width), f32),
        ((row_len, width), b16),
        ((heads, chunks, CHUNK, CHUNK), f32),
        ((heads, chunks, DK, DK), f32),
        ((heads, chunks, CHUNK, DK), f32),
        ((rows_axis, seqs, width, shard), b16),
        ((rows, model_width), f32),
    )
    scratch = [
        pltpu.VMEM((PAD + CHUNK, 3 * width), f32),
        pltpu.VMEM((heads, DK, DK), f32),
        pltpu.VMEM((width, model_width), b16),
        pltpu.VMEM((rows, model_width), b16),
        pltpu.VMEM((beta.shape[2], model_width), b16),
    ]
    scratch = scratch + scatter_scratch(seqs, cores, rows, model_width) + [dma_sems(4)]
    scratch = scratch + [dma_sems(6, seqs, PARTS)] * 3 + exchange_sems() * 4
    *saved, o_full, resid, n2, g_full, gate, up, down = line_call(
        functools.partial(forward_kernel, heads), 5, "mixer_forward", outs, scratch,
        (n1, qkv, beta, taps, aux, docs, gain, x, mlp_gain),
        far_args=(g, *weights),
        far_outs=(
            ((seqs, cores, rows, model_width), b16),
            ((seqs, cores, rows, model_width), b16),
            ((rows_axis,) + weights[1].shape, b16),
            ((rows_axis,) + weights[2].shape, b16),
            ((rows_axis, seqs, units, shard), b16),
        ),
    )
    n2, g_full = n2.reshape(-1, model_width), g_full.reshape(-1, model_width)
    gate, up = gate.reshape(model_width, units), up.reshape(model_width, units)
    return saved, o_full, resid, n2, g_full, gate, up, down


def run_backward(grad, o_full, saved, taps, aux, docs, gain, extra, sums):
    row_len, heads = grad.shape[0], o_full.shape[2] // DK
    model_width = grad.shape[1]
    rows_axis, seqs, _, shard = o_full.shape
    cores = lax.axis_size("tp")
    width, f32, b16 = heads * DK, jnp.float32, jnp.bfloat16
    rows, span = row_len // (seqs * cores), model_width // rows_axis
    small = (4 + heads, model_width)
    outs = (((cores * rows, model_width), b16), ((cores, seqs) + small, f32))
    far_outs = (((seqs, shard, 3 * width), b16), ((seqs, shard, width), b16))
    qkv_buffers, qkv_sems = row_sum_scratch((rows_axis, 1, span, 3 * width))
    o_buffers, o_sems = row_sum_scratch((rows_axis, 1, span, width))
    scratch = [
        pltpu.VMEM((PAD + CHUNK, 3 * width), f32),
        pltpu.VMEM((KW - 1, CHUNK + PAD, 3 * width), f32),
        pltpu.VMEM((heads, DK, DK), f32),
        pltpu.VMEM((width, model_width), b16),
        pltpu.VMEM((saved[1].shape[1], model_width), b16),
        pltpu.VMEM((KW, 3 * width), f32),
        pltpu.VMEM((1, DK), f32),
        pltpu.VMEM((row_len, 3 * width), b16),
        pltpu.VMEM(saved[1].shape, b16),
        pltpu.VMEM(small, f32),
        pltpu.VMEM((rows_axis,) + small, f32),
        pltpu.VMEM((seqs, shard, 3 * width), b16),
        pltpu.VMEM((seqs, shard, width), b16),
    ]
    scratch = scratch + scatter_scratch(seqs, cores, rows, model_width) + qkv_buffers + o_buffers
    scratch = scratch + [dma_sems(6, seqs, PARTS), dma_sems(2)]
    scratch = scratch + pair_sems("seq", 3) + pair_sems("seq", 1) * 2 + pair_sems("row", 1)
    scratch = scratch + [dma_sems(seqs - 1)] * 2 + [dma_sems(2)] + o_sems + qkv_sems
    return line_call(
        functools.partial(backward_kernel, heads), 6, "mixer_backward", outs, scratch,
        (grad, o_full, *saved, taps, aux, docs, gain, *extra),
        far_args=(sums,),
        far_outs=far_outs + ((sums.shape[1:], b16),) * 3,
    )


def row_aux(docs):
    f32 = jnp.float32
    chunks = docs.reshape(-1, CHUNK)
    prior = jnp.concatenate([jnp.full((1,), -1, jnp.int32), chunks[:-1, -1]])
    padded = jnp.concatenate([jnp.full((KW - 1,), -1, jnp.int32), docs])
    columns = [
        docs,
        docs < DOCS,
        (chunks == prior[:, None]).reshape(-1),
        (chunks == chunks[:, -1:]).reshape(-1),
    ] + [padded[KW - 1 - tap : KW - 1 - tap + docs.shape[0]] == docs for tap in range(1, KW)]
    columns = [column.astype(f32) for column in columns]
    columns += [jnp.zeros_like(columns[0])] * (8 - len(columns))
    return jnp.stack(columns, axis=1), chunks.astype(f32)


def remote(source, target, send, recv, where):
    return pltpu.make_async_remote_copy(
        src_ref=source,
        dst_ref=target,
        send_sem=send,
        recv_sem=recv,
        device_id=where,
        device_id_type=pl.DeviceIdType.MESH,
    )


def greet(partners):
    barrier = pltpu.get_barrier_semaphore()
    for partner, there in partners:

        @pl.when(there)
        def _(partner=partner):
            pl.semaphore_signal(
                barrier, inc=1, device_id=partner, device_id_type=pl.DeviceIdType.MESH
            )

    pl.semaphore_wait(barrier, sum(there.astype(jnp.int32) for _, there in partners))


def around(axis):
    count, place = lax.axis_size(axis), lax.axis_index(axis)
    return [lax.rem(place + by, count) for by in range(1, count)]


def line_partners():
    count, place, core = lax.axis_size("seq"), lax.axis_index("seq"), lax.axis_index("tp")
    return [
        ({"seq": jnp.minimum(place + 1, count - 1)}, place < count - 1),
        ({"seq": jnp.maximum(place - 1, 0)}, place > 0),
        ({"tp": 1 - core}, core >= 0),
    ]


class Line:
    def __init__(self):
        self.count, self.place = lax.axis_size("seq"), lax.axis_index("seq")
        self.core = lax.axis_index("tp")
        self.other = 1 - self.core
        self.right = {"seq": jnp.minimum(self.place + 1, self.count - 1)}
        self.left = {"seq": jnp.maximum(self.place - 1, 0)}
        self.across = {"tp": self.other}


class Gather:
    def __init__(self, line, slots, own, sems):
        self.line, self.slots, self.own, self.sems = line, slots, own, sems
        self.parts = sems.shape[2]
        self.rows = slots.shape[2] // self.parts

    def span(self, part):
        return pl.ds(part * self.rows, self.rows)

    def copy(self, kind, seq, part, own=False):
        line = self.line
        send = {"right": 0, "left": 1, "across": 2}[kind]
        recv = 4 if kind == "across" else 3
        slot = self.slots.at[seq, line.core, self.span(part)]
        where = {"right": line.right, "left": line.left, "across": line.across}[kind]
        source = self.own.at[self.span(part)] if own else slot
        return remote(
            source, slot, self.sems.at[send, seq, part], self.sems.at[recv, seq, part], where
        )

    def own_copy(self, part):
        line = self.line
        return pltpu.make_async_copy(
            self.own.at[self.span(part)],
            self.slots.at[line.place, line.core, self.span(part)],
            self.sems.at[5, 0, part],
        )

    def forward(self, seq, part, right, left, own=False):
        line = self.line
        if right:

            @pl.when(line.place < line.count - 1)
            def _():
                self.copy("right", seq, part, own).start()

        if left:

            @pl.when(line.place > 0)
            def _():
                self.copy("left", seq, part, own).start()

        self.copy("across", seq, part, own).start()

    def phase(self, by, part):
        line = self.line
        if by == 0:
            self.forward(line.place, part, True, True, own=True)
            self.own_copy(part).start()
            return

        @pl.when(line.place - by >= 0)
        def _():
            self.copy("right", line.place - by, part).wait_recv()
            self.forward(line.place - by, part, True, False)

        @pl.when(line.place + by < line.count)
        def _():
            self.copy("left", line.place + by, part).wait_recv()
            self.forward(line.place + by, part, False, True)

    def phases(self, by):
        for part in range(self.parts):
            self.phase(by, part)

    def finish(self):
        line = self.line
        for part in range(self.parts):
            self.own_copy(part).wait()
        for seq in range(line.count):
            for part in range(self.parts):

                @pl.when((line.place >= seq) & (line.place < line.count - 1))
                def _():
                    self.copy("right", seq, part).wait_send()

                @pl.when((line.place <= seq) & (line.place > 0))
                def _():
                    self.copy("left", seq, part).wait_send()

                self.copy("across", seq, part).wait()


class Scatter:
    def __init__(self, line, blocks, came, across, sems):
        self.line, self.blocks, self.came, self.across, self.sems = line, blocks, came, across, sems
        self.parts = sems.shape[2]
        self.rows = blocks.shape[2] // self.parts

    def span(self, part):
        return pl.ds(part * self.rows, self.rows)

    def over(self, seq, part):
        line, span = self.line, self.span(part)
        return remote(
            self.blocks.at[seq, line.other, span],
            self.across.at[seq, span],
            self.sems.at[0, seq, part],
            self.sems.at[1, seq, part],
            line.across,
        )

    def along(self, kind, seq, part):
        line, span = self.line, self.span(part)
        way = {"right": 0, "left": 1}[kind]
        slot = seq if way == 0 else jnp.where(seq == line.place - 1, line.count, seq)
        return remote(
            self.blocks.at[seq, line.core, span],
            self.came.at[slot, span],
            self.sems.at[2, seq, part],
            self.sems.at[3 + way, seq, part],
            line.right if way == 0 else line.left,
        )

    def nears(self, k):
        for part in range(self.parts):
            self.near(k, part)

    def fars(self, k):
        for part in range(self.parts):
            self.far(k, part)

    def product(self, left_ref, right_ref, part, order=1, tile=512, right_tile=None):
        seqs, cores, _, width = self.blocks.shape
        span = self.span(part)
        left = left_ref
        if len(left_ref.shape) == 3:
            left = left_ref[:, span].reshape(seqs * cores * self.rows, -1)

        def columns(t, _):
            across = pl.ds(pl.multiple_of(t * tile, tile), tile)
            if right_tile is not None:
                total = right_tile(left, t, across)
            elif order == 1:
                total = mul(left, right_ref[across], (1, 1))
            else:
                total = mul(left, right_ref[:, across], (1, 0))
            self.blocks[:, :, span, across] = total.astype(jnp.bfloat16).reshape(
                seqs, cores, self.rows, tile
            )
            return 0

        lax.fori_loop(0, width // tile, columns, 0)
        self.offer(part)

    def offer(self, part):
        for k in range(self.blocks.shape[0]):
            self.over(self.target(k), part).start()

    def pass_on(self, kind, seq, part):
        line, span = self.line, self.span(part)
        f32 = jnp.float32
        first = line.place == (0 if kind == "right" else line.count - 1)
        way = {"right": 0, "left": 1}[kind]
        self.over(seq, part).wait_recv()
        total = self.blocks[seq, line.core, span].astype(f32)
        total = total + self.across[seq, span].astype(f32)

        @pl.when(first)
        def _():
            self.blocks[seq, line.core, span] = total.astype(jnp.bfloat16)

        @pl.when(jnp.logical_not(first))
        def _():
            self.along(kind, seq, part).wait_recv()
            self.blocks[seq, line.core, span] = (
                total + self.came[seq, span].astype(f32)
            ).astype(jnp.bfloat16)

        self.along(kind, seq, part).start()

    def target(self, k):
        line = self.line
        return jnp.where(line.place < line.count // 2, line.count - 1 - k, k)

    def edge(self):
        return (self.line.place == 0) | (self.line.place == self.line.count - 1)

    def near(self, k, part):
        line = self.line
        low = line.place < line.count // 2

        @pl.when(low & (line.count - 1 - k > line.place))
        def _():
            self.pass_on("right", line.count - 1 - k, part)

        @pl.when(jnp.logical_not(low) & (k < line.place))
        def _():
            self.pass_on("left", k, part)

    def far(self, k, part):
        line = self.line
        low = line.place < line.count // 2

        @pl.when(low & (k < line.place))
        def _():
            self.pass_on("left", k, part)

        @pl.when(jnp.logical_not(low) & (line.count - 1 - k > line.place))
        def _():
            self.pass_on("right", line.count - 1 - k, part)

    def start_edges(self, part):
        @pl.when(self.edge())
        def _():
            for k in range(self.line.count - 1):
                self.near(k, part)

    def relay(self, k, part):
        @pl.when(jnp.logical_not(self.edge()))
        def _():
            self.near(k, part)

    def relay_back(self, part):
        @pl.when(jnp.logical_not(self.edge()))
        def _():
            for k in range(self.line.count - 1):
                self.far(k, part)

    def wait_own(self, part):
        line = self.line

        @pl.when(line.place > 0)
        def _():
            self.along("right", line.place, part).wait_recv()

        @pl.when(line.place < line.count - 1)
        def _():
            self.along("left", line.place, part).wait_recv()

        self.over(line.place, part).wait_recv()

    def own_rows(self, rows):
        line = self.line
        f32 = jnp.float32
        total = self.blocks[line.place, line.core, rows].astype(f32)
        total = total + self.across[line.place, rows].astype(f32)
        from_left = self.came[line.place, rows].astype(f32)
        from_right = self.came[line.count, rows].astype(f32)
        total = total + jnp.where(line.place > 0, from_left, 0.0)
        return total + jnp.where(line.place < line.count - 1, from_right, 0.0)

    def finish(self):
        line = self.line
        for seq in range(line.count):
            for part in range(self.parts):
                self.over(seq, part).wait_send()

                @pl.when(line.place != seq)
                def _():
                    self.along("right", seq, part).wait_send()


class Exchange:
    def __init__(self, line, source, target, sems):
        self.line, self.source, self.target = line, source, target
        self.send, self.recv, self.send_row, self.recv_row = sems
        self.row = lax.axis_index("row")
        self.seq_others, self.row_others = around("seq"), around("row")

    def spread(self, i):
        other = self.seq_others[i]
        return remote(
            self.source(other),
            self.target.at[self.row, self.line.place],
            self.send.at[i],
            self.recv.at[i],
            {"seq": other},
        )

    def share(self, i, j):
        line = self.line
        came_from = lax.rem(line.place + line.count - i, line.count)
        slot = self.target.at[self.row, came_from]
        source = self.source(line.place) if i == 0 else slot
        return remote(
            source,
            slot,
            self.send_row.at[i, j],
            self.recv_row.at[i, j],
            {"row": self.row_others[j]},
        )

    def start(self):
        for i in range(len(self.seq_others)):
            self.spread(i).start()

    def share_own(self):
        for j in range(len(self.row_others)):
            self.share(0, j).start()

    def share_came(self, i):
        self.spread(i - 1).wait_recv()
        for j in range(len(self.row_others)):
            self.share(i, j).start()

    def finish(self):
        for i in range(len(self.seq_others)):
            self.spread(i).wait_send()
        for i in range(len(self.seq_others) + 1):
            for j in range(len(self.row_others)):
                self.share(i, j).wait()


class Share:
    def __init__(self, axis, source, target, sems, own_sem):
        self.axis, self.source, self.target = axis, source, target
        self.send, self.recv = sems
        self.others = around(axis)
        self.own = pltpu.make_async_copy(source, target.at[lax.axis_index(axis)], own_sem)

    def copy(self, i):
        return remote(
            self.source,
            self.target.at[lax.axis_index(self.axis)],
            self.send.at[i],
            self.recv.at[i],
            {self.axis: self.others[i]},
        )

    def start(self):
        for i in range(len(self.others)):
            self.copy(i).start()
        self.own.start()

    def finish(self):
        for i in range(len(self.others)):
            self.copy(i).wait()
        self.own.wait()


class Swap:
    def __init__(self, axis, source, target, sems, own_sem):
        self.axis, self.source, self.target = axis, source, target
        self.send, self.recv = sems
        self.others = around(axis)
        place = lax.axis_index(axis)
        self.own = pltpu.make_async_copy(source.at[place], target.at[place], own_sem)

    def copy(self, i):
        return remote(
            self.source.at[self.others[i]],
            self.target.at[lax.axis_index(self.axis)],
            self.send.at[i],
            self.recv.at[i],
            {self.axis: self.others[i]},
        )

    def start(self):
        for i in range(len(self.others)):
            self.copy(i).start()
        self.own.start()

    def finish(self):
        for i in range(len(self.others)):
            self.copy(i).wait()
        self.own.wait()


class RowSum:
    def __init__(self, blocks, halves, came, sems):
        self.blocks, self.halves, self.came = blocks, halves, came
        self.row = lax.axis_index("row")
        even_x, even_y = lax.rem(self.row, 2) == 0, self.row < 2
        x_step, y_step = jnp.where(even_x, 1, -1), jnp.where(even_y, 2, -2)
        self.near = (self.row + x_step, self.row + y_step)
        self.far = self.row + x_step + y_step
        self.half = blocks.shape[2] // 2
        self.send_half, self.recv_half, self.send, self.recv = sems

    def rows(self, i):
        return pl.ds(i * self.half, self.half)

    def half_copy(self, i, m):
        return remote(
            self.blocks.at[self.far, m, self.rows(i)],
            self.halves.at[i, m],
            self.send_half.at[i, m],
            self.recv_half.at[i, m],
            {"row": self.near[i]},
        )

    def copy(self, i, j, m):
        return remote(
            self.blocks.at[self.near[i], m, self.rows(j)],
            self.came.at[i, m, self.rows(j)],
            self.send.at[i, j, m],
            self.recv.at[i, j, m],
            {"row": self.near[i]},
        )

    def start_far(self, m):
        for i in range(2):
            self.half_copy(i, m).start()

    def start_near(self, i, m):
        self.copy(i, i, m).start()

    def add_half(self, i, m):
        j = 1 - i
        self.half_copy(j, m).wait_recv()
        rows = self.rows(j)
        total = self.blocks[self.near[i], m, rows].astype(jnp.float32)
        total = total + self.halves[j, m].astype(jnp.float32)
        self.blocks[self.near[i], m, rows] = total.astype(jnp.bfloat16)
        self.copy(i, j, m).start()

    def start(self, step, m):
        if step == 0:
            self.start_far(m)
        elif step < 3:
            self.start_near(step - 1, m)

    def order(self):
        return (self.far, self.near[0], self.near[1], self.row)

    def add_halves(self, m):
        for i in range(2):
            self.add_half(i, m)

    def total(self, m):
        for i in range(2):
            for j in range(2):
                self.copy(i, j, m).wait_recv()
        total = self.blocks[self.row, m].astype(jnp.float32)
        for i in range(2):
            total = total + self.came[i, m].astype(jnp.float32)
        return total

    def finish(self):
        for m in range(self.blocks.shape[1]):
            for i in range(2):
                self.half_copy(i, m).wait_send()
                for j in range(2):
                    self.copy(i, j, m).wait_send()


def row_sum_scratch(shape):
    b16 = jnp.bfloat16
    _, count, rows, width = shape
    return [
        pltpu.VMEM(shape, b16),
        pltpu.VMEM((2, count, rows // 2, width), b16),
        pltpu.VMEM((2, count, rows, width), b16),
    ], [dma_sems(2, count), dma_sems(2, count), dma_sems(2, 2, count), dma_sems(2, 2, count)]


def pair_sems(axis, count):
    return [dma_sems(lax.axis_size(axis) - 1)] * (2 * count) + [dma_sems(count)]


def moves_of(kind, axis, sources, targets, sems):
    return [
        kind(axis, source, target, sems[2 * i : 2 * i + 2], sems[-1].at[i])
        for i, (source, target) in enumerate(zip(sources, targets))
    ]


def along_axis(axis):
    return [({axis: other}, other >= 0) for other in around(axis)]


def exchange_sems():
    seqs, rows = lax.axis_size("seq"), lax.axis_size("row")
    return [
        dma_sems(seqs - 1),
        dma_sems(seqs - 1),
        dma_sems(seqs, rows - 1),
        dma_sems(seqs, rows - 1),
    ]


def exchange_partners(line):
    return [({"seq": other}, other >= 0) for other in around("seq")] + [
        ({"row": other}, other >= 0) for other in around("row")
    ]


STEP = 32


def over_rows(total, part, body):
    def step(i, _):
        body(pl.ds(pl.multiple_of(part * total.rows + i * STEP, STEP), STEP))
        return 0

    lax.fori_loop(0, total.rows // STEP, step, 0)


def side_by_side(blocks_ref, out_ref):
    outer, inner, _, width = blocks_ref.shape
    for i in range(outer):
        for j in range(inner):
            out_ref[:, (i * inner + j) * width : (i * inner + j + 1) * width] = blocks_ref[i, j]


def dma_sems(*shape):
    return pltpu.SemaphoreType.DMA(shape)


class Staged:
    def __init__(self, inputs, outputs, in_sems, out_sems):
        self.loads = [
            (near, pltpu.make_async_copy(far, near, in_sems.at[i]))
            for i, (far, near) in enumerate(inputs)
        ]
        self.stores = [
            (near, pltpu.make_async_copy(near, far, out_sems.at[i]))
            for i, (far, near) in enumerate(outputs)
        ]
        self.stored = []
        for _, copy in self.loads:
            copy.start()

    def need(self, *refs):
        for ref in refs:
            (at,) = [i for i, (near, _) in enumerate(self.loads) if near is ref]
            self.loads.pop(at)[1].wait()

    def store(self, *refs):
        for ref in refs:
            (at,) = [i for i, (near, _) in enumerate(self.stores) if near is ref]
            copy = self.stores.pop(at)[1]
            copy.start()
            self.stored.append(copy)

    def finish(self):
        self.need(*[near for near, _ in self.loads])
        self.store(*[near for near, _ in self.stores])
        for copy in self.stored:
            copy.wait()


def line_call(kernel, collective_id, name, outs, scratch, args, limit=63, far_args=(), far_outs=()):
    counts = [len(args), len(far_args), len(outs), len(far_outs), len(args), len(outs)]

    def body(*refs):
        groups, at = [], 0
        for count in counts:
            groups.append(refs[at : at + count])
            at += count
        near_in, near_out, in_sems, out_sems, *rest = *groups[4:], *refs[at:]
        staged = Staged(
            list(zip(groups[0], near_in)), list(zip(groups[2], near_out)), in_sems, out_sems
        )
        kernel(staged, *near_in, *groups[1], *near_out, *groups[3], *rest)
        staged.finish()

    far = pl.BlockSpec(memory_space=pl.ANY)
    stages = [pltpu.VMEM(arg.shape, arg.dtype) for arg in args]
    stages += [pltpu.VMEM(*out) for out in outs]
    stages += [dma_sems(max(len(args), 1)), dma_sems(max(len(outs), 1))]
    return pl.pallas_call(
        body,
        out_shape=[jax.ShapeDtypeStruct(*out) for out in (*outs, *far_outs)],
        in_specs=[far] * (len(args) + len(far_args)),
        out_specs=[far] * (len(outs) + len(far_outs)),
        scratch_shapes=stages + scratch,
        compiler_params=pltpu.CompilerParams(
            collective_id=collective_id,
            has_side_effects=collective_id is not None,
            vmem_limit_bytes=limit * 1024 * 1024,
        ),
        name=name,
    )(*args, *far_args)


def scatter_scratch(seqs, cores, rows, width):
    b16 = jnp.bfloat16
    return [
        pltpu.VMEM((seqs, cores, rows, width), b16),
        pltpu.VMEM((seqs + 1, rows, width), b16),
        pltpu.VMEM((seqs, rows, width), b16),
    ]


PARTS = 2


def mlp_grad_kernel(
    staged, gate_ref, up_ref, resid_ref, gain_ref,
    down_full_ref, n2_ref, g_full_ref,
    grad_resid_ref, gain_grad_ref, result_ref,
    grad_attn_ref, sum_ref,
    grad_gate_ref, grad_up_ref, hidden_ref, down_ref, inner, g_own, attn_own, blocks, came, across, out_blocks, out_came, out_across, tokens, parts, halves, parts_came,
    sum_sems, out_sems, attn_sems, swap_sems, inner_sems, token_sems, own_sems, down_sems, *sems,
):
    line = Line()
    rows_axis, pieces, _, shard = down_full_ref.shape
    down_loads = [
        pltpu.make_async_copy(
            down_full_ref.at[i, j],
            down_ref.at[:, pl.ds((i * pieces + j) * shard, shard)],
            down_sems.at[i, j],
        )
        for i in range(rows_axis)
        for j in range(pieces)
    ]
    for copy in down_loads:
        copy.start()
    rows = resid_ref.shape[0]
    g_load = pltpu.make_async_copy(
        g_full_ref.at[line.place * lax.axis_size("tp") + line.core], g_own, own_sems.at[3]
    )
    g_load.start()
    total = Scatter(line, blocks, came, across, sum_sems)
    result = Scatter(line, out_blocks, out_came, out_across, out_sems)
    attn = Gather(line, grad_attn_ref, attn_own, attn_sems)
    sums = RowSum(parts, halves, parts_came, sems)
    units = hidden_ref.shape[2]
    group = inner.shape[1]
    groups = hidden_ref.shape[0] // group
    steps = total.parts * groups

    def inner_copy(i, step):
        part, at = step // groups, lax.rem(step, groups) * group
        span = pl.ds(pl.multiple_of(part * total.rows, total.rows), total.rows)
        ref = (n2_ref, g_full_ref)[i]
        return pltpu.make_async_copy(
            ref.at[pl.ds(at, group), span], inner.at[i], inner_sems.at[i]
        )

    for i in range(2):
        inner_copy(i, 0).start()
    greet(line_partners() + along_axis("row"))

    def ahead(i, step):
        @pl.when(step + 1 < steps)
        def _():
            inner_copy(i, step + 1).start()

    def mlp(step, _):
        part, at = step // groups, lax.rem(step, groups) * group
        span = pl.ds(pl.multiple_of(part * total.rows, total.rows), total.rows)
        width = n2_ref.shape[2]
        inner_copy(0, step).wait()
        n2 = inner[0].reshape(-1, width)
        gate = mul(n2, gate_ref[...], (1, 0))
        up = mul(n2, up_ref[...], (1, 0))
        ahead(0, step)
        inner_copy(1, step).wait()
        grad_hidden = mul(inner[1].reshape(-1, width), down_ref[...], (1, 1))
        ahead(1, step)
        sig = sigmoid(gate)
        act = gate * sig
        grad_gate = grad_hidden * up * sig * (1.0 + gate * (1.0 - sig))
        for ref, value in (
            (hidden_ref, act * up),
            (grad_up_ref, grad_hidden * act),
            (grad_gate_ref, grad_gate),
        ):
            ref[pl.ds(at, group), span] = value.astype(jnp.bfloat16).reshape(
                group, total.rows, units
            )
        return 0

    orders = sums.order()
    block_width = tokens.shape[3]

    def token_copy(i, step):
        columns = pl.ds(pl.multiple_of(orders[step] * block_width, block_width), block_width)
        ref = (g_full_ref, n2_ref)[i]
        return pltpu.make_async_copy(ref.at[:, :, columns], tokens.at[i], token_sems.at[i])

    for i in range(2):
        token_copy(i, 0).start()

    def product(part):
        left_up = grad_up_ref[:, total.span(part)].reshape(-1, units)

        def right_tile(left, t, columns):
            return mul(left, gate_ref[columns], (1, 1)) + mul(left_up, up_ref[columns], (1, 1))

        total.product(grad_gate_ref, None, part, right_tile=right_tile)
        total.start_edges(part)

    def weight_grads(step):
        to = orders[step]
        for m, (i, ref) in enumerate(((0, hidden_ref), (1, grad_gate_ref), (1, grad_up_ref))):
            if m < 2:
                token_copy(i, step).wait()
            part = mul(
                tokens[i].reshape(-1, block_width), ref[...].reshape(-1, units), (0, 0)
            )
            parts[to, m] = part.astype(jnp.bfloat16)
            if m != 1 and step + 1 < len(orders):
                token_copy(i, step + 1).start()
            sums.start(step, m)

    staged.need(gate_ref, up_ref)
    for copy in down_loads:
        copy.wait()
    lax.fori_loop(0, groups, mlp, 0)
    product(0)
    lax.fori_loop(groups, steps, mlp, 0)
    weight_grads(0)
    for part in range(1, total.parts):
        product(part)
    total.relay(0, 0)
    total.relay(1, 0)
    weight_grads(1)
    total.relay_back(0)
    weight_grads(2)
    total.relay(0, 1)
    total.relay(1, 1)
    weight_grads(3)
    total.relay_back(1)
    staged.need(resid_ref, gain_ref)
    g_load.wait()
    gain_grad_ref[...] = jnp.zeros_like(gain_grad_ref)

    def back(span):
        resid = resid_ref[span]
        grad_two = total.own_rows(span)
        scale = norm_scale(resid)
        gain_grad_ref[...] += jnp.sum(grad_two * resid * scale, axis=0, keepdims=True)
        grad = g_own[span].astype(jnp.float32) + norm_back(
            resid, scale, gain_ref[...], grad_two
        )
        grad_resid_ref[span] = grad
        attn_own[span] = grad.astype(jnp.bfloat16)

    for part in range(total.parts):
        total.wait_own(part)
        over_rows(total, part, back)
        attn.phase(0, part)
    staged.store(grad_resid_ref, gain_grad_ref)
    for part in range(result.parts):
        result.product(hidden_ref, down_ref, part, order=0)
    for m in range(parts.shape[1]):
        sums.add_halves(m)
    for k in range(1, line.count):
        attn.phases(k)
        result.nears(k - 1)
    for k in range(line.count - 1):
        result.fars(k)

    def finish(span):
        own_span = pl.ds(pl.multiple_of(line.core * rows + span.start, STEP), STEP)
        result_ref[own_span] = (resid_ref[span] + result.own_rows(span)).astype(jnp.bfloat16)

    for part in range(result.parts):
        result.wait_own(part)
        over_rows(result, part, finish)
    swap = own_swap(line, result_ref, rows, swap_sems)
    swap.start()
    own = []
    for m in range(parts.shape[1]):
        parts[sums.row, m] = sums.total(m).astype(jnp.bfloat16)
        own.append(
            pltpu.make_async_copy(parts.at[sums.row, m], sum_ref.at[m], own_sems.at[m])
        )
        own[m].start()
    total.finish()
    result.finish()
    attn.finish()
    swap.wait()
    sums.finish()
    for copy in own:
        copy.wait()


def own_swap(line, ref, rows, sems):
    own = ref.at[pl.ds(pl.multiple_of(line.core * rows, rows), rows)]
    return remote(own, own, sems.at[0], sems.at[1], line.across)


def run_mlp_grad(gate, up, down, resid, gain, n2, g_full):
    seqs, cores, (rows, width) = lax.axis_size("seq"), lax.axis_size("tp"), resid.shape
    rows_axis = lax.axis_size("row")
    piece, b16, f32 = rows * cores, jnp.bfloat16, jnp.float32
    units, span, blocks = gate.shape[1], width // rows_axis, seqs * cores
    outs = (((rows, width), f32), ((1, width), f32), ((piece, width), b16))
    sum_buffers, sum_sems = row_sum_scratch((rows_axis, 3, span, units))
    scratch = [pltpu.VMEM((blocks, rows, units), b16)] * 3
    scratch = scratch + [
        pltpu.VMEM((units, width), b16),
        pltpu.VMEM((2, blocks // 2, rows // PARTS, width), b16),
        pltpu.VMEM((rows, width), b16),
        pltpu.VMEM((rows, width), b16),
    ]
    scratch = scratch + scatter_scratch(seqs, cores, rows, width) * 2
    scratch = scratch + [pltpu.VMEM((2, blocks, rows, span), b16)] + sum_buffers
    scratch = scratch + [dma_sems(6, seqs, PARTS)] * 3 + [dma_sems(2)]
    scratch = scratch + [dma_sems(2)] * 2 + [dma_sems(4), dma_sems(rows_axis, seqs)]
    scratch = scratch + sum_sems
    grad_resid, gain_grad, result, grad_attn, sums = line_call(
        mlp_grad_kernel, 2, "mlp_grad", outs, scratch,
        (gate, up, resid, gain),
        far_args=(down, n2.reshape(blocks, rows, width), g_full.reshape(blocks, rows, width)),
        far_outs=(((seqs, cores, rows, width), b16), ((3, span, units), b16)),
    )
    return grad_resid, grad_attn.reshape(-1, width), gain_grad, result, sums


def unit_square(size):
    down = lax.broadcasted_iota(jnp.int32, (size, size), 0)
    along = lax.broadcasted_iota(jnp.int32, (size, size), 1)
    return jnp.where(down == along, 1.0, 0.0).astype(jnp.bfloat16)


def normed_kernel(
    staged, x_ref, gain_ref, beta_weight_ref, gate_up_ref, weight_ref,
    gate_parts_ref, up_parts_ref, n1_ref, qkv_ref, beta_full_ref, n1_own, beta_ref, n1_sems,
    own_sems, *sems,
):
    line = Line()
    row = lax.axis_index("row")
    greet(exchange_partners(line) + [(line.across, line.core >= 0)])
    width = qkv_ref.shape[-1]

    def columns(seq):
        return weight_ref.at[:, :, pl.ds(pl.multiple_of(seq * width, width), width)]

    moves = [
        Exchange(line, columns, qkv_ref, sems[:4]),
        Exchange(line, lambda seq: beta_ref.at[seq], beta_full_ref, sems[4:]),
    ]
    moves[0].start()
    staged.need(beta_weight_ref)
    beta = mul(beta_weight_ref[...], unit_square(beta_weight_ref.shape[0]), (0, 0))
    heads = beta.shape[0] // line.count
    empty = jnp.zeros((beta_ref.shape[1] - heads, beta.shape[1]), jnp.float32)
    for seq in range(line.count):
        own_heads = beta[seq * heads : (seq + 1) * heads]
        beta_ref[seq] = jnp.concatenate([own_heads, empty], axis=0).astype(jnp.bfloat16)
    moves[1].start()
    own = [
        pltpu.make_async_copy(
            move.source(line.place), move.target.at[row, line.place], own_sems.at[i]
        )
        for i, move in enumerate(moves)
    ]
    for copy in own:
        copy.start()
    rows = n1_ref.shape[2]
    n1 = Gather(line, n1_ref, n1_own, n1_sems)
    staged.need(x_ref, gain_ref)

    def normed(span):
        x_span = pl.ds(pl.multiple_of(line.core * rows + span.start, STEP), STEP)
        x = x_ref[x_span].astype(jnp.float32)
        n1_own[span] = (x * norm_scale(x) * gain_ref[...]).astype(jnp.bfloat16)

    for part in range(n1.parts):
        over_rows(n1, part, normed)
        n1.phase(0, part)
    for move in moves:
        move.share_own()
    staged.need(gate_up_ref)
    units = gate_parts_ref.shape[2]
    for i, ref in enumerate((gate_parts_ref, up_parts_ref)):
        weight = gate_up_ref[i].astype(jnp.float32)
        for seq in range(line.count):
            ref[seq] = weight[:, seq * units : (seq + 1) * units].astype(jnp.bfloat16)
    staged.store(gate_parts_ref, up_parts_ref)
    for k in range(1, line.count):
        for move in moves:
            move.share_came(k)
        n1.phases(k)
    for move in moves:
        move.finish()
    for copy in own:
        copy.wait()
    n1.finish()


def run_normed(x, gain, weight, beta, gate_up):
    rows_axis, seqs, cores = (lax.axis_size(axis) for axis in ("row", "seq", "tp"))
    piece, width = x.shape
    shard, units = gate_up.shape[1], gate_up.shape[2] // seqs
    b16 = jnp.bfloat16
    outs = (((seqs, shard, units), b16),) * 2
    far_outs = (
        ((seqs, cores, piece // cores, width), b16),
        ((rows_axis, seqs) + weight.shape[:2] + (weight.shape[2] // seqs,), b16),
        ((rows_axis, seqs, 16, shard), b16),
    )
    gate, up, n1, qkv, beta_full = line_call(
        normed_kernel, 4, "norm_gather", outs,
        [
            pltpu.VMEM((piece // cores, width), b16),
            pltpu.VMEM((seqs, 16, shard), b16),
            dma_sems(6, seqs, PARTS),
            dma_sems(2),
        ]
        + exchange_sems() * 2,
        (x, gain, beta, gate_up),
        far_args=(weight,),
        far_outs=far_outs,
    )
    return gate, up, n1.reshape(-1, width), qkv, beta_full


def finish_kernel(
    staged, small_ref, qkv_ref, o_ref, gate_ref, up_ref, down_ref, result_ref, input_grad_ref,
    attn_gain_ref, mlp_gain_ref, out_gain_ref, conv_ref, qkv_out, o_out, gate_up_out, down_out,
    beta_out, result_out, input_grad_out,
):
    f32 = jnp.float32
    cores, seqs, _, _ = small_ref.shape
    _, shard, width3 = qkv_ref.shape
    width, units = width3 // 3, gate_ref.shape[2]
    heads = width // DK
    unit = unit_square(shard)
    for i, ref in enumerate((gate_ref, up_ref)):
        staged.need(ref)
        gate_up_out[i] = jnp.concatenate([ref[seq].astype(f32) for seq in range(seqs)], axis=1)
    staged.store(gate_up_out)
    staged.need(down_ref, o_ref)
    for seq in range(seqs):
        down_out[seq * units : (seq + 1) * units] = mul(down_ref[seq], unit, (0, 0))
        o_out[seq * width : (seq + 1) * width] = mul(o_ref[seq], unit, (0, 0))
    staged.store(down_out, o_out)
    staged.need(qkv_ref)
    for seq in range(seqs):
        for c in range(3):
            qkv_out[c, :, seq * width : (seq + 1) * width] = qkv_ref[
                seq, :, c * width : (c + 1) * width
            ].astype(f32)
    staged.store(qkv_out)
    staged.need(result_ref, input_grad_ref)
    result_out[...] = result_ref[...]
    input_grad_out[...] = input_grad_ref[...]
    staged.store(result_out, input_grad_out)
    staged.need(small_ref)
    at = 2 + heads
    for ref, rows, lanes in (
        (attn_gain_ref, slice(0, 1), slice(None)),
        (mlp_gain_ref, slice(1, 2), slice(None)),
        (out_gain_ref, slice(at, at + 1), slice(2 * width3, 2 * width3 + DK)),
    ):
        total = small_ref[0, 0, rows, lanes]
        for i in range(1, cores * seqs):
            total = total + small_ref[i // seqs, i % seqs, rows, lanes]
        ref[...] = total
    for core in range(cores):
        for seq in range(seqs):
            for c in range(3):
                for tap in range(KW):
                    row, lane = at + tap // 2, (tap % 2) * width3 + c * width
                    to = (core * seqs + seq) * width
                    conv_ref[c, tap : tap + 1, to : to + width] = small_ref[
                        core, seq, row : row + 1, lane : lane + width
                    ]
    block = lax.axis_index("row") * seqs + lax.axis_index("seq")
    columns = pl.ds(pl.multiple_of(block * shard, shard), shard)
    beta = jnp.concatenate(
        [small_ref[lax.axis_index("tp"), seq, 2 : 2 + heads, columns] for seq in range(seqs)], axis=0
    )
    beta_out[...] = fine(unit_square(shard).astype(f32), beta, (1, 1))


def run_finish(small, qkv, o, gate, up, down, result, input_grad):
    f32 = jnp.float32
    cores, seqs, _, model_width = small.shape
    _, shard, width3 = qkv.shape
    units = gate.shape[2]
    shapes = (
        (1, model_width),
        (1, model_width),
        (1, DK),
        (3, KW, model_width),
        (3, shard, seqs * width3 // 3),
        (seqs * width3 // 3, shard),
        (2, shard, seqs * units),
        (seqs * units, shard),
        (shard, seqs * width3 // (3 * DK)),
    )
    return line_call(
        finish_kernel, None, "finish",
        [(shape, f32) for shape in shapes] + [(result.shape, result.dtype)] * 2, [],
        (small, qkv, o, gate, up, down, result, input_grad),
    )


def local_heads(
    block_input,
    grad_out,
    doc_lengths,
    attn_gain,
    mlp_gain,
    out_gain,
    conv_weight,
    qkv_weight,
    beta_weight,
    o_weight,
    gate_up_weight,
    down_weight,
):
    tok_rows, model_width = block_input.shape[1:]
    pieces, cores = lax.axis_size("seq"), lax.axis_size("tp")
    piece, core = lax.axis_index("seq"), lax.axis_index("tp")
    row_len = pieces * tok_rows
    shard_rows = qkv_weight.shape[1]
    width = qkv_weight.shape[2] // pieces
    heads = width // DK
    units = gate_up_weight.shape[2] // pieces
    f32, b16 = jnp.float32, jnp.bfloat16

    x_piece, g_piece = block_input[0], grad_out[0]
    gate_parts, up_parts, normed_one, qkv_full, beta_full = run_normed(
        x_piece, attn_gain[None], qkv_weight, beta_weight, gate_up_weight
    )

    ends = jnp.cumsum(doc_lengths[0])
    places = jnp.arange(row_len, dtype=jnp.int32)
    docs = jnp.sum((places[:, None] >= ends[None, :]).astype(jnp.int32), axis=1)
    aux, doc_rows = row_aux(docs)
    gain_row = out_gain[None]
    taps = lax.dynamic_slice_in_dim(conv_weight, piece * width, width, axis=2)
    taps = taps.transpose(1, 0, 2).reshape(KW, 3 * width)

    saved, o_full, resid, normed_two, g_full, gate_full, up_full, down_full = run_forward(
        normed_one, qkv_full, beta_full, taps, aux, doc_rows, gain_row,
        x_piece, g_piece, mlp_gain[None],
        (o_weight, gate_parts, up_parts, down_weight),
    )
    proj, logit, mixed, normed_mix, inverse, states, written = saved
    grad_resid, grad_attn, mlp_gain_part, result, sums = run_mlp_grad(
        gate_full, up_full, down_full, resid, mlp_gain[None], normed_two, g_full
    )
    input_grad, small, qkv_sum, o_sum, down_sum, gate_sum, up_sum = run_backward(
        grad_attn,
        o_full,
        (proj, logit, mixed, inverse, states, written),
        taps,
        aux,
        doc_rows,
        gain_row,
        (
            normed_mix, normed_one, qkv_full, beta_full, attn_gain[None], mlp_gain_part,
            x_piece, grad_resid,
        ),
        sums.reshape(3, pieces, shard_rows, units),
    )
    (
        attn_gain_grad, mlp_gain_grad, out_gain_grad, conv_grad, qkv_grad, o_grad, gate_up_grad,
        down_grad, beta_grad, result, input_grad,
    ) = run_finish(small, qkv_sum, o_sum, gate_sum, up_sum, down_sum, result, input_grad)
    return (
        result[None],
        input_grad[None],
        attn_gain_grad[0],
        mlp_gain_grad[0],
        out_gain_grad[0],
        conv_grad,
        qkv_grad,
        beta_grad,
        o_grad,
        gate_up_grad,
        down_grad,
    )


def splits_heads(mesh, heads=16, units=5632):
    return (
        mesh.shape["tp"] == 2
        and heads % (mesh.shape["seq"] * 2) == 0
        and units % (mesh.shape["seq"] * 2) == 0
    )


def solution(mesh):
    in_specs = (
        P("row", "seq", None),
        P("row", "seq", None),
        P("row", None),
        P(),
        P(),
        P(),
        P(None, None, "tp"),
        P(None, ("row", "seq"), "tp"),
        P(("row", "seq"), "tp"),
        P("tp", ("row", "seq")),
        P(None, ("row", "seq"), "tp"),
        P("tp", ("row", "seq")),
    )
    out_specs = (
        P("row", "seq", None),
        P("row", "seq", None),
        P(),
        P(),
        P(),
        P(),
        P(None, ("row", "seq"), "tp"),
        P(("row", "seq"), "tp"),
        P("tp", ("row", "seq")),
        P(None, ("row", "seq"), "tp"),
        P("tp", ("row", "seq")),
    )
    local = local_heads if splits_heads(mesh) else local_pieces
    return jax.shard_map(local, mesh=mesh, in_specs=in_specs, out_specs=out_specs, check_vma=False)
```

```python
import functools

import jax
import jax.numpy as jnp
from jax import lax
from jax.experimental import pallas as pl
from jax.experimental.pallas import tpu as pltpu
from jax.sharding import PartitionSpec as P

DK = 128
KW = 4
GROUP = 64
DOCS = 8


eps = 1e-06
mix_floor = 0.01
precise = lax.Precision.HIGHEST


def from_behind(shard, axis, by):
    devices = lax.axis_size(axis)
    pairs = [(i, i + by) for i in range(devices) if 0 <= i + by < devices]
    return lax.ppermute(shard, axis, pairs)


def prefix(shard, axis, combine, identity, reverse):
    devices, place = (lax.axis_size(axis), lax.axis_index(axis))
    everything = jax.tree.map(
        lambda part, kind: lax.all_gather(part.astype(kind), axis),
        shard,
        (jnp.bfloat16, jnp.bfloat16),
    )
    start = jax.tree.map(
        lambda part, zero: jnp.broadcast_to(jnp.asarray(zero, part.dtype), part.shape),
        shard,
        identity,
    )

    def step(k, before):
        at = devices - 1 - k if reverse else k
        reached = at > place if reverse else at < place
        new = combine(
            before, jax.tree.map(lambda part, own: part[at].astype(own.dtype), everything, shard)
        )
        return jax.tree.map(lambda a, b: jnp.where(reached, a, b), new, before)

    return lax.fori_loop(0, devices, step, start)


def norm_scale(values):
    return lax.rsqrt(jnp.mean(values * values, axis=-1, keepdims=True) + eps)


def norm_back(values, scale, gain, grad):
    weighted = gain * grad
    return scale * weighted - values * scale**3 * jnp.mean(
        weighted * values, axis=-1, keepdims=True
    )


def batch_mul(left, right):
    return jnp.einsum("hij,hjk->hik", left, right, precision=precise)


def batch_mul_t(left, right):
    return jnp.einsum("hji,hjk->hik", left, right, precision=precise)


def compose(earlier, later):
    return (batch_mul(later[0], earlier[0]), batch_mul(later[0], earlier[1]) + later[1])


def over_heads(function, shared):
    return jax.vmap(jax.vmap(function), in_axes=shared)


def tp_total(term):
    return lax.psum(term.astype(jnp.bfloat16), "tp").astype(jnp.float32)


def group_parts(key_rows, value_rows, rates, same_doc, carry_mask):
    size = key_rows.shape[0]
    strict = jnp.tril(jnp.ones((size, size), jnp.float32), -1) * same_doc
    inner = jnp.dot(key_rows, key_rows.T, precision=precise)
    system = jnp.eye(size, dtype=jnp.float32) + rates[:, None] * inner * strict
    right_side = jnp.concatenate(
        [rates[:, None] * value_rows, (rates * carry_mask)[:, None] * key_rows], axis=1
    )
    solved = jax.scipy.linalg.solve_triangular(system, right_side, lower=True)
    base_rows = solved[:, : value_rows.shape[1]]
    wy_rows = solved[:, value_rows.shape[1] :]
    tail_keys = same_doc[size - 1][:, None] * key_rows
    identity_mat = jnp.eye(key_rows.shape[1], dtype=jnp.float32)
    transition = carry_mask[size - 1] * identity_mat - jnp.dot(
        tail_keys.T, wy_rows, precision=precise
    )
    contribution = jnp.dot(tail_keys.T, base_rows, precision=precise)
    return (transition, contribution, base_rows, wy_rows)


def group_output(queries, key_rows, same_doc, carry_mask, base_rows, wy_rows, state_in):
    size = key_rows.shape[0]
    lower = jnp.tril(jnp.ones((size, size), jnp.float32)) * same_doc
    written = base_rows - jnp.dot(wy_rows, state_in, precision=precise)
    scores = jnp.dot(queries, key_rows.T, precision=precise) * lower
    carried = carry_mask[:, None] * jnp.dot(queries, state_in, precision=precise)
    return carried + jnp.dot(scores, written, precision=precise)


def group_full(queries, key_rows, value_rows, rates, same_doc, carry_mask, state_in):
    transition, contribution, base_rows, wy_rows = group_parts(
        key_rows, value_rows, rates, same_doc, carry_mask
    )
    outputs = group_output(queries, key_rows, same_doc, carry_mask, base_rows, wy_rows, state_in)
    return (outputs, jnp.dot(transition, state_in, precision=precise) + contribution)


def state_pull(queries, key_rows, same_doc, carry_mask, wy_rows, grad_rows):
    size = key_rows.shape[0]
    lower = jnp.tril(jnp.ones((size, size), jnp.float32)) * same_doc
    scores = jnp.dot(queries, key_rows.T, precision=precise) * lower
    pulled = jnp.dot(scores.T, grad_rows, precision=precise)
    direct = jnp.dot((carry_mask[:, None] * queries).T, grad_rows, precision=precise)
    return direct - jnp.dot(wy_rows.T, pulled, precision=precise)


def group_grads(
    queries, key_rows, value_rows, rates, same_doc, carry_mask, state_in, grad_rows, grad_end
):

    def group_local(query_in, key_in, value_in, rate_in):
        return group_full(query_in, key_in, value_in, rate_in, same_doc, carry_mask, state_in)

    outputs, pullback = jax.vjp(group_local, queries, key_rows, value_rows, rates)
    return pullback((grad_rows, grad_end))


def local_pieces(
    block_input,
    grad_out,
    doc_lengths,
    attn_gain,
    mlp_gain,
    out_gain,
    conv_weight,
    qkv_weight,
    beta_weight,
    o_weight,
    gate_up_weight,
    down_weight,
):
    tok_rows = block_input.shape[1]
    model_width = block_input.shape[2]
    blocks = tok_rows // GROUP
    unit_floor = DK / 16.0
    x_rows = block_input[0].astype(jnp.float32)
    grad_rows_out = grad_out[0]
    qkv_full, beta_full, o_full, gate_up_full, down_full = (
        lax.all_gather(qkv_weight, ("row", "seq"), axis=1, tiled=True),
        lax.all_gather(beta_weight, ("row", "seq"), axis=0, tiled=True),
        lax.all_gather(o_weight, ("row", "seq"), axis=1, tiled=True),
        lax.all_gather(gate_up_weight, ("row", "seq"), axis=1, tiled=True),
        lax.all_gather(down_weight, ("row", "seq"), axis=1, tiled=True),
    )
    local_width = qkv_full.shape[2]
    head_count = local_width // DK
    lead_mask = (lax.axis_index("tp") == 0).astype(jnp.float32)
    ends = jnp.cumsum(doc_lengths[0])
    places = (
        lax.axis_index("seq") * tok_rows + jnp.arange(tok_rows + KW - 1, dtype=jnp.int32) - (KW - 1)
    )
    doc_ids = jnp.sum((places[:, None] >= ends[None, :]).astype(jnp.int32), axis=1)
    doc_ids = jnp.where(places < 0, -1, doc_ids)
    own_docs = doc_ids[KW - 1 :]
    prior_docs = doc_ids[KW - 2 : KW - 2 + tok_rows]
    valid = (own_docs < DOCS).astype(jnp.float32)
    fresh = (own_docs != prior_docs).astype(jnp.int32)
    tap_masks = [
        (doc_ids[KW - 1 - tap : KW - 1 - tap + tok_rows] == own_docs).astype(jnp.float32)
        for tap in range(KW)
    ]
    own_blocks = own_docs.reshape(blocks, GROUP)
    same_doc = (own_blocks[:, :, None] == own_blocks[:, None, :]).astype(jnp.float32)
    carry_mask = (jnp.cumsum(fresh.reshape(blocks, GROUP), axis=1) == 0).astype(jnp.float32)

    def to_blocks(array):
        return array.reshape(blocks, GROUP, head_count, -1).transpose(2, 0, 1, 3)

    def from_blocks(array):
        return array.transpose(1, 2, 0, 3).reshape(tok_rows, head_count, -1)

    scale_one = norm_scale(x_rows)
    normed_one = (x_rows * scale_one * attn_gain).astype(jnp.bfloat16)
    proj_low = jnp.einsum(
        "td,cde->cte", normed_one, qkv_full, preferred_element_type=jnp.float32
    ).astype(jnp.bfloat16)
    logit = jnp.dot(normed_one, beta_full, preferred_element_type=jnp.float32)
    rim_rows = from_behind(proj_low[:, tok_rows - (KW - 1) :, :], "seq", 1)
    extended = jnp.concatenate([rim_rows, proj_low], axis=1).astype(jnp.float32)
    conv_out = jnp.zeros((3, tok_rows, local_width), jnp.float32)
    for tap in range(KW):
        window = extended[:, KW - 1 - tap : KW - 1 - tap + tok_rows]
        conv_out = (
            conv_out + conv_weight[:, tap][:, None, :] * window * tap_masks[tap][None, :, None]
        )
    conv_sig = jax.nn.sigmoid(conv_out)
    activated = conv_out * conv_sig
    query_raw = activated[0].reshape(tok_rows, head_count, DK)
    key_raw = activated[1].reshape(tok_rows, head_count, DK)
    query_sq = jnp.sum(query_raw * query_raw, axis=-1, keepdims=True)
    key_sq = jnp.sum(key_raw * key_raw, axis=-1, keepdims=True)
    query_scale = lax.rsqrt(jnp.maximum(query_sq, unit_floor))
    key_scale = lax.rsqrt(jnp.maximum(key_sq, unit_floor))
    query_live = (query_sq > unit_floor).astype(jnp.float32)
    key_live = (key_sq > unit_floor).astype(jnp.float32)
    query_blocks = to_blocks(query_raw * query_scale)
    key_blocks = to_blocks(key_raw * key_scale)
    value_blocks = to_blocks(activated[2].reshape(tok_rows, head_count, DK))
    rate_sig = jax.nn.sigmoid(logit)
    rate_blocks = (rate_sig * valid[:, None]).reshape(blocks, GROUP, head_count).transpose(2, 0, 1)
    transition, contribution, base_rows, wy_rows = over_heads(group_parts, (0, 0, 0, None, None))(
        key_blocks, value_blocks, rate_blocks, same_doc, carry_mask
    )
    identity_mat = jnp.broadcast_to(jnp.eye(DK, dtype=jnp.float32), (head_count, DK, DK))
    zero_state = jnp.zeros((head_count, DK, DK), jnp.float32)
    transition_steps = jnp.moveaxis(transition, 1, 0)

    def chain(running, pair):
        product, partial_state = running
        step_trans, step_contrib = pair
        advanced = (
            batch_mul(step_trans, product),
            batch_mul(step_trans, partial_state) + step_contrib,
        )
        return (advanced, (product, partial_state))

    (dev_trans, dev_state), (products, partials) = lax.scan(
        chain, (identity_mat, zero_state), (transition_steps, jnp.moveaxis(contribution, 1, 0))
    )
    incoming = prefix((dev_trans, dev_state), "seq", compose, (identity_mat, zero_state), False)[1]
    group_starts = partials + jnp.einsum("nhij,hjk->nhik", products, incoming, precision=precise)
    start_blocks = jnp.moveaxis(group_starts, 0, 1)
    mix_blocks = over_heads(group_output, (0, 0, None, None, 0, 0, 0))(
        query_blocks, key_blocks, same_doc, carry_mask, base_rows, wy_rows, start_blocks
    )
    mixed = from_blocks(mix_blocks) * valid[:, None, None]
    mix_sq = jnp.mean(mixed * mixed, axis=-1, keepdims=True)
    mix_scale = lax.rsqrt(jnp.maximum(mix_sq, mix_floor))
    mix_live = (mix_sq > mix_floor).astype(jnp.float32)
    normed_mix = (mixed * mix_scale * out_gain).astype(jnp.bfloat16).reshape(tok_rows, local_width)
    o_term = jnp.dot(normed_mix, o_full, preferred_element_type=jnp.float32)
    resid = x_rows + tp_total(o_term)
    scale_two = norm_scale(resid)
    normed_local = (resid * scale_two * mlp_gain).astype(jnp.bfloat16)
    gate_up = jnp.einsum(
        "td,cdf->ctf", normed_local, gate_up_full, preferred_element_type=jnp.float32
    )
    gate_sig = jax.nn.sigmoid(gate_up[0])
    gate_act = gate_up[0] * gate_sig
    hidden = (gate_act * gate_up[1]).astype(jnp.bfloat16)
    down_term = jnp.dot(hidden, down_full, preferred_element_type=jnp.float32)
    mlp_out = tp_total(down_term)
    result = (resid + mlp_out).astype(jnp.bfloat16)
    grad_hidden = jnp.einsum(
        "td,fd->tf", grad_rows_out, down_full, preferred_element_type=jnp.float32
    )
    grad_gate = grad_hidden * gate_up[1] * gate_sig * (1.0 + gate_up[0] * (1.0 - gate_sig))
    grad_up = grad_hidden * gate_act
    grad_gate_up = jnp.stack([grad_gate, grad_up]).astype(jnp.bfloat16)
    down_part = jnp.einsum("tf,td->fd", hidden, grad_rows_out, preferred_element_type=jnp.float32)
    gate_up_part = jnp.einsum(
        "td,ctf->cdf", normed_local, grad_gate_up, preferred_element_type=jnp.float32
    )
    two_term = jnp.einsum(
        "ctf,cdf->td", grad_gate_up, gate_up_full, preferred_element_type=jnp.float32
    )
    grad_two = tp_total(two_term)
    mlp_gain_part = jnp.sum(grad_two * resid * scale_two, axis=0)
    grad_resid = grad_rows_out.astype(jnp.float32) + norm_back(resid, scale_two, mlp_gain, grad_two)
    grad_attn_local = grad_resid.astype(jnp.bfloat16)
    o_part = jnp.einsum(
        "te,td->ed", normed_mix, grad_attn_local, preferred_element_type=jnp.float32
    )
    grad_normed = jnp.einsum(
        "td,ed->te", grad_attn_local, o_full, preferred_element_type=jnp.float32
    ).reshape(tok_rows, head_count, DK)
    out_gain_part = jnp.sum(grad_normed * mixed * mix_scale, axis=(0, 1))
    weighted_mix = out_gain * grad_normed
    grad_mixed = (
        mix_scale * weighted_mix
        - mixed * mix_scale**3 * mix_live * jnp.mean(weighted_mix * mixed, axis=-1, keepdims=True)
    ) * valid[:, None, None]
    grad_blocks = to_blocks(grad_mixed)
    pulls = over_heads(state_pull, (0, 0, None, None, 0, 0))(
        query_blocks, key_blocks, same_doc, carry_mask, wy_rows, grad_blocks
    )

    def back_chain(running, pair):
        grad_end, product = running
        step_trans, step_pull = pair
        advanced = (step_pull + batch_mul_t(step_trans, grad_end), batch_mul_t(step_trans, product))
        return (advanced, (grad_end, product))

    (dev_pull, dev_back), (grad_ends, back_products) = lax.scan(
        back_chain,
        (zero_state, identity_mat),
        (transition_steps, jnp.moveaxis(pulls, 1, 0)),
        reverse=True,
    )
    outgoing = prefix((dev_back, dev_pull), "seq", compose, (identity_mat, zero_state), True)[1]
    end_grads = grad_ends + jnp.einsum("nhij,hjk->nhik", back_products, outgoing, precision=precise)
    grad_query, grad_key, grad_value, grad_rate = over_heads(
        group_grads, (0, 0, 0, 0, None, None, 0, 0, 0)
    )(
        query_blocks,
        key_blocks,
        value_blocks,
        rate_blocks,
        same_doc,
        carry_mask,
        start_blocks,
        grad_blocks,
        jnp.moveaxis(end_grads, 0, 1),
    )
    grad_query = from_blocks(grad_query)
    grad_key = from_blocks(grad_key)
    grad_query_raw = query_scale * grad_query - query_raw * query_scale**3 * query_live * jnp.sum(
        query_raw * grad_query, axis=-1, keepdims=True
    )
    grad_key_raw = key_scale * grad_key - key_raw * key_scale**3 * key_live * jnp.sum(
        key_raw * grad_key, axis=-1, keepdims=True
    )
    grad_activated = jnp.stack(
        [
            grad_query_raw.reshape(tok_rows, local_width),
            grad_key_raw.reshape(tok_rows, local_width),
            from_blocks(grad_value).reshape(tok_rows, local_width),
        ]
    )
    grad_conv = grad_activated * conv_sig * (1.0 + conv_out * (1.0 - conv_sig))
    grad_extended = jnp.zeros((3, tok_rows + KW - 1, local_width), jnp.float32)
    tap_grads = []
    for tap in range(KW):
        masked = grad_conv * tap_masks[tap][None, :, None]
        window = extended[:, KW - 1 - tap : KW - 1 - tap + tok_rows]
        tap_grads.append(jnp.sum(masked * window, axis=1))
        grad_extended = grad_extended + jnp.pad(
            conv_weight[:, tap][:, None, :] * masked, ((0, 0), (KW - 1 - tap, tap), (0, 0))
        )
    conv_part = jnp.stack(tap_grads, axis=1)
    rim_back = from_behind(grad_extended[:, : KW - 1], "seq", -1)
    grad_proj = jnp.concatenate(
        [grad_extended[:, KW - 1 : tok_rows], grad_extended[:, tok_rows:] + rim_back], axis=1
    ).astype(jnp.bfloat16)
    rate_grad = grad_rate.transpose(1, 2, 0).reshape(tok_rows, head_count)
    grad_logit = (rate_grad * valid[:, None] * rate_sig * (1.0 - rate_sig)).astype(jnp.bfloat16)
    qkv_part = jnp.einsum("td,cte->cde", normed_one, grad_proj, preferred_element_type=jnp.float32)
    beta_part = jnp.einsum("td,th->dh", normed_one, grad_logit, preferred_element_type=jnp.float32)
    grad_one_part = jnp.einsum(
        "cte,cde->td", grad_proj, qkv_full, preferred_element_type=jnp.float32
    ) + jnp.einsum("th,dh->td", grad_logit, beta_full, preferred_element_type=jnp.float32)
    grad_one = tp_total(grad_one_part)
    attn_gain_part = jnp.sum(grad_one * x_rows * scale_one, axis=0)
    input_local = (grad_resid + norm_back(x_rows, scale_one, attn_gain, grad_one)).astype(
        jnp.bfloat16
    )
    conv_whole = lax.dynamic_update_slice(
        jnp.zeros((3, KW, model_width), jnp.float32),
        conv_part,
        (0, 0, lax.axis_index("tp") * local_width),
    )
    attn_gain_grad, mlp_gain_grad, out_gain_grad, conv_grad = lax.psum(
        (attn_gain_part * lead_mask, mlp_gain_part * lead_mask, out_gain_part, conv_whole),
        ("row", "seq", "tp"),
    )
    qkv_sum, beta_sum, o_sum, gate_up_sum, down_sum = (
        lax.psum_scatter(
            qkv_part.astype(jnp.bfloat16), ("row", "seq"), scatter_dimension=1, tiled=True
        ).astype(jnp.float32),
        lax.psum_scatter(
            beta_part.astype(jnp.bfloat16), ("row", "seq"), scatter_dimension=0, tiled=True
        ).astype(jnp.float32),
        lax.psum_scatter(
            o_part.astype(jnp.bfloat16), ("row", "seq"), scatter_dimension=1, tiled=True
        ).astype(jnp.float32),
        lax.psum_scatter(
            gate_up_part.astype(jnp.bfloat16), ("row", "seq"), scatter_dimension=1, tiled=True
        ).astype(jnp.float32),
        lax.psum_scatter(
            down_part.astype(jnp.bfloat16), ("row", "seq"), scatter_dimension=1, tiled=True
        ).astype(jnp.float32),
    )
    return (
        result[None],
        input_local[None],
        attn_gain_grad,
        mlp_gain_grad,
        out_gain_grad,
        conv_grad,
        qkv_sum,
        beta_sum,
        o_sum,
        gate_up_sum,
        down_sum,
    )


CHUNK = 128
PAD = 8


def mul(left, right, dims):
    return lax.dot_general(
        left, right, ((dims[:1], dims[1:]), ((), ())), preferred_element_type=jnp.float32
    )


def fine(left, right, dims=(1, 0)):
    left_high, right_high = left.astype(jnp.bfloat16), right.astype(jnp.bfloat16)
    left_rest = (left - left_high.astype(jnp.float32)).astype(jnp.bfloat16)
    right_rest = (right - right_high.astype(jnp.float32)).astype(jnp.bfloat16)
    rest = mul(left_high, right_rest, dims) + mul(left_rest, right_high, dims)
    return mul(left_high, right_high, dims) + rest


def plain(left, right, dims=(1, 0)):
    return mul(left.astype(jnp.bfloat16), right.astype(jnp.bfloat16), dims)


def chunk_masks(doc_col, doc_row):
    same = doc_col == doc_row
    down = lax.broadcasted_iota(jnp.int32, (CHUNK, CHUNK), 0)
    along = lax.broadcasted_iota(jnp.int32, (CHUNK, CHUNK), 1)
    lower = jnp.where(same & (down >= along), 1.0, 0.0)
    strict = jnp.where(same & (down > along), 1.0, 0.0)
    return lower, strict, down, along


def lower_inverse(systems, down, along):
    at_one = (down // 2 == along // 2) & (down != along)
    unit = jnp.where(down == along, 1.0, 0.0)
    inverses = [unit - jnp.where(at_one, system, 0.0) for system in systems]
    half = 2
    while half < CHUNK:
        joins = (down // (2 * half) == along // (2 * half)) & (down // half != along // half)
        inner = [
            fine(jnp.where(joins, system, 0.0), inverse)
            for system, inverse in zip(systems, inverses)
        ]
        inverses = [inverse - fine(inverse, part) for inverse, part in zip(inverses, inner)]
        half *= 2
    return inverses


def tap_mask(aux, tap):
    return 1.0 if tap == 0 else aux[:, 3 + tap : 4 + tap]


def convolved(window, taps, aux):
    total = 0.0
    for tap in range(KW):
        total = total + (
            taps[tap : tap + 1] * window[PAD - tap : PAD - tap + CHUNK] * tap_mask(aux, tap)
        )
    return total


def sigmoid(values):
    return 1.0 / (1.0 + jnp.exp(-values))


def unit_scale(values):
    total = jnp.sum(values * values, axis=1, keepdims=True)
    floor = DK / 16.0
    return lax.rsqrt(jnp.maximum(total, floor)), jnp.where(total > floor, 1.0, 0.0)


def mix_norm(mixed):
    mean = jnp.mean(mixed * mixed, axis=1, keepdims=True)
    return lax.rsqrt(jnp.maximum(mean, mix_floor)), jnp.where(mean > mix_floor, 1.0, 0.0)


def forward_kernel(
    heads,
    staged,
    n1_ref,
    qkv_ref,
    beta_blocks_ref,
    taps_ref,
    aux_ref,
    docs_ref,
    gain_ref,
    x_ref,
    mlp_gain_ref,
    g_ref,
    o_weight_ref,
    gate_ref,
    up_ref,
    down_ref,
    proj_ref,
    logit_ref,
    mixed_ref,
    normed_ref,
    inverse_ref,
    states_ref,
    written_ref,
    o_ref,
    resid_ref,
    n2_ref,
    g_full_ref,
    gate_out,
    up_out,
    down_out,
    window_ref,
    state_ref,
    o_rows,
    n2_own,
    beta_ref,
    blocks,
    came,
    across,
    own_sems,
    sum_sems,
    n2_sems,
    g_sems,
    *sems,
):
    width = heads * DK
    line = Line()
    greet(exchange_partners(line) + along_axis("tp"))
    row = lax.axis_index("row")
    rows = n2_ref.shape[2]
    units = down_out.shape[2]

    def rows_of(ref, count):
        return lambda seq: ref.at[pl.ds(pl.multiple_of(seq * count, count), count)]

    o_move = Exchange(line, rows_of(o_weight_ref, width), o_ref, sems[:4])
    gate_move = Exchange(line, lambda seq: gate_ref.at[seq], gate_out, sems[4:8])
    up_move = Exchange(line, lambda seq: up_ref.at[seq], up_out, sems[8:12])
    down_move = Exchange(line, rows_of(down_ref, units), down_out, sems[12:16])
    moves = (o_move, gate_move, up_move, down_move)
    total = Scatter(line, blocks, came, across, sum_sems)
    n2 = Gather(line, n2_ref, n2_own, n2_sems)
    g_own = g_ref.at[pl.ds(pl.multiple_of(line.core * rows, rows), rows)]
    grads = Gather(line, g_full_ref, g_own, g_sems)
    own = []
    for i, move in enumerate(moves):
        target = move.target.at[row, line.place]
        own.append(pltpu.make_async_copy(move.source(line.place), target, own_sems.at[i]))
        own[i].start()
    o_move.start()
    gate_move.start()
    grads.phases(0)
    for move in moves:
        move.share_own()
    window_ref[0:PAD] = jnp.zeros((PAD, 3 * width), jnp.float32)
    state_ref[...] = jnp.zeros_like(state_ref)

    def prepare(n):
        rows = pl.ds(pl.multiple_of(n * CHUNK, CHUNK), CHUNK)
        n1 = n1_ref[rows]
        proj = jnp.concatenate(
            [mul(n1, qkv_ref[:, :, c].reshape(-1, width), (1, 0)) for c in range(3)], axis=1
        ).astype(jnp.bfloat16)
        proj_ref[rows] = proj
        window_ref[PAD : PAD + CHUNK] = proj.astype(jnp.float32)
        logit = mul(n1, beta_ref[...], (1, 1))
        logit_ref[rows] = logit
        aux = aux_ref[rows]
        conv = convolved(window_ref[...], taps_ref[...], aux)
        act = conv * sigmoid(conv)
        window_ref[0:PAD] = window_ref[CHUNK : CHUNK + PAD]
        valid, carry, tail = aux[:, 1:2], aux[:, 2:3], aux[:, 3:4]
        lower, strict, down, along = chunk_masks(aux[:, 0:1], docs_ref[pl.ds(n, 1)])
        rate_all = sigmoid(logit) * valid
        parts = []
        for h in range(heads):
            query = act[:, h * DK : (h + 1) * DK]
            key = act[:, width + h * DK : width + (h + 1) * DK]
            value = act[:, 2 * width + h * DK : 2 * width + (h + 1) * DK]
            query = query * unit_scale(query)[0]
            key = key * unit_scale(key)[0]
            rate = rate_all[:, h : h + 1]
            scores = plain(query, key, (1, 1)) * lower
            system = rate * fine(key, key, (1, 1)) * strict
            parts.append((query, key, value, rate, scores, system))
        return rows, valid, carry, tail, parts, down, along

    def advance(n, rows, valid, carry, tail, parts, inverses):
        carry_last = carry[CHUNK - 1 :]
        for h, (query, key, value, rate, scores, _) in enumerate(parts):
            inverse = inverses[h]
            state = state_ref[h]
            written = fine(inverse, rate * (value - fine(carry * key, state)))
            mixed = (carry * plain(query, state) + plain(scores, written)) * valid
            states_ref[h, n] = state
            written_ref[h, n] = written
            inverse_ref[h, n] = inverse
            state_ref[h] = carry_last * state + fine(tail * key, written, (0, 0))
            columns = pl.ds(h * DK, DK)
            mixed_ref[rows, columns] = mixed
            normed_ref[rows, columns] = (
                mixed * mix_norm(mixed)[0] * gain_ref[...]
            ).astype(jnp.bfloat16)

    chunks = n1_ref.shape[0] // CHUNK
    together = 4 if chunks % 4 == 0 else 1

    def several(m, _):
        ready = [prepare(together * m + i) for i in range(together)]
        down, along = ready[0][5:]
        inverses = lower_inverse([part[5] for one in ready for part in one[4]], down, along)
        for i, one in enumerate(ready):
            advance(together * m + i, *one[:5], inverses[i * heads : (i + 1) * heads])
        return 0

    def share_came(move):
        for i in range(1, line.count):
            move.share_came(i)

    half = chunks // together // 2
    staged.need(n1_ref, qkv_ref, beta_blocks_ref, taps_ref, aux_ref, docs_ref, gain_ref)
    side_by_side(beta_blocks_ref, beta_ref)
    lax.fori_loop(0, half, several, 0)
    share_came(o_move)
    grads.phases(1)
    up_move.start()
    lax.fori_loop(half, chunks // together, several, 0)
    staged.store(
        proj_ref, logit_ref, mixed_ref, normed_ref, inverse_ref, states_ref, written_ref
    )
    share_came(gate_move)
    down_move.start()
    own[0].wait()
    o_move.finish()
    staged.store(o_ref)
    side_by_side(o_ref, o_rows)
    for part in range(total.parts):
        total.product(part_rows(normed_ref, total, part), o_rows, part, order=0)
        total.start_edges(part)
    grads.phases(2)
    total.relay(0, 0)
    total.relay(1, 0)
    share_came(up_move)
    total.relay_back(0)
    grads.phases(3)
    total.relay(0, 1)
    total.relay(1, 1)
    share_came(down_move)
    total.relay_back(1)
    staged.need(x_ref, mlp_gain_ref)

    def normed(span):
        x_span = pl.ds(pl.multiple_of(line.core * rows + span.start, STEP), STEP)
        resid = x_ref[x_span].astype(jnp.float32) + total.own_rows(span)
        resid_ref[span] = resid
        n2_own[span] = (resid * norm_scale(resid) * mlp_gain_ref[...]).astype(jnp.bfloat16)

    for part in range(total.parts):
        total.wait_own(part)
        over_rows(total, part, normed)
        n2.phase(0, part)
    staged.store(resid_ref)
    for k in range(1, line.count):
        n2.phases(k)
    total.finish()
    n2.finish()
    grads.finish()
    for i, move in enumerate(moves[1:]):
        own[i + 1].wait()
        move.finish()


def part_rows(ref, total, part):
    seqs, cores, rows, _ = total.blocks.shape
    return jnp.concatenate(
        [ref[pl.ds(i * rows + part * total.rows, total.rows)] for i in range(seqs * cores)], axis=0
    )


def backward_kernel(
    heads,
    staged,
    grad_ref,
    o_ref,
    proj_ref,
    logit_ref,
    mixed_ref,
    inverse_ref,
    states_ref,
    written_ref,
    taps_ref,
    aux_ref,
    docs_ref,
    gain_ref,
    normed_mix_ref,
    n1_ref,
    qkv_ref,
    beta_blocks_ref,
    attn_gain_ref,
    mlp_grad_ref,
    x_ref,
    grad_resid_ref,
    sum_ref,
    input_grad_ref,
    small_all_ref,
    qkv_came_ref,
    o_came_ref,
    down_came_ref,
    gate_came_ref,
    up_came_ref,
    window_ref,
    masked_ref,
    state_ref,
    o_rows,
    beta_ref,
    conv_grad_ref,
    gain_grad_ref,
    grad_proj_ref,
    grad_logit_ref,
    small_ref,
    small_rows,
    qkv_sum,
    o_sum,
    blocks,
    came,
    across,
    qkv_parts,
    qkv_halves,
    qkv_rows_came,
    o_parts,
    o_halves,
    o_rows_came,
    sum_sems,
    swap_sems,
    *sems,
):
    width = heads * DK
    line = Line()
    greet(along_axis("seq") + along_axis("row") + along_axis("tp"))
    moves = moves_of(
        Swap,
        "seq",
        [sum_ref.at[m] for m in range(3)],
        (down_came_ref, gate_came_ref, up_came_ref),
        sems[:7],
    )
    for move in moves:
        move.start()
    (o_move,) = moves_of(Swap, "seq", (o_sum,), (o_came_ref,), sems[7:10])
    (qkv_move,) = moves_of(Swap, "seq", (qkv_sum,), (qkv_came_ref,), sems[10:13])
    (small_row,) = moves_of(Share, "row", (small_ref,), (small_rows,), sems[13:16])
    own_small = small_all_ref.at[line.core, line.place]
    small_seq = [
        remote(own_small, own_small, sems[16].at[i], sems[17].at[i], {"seq": other})
        for i, other in enumerate(around("seq"))
    ]
    core_small = small_all_ref.at[line.core]
    small_core = remote(core_small, core_small, sems[18].at[0], sems[18].at[1], line.across)
    o_sums = RowSum(o_parts, o_halves, o_rows_came, sems[19:23])
    qkv_sums = RowSum(qkv_parts, qkv_halves, qkv_rows_came, sems[23:27])
    total = Scatter(line, blocks, came, across, sum_sems)
    span = o_parts.shape[2]

    def own_columns(index):
        return pl.ds(pl.multiple_of(index * span, span), span)

    staged.need(grad_ref, normed_mix_ref)
    for step, index in enumerate(o_sums.order()):
        part = mul(grad_ref[:, own_columns(index)], normed_mix_ref[...], (0, 0))
        o_parts[index, 0] = part.astype(jnp.bfloat16)
        o_sums.start(step, 0)
    chunks = grad_ref.shape[0] // CHUNK
    staged.need(
        o_ref, proj_ref, logit_ref, mixed_ref, inverse_ref, states_ref, written_ref, taps_ref,
        aux_ref, docs_ref, gain_ref,
    )
    side_by_side(o_ref, o_rows)
    state_ref[...] = jnp.zeros_like(state_ref)
    masked_ref[...] = jnp.zeros_like(masked_ref)
    conv_grad_ref[...] = jnp.zeros_like(conv_grad_ref)
    gain_grad_ref[...] = jnp.zeros_like(gain_grad_ref)

    def chunk(step, _):
        n = chunks - 1 - step
        rows = pl.ds(pl.multiple_of(n * CHUNK, CHUNK), CHUNK)
        before = jnp.maximum(n - 1, 0)
        aux = aux_ref[rows]
        grad_normed = mul(grad_ref[rows], o_rows[...], (1, 1))
        prior = proj_ref[pl.ds(pl.multiple_of(before * CHUNK + CHUNK - 16, 16), 16)]
        window_ref[0:PAD] = prior.astype(jnp.float32)[16 - PAD :]
        window_ref[PAD : PAD + CHUNK] = proj_ref[rows].astype(jnp.float32)
        window = window_ref[...]
        taps = taps_ref[...]
        conv = convolved(window, taps, aux)
        conv_sig = sigmoid(conv)
        act = conv * conv_sig
        valid, carry, tail = aux[:, 1:2], aux[:, 2:3], aux[:, 3:4]
        carry_last = carry[CHUNK - 1 :]
        lower, strict, down, along = chunk_masks(aux[:, 0:1], docs_ref[pl.ds(n, 1)])
        rate_sig = sigmoid(logit_ref[rows])
        rate_all = rate_sig * valid
        lanes = lax.broadcasted_iota(jnp.int32, rate_all.shape, 1)
        grad_rates = jnp.zeros_like(rate_all)
        grads = [[], [], []]
        for h in range(heads):
            columns = pl.ds(h * DK, DK)
            mixed = mixed_ref[rows, columns]
            mix_scale, mix_live = mix_norm(mixed)
            grad_out = grad_normed[:, h * DK : (h + 1) * DK]
            scaled = mixed * mix_scale
            gain_grad_ref[...] += jnp.sum(grad_out * scaled, axis=0, keepdims=True)
            weighted = gain_ref[...] * grad_out
            grad_mix = (
                mix_scale * weighted
                - scaled
                * (mix_scale * mix_scale * mix_live)
                * jnp.mean(weighted * mixed, axis=1, keepdims=True)
            ) * valid
            query_raw = act[:, h * DK : (h + 1) * DK]
            key_raw = act[:, width + h * DK : width + (h + 1) * DK]
            value = act[:, 2 * width + h * DK : 2 * width + (h + 1) * DK]
            query_scale, query_live = unit_scale(query_raw)
            key_scale, key_live = unit_scale(key_raw)
            query = query_raw * query_scale
            key = key_raw * key_scale
            rate = rate_all[:, h : h + 1]
            inverse = inverse_ref[h, n]
            state = states_ref[h, n]
            written = written_ref[h, n]
            grad_state = state_ref[h]
            tail_key = tail * key
            carried_key = carry * key
            scores = plain(query, key, (1, 1)) * lower
            pulled = plain(scores, grad_mix, (0, 0)) + fine(tail_key, grad_state)
            solved = fine(inverse, pulled, (0, 0))
            state_ref[h] = (
                carry_last * grad_state
                + plain(carry * query, grad_mix, (0, 0))
                - fine(rate * carried_key, solved, (0, 0))
            )
            grad_scores = plain(grad_mix, written, (1, 1)) * lower
            grad_query = carry * plain(grad_mix, state, (1, 1)) + plain(grad_scores, key)
            guess_error = value - plain(carried_key, state)
            gram = plain(key, key, (1, 1)) * strict
            grad_system = plain(solved, written, (1, 1)) * strict
            grad_rate = jnp.sum(solved * guess_error, axis=1, keepdims=True) - jnp.sum(
                grad_system * gram, axis=1, keepdims=True
            )
            grad_gram = rate * grad_system
            grad_key = (
                plain(grad_scores, query, (0, 0))
                + tail * plain(written, grad_state, (1, 1))
                - rate * carry * plain(solved, state, (1, 1))
                - plain(grad_gram, key)
                - plain(grad_gram, key, (0, 0))
            )
            grads[0].append(
                query_scale
                * (
                    grad_query
                    - query
                    * query_live
                    * jnp.sum(query * grad_query, axis=1, keepdims=True)
                )
            )
            grads[1].append(
                key_scale
                * (grad_key - key * key_live * jnp.sum(key * grad_key, axis=1, keepdims=True))
            )
            grads[2].append(rate * solved)
            grad_rates = grad_rates + jnp.where(lanes == h, grad_rate, 0.0)
        grad_act = jnp.concatenate(grads[0] + grads[1] + grads[2], axis=1)
        grad_conv = grad_act * conv_sig * (1.0 + conv * (1.0 - conv_sig))
        grad_proj = taps[0:1] * grad_conv
        conv_grad_ref[0:1] += jnp.sum(
            grad_conv * window[PAD : PAD + CHUNK], axis=0, keepdims=True
        )
        for tap in range(1, KW):
            masked = grad_conv * tap_mask(aux, tap)
            conv_grad_ref[tap : tap + 1] += jnp.sum(
                masked * window[PAD - tap : PAD - tap + CHUNK], axis=0, keepdims=True
            )
            masked_ref[tap - 1, CHUNK : CHUNK + PAD] = masked_ref[tap - 1, 0:PAD]
            masked_ref[tap - 1, 0:CHUNK] = masked
            grad_proj = grad_proj + taps[tap : tap + 1] * masked_ref[tap - 1, tap : tap + CHUNK]
        grad_proj_ref[rows] = grad_proj.astype(jnp.bfloat16)
        grad_logit_ref[rows] = (grad_rates * rate_sig * (1.0 - rate_sig) * valid).astype(
            jnp.bfloat16
        )
        return 0

    early, late = chunks // 4, chunks // 2
    lax.fori_loop(0, early, chunk, 0)
    o_sums.add_halves(0)
    lax.fori_loop(early, late, chunk, 0)
    o_sum[...] = o_sums.total(0).astype(jnp.bfloat16).reshape(o_sum.shape)
    o_move.start()
    lax.fori_loop(late, chunks, chunk, 0)
    staged.need(
        n1_ref, qkv_ref, beta_blocks_ref, attn_gain_ref, mlp_grad_ref, x_ref, grad_resid_ref
    )
    side_by_side(beta_blocks_ref, beta_ref)

    def product(part):
        left = part_rows(grad_proj_ref, total, part)
        logit = part_rows(grad_logit_ref, total, part)

        def right_tile(left, t, across):
            weights = qkv_ref[t]
            out = mul(logit, beta_ref[:, across], (1, 0))
            for c in range(3):
                out = out + mul(
                    left[:, c * width : (c + 1) * width], weights[:, c].reshape(-1, width), (1, 1)
                )
            return out

        total.product(left, None, part, tile=span, right_tile=right_tile)
        total.start_edges(part)

    def qkv_grads(step):
        index = qkv_sums.order()[step]
        columns = own_columns(index)
        n1 = n1_ref[:, columns]
        part = mul(n1, grad_proj_ref[...], (0, 0))
        qkv_parts[index, 0] = part.astype(jnp.bfloat16)
        qkv_sums.start(step, 0)
        weights = qkv_ref[index]
        terms = 0.0
        for c in range(3):
            weight = weights[:, c].reshape(span, width).astype(jnp.float32)
            terms = terms + weight * part[:, c * width : (c + 1) * width]
        terms = fine(jnp.ones((8, width), jnp.float32), terms, (1, 1))[0:1]
        beta_part = mul(grad_logit_ref[...], n1, (0, 0))
        terms = terms + jnp.sum(
            beta_part * beta_ref[:, columns].astype(jnp.float32), axis=0, keepdims=True
        )
        small_ref[0:1, columns] = terms / attn_gain_ref[:, columns]
        small_ref[2 : 2 + heads, columns] = beta_part[:heads]

    product(0)
    qkv_grads(0)
    product(1)
    qkv_grads(1)
    total.relay(0, 0)
    total.relay(1, 0)
    qkv_grads(2)
    qkv_grads(3)
    small_ref[1:2] = mlp_grad_ref[...]
    at = 2 + heads
    for tap in range(KW):
        lanes = pl.ds((tap % 2) * 3 * width, 3 * width)
        small_ref[at + tap // 2 : at + tap // 2 + 1, lanes] = conv_grad_ref[tap : tap + 1]
    small_ref[at : at + 1, 6 * width : 6 * width + DK] = gain_grad_ref[...]
    small_row.start()
    total.relay_back(0)
    qkv_sums.add_halves(0)
    total.relay(0, 1)
    total.relay(1, 1)
    small_row.finish()
    small = small_rows[0]
    for i in range(1, small_rows.shape[0]):
        small = small + small_rows[i]
    small_all_ref[line.core, line.place] = small
    for copy in small_seq:
        copy.start()
    total.relay_back(1)
    qkv_sum[...] = qkv_sums.total(0).astype(jnp.bfloat16).reshape(qkv_sum.shape)
    qkv_move.start()
    rows = grad_resid_ref.shape[0]

    def back(inner):
        own_span = pl.ds(pl.multiple_of(line.core * rows + inner.start, STEP), STEP)
        x = x_ref[own_span].astype(jnp.float32)
        input_grad_ref[own_span] = (
            grad_resid_ref[inner]
            + norm_back(x, norm_scale(x), attn_gain_ref[...], total.own_rows(inner))
        ).astype(jnp.bfloat16)

    for part in range(total.parts):
        total.wait_own(part)
        over_rows(total, part, back)
    swap = own_swap(line, input_grad_ref, rows, swap_sems)
    swap.start()
    for copy in small_seq:
        copy.wait()
    small_core.start()
    total.finish()
    o_sums.finish()
    qkv_sums.finish()
    for move in moves + [o_move, qkv_move]:
        move.finish()
    swap.wait()
    small_core.wait()


def in_vmem(count):
    return [pl.BlockSpec(memory_space=pltpu.VMEM)] * count


def run_forward(n1, qkv, beta, taps, aux, docs, gain, x, g, mlp_gain, weights):
    row_len, heads = n1.shape[0], qkv.shape[-1] // DK
    rows_axis, seqs, _, shard, _ = qkv.shape
    cores, (piece, model_width) = lax.axis_size("tp"), x.shape
    rows = piece // cores
    chunks, width, f32, b16 = row_len // CHUNK, heads * DK, jnp.float32, jnp.bfloat16
    units = weights[3].shape[0] // seqs
    outs = (
        ((row_len, 3 * width), b16),
        ((row_len, beta.shape[2]), f32),
        ((row_len, width), f32),
        ((row_len, width), b16),
        ((heads, chunks, CHUNK, CHUNK), f32),
        ((heads, chunks, DK, DK), f32),
        ((heads, chunks, CHUNK, DK), f32),
        ((rows_axis, seqs, width, shard), b16),
        ((rows, model_width), f32),
    )
    scratch = [
        pltpu.VMEM((PAD + CHUNK, 3 * width), f32),
        pltpu.VMEM((heads, DK, DK), f32),
        pltpu.VMEM((width, model_width), b16),
        pltpu.VMEM((rows, model_width), b16),
        pltpu.VMEM((beta.shape[2], model_width), b16),
    ]
    scratch = scratch + scatter_scratch(seqs, cores, rows, model_width) + [dma_sems(4)]
    scratch = scratch + [dma_sems(6, seqs, PARTS)] * 3 + exchange_sems() * 4
    *saved, o_full, resid, n2, g_full, gate, up, down = line_call(
        functools.partial(forward_kernel, heads), 5, "mixer_forward", outs, scratch,
        (n1, qkv, beta, taps, aux, docs, gain, x, mlp_gain),
        far_args=(g, *weights),
        far_outs=(
            ((seqs, cores, rows, model_width), b16),
            ((seqs, cores, rows, model_width), b16),
            ((rows_axis,) + weights[1].shape, b16),
            ((rows_axis,) + weights[2].shape, b16),
            ((rows_axis, seqs, units, shard), b16),
        ),
    )
    n2, g_full = n2.reshape(-1, model_width), g_full.reshape(-1, model_width)
    gate, up = gate.reshape(model_width, units), up.reshape(model_width, units)
    return saved, o_full, resid, n2, g_full, gate, up, down


def run_backward(grad, o_full, saved, taps, aux, docs, gain, extra, sums):
    row_len, heads = grad.shape[0], o_full.shape[2] // DK
    model_width = grad.shape[1]
    rows_axis, seqs, _, shard = o_full.shape
    cores = lax.axis_size("tp")
    width, f32, b16 = heads * DK, jnp.float32, jnp.bfloat16
    rows, span = row_len // (seqs * cores), model_width // rows_axis
    small = (4 + heads, model_width)
    outs = (((cores * rows, model_width), b16), ((cores, seqs) + small, f32))
    far_outs = (((seqs, shard, 3 * width), b16), ((seqs, shard, width), b16))
    qkv_buffers, qkv_sems = row_sum_scratch((rows_axis, 1, span, 3 * width))
    o_buffers, o_sems = row_sum_scratch((rows_axis, 1, span, width))
    scratch = [
        pltpu.VMEM((PAD + CHUNK, 3 * width), f32),
        pltpu.VMEM((KW - 1, CHUNK + PAD, 3 * width), f32),
        pltpu.VMEM((heads, DK, DK), f32),
        pltpu.VMEM((width, model_width), b16),
        pltpu.VMEM((saved[1].shape[1], model_width), b16),
        pltpu.VMEM((KW, 3 * width), f32),
        pltpu.VMEM((1, DK), f32),
        pltpu.VMEM((row_len, 3 * width), b16),
        pltpu.VMEM(saved[1].shape, b16),
        pltpu.VMEM(small, f32),
        pltpu.VMEM((rows_axis,) + small, f32),
        pltpu.VMEM((seqs, shard, 3 * width), b16),
        pltpu.VMEM((seqs, shard, width), b16),
    ]
    scratch = scratch + scatter_scratch(seqs, cores, rows, model_width) + qkv_buffers + o_buffers
    scratch = scratch + [dma_sems(6, seqs, PARTS), dma_sems(2)]
    scratch = scratch + pair_sems("seq", 3) + pair_sems("seq", 1) * 2 + pair_sems("row", 1)
    scratch = scratch + [dma_sems(seqs - 1)] * 2 + [dma_sems(2)] + o_sems + qkv_sems
    return line_call(
        functools.partial(backward_kernel, heads), 6, "mixer_backward", outs, scratch,
        (grad, o_full, *saved, taps, aux, docs, gain, *extra),
        far_args=(sums,),
        far_outs=far_outs + ((sums.shape[1:], b16),) * 3,
    )


def row_aux(docs):
    f32 = jnp.float32
    chunks = docs.reshape(-1, CHUNK)
    prior = jnp.concatenate([jnp.full((1,), -1, jnp.int32), chunks[:-1, -1]])
    padded = jnp.concatenate([jnp.full((KW - 1,), -1, jnp.int32), docs])
    columns = [
        docs,
        docs < DOCS,
        (chunks == prior[:, None]).reshape(-1),
        (chunks == chunks[:, -1:]).reshape(-1),
    ] + [padded[KW - 1 - tap : KW - 1 - tap + docs.shape[0]] == docs for tap in range(1, KW)]
    columns = [column.astype(f32) for column in columns]
    columns += [jnp.zeros_like(columns[0])] * (8 - len(columns))
    return jnp.stack(columns, axis=1), chunks.astype(f32)


def remote(source, target, send, recv, where):
    return pltpu.make_async_remote_copy(
        src_ref=source,
        dst_ref=target,
        send_sem=send,
        recv_sem=recv,
        device_id=where,
        device_id_type=pl.DeviceIdType.MESH,
    )


def greet(partners):
    barrier = pltpu.get_barrier_semaphore()
    for partner, there in partners:

        @pl.when(there)
        def _(partner=partner):
            pl.semaphore_signal(
                barrier, inc=1, device_id=partner, device_id_type=pl.DeviceIdType.MESH
            )

    pl.semaphore_wait(barrier, sum(there.astype(jnp.int32) for _, there in partners))


def around(axis):
    count, place = lax.axis_size(axis), lax.axis_index(axis)
    return [lax.rem(place + by, count) for by in range(1, count)]


def line_partners():
    count, place, core = lax.axis_size("seq"), lax.axis_index("seq"), lax.axis_index("tp")
    return [
        ({"seq": jnp.minimum(place + 1, count - 1)}, place < count - 1),
        ({"seq": jnp.maximum(place - 1, 0)}, place > 0),
        ({"tp": 1 - core}, core >= 0),
    ]


class Line:
    def __init__(self):
        self.count, self.place = lax.axis_size("seq"), lax.axis_index("seq")
        self.core = lax.axis_index("tp")
        self.other = 1 - self.core
        self.right = {"seq": jnp.minimum(self.place + 1, self.count - 1)}
        self.left = {"seq": jnp.maximum(self.place - 1, 0)}
        self.across = {"tp": self.other}


class Gather:
    def __init__(self, line, slots, own, sems):
        self.line, self.slots, self.own, self.sems = line, slots, own, sems
        self.parts = sems.shape[2]
        self.rows = slots.shape[2] // self.parts

    def span(self, part):
        return pl.ds(part * self.rows, self.rows)

    def copy(self, kind, seq, part, own=False):
        line = self.line
        send = {"right": 0, "left": 1, "across": 2}[kind]
        recv = 4 if kind == "across" else 3
        slot = self.slots.at[seq, line.core, self.span(part)]
        where = {"right": line.right, "left": line.left, "across": line.across}[kind]
        source = self.own.at[self.span(part)] if own else slot
        return remote(
            source, slot, self.sems.at[send, seq, part], self.sems.at[recv, seq, part], where
        )

    def own_copy(self, part):
        line = self.line
        return pltpu.make_async_copy(
            self.own.at[self.span(part)],
            self.slots.at[line.place, line.core, self.span(part)],
            self.sems.at[5, 0, part],
        )

    def forward(self, seq, part, right, left, own=False):
        line = self.line
        if right:

            @pl.when(line.place < line.count - 1)
            def _():
                self.copy("right", seq, part, own).start()

        if left:

            @pl.when(line.place > 0)
            def _():
                self.copy("left", seq, part, own).start()

        self.copy("across", seq, part, own).start()

    def phase(self, by, part):
        line = self.line
        if by == 0:
            self.forward(line.place, part, True, True, own=True)
            self.own_copy(part).start()
            return

        @pl.when(line.place - by >= 0)
        def _():
            self.copy("right", line.place - by, part).wait_recv()
            self.forward(line.place - by, part, True, False)

        @pl.when(line.place + by < line.count)
        def _():
            self.copy("left", line.place + by, part).wait_recv()
            self.forward(line.place + by, part, False, True)

    def phases(self, by):
        for part in range(self.parts):
            self.phase(by, part)

    def finish(self):
        line = self.line
        for part in range(self.parts):
            self.own_copy(part).wait()
        for seq in range(line.count):
            for part in range(self.parts):

                @pl.when((line.place >= seq) & (line.place < line.count - 1))
                def _():
                    self.copy("right", seq, part).wait_send()

                @pl.when((line.place <= seq) & (line.place > 0))
                def _():
                    self.copy("left", seq, part).wait_send()

                self.copy("across", seq, part).wait()


class Scatter:
    def __init__(self, line, blocks, came, across, sems):
        self.line, self.blocks, self.came, self.across, self.sems = line, blocks, came, across, sems
        self.parts = sems.shape[2]
        self.rows = blocks.shape[2] // self.parts

    def span(self, part):
        return pl.ds(part * self.rows, self.rows)

    def over(self, seq, part):
        line, span = self.line, self.span(part)
        return remote(
            self.blocks.at[seq, line.other, span],
            self.across.at[seq, span],
            self.sems.at[0, seq, part],
            self.sems.at[1, seq, part],
            line.across,
        )

    def along(self, kind, seq, part):
        line, span = self.line, self.span(part)
        way = {"right": 0, "left": 1}[kind]
        slot = seq if way == 0 else jnp.where(seq == line.place - 1, line.count, seq)
        return remote(
            self.blocks.at[seq, line.core, span],
            self.came.at[slot, span],
            self.sems.at[2, seq, part],
            self.sems.at[3 + way, seq, part],
            line.right if way == 0 else line.left,
        )

    def nears(self, k):
        for part in range(self.parts):
            self.near(k, part)

    def fars(self, k):
        for part in range(self.parts):
            self.far(k, part)

    def product(self, left_ref, right_ref, part, order=1, tile=512, right_tile=None):
        seqs, cores, _, width = self.blocks.shape
        span = self.span(part)
        left = left_ref
        if len(left_ref.shape) == 3:
            left = left_ref[:, span].reshape(seqs * cores * self.rows, -1)

        def columns(t, _):
            across = pl.ds(pl.multiple_of(t * tile, tile), tile)
            if right_tile is not None:
                total = right_tile(left, t, across)
            elif order == 1:
                total = mul(left, right_ref[across], (1, 1))
            else:
                total = mul(left, right_ref[:, across], (1, 0))
            self.blocks[:, :, span, across] = total.astype(jnp.bfloat16).reshape(
                seqs, cores, self.rows, tile
            )
            return 0

        lax.fori_loop(0, width // tile, columns, 0)
        self.offer(part)

    def offer(self, part):
        for k in range(self.blocks.shape[0]):
            self.over(self.target(k), part).start()

    def pass_on(self, kind, seq, part):
        line, span = self.line, self.span(part)
        f32 = jnp.float32
        first = line.place == (0 if kind == "right" else line.count - 1)
        way = {"right": 0, "left": 1}[kind]
        self.over(seq, part).wait_recv()
        total = self.blocks[seq, line.core, span].astype(f32)
        total = total + self.across[seq, span].astype(f32)

        @pl.when(first)
        def _():
            self.blocks[seq, line.core, span] = total.astype(jnp.bfloat16)

        @pl.when(jnp.logical_not(first))
        def _():
            self.along(kind, seq, part).wait_recv()
            self.blocks[seq, line.core, span] = (
                total + self.came[seq, span].astype(f32)
            ).astype(jnp.bfloat16)

        self.along(kind, seq, part).start()

    def target(self, k):
        line = self.line
        return jnp.where(line.place < line.count // 2, line.count - 1 - k, k)

    def edge(self):
        return (self.line.place == 0) | (self.line.place == self.line.count - 1)

    def near(self, k, part):
        line = self.line
        low = line.place < line.count // 2

        @pl.when(low & (line.count - 1 - k > line.place))
        def _():
            self.pass_on("right", line.count - 1 - k, part)

        @pl.when(jnp.logical_not(low) & (k < line.place))
        def _():
            self.pass_on("left", k, part)

    def far(self, k, part):
        line = self.line
        low = line.place < line.count // 2

        @pl.when(low & (k < line.place))
        def _():
            self.pass_on("left", k, part)

        @pl.when(jnp.logical_not(low) & (line.count - 1 - k > line.place))
        def _():
            self.pass_on("right", line.count - 1 - k, part)

    def start_edges(self, part):
        @pl.when(self.edge())
        def _():
            for k in range(self.line.count - 1):
                self.near(k, part)

    def relay(self, k, part):
        @pl.when(jnp.logical_not(self.edge()))
        def _():
            self.near(k, part)

    def relay_back(self, part):
        @pl.when(jnp.logical_not(self.edge()))
        def _():
            for k in range(self.line.count - 1):
                self.far(k, part)

    def wait_own(self, part):
        line = self.line

        @pl.when(line.place > 0)
        def _():
            self.along("right", line.place, part).wait_recv()

        @pl.when(line.place < line.count - 1)
        def _():
            self.along("left", line.place, part).wait_recv()

        self.over(line.place, part).wait_recv()

    def own_rows(self, rows):
        line = self.line
        f32 = jnp.float32
        total = self.blocks[line.place, line.core, rows].astype(f32)
        total = total + self.across[line.place, rows].astype(f32)
        from_left = self.came[line.place, rows].astype(f32)
        from_right = self.came[line.count, rows].astype(f32)
        total = total + jnp.where(line.place > 0, from_left, 0.0)
        return total + jnp.where(line.place < line.count - 1, from_right, 0.0)

    def finish(self):
        line = self.line
        for seq in range(line.count):
            for part in range(self.parts):
                self.over(seq, part).wait_send()

                @pl.when(line.place != seq)
                def _():
                    self.along("right", seq, part).wait_send()


class Exchange:
    def __init__(self, line, source, target, sems):
        self.line, self.source, self.target = line, source, target
        self.send, self.recv, self.send_row, self.recv_row = sems
        self.row = lax.axis_index("row")
        self.seq_others, self.row_others = around("seq"), around("row")

    def spread(self, i):
        other = self.seq_others[i]
        return remote(
            self.source(other),
            self.target.at[self.row, self.line.place],
            self.send.at[i],
            self.recv.at[i],
            {"seq": other},
        )

    def share(self, i, j):
        line = self.line
        came_from = lax.rem(line.place + line.count - i, line.count)
        slot = self.target.at[self.row, came_from]
        source = self.source(line.place) if i == 0 else slot
        return remote(
            source,
            slot,
            self.send_row.at[i, j],
            self.recv_row.at[i, j],
            {"row": self.row_others[j]},
        )

    def start(self):
        for i in range(len(self.seq_others)):
            self.spread(i).start()

    def share_own(self):
        for j in range(len(self.row_others)):
            self.share(0, j).start()

    def share_came(self, i):
        self.spread(i - 1).wait_recv()
        for j in range(len(self.row_others)):
            self.share(i, j).start()

    def finish(self):
        for i in range(len(self.seq_others)):
            self.spread(i).wait_send()
        for i in range(len(self.seq_others) + 1):
            for j in range(len(self.row_others)):
                self.share(i, j).wait()


class Share:
    def __init__(self, axis, source, target, sems, own_sem):
        self.axis, self.source, self.target = axis, source, target
        self.send, self.recv = sems
        self.others = around(axis)
        self.own = pltpu.make_async_copy(source, target.at[lax.axis_index(axis)], own_sem)

    def copy(self, i):
        return remote(
            self.source,
            self.target.at[lax.axis_index(self.axis)],
            self.send.at[i],
            self.recv.at[i],
            {self.axis: self.others[i]},
        )

    def start(self):
        for i in range(len(self.others)):
            self.copy(i).start()
        self.own.start()

    def finish(self):
        for i in range(len(self.others)):
            self.copy(i).wait()
        self.own.wait()


class Swap:
    def __init__(self, axis, source, target, sems, own_sem):
        self.axis, self.source, self.target = axis, source, target
        self.send, self.recv = sems
        self.others = around(axis)
        place = lax.axis_index(axis)
        self.own = pltpu.make_async_copy(source.at[place], target.at[place], own_sem)

    def copy(self, i):
        return remote(
            self.source.at[self.others[i]],
            self.target.at[lax.axis_index(self.axis)],
            self.send.at[i],
            self.recv.at[i],
            {self.axis: self.others[i]},
        )

    def start(self):
        for i in range(len(self.others)):
            self.copy(i).start()
        self.own.start()

    def finish(self):
        for i in range(len(self.others)):
            self.copy(i).wait()
        self.own.wait()


class RowSum:
    def __init__(self, blocks, halves, came, sems):
        self.blocks, self.halves, self.came = blocks, halves, came
        self.row = lax.axis_index("row")
        even_x, even_y = lax.rem(self.row, 2) == 0, self.row < 2
        x_step, y_step = jnp.where(even_x, 1, -1), jnp.where(even_y, 2, -2)
        self.near = (self.row + x_step, self.row + y_step)
        self.far = self.row + x_step + y_step
        self.half = blocks.shape[2] // 2
        self.send_half, self.recv_half, self.send, self.recv = sems

    def rows(self, i):
        return pl.ds(i * self.half, self.half)

    def half_copy(self, i, m):
        return remote(
            self.blocks.at[self.far, m, self.rows(i)],
            self.halves.at[i, m],
            self.send_half.at[i, m],
            self.recv_half.at[i, m],
            {"row": self.near[i]},
        )

    def copy(self, i, j, m):
        return remote(
            self.blocks.at[self.near[i], m, self.rows(j)],
            self.came.at[i, m, self.rows(j)],
            self.send.at[i, j, m],
            self.recv.at[i, j, m],
            {"row": self.near[i]},
        )

    def start_far(self, m):
        for i in range(2):
            self.half_copy(i, m).start()

    def start_near(self, i, m):
        self.copy(i, i, m).start()

    def add_half(self, i, m):
        j = 1 - i
        self.half_copy(j, m).wait_recv()
        rows = self.rows(j)
        total = self.blocks[self.near[i], m, rows].astype(jnp.float32)
        total = total + self.halves[j, m].astype(jnp.float32)
        self.blocks[self.near[i], m, rows] = total.astype(jnp.bfloat16)
        self.copy(i, j, m).start()

    def start(self, step, m):
        if step == 0:
            self.start_far(m)
        elif step < 3:
            self.start_near(step - 1, m)

    def order(self):
        return (self.far, self.near[0], self.near[1], self.row)

    def add_halves(self, m):
        for i in range(2):
            self.add_half(i, m)

    def total(self, m):
        for i in range(2):
            for j in range(2):
                self.copy(i, j, m).wait_recv()
        total = self.blocks[self.row, m].astype(jnp.float32)
        for i in range(2):
            total = total + self.came[i, m].astype(jnp.float32)
        return total

    def finish(self):
        for m in range(self.blocks.shape[1]):
            for i in range(2):
                self.half_copy(i, m).wait_send()
                for j in range(2):
                    self.copy(i, j, m).wait_send()


def row_sum_scratch(shape):
    b16 = jnp.bfloat16
    _, count, rows, width = shape
    return [
        pltpu.VMEM(shape, b16),
        pltpu.VMEM((2, count, rows // 2, width), b16),
        pltpu.VMEM((2, count, rows, width), b16),
    ], [dma_sems(2, count), dma_sems(2, count), dma_sems(2, 2, count), dma_sems(2, 2, count)]


def pair_sems(axis, count):
    return [dma_sems(lax.axis_size(axis) - 1)] * (2 * count) + [dma_sems(count)]


def moves_of(kind, axis, sources, targets, sems):
    return [
        kind(axis, source, target, sems[2 * i : 2 * i + 2], sems[-1].at[i])
        for i, (source, target) in enumerate(zip(sources, targets))
    ]


def along_axis(axis):
    return [({axis: other}, other >= 0) for other in around(axis)]


def exchange_sems():
    seqs, rows = lax.axis_size("seq"), lax.axis_size("row")
    return [
        dma_sems(seqs - 1),
        dma_sems(seqs - 1),
        dma_sems(seqs, rows - 1),
        dma_sems(seqs, rows - 1),
    ]


def exchange_partners(line):
    return [({"seq": other}, other >= 0) for other in around("seq")] + [
        ({"row": other}, other >= 0) for other in around("row")
    ]


STEP = 32


def over_rows(total, part, body):
    def step(i, _):
        body(pl.ds(pl.multiple_of(part * total.rows + i * STEP, STEP), STEP))
        return 0

    lax.fori_loop(0, total.rows // STEP, step, 0)


def side_by_side(blocks_ref, out_ref):
    outer, inner, _, width = blocks_ref.shape
    for i in range(outer):
        for j in range(inner):
            out_ref[:, (i * inner + j) * width : (i * inner + j + 1) * width] = blocks_ref[i, j]


def dma_sems(*shape):
    return pltpu.SemaphoreType.DMA(shape)


class Staged:
    def __init__(self, inputs, outputs, in_sems, out_sems):
        self.loads = [
            (near, pltpu.make_async_copy(far, near, in_sems.at[i]))
            for i, (far, near) in enumerate(inputs)
        ]
        self.stores = [
            (near, pltpu.make_async_copy(near, far, out_sems.at[i]))
            for i, (far, near) in enumerate(outputs)
        ]
        self.stored = []
        for _, copy in self.loads:
            copy.start()

    def need(self, *refs):
        for ref in refs:
            (at,) = [i for i, (near, _) in enumerate(self.loads) if near is ref]
            self.loads.pop(at)[1].wait()

    def store(self, *refs):
        for ref in refs:
            (at,) = [i for i, (near, _) in enumerate(self.stores) if near is ref]
            copy = self.stores.pop(at)[1]
            copy.start()
            self.stored.append(copy)

    def finish(self):
        self.need(*[near for near, _ in self.loads])
        self.store(*[near for near, _ in self.stores])
        for copy in self.stored:
            copy.wait()


def line_call(kernel, collective_id, name, outs, scratch, args, limit=63, far_args=(), far_outs=()):
    counts = [len(args), len(far_args), len(outs), len(far_outs), len(args), len(outs)]

    def body(*refs):
        groups, at = [], 0
        for count in counts:
            groups.append(refs[at : at + count])
            at += count
        near_in, near_out, in_sems, out_sems, *rest = *groups[4:], *refs[at:]
        staged = Staged(
            list(zip(groups[0], near_in)), list(zip(groups[2], near_out)), in_sems, out_sems
        )
        kernel(staged, *near_in, *groups[1], *near_out, *groups[3], *rest)
        staged.finish()

    far = pl.BlockSpec(memory_space=pl.ANY)
    stages = [pltpu.VMEM(arg.shape, arg.dtype) for arg in args]
    stages += [pltpu.VMEM(*out) for out in outs]
    stages += [dma_sems(max(len(args), 1)), dma_sems(max(len(outs), 1))]
    return pl.pallas_call(
        body,
        out_shape=[jax.ShapeDtypeStruct(*out) for out in (*outs, *far_outs)],
        in_specs=[far] * (len(args) + len(far_args)),
        out_specs=[far] * (len(outs) + len(far_outs)),
        scratch_shapes=stages + scratch,
        compiler_params=pltpu.CompilerParams(
            collective_id=collective_id,
            has_side_effects=collective_id is not None,
            vmem_limit_bytes=limit * 1024 * 1024,
        ),
        name=name,
    )(*args, *far_args)


def scatter_scratch(seqs, cores, rows, width):
    b16 = jnp.bfloat16
    return [
        pltpu.VMEM((seqs, cores, rows, width), b16),
        pltpu.VMEM((seqs + 1, rows, width), b16),
        pltpu.VMEM((seqs, rows, width), b16),
    ]


PARTS = 2


def mlp_grad_kernel(
    staged, gate_ref, up_ref, resid_ref, gain_ref,
    down_full_ref, n2_ref, g_full_ref,
    grad_resid_ref, gain_grad_ref, result_ref,
    grad_attn_ref, sum_ref,
    grad_gate_ref, grad_up_ref, hidden_ref, down_ref, inner, g_own, attn_own, blocks, came, across, out_blocks, out_came, out_across, tokens, parts, halves, parts_came,
    sum_sems, out_sems, attn_sems, swap_sems, inner_sems, token_sems, own_sems, down_sems, *sems,
):
    line = Line()
    rows_axis, pieces, _, shard = down_full_ref.shape
    down_loads = [
        pltpu.make_async_copy(
            down_full_ref.at[i, j],
            down_ref.at[:, pl.ds((i * pieces + j) * shard, shard)],
            down_sems.at[i, j],
        )
        for i in range(rows_axis)
        for j in range(pieces)
    ]
    for copy in down_loads:
        copy.start()
    rows = resid_ref.shape[0]
    g_load = pltpu.make_async_copy(
        g_full_ref.at[line.place * lax.axis_size("tp") + line.core], g_own, own_sems.at[3]
    )
    g_load.start()
    total = Scatter(line, blocks, came, across, sum_sems)
    result = Scatter(line, out_blocks, out_came, out_across, out_sems)
    attn = Gather(line, grad_attn_ref, attn_own, attn_sems)
    sums = RowSum(parts, halves, parts_came, sems)
    units = hidden_ref.shape[2]
    group = inner.shape[1]
    groups = hidden_ref.shape[0] // group
    steps = total.parts * groups

    def inner_copy(i, step):
        part, at = step // groups, lax.rem(step, groups) * group
        span = pl.ds(pl.multiple_of(part * total.rows, total.rows), total.rows)
        ref = (n2_ref, g_full_ref)[i]
        return pltpu.make_async_copy(
            ref.at[pl.ds(at, group), span], inner.at[i], inner_sems.at[i]
        )

    for i in range(2):
        inner_copy(i, 0).start()
    greet(line_partners() + along_axis("row"))

    def ahead(i, step):
        @pl.when(step + 1 < steps)
        def _():
            inner_copy(i, step + 1).start()

    def mlp(step, _):
        part, at = step // groups, lax.rem(step, groups) * group
        span = pl.ds(pl.multiple_of(part * total.rows, total.rows), total.rows)
        width = n2_ref.shape[2]
        inner_copy(0, step).wait()
        n2 = inner[0].reshape(-1, width)
        gate = mul(n2, gate_ref[...], (1, 0))
        up = mul(n2, up_ref[...], (1, 0))
        ahead(0, step)
        inner_copy(1, step).wait()
        grad_hidden = mul(inner[1].reshape(-1, width), down_ref[...], (1, 1))
        ahead(1, step)
        sig = sigmoid(gate)
        act = gate * sig
        grad_gate = grad_hidden * up * sig * (1.0 + gate * (1.0 - sig))
        for ref, value in (
            (hidden_ref, act * up),
            (grad_up_ref, grad_hidden * act),
            (grad_gate_ref, grad_gate),
        ):
            ref[pl.ds(at, group), span] = value.astype(jnp.bfloat16).reshape(
                group, total.rows, units
            )
        return 0

    orders = sums.order()
    block_width = tokens.shape[3]

    def token_copy(i, step):
        columns = pl.ds(pl.multiple_of(orders[step] * block_width, block_width), block_width)
        ref = (g_full_ref, n2_ref)[i]
        return pltpu.make_async_copy(ref.at[:, :, columns], tokens.at[i], token_sems.at[i])

    for i in range(2):
        token_copy(i, 0).start()

    def product(part):
        left_up = grad_up_ref[:, total.span(part)].reshape(-1, units)

        def right_tile(left, t, columns):
            return mul(left, gate_ref[columns], (1, 1)) + mul(left_up, up_ref[columns], (1, 1))

        total.product(grad_gate_ref, None, part, right_tile=right_tile)
        total.start_edges(part)

    def weight_grads(step):
        to = orders[step]
        for m, (i, ref) in enumerate(((0, hidden_ref), (1, grad_gate_ref), (1, grad_up_ref))):
            if m < 2:
                token_copy(i, step).wait()
            part = mul(
                tokens[i].reshape(-1, block_width), ref[...].reshape(-1, units), (0, 0)
            )
            parts[to, m] = part.astype(jnp.bfloat16)
            if m != 1 and step + 1 < len(orders):
                token_copy(i, step + 1).start()
            sums.start(step, m)

    staged.need(gate_ref, up_ref)
    for copy in down_loads:
        copy.wait()
    lax.fori_loop(0, groups, mlp, 0)
    product(0)
    lax.fori_loop(groups, steps, mlp, 0)
    weight_grads(0)
    for part in range(1, total.parts):
        product(part)
    total.relay(0, 0)
    total.relay(1, 0)
    weight_grads(1)
    total.relay_back(0)
    weight_grads(2)
    total.relay(0, 1)
    total.relay(1, 1)
    weight_grads(3)
    total.relay_back(1)
    staged.need(resid_ref, gain_ref)
    g_load.wait()
    gain_grad_ref[...] = jnp.zeros_like(gain_grad_ref)

    def back(span):
        resid = resid_ref[span]
        grad_two = total.own_rows(span)
        scale = norm_scale(resid)
        gain_grad_ref[...] += jnp.sum(grad_two * resid * scale, axis=0, keepdims=True)
        grad = g_own[span].astype(jnp.float32) + norm_back(
            resid, scale, gain_ref[...], grad_two
        )
        grad_resid_ref[span] = grad
        attn_own[span] = grad.astype(jnp.bfloat16)

    for part in range(total.parts):
        total.wait_own(part)
        over_rows(total, part, back)
        attn.phase(0, part)
    staged.store(grad_resid_ref, gain_grad_ref)
    for part in range(result.parts):
        result.product(hidden_ref, down_ref, part, order=0)
    for m in range(parts.shape[1]):
        sums.add_halves(m)
    for k in range(1, line.count):
        attn.phases(k)
        result.nears(k - 1)
    for k in range(line.count - 1):
        result.fars(k)

    def finish(span):
        own_span = pl.ds(pl.multiple_of(line.core * rows + span.start, STEP), STEP)
        result_ref[own_span] = (resid_ref[span] + result.own_rows(span)).astype(jnp.bfloat16)

    for part in range(result.parts):
        result.wait_own(part)
        over_rows(result, part, finish)
    swap = own_swap(line, result_ref, rows, swap_sems)
    swap.start()
    own = []
    for m in range(parts.shape[1]):
        parts[sums.row, m] = sums.total(m).astype(jnp.bfloat16)
        own.append(
            pltpu.make_async_copy(parts.at[sums.row, m], sum_ref.at[m], own_sems.at[m])
        )
        own[m].start()
    total.finish()
    result.finish()
    attn.finish()
    swap.wait()
    sums.finish()
    for copy in own:
        copy.wait()


def own_swap(line, ref, rows, sems):
    own = ref.at[pl.ds(pl.multiple_of(line.core * rows, rows), rows)]
    return remote(own, own, sems.at[0], sems.at[1], line.across)


def run_mlp_grad(gate, up, down, resid, gain, n2, g_full):
    seqs, cores, (rows, width) = lax.axis_size("seq"), lax.axis_size("tp"), resid.shape
    rows_axis = lax.axis_size("row")
    piece, b16, f32 = rows * cores, jnp.bfloat16, jnp.float32
    units, span, blocks = gate.shape[1], width // rows_axis, seqs * cores
    outs = (((rows, width), f32), ((1, width), f32), ((piece, width), b16))
    sum_buffers, sum_sems = row_sum_scratch((rows_axis, 3, span, units))
    scratch = [pltpu.VMEM((blocks, rows, units), b16)] * 3
    scratch = scratch + [
        pltpu.VMEM((units, width), b16),
        pltpu.VMEM((2, blocks // 2, rows // PARTS, width), b16),
        pltpu.VMEM((rows, width), b16),
        pltpu.VMEM((rows, width), b16),
    ]
    scratch = scratch + scatter_scratch(seqs, cores, rows, width) * 2
    scratch = scratch + [pltpu.VMEM((2, blocks, rows, span), b16)] + sum_buffers
    scratch = scratch + [dma_sems(6, seqs, PARTS)] * 3 + [dma_sems(2)]
    scratch = scratch + [dma_sems(2)] * 2 + [dma_sems(4), dma_sems(rows_axis, seqs)]
    scratch = scratch + sum_sems
    grad_resid, gain_grad, result, grad_attn, sums = line_call(
        mlp_grad_kernel, 2, "mlp_grad", outs, scratch,
        (gate, up, resid, gain),
        far_args=(down, n2.reshape(blocks, rows, width), g_full.reshape(blocks, rows, width)),
        far_outs=(((seqs, cores, rows, width), b16), ((3, span, units), b16)),
    )
    return grad_resid, grad_attn.reshape(-1, width), gain_grad, result, sums


def unit_square(size):
    down = lax.broadcasted_iota(jnp.int32, (size, size), 0)
    along = lax.broadcasted_iota(jnp.int32, (size, size), 1)
    return jnp.where(down == along, 1.0, 0.0).astype(jnp.bfloat16)


def normed_kernel(
    staged, x_ref, gain_ref, beta_weight_ref, gate_up_ref, weight_ref,
    gate_parts_ref, up_parts_ref, n1_ref, qkv_ref, beta_full_ref, n1_own, beta_ref, n1_sems,
    own_sems, *sems,
):
    line = Line()
    row = lax.axis_index("row")
    greet(exchange_partners(line) + [(line.across, line.core >= 0)])
    width = qkv_ref.shape[-1]

    def columns(seq):
        return weight_ref.at[:, :, pl.ds(pl.multiple_of(seq * width, width), width)]

    moves = [
        Exchange(line, columns, qkv_ref, sems[:4]),
        Exchange(line, lambda seq: beta_ref.at[seq], beta_full_ref, sems[4:]),
    ]
    moves[0].start()
    staged.need(beta_weight_ref)
    beta = mul(beta_weight_ref[...], unit_square(beta_weight_ref.shape[0]), (0, 0))
    heads = beta.shape[0] // line.count
    empty = jnp.zeros((beta_ref.shape[1] - heads, beta.shape[1]), jnp.float32)
    for seq in range(line.count):
        own_heads = beta[seq * heads : (seq + 1) * heads]
        beta_ref[seq] = jnp.concatenate([own_heads, empty], axis=0).astype(jnp.bfloat16)
    moves[1].start()
    own = [
        pltpu.make_async_copy(
            move.source(line.place), move.target.at[row, line.place], own_sems.at[i]
        )
        for i, move in enumerate(moves)
    ]
    for copy in own:
        copy.start()
    rows = n1_ref.shape[2]
    n1 = Gather(line, n1_ref, n1_own, n1_sems)
    staged.need(x_ref, gain_ref)

    def normed(span):
        x_span = pl.ds(pl.multiple_of(line.core * rows + span.start, STEP), STEP)
        x = x_ref[x_span].astype(jnp.float32)
        n1_own[span] = (x * norm_scale(x) * gain_ref[...]).astype(jnp.bfloat16)

    for part in range(n1.parts):
        over_rows(n1, part, normed)
        n1.phase(0, part)
    for move in moves:
        move.share_own()
    staged.need(gate_up_ref)
    units = gate_parts_ref.shape[2]
    for i, ref in enumerate((gate_parts_ref, up_parts_ref)):
        weight = gate_up_ref[i].astype(jnp.float32)
        for seq in range(line.count):
            ref[seq] = weight[:, seq * units : (seq + 1) * units].astype(jnp.bfloat16)
    staged.store(gate_parts_ref, up_parts_ref)
    for k in range(1, line.count):
        for move in moves:
            move.share_came(k)
        n1.phases(k)
    for move in moves:
        move.finish()
    for copy in own:
        copy.wait()
    n1.finish()


def run_normed(x, gain, weight, beta, gate_up):
    rows_axis, seqs, cores = (lax.axis_size(axis) for axis in ("row", "seq", "tp"))
    piece, width = x.shape
    shard, units = gate_up.shape[1], gate_up.shape[2] // seqs
    b16 = jnp.bfloat16
    outs = (((seqs, shard, units), b16),) * 2
    far_outs = (
        ((seqs, cores, piece // cores, width), b16),
        ((rows_axis, seqs) + weight.shape[:2] + (weight.shape[2] // seqs,), b16),
        ((rows_axis, seqs, 16, shard), b16),
    )
    gate, up, n1, qkv, beta_full = line_call(
        normed_kernel, 4, "norm_gather", outs,
        [
            pltpu.VMEM((piece // cores, width), b16),
            pltpu.VMEM((seqs, 16, shard), b16),
            dma_sems(6, seqs, PARTS),
            dma_sems(2),
        ]
        + exchange_sems() * 2,
        (x, gain, beta, gate_up),
        far_args=(weight,),
        far_outs=far_outs,
    )
    return gate, up, n1.reshape(-1, width), qkv, beta_full


def finish_kernel(
    staged, small_ref, qkv_ref, o_ref, gate_ref, up_ref, down_ref, result_ref, input_grad_ref,
    attn_gain_ref, mlp_gain_ref, out_gain_ref, conv_ref, qkv_out, o_out, gate_up_out, down_out,
    beta_out, result_out, input_grad_out,
):
    f32 = jnp.float32
    cores, seqs, _, _ = small_ref.shape
    _, shard, width3 = qkv_ref.shape
    width, units = width3 // 3, gate_ref.shape[2]
    heads = width // DK
    unit = unit_square(shard)
    for i, ref in enumerate((gate_ref, up_ref)):
        staged.need(ref)
        gate_up_out[i] = jnp.concatenate([ref[seq].astype(f32) for seq in range(seqs)], axis=1)
    staged.store(gate_up_out)
    staged.need(down_ref, o_ref)
    for seq in range(seqs):
        down_out[seq * units : (seq + 1) * units] = mul(down_ref[seq], unit, (0, 0))
        o_out[seq * width : (seq + 1) * width] = mul(o_ref[seq], unit, (0, 0))
    staged.store(down_out, o_out)
    staged.need(qkv_ref)
    for seq in range(seqs):
        for c in range(3):
            qkv_out[c, :, seq * width : (seq + 1) * width] = qkv_ref[
                seq, :, c * width : (c + 1) * width
            ].astype(f32)
    staged.store(qkv_out)
    staged.need(result_ref, input_grad_ref)
    result_out[...] = result_ref[...]
    input_grad_out[...] = input_grad_ref[...]
    staged.store(result_out, input_grad_out)
    staged.need(small_ref)
    at = 2 + heads
    for ref, rows, lanes in (
        (attn_gain_ref, slice(0, 1), slice(None)),
        (mlp_gain_ref, slice(1, 2), slice(None)),
        (out_gain_ref, slice(at, at + 1), slice(2 * width3, 2 * width3 + DK)),
    ):
        total = small_ref[0, 0, rows, lanes]
        for i in range(1, cores * seqs):
            total = total + small_ref[i // seqs, i % seqs, rows, lanes]
        ref[...] = total
    for core in range(cores):
        for seq in range(seqs):
            for c in range(3):
                for tap in range(KW):
                    row, lane = at + tap // 2, (tap % 2) * width3 + c * width
                    to = (core * seqs + seq) * width
                    conv_ref[c, tap : tap + 1, to : to + width] = small_ref[
                        core, seq, row : row + 1, lane : lane + width
                    ]
    block = lax.axis_index("row") * seqs + lax.axis_index("seq")
    columns = pl.ds(pl.multiple_of(block * shard, shard), shard)
    beta = jnp.concatenate(
        [small_ref[lax.axis_index("tp"), seq, 2 : 2 + heads, columns] for seq in range(seqs)], axis=0
    )
    beta_out[...] = beta


def run_finish(small, qkv, o, gate, up, down, result, input_grad):
    f32 = jnp.float32
    cores, seqs, _, model_width = small.shape
    _, shard, width3 = qkv.shape
    units = gate.shape[2]
    shapes = (
        (1, model_width),
        (1, model_width),
        (1, DK),
        (3, KW, model_width),
        (3, shard, seqs * width3 // 3),
        (seqs * width3 // 3, shard),
        (2, shard, seqs * units),
        (seqs * units, shard),
        (seqs * width3 // (3 * DK), shard),
    )
    return line_call(
        finish_kernel, None, "finish",
        [(shape, f32) for shape in shapes] + [(result.shape, result.dtype)] * 2, [],
        (small, qkv, o, gate, up, down, result, input_grad),
    )


def local_heads(
    block_input,
    grad_out,
    doc_lengths,
    attn_gain,
    mlp_gain,
    out_gain,
    conv_weight,
    qkv_weight,
    beta_weight,
    o_weight,
    gate_up_weight,
    down_weight,
):
    tok_rows, model_width = block_input.shape[1:]
    pieces, cores = lax.axis_size("seq"), lax.axis_size("tp")
    piece, core = lax.axis_index("seq"), lax.axis_index("tp")
    row_len = pieces * tok_rows
    shard_rows = qkv_weight.shape[1]
    width = qkv_weight.shape[2] // pieces
    heads = width // DK
    units = gate_up_weight.shape[2] // pieces
    f32, b16 = jnp.float32, jnp.bfloat16

    x_piece, g_piece = block_input[0], grad_out[0]
    gate_parts, up_parts, normed_one, qkv_full, beta_full = run_normed(
        x_piece, attn_gain[None], qkv_weight, beta_weight, gate_up_weight
    )

    ends = jnp.cumsum(doc_lengths[0])
    places = jnp.arange(row_len, dtype=jnp.int32)
    docs = jnp.sum((places[:, None] >= ends[None, :]).astype(jnp.int32), axis=1)
    aux, doc_rows = row_aux(docs)
    gain_row = out_gain[None]
    taps = lax.dynamic_slice_in_dim(conv_weight, piece * width, width, axis=2)
    taps = taps.transpose(1, 0, 2).reshape(KW, 3 * width)

    saved, o_full, resid, normed_two, g_full, gate_full, up_full, down_full = run_forward(
        normed_one, qkv_full, beta_full, taps, aux, doc_rows, gain_row,
        x_piece, g_piece, mlp_gain[None],
        (o_weight, gate_parts, up_parts, down_weight),
    )
    proj, logit, mixed, normed_mix, inverse, states, written = saved
    grad_resid, grad_attn, mlp_gain_part, result, sums = run_mlp_grad(
        gate_full, up_full, down_full, resid, mlp_gain[None], normed_two, g_full
    )
    input_grad, small, qkv_sum, o_sum, down_sum, gate_sum, up_sum = run_backward(
        grad_attn,
        o_full,
        (proj, logit, mixed, inverse, states, written),
        taps,
        aux,
        doc_rows,
        gain_row,
        (
            normed_mix, normed_one, qkv_full, beta_full, attn_gain[None], mlp_gain_part,
            x_piece, grad_resid,
        ),
        sums.reshape(3, pieces, shard_rows, units),
    )
    (
        attn_gain_grad, mlp_gain_grad, out_gain_grad, conv_grad, qkv_grad, o_grad, gate_up_grad,
        down_grad, beta_grad, result, input_grad,
    ) = run_finish(small, qkv_sum, o_sum, gate_sum, up_sum, down_sum, result, input_grad)
    return (
        result[None],
        input_grad[None],
        attn_gain_grad[0],
        mlp_gain_grad[0],
        out_gain_grad[0],
        conv_grad,
        qkv_grad,
        beta_grad.T,
        o_grad,
        gate_up_grad,
        down_grad,
    )


def splits_heads(mesh, heads=16, units=5632):
    return (
        mesh.shape["tp"] == 2
        and heads % (mesh.shape["seq"] * 2) == 0
        and units % (mesh.shape["seq"] * 2) == 0
    )


def solution(mesh):
    in_specs = (
        P("row", "seq", None),
        P("row", "seq", None),
        P("row", None),
        P(),
        P(),
        P(),
        P(None, None, "tp"),
        P(None, ("row", "seq"), "tp"),
        P(("row", "seq"), "tp"),
        P("tp", ("row", "seq")),
        P(None, ("row", "seq"), "tp"),
        P("tp", ("row", "seq")),
    )
    out_specs = (
        P("row", "seq", None),
        P("row", "seq", None),
        P(),
        P(),
        P(),
        P(),
        P(None, ("row", "seq"), "tp"),
        P(("row", "seq"), "tp"),
        P("tp", ("row", "seq")),
        P(None, ("row", "seq"), "tp"),
        P("tp", ("row", "seq")),
    )
    local = local_heads if splits_heads(mesh) else local_pieces
    return jax.shard_map(local, mesh=mesh, in_specs=in_specs, out_specs=out_specs, check_vma=False)
```
